32 devices in a mesh: wide: 8 (over z, y), narrow: 4 (over x, core).
Axes of the slice: x: 2, y: 2, z: 4, core: 2. Of those that a mesh axis runs over, the one named last changes fastest.
Arguments:
- frames: bfloat16 [128, 8, 5, 32, 32, 3], P(('wide', 'narrow')), may hold values from -11 to 11
- tokens: bfloat16 [50176, 2048], P(('wide', 'narrow')), may hold values from -11 to 11
- stem_cotangent: bfloat16 [262144, 64], P(('wide', 'narrow')), may hold values from -6 to 6
- crop_counts: int32 [64], replicated, may hold values from 1 to 5, 128 in all
- labels: int32 [64], replicated, may hold values from 0 to 173
- stem_weight: bfloat16 [588, 64], P(None, 'wide'), may hold values from -0.25 to 0.25
- stem_gain: bfloat16 [64], P('wide'), may hold values from 0.099609375 to 1.8984375
- stem_shift: bfloat16 [64], P('wide'), may hold values from -2 to 2
- w_squeeze: bfloat16 [2048, 512], P('wide'), may hold values from -0.125 to 0.125
- next_kernel: bfloat16 [9, 512], P(None, 'wide'), may hold values from -2 to 2
- scale_kernel: bfloat16 [9, 512], P(None, 'wide'), may hold values from -2 to 2
- w_expand: bfloat16 [512, 2048], P(None, 'wide'), may hold values from -0.25 to 0.25
- w_reduce: bfloat16 [2048, 512], P('wide'), may hold values from -0.125 to 0.125
- gain_one: bfloat16 [512], P('wide'), may hold values from 0.099609375 to 1.8984375
- shift_one: bfloat16 [512], P('wide'), may hold values from -2 to 2
- w_spatial: bfloat16 [9, 512, 512], P(None, 'wide'), may hold values from -0.09375 to 0.09375
- gain_two: bfloat16 [512], P('wide'), may hold values from 0.099609375 to 1.8984375
- shift_two: bfloat16 [512], P('wide'), may hold values from -2 to 2
- w_restore: bfloat16 [512, 2048], P('wide'), may hold values from -0.25 to 0.25
- gain_three: bfloat16 [2048], P('wide'), may hold values from 0.099609375 to 1.8984375
- shift_three: bfloat16 [2048], P('wide'), may hold values from -2 to 2
- w_class: bfloat16 [2048, 174], P('wide'), may hold values from -0.5 to 0.5
- class_bias: bfloat16 [174], replicated, may hold values from -3 to 3
Outputs:
- activations: bfloat16 [50176, 2048], P(('wide', 'narrow'))
- stem_features: bfloat16 [262144, 64], P(('wide', 'narrow'))
- tokens_grad: bfloat16 [50176, 2048], P(('wide', 'narrow'))
- stem_weight_grad: float32 [588, 64], P(None, 'wide')
- stem_gain_grad: float32 [64], P('wide')
- stem_shift_grad: float32 [64], P('wide')
- squeeze_grad: float32 [2048, 512], P('wide')
- next_kernel_grad: float32 [9, 512], P(None, 'wide')
- scale_kernel_grad: float32 [9, 512], P(None, 'wide')
- expand_grad: float32 [512, 2048], P(None, 'wide')
- reduce_grad: float32 [2048, 512], P('wide')
- gain_one_grad: float32 [512], P('wide')
- shift_one_grad: float32 [512], P('wide')
- spatial_grad: float32 [9, 512, 512], P(None, 'wide')
- gain_two_grad: float32 [512], P('wide')
- shift_two_grad: float32 [512], P('wide')
- restore_grad: float32 [512, 2048], P('wide')
- gain_three_grad: float32 [2048], P('wide')
- shift_three_grad: float32 [2048], P('wide')
- class_grad: float32 [2048, 174], P('wide')
- class_bias_grad: float32 [174], replicated
- loss: float32 [], replicated
The draws below stay inside these ranges and needn't reach their ends.
Inputs may be any that keep to these rules, and one draw needn't show every extreme that they name: `crop_counts`: the counts sum to 128, and some video has 5 views.
All inputs are finite; a program needn't handle non-finite values.
Results may differ from the reference program's by a relative error of at most 0.015.
Values may be sent and summed in bfloat16 or wider, within the bound.
No kernel may reach another device: no remote copies, remote signals or barrier semaphores. Data moves between devices by JAX's collectives and lax.ppermute only.
A program may use at most 320 MiB of HBM per device.

```python
import math
import jax
import jax.numpy as jnp
import numpy as np
from jax import lax

C = 2048
B = 512
R = 512
CLASSES = 174
STEM = 64
SEG = 8
SIDE = 7
STEM_SIDE = 16
MOST_CROPS = 5
STEM_K = 588
VIEWS = 128
VIDEOS = 64
ROWS = 50176
STEM_ROWS = 262144


def view_ramp(total_views):
    return 0.6 + 1.2 * jnp.arange(total_views, dtype=jnp.float32) / total_views


def draw_tokens(key, part):
    key = jax.random.fold_in(key, 11)
    base = jnp.clip(jax.random.normal(key, (ROWS, C), jnp.float32), -6.0, 6.0)
    scale = jnp.repeat(view_ramp(VIEWS), SEG * SIDE * SIDE)
    return (base * scale[:, None]).astype(jnp.bfloat16)


def draw_frames(key, part):
    key = jax.random.fold_in(key, 23)
    shape = (VIEWS, SEG, 5, 2 * STEM_SIDE, 2 * STEM_SIDE, 3)
    base = jnp.clip(jax.random.normal(key, shape, jnp.float32), -6.0, 6.0)
    scale = view_ramp(VIEWS)
    return (base * scale[:, None, None, None, None, None]).astype(jnp.bfloat16)


def plant(values, key, low, high):
    longest = values.shape.index(max(values.shape))
    spots = []
    for shift in (0, 1):
        where = [jax.random.randint(jax.random.fold_in(key, axis), (), 0, length) for axis, length in enumerate(values.shape)]
        where[longest] = (where[longest] + shift) % values.shape[longest]
        spots.append(tuple(where))
    return values.at[spots[0]].set(low).at[spots[1]].set(high)


def shard_levels(key, shape, cuts, low, high):
    level, own = 1.0, jax.random.fold_in(key, 6)
    for dim, blocks in cuts:
        steps = jnp.exp(jax.random.uniform(jax.random.fold_in(own, dim), (blocks,), jnp.float32, low / len(cuts), high / len(cuts)))
        level = level * jnp.repeat(steps, shape[dim] // blocks).reshape([-1 if axis == dim else 1 for axis in range(len(shape))])
    return level


def profile(number_of, total, reach, slope):
    portions = [(1 << 20) // math.isqrt(rank ** slope) + 1 for rank in range(2, number_of + 1)]
    rest, given = total - reach - (number_of - 1), [1] * (number_of - 1)
    while rest > 0:
        movable = [i for i in range(number_of - 1) if given[i] < reach]
        pool, budget = sum([portions[i] for i in movable]), rest
        for i in movable:
            extra = min(reach - given[i], max(1, budget * portions[i] // pool), rest)
            given[i] = given[i] + extra
            rest = rest - extra
    return np.array([reach] + given)


def uneven_parts(own_key, count, total, bound, slope):
    if count == 2:
        one = jax.random.randint(own_key, (), max(1, total - bound), min(bound, total - 1) + 1)
        return jnp.stack([one, total - one])
    lengths = jnp.asarray(profile(count, total, bound, slope), jnp.int32)
    couples = (count - 1) // 2
    donor, receiver = lengths[1:1 + 2 * couples:2], lengths[2:2 + 2 * couples:2]
    margin = jnp.minimum(donor - 1, bound - receiver)
    passed = jax.random.randint(jax.random.fold_in(own_key, 1), (couples,), 0, 1 << 20) % (margin + 1)
    lengths = lengths.at[1:1 + 2 * couples:2].set(donor - passed).at[2:2 + 2 * couples:2].set(receiver + passed)
    return lengths[jax.random.permutation(jax.random.fold_in(own_key, 2), count)]


def centred(own_key, shape, scale, limit, shards=(), kind=jnp.bfloat16):
    drawn = scale * jax.random.normal(own_key, shape, jnp.float32)
    if shards:
        drawn = drawn * shard_levels(own_key, shape, shards, -0.22, 0.18)
    return jnp.clip(drawn, -limit, limit).astype(kind)


def setup_inputs(seed: int = 0) -> dict:
    keys = jax.random.split(jax.random.key(seed), 24)
    return {
        "frames": draw_frames(jax.random.fold_in(keys[23], 71), 0),
        "tokens": draw_tokens(jax.random.fold_in(keys[23], 71), 0),
        "stem_cotangent": centred(keys[2], (STEM_ROWS, STEM), 1.0, 6.0, ((0, 32),)),
        "crop_counts": uneven_parts(keys[3], VIDEOS, VIEWS, MOST_CROPS, 1).astype(jnp.int32),
        "labels": plant(jax.random.randint(keys[4], (VIDEOS,), 0, CLASSES), jax.random.fold_in(keys[4], 1), 0, CLASSES - 1).astype(jnp.int32),
        "stem_weight": centred(keys[5], (STEM_K, STEM), STEM_K ** -0.5, 0.25, ((1, 8),)),
        "stem_gain": jnp.clip(1.0 + 0.18 * jax.random.normal(keys[6], (STEM,), jnp.float32), 0.099609375, 1.8984375).astype(jnp.bfloat16),
        "stem_shift": centred(keys[7], (STEM,), 0.3, 2.0, ((0, 8),)),
        "w_squeeze": centred(keys[8], (C, R), C ** -0.5, 0.125, ((0, 8),)),
        "next_kernel": centred(keys[9], (9, R), 9 ** -0.5, 2.0, ((1, 8),)),
        "scale_kernel": centred(keys[10], (9, R), 9 ** -0.5, 2.0, ((1, 8),)),
        "w_expand": centred(keys[11], (R, C), R ** -0.5, 0.25, ((1, 8),)),
        "w_reduce": centred(keys[12], (C, B), C ** -0.5, 0.125, ((0, 8),)),
        "gain_one": jnp.clip(1.0 + 0.18 * jax.random.normal(keys[13], (B,), jnp.float32), 0.099609375, 1.8984375).astype(jnp.bfloat16),
        "shift_one": centred(keys[14], (B,), 0.3, 2.0, ((0, 8),)),
        "w_spatial": centred(keys[15], (9, B, B), (9 * B) ** -0.5, 0.09375, ((1, 8),)),
        "gain_two": jnp.clip(1.0 + 0.18 * jax.random.normal(keys[16], (B,), jnp.float32), 0.099609375, 1.8984375).astype(jnp.bfloat16),
        "shift_two": centred(keys[17], (B,), 0.3, 2.0, ((0, 8),)),
        "w_restore": centred(keys[18], (B, C), B ** -0.5, 0.25, ((0, 8),)),
        "gain_three": jnp.clip(1.0 + 0.18 * jax.random.normal(keys[19], (C,), jnp.float32), 0.099609375, 1.8984375).astype(jnp.bfloat16),
        "shift_three": centred(keys[20], (C,), 0.3, 2.0, ((0, 8),)),
        "w_class": centred(keys[21], (C, CLASSES), (C // 16) ** -0.5, 0.5, ((0, 8),)),
        "class_bias": centred(keys[22], (CLASSES,), 0.5, 3.0),
    }


epsilon = 1e-05
loss_scale = 1024.0

@jax.custom_vjp
def low(v):
    return lax.optimization_barrier(v.astype(jnp.bfloat16)).astype(jnp.float32)

@jax.custom_vjp
def low_back(v):
    return v

def low_keep(v):
    return (low(v), None)

def low_pass(kept, grad):
    return (grad,)

def back_keep(v):
    return (v, None)

def back_low(kept, grad):
    return (low(grad),)
low.defvjp(low_keep, low_pass)
low_back.defvjp(back_keep, back_low)

def matmul(first_operand, second_operand):
    return jnp.dot(first_operand, second_operand, precision=lax.Precision.HIGHEST, preferred_element_type=jnp.float32)

def depthwise(feature, kernel):
    extent = feature.shape[2]
    padded = jnp.pad(feature, ((0, 0), (0, 0), (1, 1), (1, 1), (0, 0)))
    accumulated = jnp.zeros_like(feature)
    for offset in range(9):
        accumulated = accumulated + padded[:, :, offset // 3:offset // 3 + extent, offset % 3:offset % 3 + extent, :] * kernel[offset]
    return accumulated

def temporal(squeezed, next_kernel, scale_kernel):
    upcoming = jnp.concatenate([squeezed[:, 1:], jnp.zeros_like(squeezed[:, :1])], axis=1)
    differ = depthwise(upcoming, next_kernel) - squeezed
    return differ + depthwise(differ, scale_kernel) + lax.optimization_barrier(jnp.mean(differ, axis=(2, 3), keepdims=True))

def columns(feature):
    extent = feature.shape[2]
    padded = jnp.pad(feature, ((0, 0), (0, 0), (1, 1), (1, 1), (0, 0)))
    pieces = [padded[:, :, offset // 3:offset // 3 + extent, offset % 3:offset % 3 + extent, :] for offset in range(9)]
    return jnp.concatenate(pieces, axis=-1).reshape(-1, 9 * feature.shape[-1])

def stem_patches(frames):
    differ = jnp.concatenate([frames[:, :, index + 1] - frames[:, :, index] for index in range(4)], axis=-1)
    extent = differ.shape[2] // 2
    padded = jnp.pad(differ, ((0, 0), (0, 0), (3, 3), (3, 3), (0, 0)))
    pieces = [padded[:, :, offset // 7:offset // 7 + 2 * extent:2, offset % 7:offset % 7 + 2 * extent:2, :] for offset in range(49)]
    return jnp.concatenate(pieces, axis=-1).reshape(-1, 49 * differ.shape[-1])

def batch_norm(values, gain, shift):
    mean = lax.optimization_barrier(jnp.mean(values, 0))
    variance = lax.optimization_barrier(jnp.mean(values * values, 0)) - mean * mean
    return (values - mean) * lax.rsqrt(variance + epsilon) * gain + shift

def forward(frames, tokens, params, member, counts, target):
    stem_weight, stem_gain, stem_shift, w_squeeze, next_kernel, scale_kernel, w_expand, w_reduce, gain_one, shift_one, w_spatial, gain_two, shift_two, w_restore, gain_three, shift_three, w_class, class_bias = params
    blocks = VIEWS // 8
    per_block = 8 * SEG * SIDE * SIDE

    def stem_block(frame_block):
        return low_back(matmul(low(stem_patches(frame_block)), stem_weight))
    stem_pre = lax.map(jax.checkpoint(stem_block), frames.reshape((blocks, 8) + frames.shape[1:])).reshape(-1, STEM)
    stem_out = jax.nn.silu(batch_norm(stem_pre, stem_gain, stem_shift))

    def first_block(token_block):
        squeezed = low_back(matmul(token_block, w_squeeze))
        mixed = temporal(squeezed.reshape(8, SEG, SIDE, SIDE, R), next_kernel, scale_kernel).reshape(per_block, R)
        gate = jax.nn.sigmoid(low_back(matmul(low(mixed), w_expand)))
        gated = token_block + token_block * gate
        return (low_back(matmul(low(gated), w_reduce)), gated)
    pre_one, gated = lax.map(jax.checkpoint(first_block), tokens.reshape(blocks, per_block, C))
    hidden_one = jax.nn.silu(batch_norm(pre_one.reshape(-1, B), gain_one, shift_one))

    def second_block(hidden_block):
        patches = columns(low(hidden_block).reshape(8, SEG, SIDE, SIDE, B))
        return low_back(matmul(patches, w_spatial.reshape(9 * B, B)))
    pre_two = lax.map(jax.checkpoint(second_block), hidden_one.reshape(blocks, per_block, B)).reshape(-1, B)
    hidden_two = jax.nn.silu(batch_norm(pre_two, gain_two, shift_two))

    def third_block(hidden_block):
        return low_back(matmul(low(hidden_block), w_restore))
    pre_three = lax.map(jax.checkpoint(third_block), hidden_two.reshape(blocks, per_block, B)).reshape(-1, C)
    output = jax.nn.silu(batch_norm(pre_three, gain_three, shift_three) + gated.reshape(-1, C))
    pooled = lax.optimization_barrier(jnp.mean(output.reshape(VIEWS, SEG * SIDE * SIDE, C), 1))
    view_logits = low_back(matmul(low(pooled), w_class)) + class_bias
    video_logits = matmul(member.T, view_logits) / counts[:, None]
    log_probs = jax.nn.log_softmax(video_logits, axis=-1)
    entropy = -lax.optimization_barrier(jnp.sum(target * log_probs, axis=-1))
    return (loss_scale * jnp.sum(entropy), stem_out, output, jnp.mean(entropy))

def reference(frames, tokens, stem_cotangent, crop_counts, labels, stem_weight, stem_gain, stem_shift, w_squeeze, next_kernel, scale_kernel, w_expand, w_reduce, gain_one, shift_one, w_spatial, gain_two, shift_two, w_restore, gain_three, shift_three, w_class, class_bias):
    params = (stem_weight, stem_gain, stem_shift, w_squeeze, next_kernel, scale_kernel, w_expand, w_reduce, gain_one, shift_one, w_spatial, gain_two, shift_two, w_restore, gain_three, shift_three, w_class, class_bias)
    floats = tuple((weight.astype(jnp.float32) for weight in params))
    ends = jnp.cumsum(crop_counts).astype(jnp.int32)
    starts = ends - crop_counts
    positions = jnp.arange(VIEWS, dtype=jnp.int32)
    member = ((positions[:, None] >= starts[None, :]) & (positions[:, None] < ends[None, :])).astype(jnp.float32)
    counts = crop_counts.astype(jnp.float32)
    target = (labels[:, None] == jnp.arange(CLASSES, dtype=jnp.int32)[None, :]).astype(jnp.float32)
    frame_values = frames.astype(jnp.float32)

    def objective(token_values, param_values):
        return forward(frame_values, token_values, param_values, member, counts, target)
    primal, backward = jax.vjp(objective, tokens.astype(jnp.float32), floats)
    total, stem_out, output, loss = primal
    token_grad, grads = backward((jnp.ones_like(total), stem_cotangent.astype(jnp.float32), jnp.zeros_like(output), jnp.zeros_like(loss)))
    return (output.astype(jnp.bfloat16), stem_out.astype(jnp.bfloat16), token_grad.astype(jnp.bfloat16), grads[0], grads[1], grads[2], grads[3], grads[4], grads[5], grads[6], grads[7], grads[8], grads[9], grads[10], grads[11], grads[12], grads[13], grads[14], grads[15], grads[16], grads[17], loss)
```

```python
import jax
import jax.numpy as jnp
from jax import lax
from jax.sharding import PartitionSpec as P

C = 2048
B = 512
R = 512
CLASSES = 174
SEG = 8
SIDE = 7
PER_VIEW = SEG * SIDE * SIDE

epsilon = 1e-05
loss_scale = 1024.0

AXES = ("wide", "narrow")
f32 = jnp.float32
bf16 = jnp.bfloat16


def product(first_operand, second_operand):
    return jnp.dot(first_operand, second_operand, preferred_element_type=f32)


def product_left(first_operand, second_operand):
    return lax.dot_general(
        first_operand, second_operand, (((0,), (0,)), ((), ())), preferred_element_type=f32
    )


def product_right(first_operand, second_operand):
    return lax.dot_general(
        first_operand, second_operand, (((1,), (1,)), ((), ())), preferred_element_type=f32
    )


def bit_count(size):
    return size.bit_length() - 1


def device_bits():
    return bit_count(lax.axis_size(AXES))


def exchange(values, mask):
    size = lax.axis_size(AXES)
    return lax.ppermute(values, AXES, [(index, index ^ mask) for index in range(size)])


def own_bit(bit):
    return (lax.axis_index(AXES) >> bit) & 1


def total(values):
    bits = device_bits()
    values = values + exchange(values, 1)
    for bit in range(1, bits, 2):
        masks = [1 << bit]
        if bit + 1 < bits:
            masks += [2 << bit, 3 << bit]
        parts = [exchange(values, mask) for mask in masks]
        for part in parts:
            values = values + part
    return values


def total_of(*arrays):
    flat = jnp.concatenate([array.reshape(-1) for array in arrays])
    flat = total(flat)
    found, at = [], 0
    for array in arrays:
        found.append(flat[at : at + array.size].reshape(array.shape))
        at += array.size
    return found


def gather_tree(block, order, lead=0):
    done = []
    for bit in order:
        other = exchange(block, 1 << bit)
        low = own_bit(bit) == 0
        place = lead + sum(1 for known in done if known > bit)
        block = jnp.stack(
            [jnp.where(low, block, other), jnp.where(low, other, block)], axis=place
        )
        done.append(bit)
    shape = block.shape
    return block.reshape(shape[:lead] + (1 << len(done),) + shape[lead + len(done) :])


def scatter_tree(values, order, lead=0):
    shape = values.shape
    values = values.reshape(shape[:lead] + (2,) * len(order) + shape[lead + 1 :])
    left = sorted(order, reverse=True)
    for bit in order:
        place = lead + left.index(bit)
        mine = own_bit(bit)
        keep = lax.dynamic_index_in_dim(values, mine, place, keepdims=False)
        send = lax.dynamic_index_in_dim(values, 1 - mine, place, keepdims=False)
        values = keep + exchange(send, 1 << bit)
        left.remove(bit)
    return values


def own_part(values, axis):
    width = values.shape[axis] // lax.axis_size("narrow")
    return lax.dynamic_slice_in_dim(values, lax.axis_index("narrow") * width, width, axis)


def own_slice(values, width):
    return lax.dynamic_slice_in_dim(values, lax.axis_index("wide") * width, width)


def depthwise(feature, kernel):
    extent = feature.shape[2]
    padded = jnp.pad(feature, ((0, 0), (0, 0), (1, 1), (1, 1), (0, 0)))
    accumulated = jnp.zeros_like(feature)
    for offset in range(9):
        accumulated = (
            accumulated
            + padded[:, :, offset // 3 : offset // 3 + extent, offset % 3 : offset % 3 + extent, :]
            * kernel[offset]
        )
    return accumulated


def temporal(squeezed, next_kernel, scale_kernel):
    upcoming = jnp.concatenate([squeezed[:, 1:], jnp.zeros_like(squeezed[:, :1])], axis=1)
    differ = depthwise(upcoming, next_kernel) - squeezed
    return differ + depthwise(differ, scale_kernel) + jnp.mean(differ, axis=(2, 3), keepdims=True)


def columns(feature):
    extent = feature.shape[2]
    padded = jnp.pad(feature, ((0, 0), (0, 0), (1, 1), (1, 1), (0, 0)))
    pieces = [
        padded[:, :, offset // 3 : offset // 3 + extent, offset % 3 : offset % 3 + extent, :]
        for offset in range(9)
    ]
    return jnp.concatenate(pieces, axis=-1).reshape(-1, 9 * feature.shape[-1])


def frame_differ(frames):
    differ = jnp.concatenate(
        [frames[:, :, index + 1] - frames[:, :, index] for index in range(4)], axis=-1
    )
    return differ.reshape((-1,) + differ.shape[2:])


def stem_conv(differ, kernel):
    return lax.conv_general_dilated(
        differ,
        kernel,
        (2, 2),
        ((3, 3), (3, 3)),
        dimension_numbers=("NHWC", "HWIO", "NHWC"),
        preferred_element_type=f32,
    )


def silu_slope(values):
    sigma = jax.nn.sigmoid(values)
    return sigma * (1.0 + values * (1.0 - sigma))


def moments(values):
    return jnp.sum(values, 0), jnp.sum(values * values, 0)


def normalize(values, sums, squares, gain, shift, count):
    mean = sums / count
    inverse = lax.rsqrt(squares / count - mean * mean + epsilon)
    unit = (values - mean) * inverse
    return unit * gain + shift, unit, inverse


def grad_moments(grad, unit):
    return jnp.sum(grad, 0), jnp.sum(grad * unit, 0)


def input_grad(grad, unit, inverse, gain, shift_grad, gain_grad, count):
    return gain * inverse * (grad - shift_grad / count - unit * gain_grad / count)


def shards(
    frames,
    tokens,
    stem_cotangent,
    crop_counts,
    labels,
    stem_weight,
    stem_gain,
    stem_shift,
    w_squeeze,
    next_kernel,
    scale_kernel,
    w_expand,
    w_reduce,
    gain_one,
    shift_one,
    w_spatial,
    gain_two,
    shift_two,
    w_restore,
    gain_three,
    shift_three,
    w_class,
    class_bias,
):
    view_count = frames.shape[0]
    row_count = tokens.shape[0]
    devices = lax.axis_size(AXES)
    wide = lax.axis_size("wide")
    narrow = lax.axis_size("narrow")
    count = float(row_count * devices)
    bits = device_bits()
    outward = list(reversed(range(bits)))
    wide_bits = [bit for bit in outward if bit >= bit_count(narrow)]
    narrow_bits = [bit for bit in outward if bit < bit_count(narrow)]

    small = [
        stem_weight, stem_gain, stem_shift, next_kernel, scale_kernel, gain_one, shift_one,
        gain_two, shift_two, gain_three, shift_three,
    ]
    pack = jnp.concatenate([value.reshape(-1) for value in small])
    pack = jnp.pad(pack, (0, -pack.size % 1024))
    packs = gather_tree(pack.reshape(-1, 128), wide_bits).reshape(wide, -1)
    full, at = [], 0
    for value in small:
        piece = packs[:, at : at + value.size].reshape((wide,) + value.shape)
        at += value.size
        full.append(
            piece.reshape(-1)
            if value.ndim == 1
            else piece.transpose(1, 0, 2).reshape(value.shape[0], -1)
        )
    full_stem = full[0]
    (
        full_stem_gain, full_stem_shift, full_next, full_scale, full_gain_one, full_shift_one,
        full_gain_two, full_shift_two, full_gain_three, full_shift_three,
    ) = (value.astype(f32) for value in full[1:])

    full_squeeze = gather_tree(own_part(w_squeeze, 0), outward).reshape(C, R)
    full_expand = gather_tree(own_part(w_expand, 0), outward)
    full_expand = full_expand.reshape(wide, R, -1).transpose(1, 0, 2).reshape(R, C)
    full_reduce = gather_tree(own_part(w_reduce, 0), outward).reshape(C, B)
    full_spatial = gather_tree(own_part(w_spatial, 1), outward, 1).reshape(9 * B, B)
    full_restore = gather_tree(own_part(w_restore, 0), outward).reshape(B, C)
    full_class = gather_tree(own_part(w_class, 0), outward).reshape(C, CLASSES)

    differ_low = frame_differ(frames.astype(f32)).astype(bf16)
    stem_width_all = full_stem.shape[1]
    stem_kernel = full_stem.reshape(7, 7, differ_low.shape[-1], stem_width_all)
    stem_pre = stem_conv(differ_low, stem_kernel).reshape(-1, stem_width_all)
    stem_count = float(stem_pre.shape[0] * devices)

    squeezed = product(tokens, full_squeeze)

    def mixing(squeezed_values, next_values, scale_values):
        return temporal(
            squeezed_values.reshape(view_count, SEG, SIDE, SIDE, R), next_values, scale_values
        ).reshape(row_count, R)

    mixed, mixing_back = jax.vjp(mixing, squeezed, full_next, full_scale)
    mixed_low = mixed.astype(bf16)
    gate = jax.nn.sigmoid(product(mixed_low, full_expand))
    token_values = tokens.astype(f32)
    gated = token_values + token_values * gate
    gated_low = gated.astype(bf16)
    pre_one = product(gated_low, full_reduce)

    one_sums, one_squares, stem_sums, stem_squares = total_of(
        *moments(pre_one), *moments(stem_pre)
    )
    norm_one, unit_one, inverse_one = normalize(
        pre_one, one_sums, one_squares, full_gain_one, full_shift_one, count
    )
    stem_norm, stem_unit, stem_inverse = normalize(
        stem_pre, stem_sums, stem_squares, full_stem_gain, full_stem_shift, stem_count
    )
    stem_out = jax.nn.silu(stem_norm)
    stem_norm_grad = stem_cotangent.astype(f32) * silu_slope(stem_norm)

    hidden_one = jax.nn.silu(norm_one).astype(bf16)
    spread_cols = columns(hidden_one.reshape(view_count, SEG, SIDE, SIDE, B))
    pre_two = product(spread_cols, full_spatial)
    two_sums, two_squares = total_of(*moments(pre_two))
    norm_two, unit_two, inverse_two = normalize(
        pre_two, two_sums, two_squares, full_gain_two, full_shift_two, count
    )
    hidden_two = jax.nn.silu(norm_two).astype(bf16)
    pre_three = product(hidden_two, full_restore)
    three_sums, three_squares, stem_shift_grad, stem_gain_grad = total_of(
        *moments(pre_three), *grad_moments(stem_norm_grad, stem_unit)
    )
    norm_three, unit_three, inverse_three = normalize(
        pre_three, three_sums, three_squares, full_gain_three, full_shift_three, count
    )
    summed = norm_three + gated
    output = jax.nn.silu(summed)
    pooled = jnp.mean(output.reshape(view_count, PER_VIEW, C), 1)
    pooled_low = pooled.astype(bf16)
    view_logits = product(pooled_low, full_class) + class_bias.astype(f32)

    ends = jnp.cumsum(crop_counts)
    starts = ends - crop_counts
    index = lax.axis_index(AXES)
    positions = (index - 1) * view_count + jnp.arange(3 * view_count, dtype=jnp.int32)
    video = jnp.sum((ends[None, :] <= positions[:, None]).astype(jnp.int32), 1)
    own_video = video[view_count : 2 * view_count]
    belongs = (
        own_video[:, None] == jnp.arange(crop_counts.shape[0], dtype=jnp.int32)[None, :]
    ).astype(jnp.int32)
    own_count = jnp.sum(belongs * crop_counts[None, :], 1).astype(f32)
    own_label = jnp.sum(belongs * labels[None, :], 1)
    own_start = jnp.sum(belongs * starts[None, :], 1)
    first = (own_start == positions[view_count : 2 * view_count]).astype(f32)
    same = (own_video[:, None] == video[None, :]).astype(f32) / own_count[:, None]
    target = (own_label[:, None] == jnp.arange(CLASSES, dtype=jnp.int32)[None, :]).astype(f32)

    before = lax.ppermute(view_logits, AXES, [(i, i + 1) for i in range(devices - 1)])
    after = lax.ppermute(view_logits, AXES, [(i + 1, i) for i in range(devices - 1)])
    near = jnp.concatenate([before, view_logits, after])
    video_logits = jnp.sum(same[:, :, None] * near[None, :, :], 1)
    log_probs = jax.nn.log_softmax(video_logits, axis=-1)
    entropy_part = jnp.sum(first * -jnp.sum(target * log_probs, axis=-1))
    video_grad = loss_scale * (jnp.exp(log_probs) - target)
    bias_part = jnp.sum(first[:, None] * video_grad, 0)
    view_grad_low = (video_grad / own_count[:, None]).astype(bf16)

    class_grad = product_left(pooled_low, view_grad_low)
    pooled_grad = product_right(view_grad_low, full_class)
    output_grad = jnp.broadcast_to(
        (pooled_grad / PER_VIEW)[:, None, :], (view_count, PER_VIEW, C)
    ).reshape(row_count, C)
    summed_grad = output_grad * silu_slope(summed)
    shift_three_grad, gain_three_grad, class_bias_grad, entropy_sum = total_of(
        *grad_moments(summed_grad, unit_three), bias_part, entropy_part
    )
    loss = entropy_sum / crop_counts.shape[0]
    low_three = input_grad(
        summed_grad, unit_three, inverse_three, full_gain_three, shift_three_grad,
        gain_three_grad, count,
    ).astype(bf16)
    restore_grad = product_left(hidden_two, low_three)
    hidden_two_grad = product_right(low_three, full_restore)
    norm_two_grad = hidden_two_grad * silu_slope(norm_two)
    shift_two_grad, gain_two_grad = total_of(*grad_moments(norm_two_grad, unit_two))
    low_two = input_grad(
        norm_two_grad, unit_two, inverse_two, full_gain_two, shift_two_grad, gain_two_grad, count
    ).astype(bf16)
    spatial_grad = product_left(spread_cols, low_two).reshape(9, -1, B)
    cols_grad = product_right(low_two, full_spatial)
    spread_back = jax.vjp(columns, jnp.zeros((view_count, SEG, SIDE, SIDE, B), f32))[1]
    hidden_one_grad = spread_back(cols_grad)[0].reshape(row_count, B)
    norm_one_grad = hidden_one_grad * silu_slope(norm_one)
    shift_one_grad, gain_one_grad = total_of(*grad_moments(norm_one_grad, unit_one))
    low_one = input_grad(
        norm_one_grad, unit_one, inverse_one, full_gain_one, shift_one_grad, gain_one_grad, count
    ).astype(bf16)
    reduce_grad = product_left(gated_low, low_one)
    gated_grad = product_right(low_one, full_reduce) + summed_grad
    gate_logit_grad = (gated_grad * token_values * gate * (1.0 - gate)).astype(bf16)
    expand_grad = product_left(mixed_low, gate_logit_grad)
    mixed_grad = product_right(gate_logit_grad, full_expand)
    squeezed_grad, next_grad, scale_grad = mixing_back(mixed_grad)
    low_squeezed = squeezed_grad.astype(bf16)
    squeeze_grad = product_left(tokens, low_squeezed)
    tokens_grad = (gated_grad * (1.0 + gate) + product_right(low_squeezed, full_squeeze)).astype(
        bf16
    )
    stem_pre_low = input_grad(
        stem_norm_grad, stem_unit, stem_inverse, full_stem_gain, stem_shift_grad, stem_gain_grad,
        stem_count,
    ).astype(bf16).astype(f32)
    differ_values = differ_low.astype(f32)

    def stem_map(kernel_values):
        return stem_conv(differ_values, kernel_values)

    stem_map_back = jax.vjp(stem_map, stem_kernel.astype(f32))[1]
    stem_grad = stem_map_back(
        stem_pre_low.reshape(
            differ_low.shape[0], differ_low.shape[1] // 2, differ_low.shape[2] // 2, stem_width_all
        )
    )[0].reshape(-1, stem_width_all)

    inward = list(range(bits))

    def reduced(grad, lead):
        shape = grad.shape
        rows = shape[lead] // devices
        parts = grad.astype(bf16).reshape(shape[:lead] + (devices, rows) + shape[lead + 1 :])
        part = scatter_tree(parts, inward, lead)
        whole = gather_tree(part, narrow_bits, lead)
        return whole.reshape(shape[:lead] + (narrow * rows,) + shape[lead + 1 :]).astype(f32)

    sum_restore = reduced(restore_grad, 0)
    sum_class = reduced(class_grad, 0)
    sum_spatial = reduced(spatial_grad, 1)
    sum_reduce = reduced(reduce_grad, 0)
    tiles = expand_grad.reshape(R, wide, -1).transpose(1, 0, 2)
    sum_expand = reduced(tiles.reshape(wide * R, -1), 0)
    sum_squeeze = reduced(squeeze_grad, 0)

    def cut(grad):
        return grad.reshape(grad.shape[0], wide, -1).transpose(1, 0, 2).reshape(wide, -1)

    cuts = [cut(stem_grad), cut(next_grad), cut(scale_grad)]
    joined = jnp.concatenate(cuts, 1)
    joined = jnp.pad(joined, ((0, 0), (0, -joined.shape[1] % 1024))).astype(bf16)
    parts = joined.reshape(wide, -1, 128)
    for bit in narrow_bits:
        parts = parts + exchange(parts, 1 << bit)
    mine = scatter_tree(parts, list(reversed(wide_bits))).reshape(-1).astype(f32)
    sizes = [piece.shape[1] for piece in cuts]
    sum_stem = mine[: sizes[0]].reshape(stem_weight.shape)
    sum_next = mine[sizes[0] : sizes[0] + sizes[1]].reshape(next_kernel.shape)
    sum_scale = mine[sizes[0] + sizes[1] : sum(sizes)].reshape(scale_kernel.shape)

    stem_width = stem_gain.shape[0]
    inner_width = gain_one.shape[0]
    outer_width = gain_three.shape[0]
    return (
        output.astype(bf16),
        stem_out.astype(bf16),
        tokens_grad,
        sum_stem,
        own_slice(stem_gain_grad, stem_width),
        own_slice(stem_shift_grad, stem_width),
        sum_squeeze,
        sum_next,
        sum_scale,
        sum_expand,
        sum_reduce,
        own_slice(gain_one_grad, inner_width),
        own_slice(shift_one_grad, inner_width),
        sum_spatial,
        own_slice(gain_two_grad, inner_width),
        own_slice(shift_two_grad, inner_width),
        sum_restore,
        own_slice(gain_three_grad, outer_width),
        own_slice(shift_three_grad, outer_width),
        sum_class,
        class_bias_grad,
        loss,
    )


def solution(mesh):
    in_specs = (
        P(("wide", "narrow"), None, None, None, None, None),
        P(("wide", "narrow"), None),
        P(("wide", "narrow"), None),
        P(),
        P(),
        P(None, "wide"),
        P("wide"),
        P("wide"),
        P("wide", None),
        P(None, "wide"),
        P(None, "wide"),
        P(None, "wide"),
        P("wide", None),
        P("wide"),
        P("wide"),
        P(None, "wide", None),
        P("wide"),
        P("wide"),
        P("wide", None),
        P("wide"),
        P("wide"),
        P("wide", None),
        P(),
    )
    out_specs = (
        P(("wide", "narrow"), None),
        P(("wide", "narrow"), None),
        P(("wide", "narrow"), None),
        P(None, "wide"),
        P("wide"),
        P("wide"),
        P("wide", None),
        P(None, "wide"),
        P(None, "wide"),
        P(None, "wide"),
        P("wide", None),
        P("wide"),
        P("wide"),
        P(None, "wide", None),
        P("wide"),
        P("wide"),
        P("wide", None),
        P("wide"),
        P("wide"),
        P("wide", None),
        P(),
        P(),
    )
    return jax.shard_map(shards, mesh=mesh, in_specs=in_specs, out_specs=out_specs, check_vma=False)
```

```python
import functools

import jax
import jax.numpy as jnp
from jax import lax
from jax.experimental import pallas as pl
from jax.experimental.pallas import tpu as pltpu
from jax.sharding import PartitionSpec as P

C = 2048
B = 512
R = 512
CLASSES = 174
SEG = 8
SIDE = 7
PER_VIEW = SEG * SIDE * SIDE

epsilon = 1e-05
loss_scale = 1024.0

AXES = ("wide", "narrow")
f32 = jnp.float32
bf16 = jnp.bfloat16


def product(first_operand, second_operand):
    return jnp.dot(first_operand, second_operand, preferred_element_type=f32)


def product_left(first_operand, second_operand):
    return lax.dot_general(
        first_operand, second_operand, (((0,), (0,)), ((), ())), preferred_element_type=f32
    )


def product_right(first_operand, second_operand):
    return lax.dot_general(
        first_operand, second_operand, (((1,), (1,)), ((), ())), preferred_element_type=f32
    )


def exchange(values, mask):
    size = lax.axis_size(AXES)
    return lax.ppermute(values, AXES, [(index, index ^ mask) for index in range(size)])


def own_bit(bit):
    return (lax.axis_index(AXES) >> bit) & 1


def total(values):
    bits = lax.axis_size(AXES).bit_length() - 1
    values = values + exchange(values, 1)
    for bit in range(1, bits, 2):
        masks = [1 << bit]
        if bit + 1 < bits:
            masks += [2 << bit, 3 << bit]
        parts = [exchange(values, mask) for mask in masks]
        for part in parts:
            values = values + part
    return values


def block_tree(block):
    four = jnp.stack([block] + [exchange(block, mask) for mask in (8, 16, 24)])
    eight = jnp.concatenate([four, exchange(four, 4)])
    over_x = exchange(eight, 2)
    return eight, over_x, exchange(eight, 1), exchange(over_x, 1)


def wide_tree(block):
    four = jnp.stack([block] + [exchange(block, mask) for mask in (8, 16, 24)])
    four = four.reshape((2, 2) + block.shape)
    eight = jnp.stack([four, exchange(four, 4)], axis=2)
    for axis, bit in ((0, 4), (1, 3), (2, 2)):
        eight = jnp.where(own_bit(bit) == 1, jnp.flip(eight, axis), eight)
    return eight.reshape((8,) + block.shape)


def split_stage(values, axis, bit):
    mine = own_bit(bit)
    keep = lax.dynamic_index_in_dim(values, mine, axis, keepdims=False)
    send = lax.dynamic_index_in_dim(values, 1 - mine, axis, keepdims=False)
    got = exchange(send.astype(bf16), 1 << bit)
    return keep + got.astype(f32), got


def depth_stage(values, axis):
    mine = (lax.axis_index(AXES) >> 3) & 3
    found = lax.dynamic_index_in_dim(values, mine, axis, keepdims=False)
    got = [
        exchange(
            lax.dynamic_index_in_dim(values, mine ^ mask, axis, keepdims=False).astype(bf16),
            mask << 3,
        )
        for mask in (1, 2, 3)
    ]
    for part in got:
        found = found + part.astype(f32)
    return found, got[-1]


def narrow_gather(part):
    part = part.astype(bf16)
    own, core, over_x, both = part, exchange(part, 1), exchange(part, 2), exchange(part, 3)
    odd, far = own_bit(0) == 1, own_bit(1) == 1
    near = [jnp.where(odd, core, own), jnp.where(odd, own, core)]
    away = [jnp.where(odd, both, over_x), jnp.where(odd, over_x, both)]
    return jnp.stack(
        [jnp.where(far, away[0], near[0]), jnp.where(far, away[1], near[1]),
         jnp.where(far, near[0], away[0]), jnp.where(far, near[1], away[1])]
    ).astype(f32)


def halves_tree(half, shape, lead, order):
    keep, send = half
    came = [exchange(send, 1)]
    values = (keep + came[0].astype(f32)).reshape(shape)
    axes = "zyx"
    for letter in order:
        place = lead + axes.index(letter)
        axes = axes.replace(letter, "")
        if letter == "z":
            values, got = depth_stage(values, place)
        else:
            values, got = split_stage(values, place, 1 if letter == "x" else 2)
        came.append(got)
    return narrow_gather(values), came


def small_scatter(parts):
    parts = parts.reshape((4, 2) + parts.shape[1:])
    parts, _ = split_stage(parts, 1, 2)
    parts, _ = depth_stage(parts, 0)
    for mask in (1, 2):
        parts = parts + exchange(parts, mask)
    return parts


SMALL_LANES = 640


def small_pack(stem_weight, next_kernel, scale_kernel, outer, inner):
    def row(vectors):
        found = jnp.concatenate(vectors)[None]
        return jnp.pad(found, ((0, 0), (0, SMALL_LANES - found.shape[1])))

    def aligned(kernel, width):
        return jnp.pad(kernel, ((0, 0), (0, width - kernel.shape[1])))

    stem = stem_weight.T
    taps = jnp.concatenate(
        [aligned(next_kernel, 128), aligned(scale_kernel, SMALL_LANES - 128)], axis=1
    )
    return jnp.concatenate(
        [aligned(stem, SMALL_LANES), taps, row(outer), row(inner)]
    ).astype(f32)


def gathered(w_squeeze, w_expand, w_reduce, w_spatial, w_restore, w_class):
    def whole(weight, axis):
        return lax.all_gather(weight, "wide", axis=axis, tiled=True)

    def as_blocks(blocks):
        ordered = blocks.reshape((4, 2, 2, 2) + blocks.shape[1:])
        return [
            ordered[:, :, far, core].swapaxes(0, 1).reshape((8,) + blocks.shape[1:])
            for core in range(2)
            for far in range(2)
        ]

    squeeze = whole(w_squeeze, 0).reshape(32, -1, R)
    expand = whole(w_expand, 1).reshape(R, 8, TILE).swapaxes(0, 1).reshape(32, -1, TILE)
    reduce = whole(w_reduce, 0).reshape(32, -1, B)
    spatial = whole(w_spatial, 1).reshape(9, 32, 16, B).swapaxes(0, 1).reshape(32, -1, B)
    restore = whole(w_restore, 0).reshape(8, 64, 4, B).swapaxes(1, 2).reshape(32, 64, B)
    classes = jnp.pad(whole(w_class, 0), ((0, 0), (0, TILE - CLASSES)))
    classes = classes.reshape(32, 2, CLASS_ROWS, TILE).swapaxes(1, 2).reshape(32, CLASS_ROWS, B)
    pack = jnp.concatenate([spatial, restore, classes], axis=1)
    return as_blocks(squeeze), as_blocks(expand), as_blocks(reduce), pack


def reduced(restore_half, spatial_half, pair_half, squeeze_half):
    def whole(half, grain):
        keep, send = (part.astype(bf16) for part in half)
        shape = keep.shape[:1] + (-1, grain) + keep.shape[2:]
        both = jnp.stack([keep.reshape(shape), send.reshape(shape)], axis=2)
        return both.reshape(keep.shape[:1] + (-1,) + keep.shape[2:])

    def scattered(grad, axis):
        part = lax.psum_scatter(grad, "wide", scatter_dimension=axis, tiled=True)
        return lax.psum(part, "narrow").astype(f32)

    def columns(tiles):
        return tiles.swapaxes(0, 1).reshape(tiles.shape[1], -1)

    pair = whole(pair_half, 128)
    return (
        scattered(columns(whole(restore_half, 16)), 0),
        scattered(whole(spatial_half, 16), 1),
        scattered(columns(pair[:8]), 1).T,
        scattered(columns(pair[8:]), 1),
        scattered(columns(whole(squeeze_half, 128)), 1).T,
    )


CELLS = SIDE * SIDE
HALF = 2 * PER_VIEW
PADDED = SIDE + 2
MIB = 1 << 20
LANES = 128
TILE = 256


def cell_place(cell):
    return (cell // SIDE + 1) * PADDED + cell % SIDE + 1


def tap_place(cell, tap):
    return cell_place(cell) + (tap // 3 - 1) * PADDED + tap % 3 - 1


def dot_nt(first_operand, second_operand):
    return lax.dot_general(
        first_operand, second_operand, (((1,), (1,)), ((), ())), preferred_element_type=f32
    )


def dot_tn(first_operand, second_operand):
    return lax.dot_general(
        first_operand, second_operand, (((0,), (0,)), ((), ())), preferred_element_type=f32
    )


def sigmoid(values):
    return 1.0 / (1.0 + jnp.exp(-values))


def constants(sums, affine, count):
    mean = sums[0:1] / count
    inverse = lax.rsqrt(sums[1:2] / count - mean * mean + epsilon)
    return mean, inverse, affine[0:1], affine[1:2]


def spread(row, rows=16):
    return jnp.broadcast_to(row, (rows, row.shape[1]))


def lanes(index, width):
    return pl.ds(pl.multiple_of(index * width, width), width)


def clear_border(ref):
    zero = jnp.zeros(ref.shape[1:], ref.dtype)
    for place in range(PADDED * PADDED):
        if place // PADDED in (0, PADDED - 1) or place % PADDED in (0, PADDED - 1):
            ref[place] = zero


def fold(values):
    return values[0:8] + values[8:16]


def half_spec(width):
    return pl.BlockSpec((HALF, width), lambda step: (step, 0))


def whole_spec(shape):
    return pl.BlockSpec(shape, lambda step: (0,) * len(shape), pipeline_mode=pl.Buffered(1))


def whole_out(shape):
    return pl.BlockSpec(shape, lambda step: (0,) * len(shape))


ANY = pl.BlockSpec(memory_space=pl.ANY)
SCALAR = pl.BlockSpec(memory_space=pltpu.SMEM)


def kernel_call(kernel, steps, in_specs, out_specs, out_shapes, scratch, flops,
                transcendentals=0, after=()):
    known = len(in_specs)

    def body(*refs):
        kernel(*refs[:known], *refs[known + len(after) :])

    call = pl.pallas_call(
        body,
        grid=(steps,),
        in_specs=list(in_specs) + [ANY] * len(after),
        out_specs=out_specs,
        out_shape=out_shapes,
        scratch_shapes=scratch,
        compiler_params=pltpu.CompilerParams(
            dimension_semantics=("arbitrary",), vmem_limit_bytes=60 * MIB
        ),
        cost_estimate=pl.CostEstimate(
            flops=2 * flops, bytes_accessed=16 * MIB, transcendentals=transcendentals
        ),
    )
    return lambda *operands: call(*operands, *after)


LOW_MASKS = (0, 2, 1, 3)


def block_copies(me, sources, target, semaphores):
    copies = []
    for low_mask, source in zip(LOW_MASKS, sources):
        for entry in range(8):
            mask = low_mask | ((entry // 4) << 2) | ((entry % 4) << 3)
            copies.append(
                pltpu.make_async_copy(
                    source.at[entry], target.at[me ^ mask], semaphores.at[len(copies)]
                )
            )
    return copies


def start(copies):
    for copy in copies:
        copy.start()


def wait(copies):
    for copy in copies:
        copy.wait()


def first_step():
    return pl.program_id(0) == 0


def add_moments(sums_ref, where, first, second):
    sums_ref[0:1, where] += jnp.sum(first, 0, keepdims=True)
    sums_ref[1:2, where] += jnp.sum(second, 0, keepdims=True)


def mixing_kernel(
    me_ref, block_a, block_b, block_c, block_d, tokens_ref, next_ref, scale_ref,
    upcoming_ref, differ_ref, mixed_ref, natural, ahead, padded, squeeze_ref, semaphores,
):
    @pl.when(first_step())
    def _():
        copies = block_copies(
            me_ref[0], (block_a, block_b, block_c, block_d), squeeze_ref, semaphores
        )
        start(copies)
        natural[:, HALF:] = jnp.zeros((4, natural.shape[1] - HALF, LANES), f32)
        clear_border(ahead)
        clear_border(padded)
        wait(copies)

    def squeeze_step(step, carry):
        squeezed = product(
            tokens_ref[...], squeeze_ref[:, :, lanes(step, TILE)].reshape(C, TILE)
        )
        natural[2 * step, 0:HALF] = squeezed[:, 0:LANES]
        natural[2 * step + 1, 0:HALF] = squeezed[:, LANES:TILE]
        return carry

    lax.fori_loop(0, 2, squeeze_step, 0)
    segment = lax.broadcasted_iota(jnp.int32, (16, LANES), 0) % SEG
    not_last = (segment != SEG - 1).astype(f32)

    def mixing_step(step, carry):
        where = lanes(step, LANES)
        next_rows = [spread(next_ref[tap : tap + 1, where]) for tap in range(9)]
        for cell in range(CELLS):
            upcoming = natural[step, pl.ds(cell + CELLS, 16, stride=CELLS)] * not_last
            ahead[cell_place(cell)] = upcoming
            upcoming_ref[cell * 16 : cell * 16 + 16, where] = upcoming
        mean = jnp.zeros((16, LANES), f32)
        for cell in range(CELLS):
            differ = -natural[step, pl.ds(cell, 16, stride=CELLS)]
            for tap in range(9):
                differ = differ + ahead[tap_place(cell, tap)] * next_rows[tap]
            padded[cell_place(cell)] = differ
            differ_ref[cell * 16 : cell * 16 + 16, where] = differ
            mean = mean + differ
        mean = mean * (1.0 / CELLS)
        scale_rows = [spread(scale_ref[tap : tap + 1, where]) for tap in range(9)]
        for cell in range(CELLS):
            mixed = padded[cell_place(cell)] + mean
            for tap in range(9):
                mixed = mixed + padded[tap_place(cell, tap)] * scale_rows[tap]
            natural[step, pl.ds(cell, 16, stride=CELLS)] = mixed
        mixed_ref[:, where] = natural[step, 0:HALF].astype(bf16)
        return carry

    lax.fori_loop(0, 4, mixing_step, 0)


def mixing_block(me, squeeze, tokens, next_kernel, scale_kernel, after=()):
    rows = tokens.shape[0]
    return kernel_call(
        mixing_kernel,
        rows // HALF,
        [SCALAR, ANY, ANY, ANY, ANY, half_spec(C), whole_spec((9, R)), whole_spec((9, R))],
        [half_spec(R), half_spec(R), half_spec(R)],
        [jax.ShapeDtypeStruct((rows, R), f32), jax.ShapeDtypeStruct((rows, R), f32),
         jax.ShapeDtypeStruct((rows, R), bf16)],
        [pltpu.VMEM((4, HALF + CELLS + 7, LANES), f32),
         pltpu.VMEM((PADDED * PADDED, 16, LANES), f32),
         pltpu.VMEM((PADDED * PADDED, 16, LANES), f32),
         pltpu.VMEM((32, C // 32, R), bf16), pltpu.SemaphoreType.DMA((32,))],
        2 * rows * C * R,
        after=after,
    )(me, *squeeze, tokens, next_kernel, scale_kernel)


def gate_kernel(
    me_ref, expand_a, expand_b, expand_c, expand_d, reduce_a, reduce_b, reduce_c, reduce_d,
    tokens_ref, mixed_ref, logit_ref, gated_ref, pre_ref, sums_ref,
    tile, expand_ref, reduce_ref, expand_semaphores, reduce_semaphores,
):
    me = me_ref[0]
    expand_copies = block_copies(
        me, (expand_a, expand_b, expand_c, expand_d), expand_ref, expand_semaphores
    )
    reduce_copies = block_copies(
        me, (reduce_a, reduce_b, reduce_c, reduce_d), reduce_ref, reduce_semaphores
    )

    @pl.when(first_step())
    def _():
        start(expand_copies)
        start(reduce_copies)
        sums_ref[...] = jnp.zeros_like(sums_ref)
        wait(expand_copies)

    def gate_step(step, carry):
        where = lanes(step, TILE)
        tile[...] = product(
            mixed_ref[...], expand_ref[pl.ds(4 * step, 4)].reshape(R, TILE)
        )
        for chunk in range(HALF // 16):
            rows = slice(chunk * 16, chunk * 16 + 16)
            logit = tile[rows]
            token = tokens_ref[rows, where].astype(f32)
            logit_ref[rows, where] = logit.astype(bf16)
            gated_ref[rows, where] = (token + token * sigmoid(logit)).astype(bf16)
        return carry

    lax.fori_loop(0, C // TILE, gate_step, 0)

    @pl.when(first_step())
    def _():
        wait(reduce_copies)

    def reduce_step(step, carry):
        where = lanes(step, TILE)
        tile[...] = product(gated_ref[...], reduce_ref[:, :, where].reshape(C, TILE))
        first = jnp.zeros((8, TILE), f32)
        second = jnp.zeros((8, TILE), f32)
        for chunk in range(HALF // 16):
            rows = slice(chunk * 16, chunk * 16 + 16)
            value = tile[rows]
            pre_ref[rows, where] = value
            first = first + fold(value)
            second = second + fold(value * value)
        add_moments(sums_ref, where, first, second)
        return carry

    lax.fori_loop(0, B // TILE, reduce_step, 0)


def gate_block(me, expand, reduce, tokens, mixed, after=()):
    rows = tokens.shape[0]
    return kernel_call(
        gate_kernel,
        rows // HALF,
        [SCALAR] + [ANY] * 8 + [half_spec(C), half_spec(R)],
        [half_spec(C), half_spec(C), half_spec(B), whole_out((2, B))],
        [jax.ShapeDtypeStruct((rows, C), bf16), jax.ShapeDtypeStruct((rows, C), bf16),
         jax.ShapeDtypeStruct((rows, B), f32), jax.ShapeDtypeStruct((2, B), f32)],
        [pltpu.VMEM((HALF, TILE), f32), pltpu.VMEM((32, R // 4, TILE), bf16),
         pltpu.VMEM((32, C // 32, B), bf16), pltpu.SemaphoreType.DMA((32,)),
         pltpu.SemaphoreType.DMA((32,))],
        4 * rows * C * R,
        2 * rows * C,
        after=after,
    )(me, *expand, *reduce, tokens, mixed)


SPATIAL_ROWS = 9 * 16
RESTORE_ROWS = 64
CLASS_ROWS = 32
PACK_ROWS = SPATIAL_ROWS + RESTORE_ROWS + CLASS_ROWS


def spatial_copy(pack_ref, target, semaphore):
    return pltpu.make_async_copy(pack_ref.at[:, 0:SPATIAL_ROWS], target, semaphore)


def restore_copy(pack_ref, target, semaphore):
    return pltpu.make_async_copy(
        pack_ref.at[:, SPATIAL_ROWS : SPATIAL_ROWS + RESTORE_ROWS], target, semaphore
    )


def second_kernel(count, pre_ref, in_sums_ref, affine_ref, pack_ref,
                  hidden_ref, out_ref, sums_ref, natural, padded, tile, spatial_ref, semaphore):
    copy = spatial_copy(pack_ref, spatial_ref, semaphore)

    @pl.when(first_step())
    def _():
        copy.start()
        sums_ref[...] = jnp.zeros_like(sums_ref)
        clear_border(padded)

    border = SIDE * 16
    hidden_ref[0, 0:border] = jnp.zeros((border, 3 * B), bf16)
    hidden_ref[0, border + HALF :] = jnp.zeros((border, 3 * B), bf16)

    def hidden_step(step, carry):
        where = lanes(step, LANES)
        mean, inverse, gain, shift = (
            spread(row) for row in constants(in_sums_ref[:, where], affine_ref[:, where], count)
        )
        for chunk in range(HALF // 16):
            rows = slice(chunk * 16, chunk * 16 + 16)
            norm = (pre_ref[rows, where] - mean) * inverse * gain + shift
            natural[rows] = norm * sigmoid(norm)
        for cell in range(CELLS):
            padded[cell_place(cell)] = natural[pl.ds(cell, 16, stride=CELLS)].astype(bf16)
        for side in range(3):
            at = lanes(side * 4 + step, LANES)
            for cell in range(CELLS):
                hidden_ref[0, border + cell * 16 : border + cell * 16 + 16, at] = padded[
                    tap_place(cell, 3 + side)
                ]
        return carry

    lax.fori_loop(0, 4, hidden_step, 0)

    @pl.when(first_step())
    def _():
        copy.wait()

    def product_step(step, carry):
        where = lanes(step, TILE)
        found = None
        for row in range(3):
            taps = [
                spatial_ref[:, tap * 16 : tap * 16 + 16, where].reshape(B, TILE)
                for tap in range(3 * row, 3 * row + 3)
            ]
            part = product(
                hidden_ref[0, row * border : row * border + HALF], jnp.concatenate(taps, axis=0)
            )
            found = part if found is None else found + part
        tile[...] = found
        first = jnp.zeros((8, TILE), f32)
        second = jnp.zeros((8, TILE), f32)
        for chunk in range(HALF // 16):
            rows = slice(chunk * 16, chunk * 16 + 16)
            value = tile[rows]
            out_ref[rows, where] = value
            first = first + fold(value)
            second = second + fold(value * value)
        add_moments(sums_ref, where, first, second)
        return carry

    lax.fori_loop(0, B // TILE, product_step, 0)


def second_block(pre_one, sums, affine, pack, count, after=()):
    rows = pre_one.shape[0]
    steps = rows // HALF
    deep = HALF + 2 * SIDE * 16
    return kernel_call(
        functools.partial(second_kernel, count),
        steps,
        [half_spec(B), whole_spec(sums.shape), whole_spec((2, B)), ANY],
        [pl.BlockSpec((1, deep, 3 * B), lambda step: (step, 0, 0)), half_spec(B),
         whole_out((2, B))],
        [jax.ShapeDtypeStruct((steps, deep, 3 * B), bf16), jax.ShapeDtypeStruct((rows, B), f32),
         jax.ShapeDtypeStruct((2, B), f32)],
        [pltpu.VMEM((HALF, LANES), f32), pltpu.VMEM((PADDED * PADDED, 16, LANES), bf16),
         pltpu.VMEM((HALF, TILE), f32), pltpu.VMEM((32, SPATIAL_ROWS, B), bf16),
         pltpu.SemaphoreType.DMA(())],
        18 * rows * B * B,
        2 * rows * B,
        after=after,
    )(pre_one, sums, affine, pack)


def third_kernel(count, pre_ref, in_sums_ref, affine_ref, pack_ref,
                 hidden_ref, out_ref, sums_ref, natural, tile, restore_ref, semaphore):
    copy = restore_copy(pack_ref, restore_ref, semaphore)

    @pl.when(first_step())
    def _():
        copy.start()
        sums_ref[...] = jnp.zeros_like(sums_ref)

    def hidden_step(step, carry):
        where = lanes(step, LANES)
        mean, inverse, gain, shift = (
            spread(row) for row in constants(in_sums_ref[:, where], affine_ref[:, where], count)
        )
        for cell in range(CELLS):
            rows = slice(cell * 16, cell * 16 + 16)
            norm = (pre_ref[rows, where] - mean) * inverse * gain + shift
            natural[pl.ds(cell, 16, stride=CELLS)] = norm * sigmoid(norm)
        hidden_ref[:, where] = natural[...].astype(bf16)
        return carry

    lax.fori_loop(0, 4, hidden_step, 0)

    @pl.when(first_step())
    def _():
        copy.wait()

    blocks = restore_ref.reshape(8, 4, RESTORE_ROWS, B)

    def product_step(step, carry):
        where = lanes(step, TILE)
        columns = blocks[:, step // 2, :, lanes(step % 2, TILE)].reshape(B, TILE)
        tile[...] = product(hidden_ref[...], columns)
        first = jnp.zeros((8, TILE), f32)
        second = jnp.zeros((8, TILE), f32)
        for chunk in range(HALF // 16):
            rows = slice(chunk * 16, chunk * 16 + 16)
            value = tile[rows]
            out_ref[rows, where] = value.astype(bf16)
            first = first + fold(value)
            second = second + fold(value * value)
        add_moments(sums_ref, where, first, second)
        return carry

    lax.fori_loop(0, C // TILE, product_step, 0)


def third_block(pre_two, sums, affine, pack, count, after=()):
    rows = pre_two.shape[0]
    return kernel_call(
        functools.partial(third_kernel, count),
        rows // HALF,
        [half_spec(B), whole_spec(sums.shape), whole_spec((2, B)), ANY],
        [half_spec(B), half_spec(C), whole_out((2, C))],
        [jax.ShapeDtypeStruct((rows, B), bf16), jax.ShapeDtypeStruct((rows, C), bf16),
         jax.ShapeDtypeStruct((2, C), f32)],
        [pltpu.VMEM((HALF, LANES), f32), pltpu.VMEM((HALF, TILE), f32),
         pltpu.VMEM((32, RESTORE_ROWS, B), bf16), pltpu.SemaphoreType.DMA(())],
        2 * rows * B * C,
        2 * rows * B,
        after=after,
    )(pre_two, sums, affine, pack)


def view_rows(chunk):
    return (chunk * 16) // PER_VIEW, (chunk * 16 + 8) // PER_VIEW


def fourth_kernel(count, pre_ref, gated_ref, in_sums_ref, affine_ref,
                  out_ref, slope_ref, views_ref):
    def step_body(step, carry):
        where = lanes(step, TILE)
        mean, inverse, gain, shift = (
            spread(row) for row in constants(in_sums_ref[:, where], affine_ref[:, where], count)
        )
        totals = [[jnp.zeros((8, TILE), f32) for _ in range(2)] for _ in range(3)]
        for chunk in range(HALF // 16):
            rows = slice(chunk * 16, chunk * 16 + 16)
            unit = (pre_ref[rows, where].astype(f32) - mean) * inverse
            summed = unit * gain + shift + gated_ref[rows, where].astype(f32)
            sigma = sigmoid(summed)
            output = summed * sigma
            slope = sigma + output * (1.0 - sigma)
            out_ref[rows, where] = output.astype(bf16)
            slope_ref[rows, where] = slope.astype(bf16)
            low, high = view_rows(chunk)
            for kind, value in enumerate((output, slope, slope * unit)):
                if low == high:
                    totals[kind][low] = totals[kind][low] + fold(value)
                else:
                    totals[kind][low] = totals[kind][low] + value[0:8]
                    totals[kind][high] = totals[kind][high] + value[8:16]
        for kind in range(3):
            for view in range(2):
                at = 2 * kind + view
                views_ref[0, at : at + 1, where] = jnp.sum(totals[kind][view], 0, keepdims=True)
        views_ref[0, 6:8, where] = jnp.zeros((2, TILE), f32)
        return carry

    lax.fori_loop(0, C // TILE, step_body, 0)


def fourth_block(pre_three, gated, sums, affine, count):
    rows = pre_three.shape[0]
    steps = rows // HALF
    return kernel_call(
        functools.partial(fourth_kernel, count),
        steps,
        [half_spec(C), half_spec(C), whole_spec(sums.shape), whole_spec((2, C))],
        [half_spec(C), half_spec(C), pl.BlockSpec((1, 8, C), lambda step: (step, 0, 0))],
        [jax.ShapeDtypeStruct((rows, C), bf16), jax.ShapeDtypeStruct((rows, C), bf16),
         jax.ShapeDtypeStruct((steps, 8, C), f32)],
        [],
        20 * rows * C,
        2 * rows * C,
    )(pre_three, gated, sums, affine)


def view_scale(pooled_ref, view, where):
    return spread(pooled_ref[0, view : view + 1, where], 8)


def view_grad_rows(slope, pooled, chunk):
    low, high = view_rows(chunk)
    return slope * jnp.concatenate([pooled[low], pooled[high]], axis=0)


def fifth_kernel(count, slope_ref, pre_three_ref, pooled_ref, sums_three_ref, affine_three_ref,
                 grads_three_ref, pack_ref, pre_two_ref, sums_two_ref, affine_two_ref,
                 low_ref, out_ref, sums_ref, natural, restore_ref, semaphore):
    copy = restore_copy(pack_ref, restore_ref, semaphore)

    @pl.when(first_step())
    def _():
        copy.start()
        sums_ref[...] = jnp.zeros_like(sums_ref)

    def low_step(step, carry):
        where = lanes(step, TILE)
        mean, inverse, gain, _ = constants(
            sums_three_ref[:, where], affine_three_ref[:, where], count
        )
        scale = spread(gain * inverse)
        offset = spread(grads_three_ref[0:1, where] / count)
        along = spread(grads_three_ref[1:2, where] / count * inverse)
        mean = spread(mean)
        pooled = [view_scale(pooled_ref, view, where) for view in range(2)]
        for chunk in range(HALF // 16):
            rows = slice(chunk * 16, chunk * 16 + 16)
            grad = view_grad_rows(slope_ref[rows, where].astype(f32), pooled, chunk)
            centred = pre_three_ref[rows, where].astype(f32) - mean
            low_ref[rows, where] = (scale * (grad - offset - centred * along)).astype(bf16)
        return carry

    lax.fori_loop(0, C // TILE, low_step, 0)

    @pl.when(first_step())
    def _():
        copy.wait()

    blocks = restore_ref.reshape(8, 4, RESTORE_ROWS, B)

    def product_step(step, carry):
        grad = None
        for quarter in range(4):
            rows = blocks[pl.ds(4 * step, 4), quarter].reshape(TILE, B)
            part = dot_nt(low_ref[:, quarter * B : (quarter + 1) * B], rows)
            grad = part if grad is None else grad + part
        natural[2 * step] = grad[:, 0:LANES]
        natural[2 * step + 1] = grad[:, LANES:TILE]
        return carry

    lax.fori_loop(0, B // TILE, product_step, 0)

    def slope_step(step, carry):
        where = lanes(step, LANES)
        mean, inverse, gain, shift = (
            spread(row) for row in constants(sums_two_ref[:, where], affine_two_ref[:, where], count)
        )
        first = jnp.zeros((16, LANES), f32)
        second = jnp.zeros((16, LANES), f32)
        for cell in range(CELLS):
            rows = slice(cell * 16, cell * 16 + 16)
            unit = (pre_two_ref[rows, where] - mean) * inverse
            norm = unit * gain + shift
            sigma = sigmoid(norm)
            grad = natural[step, pl.ds(cell, 16, stride=CELLS)]
            grad = grad * (sigma * (1.0 + norm * (1.0 - sigma)))
            out_ref[rows, where] = grad
            first = first + grad
            second = second + grad * unit
        add_moments(sums_ref, where, first, second)
        return carry

    lax.fori_loop(0, 4, slope_step, 0)


def fifth_block(slope, pre_three, pooled, sums_three, affine_three, grads_three, pack,
                pre_two, sums_two, affine_two, count, after=()):
    rows = slope.shape[0]
    return kernel_call(
        functools.partial(fifth_kernel, count),
        rows // HALF,
        [half_spec(C), half_spec(C), pl.BlockSpec((1, 2, C), lambda step: (step, 0, 0)),
         whole_spec(sums_three.shape), whole_spec((2, C)), whole_spec(grads_three.shape), ANY,
         half_spec(B), whole_spec(sums_two.shape), whole_spec((2, B))],
        [half_spec(C), half_spec(B), whole_out((2, B))],
        [jax.ShapeDtypeStruct((rows, C), bf16), jax.ShapeDtypeStruct((rows, B), f32),
         jax.ShapeDtypeStruct((2, B), f32)],
        [pltpu.VMEM((4, HALF, LANES), f32), pltpu.VMEM((32, RESTORE_ROWS, B), bf16),
         pltpu.SemaphoreType.DMA(())],
        2 * rows * B * C,
        2 * rows * B,
        after=after,
    )(slope, pre_three, pooled, sums_three, affine_three, grads_three, pack,
      pre_two, sums_two, affine_two)


def sixth_kernel(count, grad_ref, pre_two_ref, sums_two_ref, affine_two_ref, grads_two_ref,
                 pack_ref, pre_one_ref, sums_one_ref, affine_one_ref,
                 low_ref, out_ref, sums_ref, padded, shifted, tile, natural, spatial_ref,
                 semaphore):
    border = SIDE * 16
    copy = spatial_copy(pack_ref, spatial_ref, semaphore)

    @pl.when(first_step())
    def _():
        copy.start()
        sums_ref[...] = jnp.zeros_like(sums_ref)
        clear_border(padded)
        shifted[0:border] = jnp.zeros((border, 3 * B), bf16)
        shifted[border + HALF :] = jnp.zeros((border, 3 * B), bf16)

    def low_step(step, carry):
        where = lanes(step, LANES)
        mean, inverse, gain, _ = constants(sums_two_ref[:, where], affine_two_ref[:, where], count)
        scale = spread(gain * inverse)
        offset = spread(grads_two_ref[0:1, where] / count)
        along = spread(grads_two_ref[1:2, where] / count * inverse)
        mean = spread(mean)
        for cell in range(CELLS):
            rows = slice(cell * 16, cell * 16 + 16)
            centred = pre_two_ref[rows, where] - mean
            low = (scale * (grad_ref[rows, where] - offset - centred * along)).astype(bf16)
            low_ref[rows, where] = low
            padded[cell_place(cell)] = low
        for side in range(3):
            at = lanes(side * 4 + step, LANES)
            for cell in range(CELLS):
                shifted[border + cell * 16 : border + cell * 16 + 16, at] = padded[
                    tap_place(cell, 3 + side)
                ]
        return carry

    lax.fori_loop(0, 4, low_step, 0)

    @pl.when(first_step())
    def _():
        copy.wait()

    def product_step(step, carry):
        grad = None
        for tap in range(9):
            top = (tap // 3) * border
            at = (tap % 3) * B
            back = (8 - tap) * 16
            rows = spatial_ref[pl.ds(16 * step, 16), back : back + 16].reshape(TILE, B)
            part = dot_nt(shifted[top : top + HALF, at : at + B], rows)
            grad = part if grad is None else grad + part
        tile[...] = grad
        for half in range(2):
            for cell in range(CELLS):
                natural[2 * step + half, pl.ds(cell, 16, stride=CELLS)] = tile[
                    cell * 16 : cell * 16 + 16, half * LANES : (half + 1) * LANES
                ]
        return carry

    lax.fori_loop(0, B // TILE, product_step, 0)

    def slope_step(step, carry):
        where = lanes(step, LANES)
        mean, inverse, gain, shift = (
            spread(row) for row in constants(sums_one_ref[:, where], affine_one_ref[:, where], count)
        )
        first = jnp.zeros((16, LANES), f32)
        second = jnp.zeros((16, LANES), f32)
        for chunk in range(HALF // 16):
            rows = slice(chunk * 16, chunk * 16 + 16)
            unit = (pre_one_ref[rows, where] - mean) * inverse
            norm = unit * gain + shift
            sigma = sigmoid(norm)
            grad = natural[step, rows] * (sigma * (1.0 + norm * (1.0 - sigma)))
            out_ref[rows, where] = grad
            first = first + grad
            second = second + grad * unit
        add_moments(sums_ref, where, first, second)
        return carry

    lax.fori_loop(0, 4, slope_step, 0)


def sixth_block(grad, pre_two, sums_two, affine_two, grads_two, pack, pre_one, sums_one,
                affine_one, count, after=()):
    rows = grad.shape[0]
    deep = HALF + 2 * SIDE * 16
    return kernel_call(
        functools.partial(sixth_kernel, count),
        rows // HALF,
        [half_spec(B), half_spec(B), whole_spec(sums_two.shape), whole_spec((2, B)),
         whole_spec(grads_two.shape), ANY, half_spec(B), whole_spec(sums_one.shape),
         whole_spec((2, B))],
        [half_spec(B), half_spec(B), whole_out((2, B))],
        [jax.ShapeDtypeStruct((rows, B), bf16), jax.ShapeDtypeStruct((rows, B), f32),
         jax.ShapeDtypeStruct((2, B), f32)],
        [pltpu.VMEM((PADDED * PADDED, 16, LANES), bf16), pltpu.VMEM((deep, 3 * B), bf16),
         pltpu.VMEM((HALF, TILE), f32), pltpu.VMEM((4, HALF, LANES), f32),
         pltpu.VMEM((32, SPATIAL_ROWS, B), bf16), pltpu.SemaphoreType.DMA(())],
        18 * rows * B * B,
        2 * rows * B,
        after=after,
    )(grad, pre_two, sums_two, affine_two, grads_two, pack, pre_one, sums_one,
      affine_one)


def low_kernel(count, grad_ref, pre_ref, sums_ref, affine_ref, grads_ref, low_ref):
    def low_step(step, carry):
        where = lanes(step, LANES)
        mean, inverse, gain, _ = constants(sums_ref[:, where], affine_ref[:, where], count)
        scale = spread(gain * inverse)
        offset = spread(grads_ref[0:1, where] / count)
        along = spread(grads_ref[1:2, where] / count * inverse)
        mean = spread(mean)
        for chunk in range(HALF // 16):
            rows = slice(chunk * 16, chunk * 16 + 16)
            centred = pre_ref[rows, where] - mean
            low_ref[rows, where] = (
                scale * (grad_ref[rows, where] - offset - centred * along)
            ).astype(bf16)
        return carry

    lax.fori_loop(0, 4, low_step, 0)


def gate_back_kernel(count, me_ref, block_a, block_b, block_c, block_d,
                     grad_ref, pre_one_ref, sums_one_ref, affine_one_ref, grads_one_ref,
                     slope_ref, pooled_ref, tokens_ref, logit_ref,
                     low_ref, logit_grad_ref, part_ref, tile, reduce_ref, semaphores):
    copies = block_copies(me_ref[0], (block_a, block_b, block_c, block_d), reduce_ref, semaphores)

    @pl.when(first_step())
    def _():
        start(copies)

    low_kernel(count, grad_ref, pre_one_ref, sums_one_ref, affine_one_ref, grads_one_ref, low_ref)

    @pl.when(first_step())
    def _():
        wait(copies)

    def gate_step(step, carry):
        where = lanes(step, TILE)
        tile[...] = dot_nt(low_ref[...], reduce_ref[pl.ds(4 * step, 4)].reshape(TILE, B))
        pooled = [view_scale(pooled_ref, view, where) for view in range(2)]
        for chunk in range(HALF // 16):
            rows = slice(chunk * 16, chunk * 16 + 16)
            grad = tile[rows] + view_grad_rows(slope_ref[rows, where].astype(f32), pooled, chunk)
            gate = sigmoid(logit_ref[rows, where].astype(f32))
            token = tokens_ref[rows, where].astype(f32)
            part = grad * gate
            part_ref[rows, where] = (grad + part).astype(bf16)
            logit_grad_ref[rows, where] = (part * (1.0 - gate) * token).astype(bf16)
        return carry

    lax.fori_loop(0, C // TILE, gate_step, 0)


def gate_back_block(me, reduce, grad, pre_one, sums_one, affine_one, grads_one, slope, pooled,
                    tokens, logit, count, after=()):
    rows = grad.shape[0]
    return kernel_call(
        functools.partial(gate_back_kernel, count),
        rows // HALF,
        [SCALAR, ANY, ANY, ANY, ANY, half_spec(B), half_spec(B), whole_spec(sums_one.shape),
         whole_spec((2, B)), whole_spec(grads_one.shape), half_spec(C),
         pl.BlockSpec((1, 2, C), lambda step: (step, 0, 0)), half_spec(C), half_spec(C)],
        [half_spec(B), half_spec(C), half_spec(C)],
        [jax.ShapeDtypeStruct((rows, B), bf16), jax.ShapeDtypeStruct((rows, C), bf16),
         jax.ShapeDtypeStruct((rows, C), bf16)],
        [pltpu.VMEM((HALF, TILE), f32), pltpu.VMEM((32, C // 32, B), bf16),
         pltpu.SemaphoreType.DMA((32,))],
        2 * rows * C * R,
        2 * rows * C,
        after=after,
    )(me, *reduce, grad, pre_one, sums_one, affine_one, grads_one, slope, pooled, tokens, logit)


def mixing_back_kernel(me_ref, block_a, block_b, block_c, block_d, logit_grad_ref,
                       upcoming_ref, differ_ref, next_ref, scale_ref, squeezed_ref, kernels_ref,
                       natural, later, ahead, padded, expand_ref, semaphores):
    @pl.when(first_step())
    def _():
        copies = block_copies(
            me_ref[0], (block_a, block_b, block_c, block_d), expand_ref, semaphores
        )
        start(copies)
        kernels_ref[...] = jnp.zeros_like(kernels_ref)
        clear_border(ahead)
        clear_border(padded)
        later[0:CELLS] = jnp.zeros((CELLS, LANES), f32)
        wait(copies)

    quarters = expand_ref.reshape(8, 4, R // 4, TILE)

    def mixed_step(step, carry):
        grad = None
        for block in range(C // TILE):
            at = slice(block * TILE, (block + 1) * TILE)
            rows = quarters[block, pl.ds(2 * step, 2)].reshape(TILE, TILE)
            part = dot_nt(logit_grad_ref[:, at], rows)
            grad = part if grad is None else grad + part
        natural[2 * step] = grad[:, 0:LANES]
        natural[2 * step + 1] = grad[:, LANES:TILE]
        return carry

    lax.fori_loop(0, R // TILE, mixed_step, 0)
    segment = lax.broadcasted_iota(jnp.int32, (16, LANES), 0) % SEG
    not_last = (segment != SEG - 1).astype(f32)

    def mixing_step(step, carry):
        where = lanes(step, LANES)
        scale_rows = [spread(scale_ref[tap : tap + 1, where]) for tap in range(9)]
        mean = jnp.zeros((16, LANES), f32)
        for cell in range(CELLS):
            grad = natural[step, pl.ds(cell, 16, stride=CELLS)]
            padded[cell_place(cell)] = grad
            mean = mean + grad
            ahead[cell_place(cell)] = differ_ref[cell * 16 : cell * 16 + 16, where]
        mean = mean * (1.0 / CELLS)
        sums = [jnp.zeros((16, LANES), f32) for _ in range(9)]
        for cell in range(CELLS):
            grad = padded[cell_place(cell)]
            for tap in range(9):
                sums[tap] = sums[tap] + ahead[tap_place(cell, tap)] * grad
        for tap in range(9):
            kernels_ref[9 + tap : 10 + tap, where] += jnp.sum(sums[tap], 0, keepdims=True)
        for cell in range(CELLS):
            grad = padded[cell_place(cell)] + mean
            for tap in range(9):
                grad = grad + padded[tap_place(cell, tap)] * scale_rows[8 - tap]
            ahead[cell_place(cell)] = grad
        next_rows = [spread(next_ref[tap : tap + 1, where]) for tap in range(9)]
        for cell in range(CELLS):
            padded[cell_place(cell)] = upcoming_ref[cell * 16 : cell * 16 + 16, where]
        sums = [jnp.zeros((16, LANES), f32) for _ in range(9)]
        for cell in range(CELLS):
            grad = ahead[cell_place(cell)]
            for tap in range(9):
                sums[tap] = sums[tap] + padded[tap_place(cell, tap)] * grad
        for tap in range(9):
            kernels_ref[tap : tap + 1, where] += jnp.sum(sums[tap], 0, keepdims=True)
        for cell in range(CELLS):
            back = ahead[tap_place(cell, 0)] * next_rows[8]
            for tap in range(1, 9):
                back = back + ahead[tap_place(cell, tap)] * next_rows[8 - tap]
            later[pl.ds(cell + CELLS, 16, stride=CELLS)] = back * not_last
            natural[step, pl.ds(cell, 16, stride=CELLS)] = -ahead[cell_place(cell)]
        for chunk in range(HALF // 16):
            rows = slice(chunk * 16, chunk * 16 + 16)
            squeezed_ref[rows, where] = (natural[step, rows] + later[rows]).astype(bf16)
        return carry

    lax.fori_loop(0, 4, mixing_step, 0)


def mixing_back_block(me, expand, logit_grad, upcoming, differ, next_kernel, scale_kernel,
                      after=()):
    rows = logit_grad.shape[0]
    return kernel_call(
        mixing_back_kernel,
        rows // HALF,
        [SCALAR, ANY, ANY, ANY, ANY, half_spec(C), half_spec(R), half_spec(R),
         whole_spec((9, R)), whole_spec((9, R))],
        [half_spec(R), whole_out((18, R))],
        [jax.ShapeDtypeStruct((rows, R), bf16), jax.ShapeDtypeStruct((18, R), f32)],
        [pltpu.VMEM((4, HALF, LANES), f32), pltpu.VMEM((HALF + CELLS + 7, LANES), f32),
         pltpu.VMEM((PADDED * PADDED, 16, LANES), f32),
         pltpu.VMEM((PADDED * PADDED, 16, LANES), f32), pltpu.VMEM((32, R // 4, TILE), bf16),
         pltpu.SemaphoreType.DMA((32,))],
        2 * rows * C * R,
        after=after,
    )(me, *expand, logit_grad, upcoming, differ, next_kernel, scale_kernel)


def tokens_kernel(me_ref, block_a, block_b, block_c, block_d, part_ref, squeezed_ref, out_ref,
                  tile, squeeze_ref, semaphores):
    @pl.when(first_step())
    def _():
        copies = block_copies(
            me_ref[0], (block_a, block_b, block_c, block_d), squeeze_ref, semaphores
        )
        start(copies)
        wait(copies)

    def step_body(step, carry):
        where = lanes(step, TILE)
        tile[...] = dot_nt(squeezed_ref[...], squeeze_ref[pl.ds(4 * step, 4)].reshape(TILE, R))
        for chunk in range(HALF // 16):
            rows = slice(chunk * 16, chunk * 16 + 16)
            out_ref[rows, where] = (tile[rows] + part_ref[rows, where].astype(f32)).astype(bf16)
        return carry

    lax.fori_loop(0, C // TILE, step_body, 0)


def tokens_block(me, squeeze, part, squeezed_grad, after=()):
    rows = part.shape[0]
    return kernel_call(
        tokens_kernel,
        rows // HALF,
        [SCALAR, ANY, ANY, ANY, ANY, half_spec(C), half_spec(R)],
        half_spec(C),
        jax.ShapeDtypeStruct((rows, C), bf16),
        [pltpu.VMEM((HALF, TILE), f32), pltpu.VMEM((32, C // 32, R), bf16),
         pltpu.SemaphoreType.DMA((32,))],
        2 * rows * C * R,
        after=after,
    )(me, *squeeze, part, squeezed_grad)


def store_halves(me, found, grain, keep_ref, send_ref, tile):
    core = me & 1
    tile[...] = found
    for group in range(tile.shape[0] // (2 * grain)):
        at = slice(group * grain, (group + 1) * grain)
        mine = pl.multiple_of((2 * group + core) * grain, grain)
        other = pl.multiple_of((2 * group + 1 - core) * grain, grain)
        keep_ref[0, at] = tile[pl.ds(mine, grain)]
        send_ref[0, at] = tile[pl.ds(other, grain)].astype(bf16)


def outer_kernel(grain, me_ref, narrow_ref, wide_ref, keep_ref, send_ref, tile, turned):
    @pl.when(first_step())
    def _():
        turned[...] = narrow_ref[...].T

    found = product(turned[...], wide_ref[...])
    store_halves(me_ref[0], found, grain, keep_ref, send_ref, tile)


def outer_block(me, narrow_values, wide_values, grain, after=()):
    rows, inner = narrow_values.shape
    blocks = wide_values.shape[1] // TILE
    half = pl.BlockSpec((1, inner // 2, TILE), lambda step: (step, 0, 0))
    return kernel_call(
        functools.partial(outer_kernel, grain),
        blocks,
        [SCALAR, whole_spec((rows, inner)), pl.BlockSpec((rows, TILE), lambda step: (0, step))],
        [half, half],
        [jax.ShapeDtypeStruct((blocks, inner // 2, TILE), f32),
         jax.ShapeDtypeStruct((blocks, inner // 2, TILE), bf16)],
        [pltpu.VMEM((inner, TILE), f32), pltpu.VMEM((inner, rows), bf16)],
        2 * rows * inner * wide_values.shape[1],
        after=after,
    )(me, narrow_values, wide_values)


def outer_pair_kernel(grain, me_ref, narrow_a, wide_a, narrow_b, wide_b, keep_ref, send_ref, tile,
                      turned):
    half = pl.num_programs(0) // 2

    @pl.when(first_step())
    def _():
        turned[...] = narrow_a[...].T

    @pl.when(pl.program_id(0) == half)
    def _():
        turned[...] = narrow_b[...].T

    @pl.when(pl.program_id(0) < half)
    def _():
        found = product(turned[...], wide_a[...])
        store_halves(me_ref[0], found, grain, keep_ref, send_ref, tile)

    @pl.when(pl.program_id(0) >= half)
    def _():
        found = product(turned[...], wide_b[...])
        store_halves(me_ref[0], found, grain, keep_ref, send_ref, tile)


def outer_pair_block(me, narrow_a, wide_a, narrow_b, wide_b, after=()):
    rows, inner = narrow_a.shape
    blocks = wide_a.shape[1] // TILE
    half = pl.BlockSpec((1, inner // 2, TILE), lambda step: (step, 0, 0))
    return kernel_call(
        functools.partial(outer_pair_kernel, inner // 4),
        2 * blocks,
        [SCALAR, whole_spec((rows, inner)),
         pl.BlockSpec((rows, TILE), lambda step: (0, jnp.minimum(step, blocks - 1))),
         whole_spec((rows, inner)),
         pl.BlockSpec((rows, TILE), lambda step: (0, jnp.maximum(step - blocks, 0)))],
        [half, half],
        [jax.ShapeDtypeStruct((2 * blocks, inner // 2, TILE), f32),
         jax.ShapeDtypeStruct((2 * blocks, inner // 2, TILE), bf16)],
        [pltpu.VMEM((inner, TILE), f32), pltpu.VMEM((inner, rows), bf16)],
        4 * rows * inner * wide_a.shape[1],
        after=after,
    )(me, narrow_a, wide_a, narrow_b, wide_b)


def spatial_kernel(me_ref, hidden_ref, low_ref, keep_ref, send_ref, tile):
    top = pl.multiple_of((pl.program_id(0) // 3) * (SIDE * 16), 16)
    found = None
    for half in range(hidden_ref.shape[0]):
        part = dot_tn(hidden_ref[half, pl.ds(top, HALF)], low_ref[half * HALF : (half + 1) * HALF])
        found = part if found is None else found + part
    store_halves(me_ref[0], found, 16, keep_ref, send_ref, tile)


def spatial_block(me, hidden, low_two, after=()):
    halves, deep, _ = hidden.shape
    half = pl.BlockSpec((1, B // 2, B), lambda tap: (tap, 0, 0))
    return kernel_call(
        spatial_kernel,
        9,
        [SCALAR, pl.BlockSpec((halves, deep, B), lambda tap: (0, 0, tap % 3)),
         whole_spec(low_two.shape)],
        [half, half],
        [jax.ShapeDtypeStruct((9, B // 2, B), f32), jax.ShapeDtypeStruct((9, B // 2, B), bf16)],
        [pltpu.VMEM((B, B), f32)],
        18 * low_two.shape[0] * B * B,
        after=after,
    )(me, hidden, low_two)


STEM = 64
STEM_SIDE = 16
CHANNELS = 12
SLABS = 19
STEM_LANES = STEM_SIDE * STEM
INPUT_LANES = CHANNELS * 2 * STEM_SIDE
WINDOW = 7


def frames_kernel(frames_ref, out_ref, rows):
    segments = frames_ref.shape[0]
    side = 2 * STEM_SIDE

    def segment_step(segment, carry):
        pieces = [
            frames_ref[segment, index + 1, colour].astype(f32)
            - frames_ref[segment, index, colour].astype(f32)
            for index in range(4)
            for colour in range(3)
        ]
        for group in range(3):
            rows[group, pl.ds(segment, side, stride=segments)] = jnp.concatenate(
                pieces[4 * group : 4 * group + 4], axis=1
            )
        return carry

    lax.fori_loop(0, segments, segment_step, 0)
    empty = jnp.zeros((segments, INPUT_LANES), bf16)
    for parity in range(2):
        for slab in (0, 1, SLABS - 1):
            out_ref[parity, slab] = empty
    for row in range(side):
        for group in range(3):
            out_ref[row % 2, row // 2 + 2, :, group * LANES : (group + 1) * LANES] = rows[
                group, row * segments : (row + 1) * segments
            ].astype(bf16)


def frames_block(frames):
    segments = frames.shape[0] * frames.shape[1]
    ordered = frames.transpose(0, 1, 2, 5, 3, 4).reshape(
        (segments, frames.shape[2], 3) + frames.shape[3:5]
    )
    shape = (2, SLABS, segments, INPUT_LANES)
    return kernel_call(
        frames_kernel,
        1,
        [whole_spec(ordered.shape)],
        whole_out(shape),
        jax.ShapeDtypeStruct(shape, bf16),
        [pltpu.VMEM((3, 2 * STEM_SIDE * segments, LANES), f32)],
        ordered.size * 100,
    )(ordered)


def stem_rows(input_ref, offset):
    parity = 1 - offset % 2
    top = (offset - 3) // 2 + 2 if parity == 0 else (offset - 4) // 2 + 2
    found = input_ref[parity, top : top + STEM_SIDE]
    return found.reshape(-1, INPUT_LANES)


def band_select():
    shape = (STEM_SIDE // 2, CHANNELS, 2 * STEM_SIDE, 2, LANES)
    pair, channel, place, which, entry = (
        lax.broadcasted_iota(jnp.int32, shape, axis) for axis in range(5)
    )
    met = (entry % CHANNELS == channel) & (entry < WINDOW * CHANNELS)
    met = met & (place == 2 * (2 * pair + which) + entry // CHANNELS - 3)
    return met.astype(bf16).reshape(STEM_SIDE // 2, INPUT_LANES, 2 * LANES)


def pair_weights(stem_weight):
    rows = stem_weight.reshape(WINDOW, WINDOW * CHANNELS, STEM)
    rows = jnp.pad(rows, ((0, 0), (0, LANES - WINDOW * CHANNELS), (0, 0)))
    none = jnp.zeros_like(rows)
    return jnp.concatenate(
        [jnp.concatenate([rows, none], 2), jnp.concatenate([none, rows], 2)], 1
    )


def stem_kernel(input_ref, select_ref, weights_ref, pre_ref, sums_ref, bands):
    def step_body(step, carry):
        where = lanes(step, TILE)
        for offset in range(WINDOW):
            for which in range(2):
                band = product(select_ref[2 * step + which], weights_ref[offset])
                bands[offset, :, which * LANES : (which + 1) * LANES] = band.astype(bf16)
        found = None
        for offset in range(WINDOW):
            part = product(stem_rows(input_ref, offset), bands[offset])
            found = part if found is None else found + part
        pre_ref[:, where] = found
        sums_ref[0:1, where] = jnp.sum(found, 0, keepdims=True)
        sums_ref[1:2, where] = jnp.sum(found * found, 0, keepdims=True)
        return carry

    lax.fori_loop(0, STEM_LANES // TILE, step_body, 0)


def stem_block(inputs, select, weights, after=()):
    rows = inputs.shape[2] * STEM_SIDE
    return kernel_call(
        stem_kernel,
        1,
        [whole_spec(inputs.shape), whole_spec(select.shape), whole_spec(weights.shape)],
        [whole_out((rows, STEM_LANES)), whole_out((2, STEM_LANES))],
        [jax.ShapeDtypeStruct((rows, STEM_LANES), f32),
         jax.ShapeDtypeStruct((2, STEM_LANES), f32)],
        [pltpu.VMEM((WINDOW, INPUT_LANES, TILE), bf16)],
        2 * WINDOW * rows * INPUT_LANES * STEM_LANES,
        after=after,
    )(inputs, select, weights)


def stem_norm_kernel(count, pre_ref, in_sums_ref, affine_ref, cotangent_ref,
                     out_ref, grad_ref, sums_ref):
    def step_body(step, carry):
        where = lanes(step, LANES)
        mean, inverse, gain, shift = (
            spread(row) for row in constants(in_sums_ref[:, where], affine_ref[:, where], count)
        )
        first = jnp.zeros((16, LANES), f32)
        second = jnp.zeros((16, LANES), f32)
        for chunk in range(pre_ref.shape[0] // 16):
            rows = slice(chunk * 16, chunk * 16 + 16)
            unit = (pre_ref[rows, where] - mean) * inverse
            norm = unit * gain + shift
            sigma = sigmoid(norm)
            output = norm * sigma
            out_ref[rows, where] = output.astype(bf16)
            grad = cotangent_ref[rows, where].astype(f32) * (sigma + output * (1.0 - sigma))
            grad_ref[rows, where] = grad
            first = first + grad
            second = second + grad * unit
        sums_ref[0:1, where] = jnp.sum(first, 0, keepdims=True)
        sums_ref[1:2, where] = jnp.sum(second, 0, keepdims=True)
        return carry

    lax.fori_loop(0, STEM_LANES // LANES, step_body, 0)


def stem_norm_block(pre, sums, affine, cotangent, count, after=()):
    shape = pre.shape
    return kernel_call(
        functools.partial(stem_norm_kernel, count),
        1,
        [whole_spec(shape), whole_spec(sums.shape), whole_spec(affine.shape), whole_spec(shape)],
        [whole_out(shape), whole_out(shape), whole_out((2, STEM_LANES))],
        [jax.ShapeDtypeStruct(shape, bf16), jax.ShapeDtypeStruct(shape, f32),
         jax.ShapeDtypeStruct((2, STEM_LANES), f32)],
        [],
        4000 * pre.size,
        after=after,
    )(pre, sums, affine, cotangent)


def stem_back_kernel(count, input_ref, select_ref, pre_ref, in_sums_ref, affine_ref, grad_ref,
                     grads_ref, out_ref, low):
    def low_step(step, carry):
        where = lanes(step, LANES)
        mean, inverse, gain, _ = constants(in_sums_ref[:, where], affine_ref[:, where], count)
        scale = spread(gain * inverse)
        offset = spread(grads_ref[0:1, where] / count)
        along = spread(grads_ref[1:2, where] / count * inverse)
        mean = spread(mean)
        for chunk in range(pre_ref.shape[0] // 16):
            rows = slice(chunk * 16, chunk * 16 + 16)
            centred = pre_ref[rows, where] - mean
            low[rows, where] = (
                scale * (grad_ref[rows, where] - offset - centred * along)
            ).astype(bf16)
        return carry

    lax.fori_loop(0, STEM_LANES // LANES, low_step, 0)
    out_ref[...] = jnp.zeros_like(out_ref)

    def step_body(step, carry):
        where = lanes(step, TILE)
        for offset in range(WINDOW):
            band = dot_tn(stem_rows(input_ref, offset), low[:, where]).astype(bf16)
            found = dot_tn(select_ref[2 * step], band[:, 0:LANES]) + dot_tn(
                select_ref[2 * step + 1], band[:, LANES:TILE]
            )
            out_ref[offset] += found
        return carry

    lax.fori_loop(0, STEM_LANES // TILE, step_body, 0)


def stem_back_block(inputs, select, pre, sums, affine, grad, grads, count, after=()):
    shape = pre.shape
    out = (WINDOW, 2 * LANES, LANES)
    return kernel_call(
        functools.partial(stem_back_kernel, count),
        1,
        [whole_spec(inputs.shape), whole_spec(select.shape), whole_spec(shape),
         whole_spec(sums.shape), whole_spec(affine.shape), whole_spec(shape),
         whole_spec(grads.shape)],
        whole_out(out),
        jax.ShapeDtypeStruct(out, f32),
        [pltpu.VMEM(shape, bf16)],
        2 * WINDOW * shape[0] * INPUT_LANES * STEM_LANES,
        after=after,
    )(inputs, select, pre, sums, affine, grad, grads)


def squeeze_cut_kernel(me_ref, squeeze_ref, squeeze_out):
    part = me_ref[0] & 3
    squeeze_out[...] = squeeze_ref[pl.ds(pl.multiple_of(part * 64, 64), 64)]


def pair_cut_kernel(me_ref, expand_ref, reduce_ref, expand_out, reduce_out):
    part = me_ref[0] & 3
    expand_out[...] = expand_ref[pl.ds(pl.multiple_of(part * 128, 128), 128)]
    reduce_out[...] = reduce_ref[pl.ds(pl.multiple_of(part * 64, 64), 64)]


def pack_cut_kernel(me_ref, spatial_ref, restore_ref, class_ref, pack_out):
    part = me_ref[0] & 3
    for tap in range(9):
        pack_out[tap * 16 : tap * 16 + 16] = spatial_ref[
            tap, pl.ds(pl.multiple_of(part * 16, 16), 16)
        ]
    pack_out[SPATIAL_ROWS : SPATIAL_ROWS + RESTORE_ROWS] = restore_ref[
        :, pl.ds(pl.multiple_of(part * B, B), B)
    ]
    top = SPATIAL_ROWS + RESTORE_ROWS
    for half in range(2):
        rows = pl.ds(pl.multiple_of(part * 64 + half * 32, 32), 32)
        pack_out[top:, half * TILE : (half + 1) * TILE] = class_ref[rows]


def cut_block(kernel, me, weights, shapes, after=()):
    return kernel_call(
        kernel,
        1,
        [SCALAR] + [whole_spec(weight.shape) for weight in weights],
        [whole_out(shape) for shape in shapes],
        [jax.ShapeDtypeStruct(shape, bf16) for shape in shapes],
        [],
        1000000,
        after=after,
    )(me, *weights)


def shards(
    frames,
    tokens,
    stem_cotangent,
    crop_counts,
    labels,
    stem_weight,
    stem_gain,
    stem_shift,
    w_squeeze,
    next_kernel,
    scale_kernel,
    w_expand,
    w_reduce,
    gain_one,
    shift_one,
    w_spatial,
    gain_two,
    shift_two,
    w_restore,
    gain_three,
    shift_three,
    w_class,
    class_bias,
):
    view_count = frames.shape[0]
    row_count = tokens.shape[0]
    devices = lax.axis_size(AXES)
    wide = lax.axis_size("wide")
    narrow = lax.axis_size("narrow")
    count = float(row_count * devices)
    segments = view_count * SEG
    stem_rows_here = segments * STEM_SIDE
    stem_count = float(stem_rows_here * STEM_SIDE * devices)
    direct = wide == C // TILE and narrow == 4
    me = lax.axis_index(AXES)
    me_array = (me if direct else 0 * me).astype(jnp.int32).reshape(1)

    vectors = (gain_three, shift_three), (
        gain_one, shift_one, gain_two, shift_two, stem_gain, stem_shift,
    )
    if direct:
        small = small_pack(stem_weight, next_kernel, scale_kernel, *vectors)
        smalls = wide_tree(small)
    else:
        small = small_pack(stem_weight, next_kernel, scale_kernel, *vectors)
        smalls = lax.all_gather(small, "wide")
    stem_width = stem_weight.shape[1]
    inner_width = gain_one.shape[0]
    outer_width = gain_three.shape[0]
    full_stem = smalls[:, 0:stem_width, : stem_weight.shape[0]]
    full_stem = full_stem.transpose(2, 0, 1).reshape(-1, STEM).astype(bf16)
    taps = smalls[:, stem_width : stem_width + 9]
    full_next = taps[:, :, 0:inner_width].transpose(1, 0, 2).reshape(9, R)
    full_scale = taps[:, :, LANES : LANES + inner_width].transpose(1, 0, 2).reshape(9, R)
    outer_row = smalls[:, stem_width + 9, 0 : 2 * outer_width]
    affine_three = outer_row.reshape(wide, 2, -1).transpose(1, 0, 2).reshape(2, C)
    inner_row = smalls[:, stem_width + 10]
    affines = inner_row[:, 0 : 4 * inner_width].reshape(wide, 4, -1)
    affines = affines.transpose(1, 0, 2).reshape(4, B)
    affine_one, affine_two = affines[0:2], affines[2:4]
    stem_affine = inner_row[:, 4 * inner_width : 4 * inner_width + 2 * stem_width]
    stem_affine = stem_affine.reshape(wide, 2, -1).transpose(1, 0, 2).reshape(2, STEM)
    stem_affine = jnp.tile(stem_affine, (1, STEM_SIDE))

    if direct:
        class_padded = jnp.pad(w_class, ((0, 0), (0, TILE - CLASSES)))
        (squeeze_own,) = cut_block(squeeze_cut_kernel, me_array, [w_squeeze], [(64, R)])
        squeeze = block_tree(squeeze_own)
        expand_own, reduce_own = cut_block(
            pair_cut_kernel, me_array, [w_expand, w_reduce], [(128, TILE), (64, B)],
            after=(squeeze[0],),
        )
        expand = block_tree(expand_own)
        reduce = block_tree(reduce_own)
        (pack_own,) = cut_block(
            pack_cut_kernel, me_array, [w_spatial, w_restore, class_padded], [(PACK_ROWS, B)],
            after=(reduce_own, smalls),
        )
        pack = lax.all_gather(pack_own, AXES)
    else:
        squeeze, expand, reduce, pack = gathered(
            w_squeeze, w_expand, w_reduce, w_spatial, w_restore, w_class
        )
    full_class = pack[:, SPATIAL_ROWS + RESTORE_ROWS :].reshape(32, CLASS_ROWS, 2, TILE)
    full_class = full_class.transpose(0, 2, 1, 3).reshape(C, TILE)[:, :CLASSES]

    inputs = frames_block(frames)
    select = band_select()
    stem_pre, stem_part = stem_block(inputs, select, pair_weights(full_stem))
    stem_part = stem_part.reshape(2, STEM_SIDE, STEM).sum(1).reshape(1, 2 * STEM)
    cotangent = stem_cotangent.reshape(segments, STEM_SIDE, STEM_LANES)
    cotangent = cotangent.transpose(1, 0, 2).reshape(stem_rows_here, STEM_LANES)

    def stem_lanes(sums):
        return jnp.tile(sums[2, : 2 * STEM].reshape(2, STEM), (1, STEM_SIDE))

    def with_row(sums, row):
        return jnp.concatenate([sums, jnp.pad(row, ((0, 0), (0, sums.shape[1] - row.shape[1])))])

    upcoming, differ, mixed_low = mixing_block(
        me_array, squeeze, tokens, full_next, full_scale, after=(stem_pre,)
    )
    logit, gated_low, pre_one, one_part = gate_block(me_array, expand, reduce, tokens, mixed_low)
    one_sums = total(with_row(one_part, stem_part))
    stem_sums = stem_lanes(one_sums)
    hidden_one, pre_two, two_part = second_block(pre_one, one_sums, affine_one, pack, count)
    stem_out, stem_norm_grad, stem_part = stem_norm_block(
        stem_pre, stem_sums, stem_affine, cotangent, stem_count
    )
    stem_part = stem_part.reshape(2, STEM_SIDE, STEM).sum(1).reshape(1, 2 * STEM)
    two_sums = total(two_part)
    hidden_two, pre_three, three_part = third_block(pre_two, two_sums, affine_two, pack, count)
    three_sums = total(with_row(three_part, stem_part))
    stem_grads = stem_lanes(three_sums)
    activations, slope, view_sums = fourth_block(
        pre_three, gated_low, three_sums, affine_three, count
    )
    stem_features = stem_out.reshape(STEM_SIDE, segments, STEM_LANES)
    stem_features = stem_features.transpose(1, 0, 2).reshape(-1, STEM)

    def of_views(kind):
        return view_sums[:, 2 * kind : 2 * kind + 2].reshape(view_count, C)

    pooled_low = (of_views(0) / PER_VIEW).astype(bf16)
    view_logits = product(pooled_low, full_class) + class_bias.astype(f32)

    ends = jnp.cumsum(crop_counts)
    starts = ends - crop_counts
    positions = (me - 1) * view_count + jnp.arange(3 * view_count, dtype=jnp.int32)
    video = jnp.sum((ends[None, :] <= positions[:, None]).astype(jnp.int32), 1)
    own_video = video[view_count : 2 * view_count]
    belongs = (
        own_video[:, None] == jnp.arange(crop_counts.shape[0], dtype=jnp.int32)[None, :]
    ).astype(jnp.int32)
    own_count = jnp.sum(belongs * crop_counts[None, :], 1).astype(f32)
    own_label = jnp.sum(belongs * labels[None, :], 1)
    own_start = jnp.sum(belongs * starts[None, :], 1)
    first = (own_start == positions[view_count : 2 * view_count]).astype(f32)
    same = (own_video[:, None] == video[None, :]).astype(f32) / own_count[:, None]
    target = (own_label[:, None] == jnp.arange(CLASSES, dtype=jnp.int32)[None, :]).astype(f32)

    before = lax.ppermute(view_logits, AXES, [(i, i + 1) for i in range(devices - 1)])
    following = lax.ppermute(view_logits, AXES, [(i + 1, i) for i in range(devices - 1)])
    near = jnp.concatenate([before, view_logits, following])
    video_logits = jnp.sum(same[:, :, None] * near[None, :, :], 1)
    log_probs = jax.nn.log_softmax(video_logits, axis=-1)
    entropy_part = jnp.sum(first * -jnp.sum(target * log_probs, axis=-1))
    video_grad = loss_scale * (jnp.exp(log_probs) - target)
    bias_part = jnp.sum(first[:, None] * video_grad, 0)
    view_grad_low = (video_grad / own_count[:, None]).astype(bf16)

    factors = jnp.concatenate(
        [pooled_low, jnp.pad(view_grad_low, ((0, 0), (0, TILE - CLASSES)))], axis=1
    )
    if direct:
        factors = jnp.concatenate(block_tree(factors)).reshape(-1, C + TILE)
    else:
        factors = lax.all_gather(factors, AXES, tiled=True)
    own_pooled = lax.dynamic_slice_in_dim(
        factors, lax.axis_index("wide") * outer_width, outer_width, 1
    )
    sum_class = product_left(own_pooled, factors[:, C : C + CLASSES])

    pooled_grad = product_right(view_grad_low, full_class) / PER_VIEW
    part_row = jnp.concatenate([bias_part, entropy_part[None]])[None]
    three_part = jnp.stack([jnp.sum(pooled_grad * of_views(kind), 0) for kind in (1, 2)])
    three_grads = total(with_row(three_part, part_row))
    class_bias_grad = three_grads[2, :CLASSES]
    loss = three_grads[2, CLASSES] / crop_counts.shape[0]
    pooled_grad = pooled_grad.reshape(-1, 2, C)

    low_three, norm_two_grad, two_part = fifth_block(
        slope, pre_three, pooled_grad, three_sums, affine_three, three_grads, pack,
        pre_two, two_sums, affine_two, count,
    )
    two_grads = total(two_part)
    restore_half = outer_block(me_array, hidden_two, low_three, RESTORE_ROWS // 4)
    low_two, norm_one_grad, one_part = sixth_block(
        norm_two_grad, pre_two, two_sums, affine_two, two_grads, pack, pre_one, one_sums,
        affine_one, count,
    )
    one_grads = total(one_part)
    spatial_half = spatial_block(me_array, hidden_one, low_two)
    if direct:
        sum_restore, restore_came = halves_tree(restore_half, (8, 4, 2, 2, 16, TILE), 1, "yxz")
        sum_spatial, spatial_came = halves_tree(spatial_half, (9, 4, 2, 2, 16, B), 1, "xyz")
    else:
        restore_came = spatial_came = [None] * 4

    def came(*arrays):
        return tuple(array for array in arrays if array is not None)

    low_one, logit_grad, tokens_part = gate_back_block(
        me_array, reduce, norm_one_grad, pre_one, one_sums, affine_one, one_grads, slope,
        pooled_grad, tokens, logit, count, after=came(restore_came[0]),
    )
    pair_half = outer_pair_block(
        me_array, low_one, gated_low, mixed_low, logit_grad,
        after=came(restore_came[1], spatial_came[0]),
    )
    low_squeezed, kernel_grads = mixing_back_block(
        me_array, expand, logit_grad, upcoming, differ, full_next, full_scale,
        after=came(restore_came[2], spatial_came[0], pair_half[0]),
    )
    if direct:
        sum_pair, pair_came = halves_tree(pair_half, (2, 4, 2, 2, 128, TILE), 1, "yxz")
    else:
        pair_came = [None] * 4
    squeeze_half = outer_block(
        me_array, low_squeezed, tokens, R // 4, after=came(spatial_came[1], pair_came[0])
    )
    if direct:
        sum_squeeze, squeeze_came = halves_tree(squeeze_half, (4, 2, 2, 128, TILE), 0, "xyz")
    else:
        squeeze_came = [None] * 4
    tokens_grad = tokens_block(
        me_array, squeeze, tokens_part, low_squeezed, after=came(squeeze_came[0], pair_came[1])
    )
    stem_back = stem_back_block(
        inputs, select, stem_pre, stem_sums, stem_affine, stem_norm_grad, stem_grads, stem_count
    )
    stem_back = stem_back[:, :LANES, :STEM] + stem_back[:, LANES:, STEM:]
    stem_grad = stem_back[:, : WINDOW * CHANNELS].reshape(-1, STEM)

    stem_cut = stem_grad.T.reshape(wide, stem_width, -1)
    kernel_cut = kernel_grads.reshape(2, 9, wide, inner_width).transpose(2, 1, 0, 3)
    kernel_cut = jnp.pad(kernel_cut, ((0, 0), (0, 0), (0, 0), (0, LANES - inner_width)))
    kernel_cut = kernel_cut.reshape(wide, 9, 2 * LANES)
    small_grads = jnp.concatenate(
        [
            jnp.pad(stem_cut, ((0, 0), (0, 0), (0, SMALL_LANES - stem_cut.shape[2]))),
            jnp.pad(kernel_cut, ((0, 0), (0, 0), (0, SMALL_LANES - 2 * LANES))),
        ],
        axis=1,
    )
    if direct:
        mine = small_scatter(small_grads)
    else:
        mine = lax.psum_scatter(small_grads, "wide", scatter_dimension=0, tiled=False)
        mine = lax.psum(mine, "narrow")
    sum_stem = mine[:stem_width, : stem_weight.shape[0]].T
    sum_next = mine[stem_width : stem_width + 9, 0:inner_width]
    sum_scale = mine[stem_width : stem_width + 9, LANES : LANES + inner_width]

    if direct:
        sum_restore = sum_restore.transpose(0, 2, 1, 3).reshape(4 * 16, C)
        sum_spatial = sum_spatial.transpose(1, 0, 2, 3).reshape(w_spatial.shape)
        sum_reduce, sum_expand = sum_pair[:, 0].reshape(B, TILE).T, sum_pair[:, 1].reshape(R, TILE)
        sum_squeeze = sum_squeeze.reshape(R, TILE).T
    else:
        sum_restore, sum_spatial, sum_reduce, sum_expand, sum_squeeze = reduced(
            restore_half, spatial_half, pair_half, squeeze_half
        )

    def own_slice(values, width):
        return lax.dynamic_slice_in_dim(values, lax.axis_index("wide") * width, width)

    return (
        activations,
        stem_features,
        tokens_grad,
        sum_stem,
        own_slice(stem_grads[1, :STEM], stem_width),
        own_slice(stem_grads[0, :STEM], stem_width),
        sum_squeeze,
        sum_next,
        sum_scale,
        sum_expand,
        sum_reduce,
        own_slice(one_grads[1], inner_width),
        own_slice(one_grads[0], inner_width),
        sum_spatial,
        own_slice(two_grads[1], inner_width),
        own_slice(two_grads[0], inner_width),
        sum_restore,
        own_slice(three_grads[1], outer_width),
        own_slice(three_grads[0], outer_width),
        sum_class,
        class_bias_grad,
        loss,
    )


def solution(mesh):
    in_specs = (
        P(("wide", "narrow"), None, None, None, None, None),
        P(("wide", "narrow"), None),
        P(("wide", "narrow"), None),
        P(),
        P(),
        P(None, "wide"),
        P("wide"),
        P("wide"),
        P("wide", None),
        P(None, "wide"),
        P(None, "wide"),
        P(None, "wide"),
        P("wide", None),
        P("wide"),
        P("wide"),
        P(None, "wide", None),
        P("wide"),
        P("wide"),
        P("wide", None),
        P("wide"),
        P("wide"),
        P("wide", None),
        P(),
    )
    out_specs = (
        P(("wide", "narrow"), None),
        P(("wide", "narrow"), None),
        P(("wide", "narrow"), None),
        P(None, "wide"),
        P("wide"),
        P("wide"),
        P("wide", None),
        P(None, "wide"),
        P(None, "wide"),
        P(None, "wide"),
        P("wide", None),
        P("wide"),
        P("wide"),
        P(None, "wide", None),
        P("wide"),
        P("wide"),
        P("wide", None),
        P("wide"),
        P("wide"),
        P("wide", None),
        P(),
        P(),
    )
    return jax.shard_map(shards, mesh=mesh, in_specs=in_specs, out_specs=out_specs, check_vma=False)
```

```python
import functools

import jax
import jax.numpy as jnp
from jax import lax
from jax.experimental import pallas as pl
from jax.experimental.pallas import tpu as pltpu
from jax.sharding import PartitionSpec as P

C = 2048
B = 512
R = 512
CLASSES = 174
SEG = 8
SIDE = 7
PER_VIEW = SEG * SIDE * SIDE

epsilon = 1e-05
loss_scale = 1024.0

AXES = ("wide", "narrow")
f32 = jnp.float32
bf16 = jnp.bfloat16


def product(first_operand, second_operand):
    return jnp.dot(first_operand, second_operand, preferred_element_type=f32)


def product_left(first_operand, second_operand):
    return lax.dot_general(
        first_operand, second_operand, (((0,), (0,)), ((), ())), preferred_element_type=f32
    )


def product_right(first_operand, second_operand):
    return lax.dot_general(
        first_operand, second_operand, (((1,), (1,)), ((), ())), preferred_element_type=f32
    )


def exchange(values, mask):
    size = lax.axis_size(AXES)
    return lax.ppermute(values, AXES, [(index, index ^ mask) for index in range(size)])


def own_bit(bit):
    return (lax.axis_index(AXES) >> bit) & 1


def total(values):
    bits = lax.axis_size(AXES).bit_length() - 1
    values = values + exchange(values, 1)
    for bit in range(1, bits, 2):
        masks = [1 << bit]
        if bit + 1 < bits:
            masks += [2 << bit, 3 << bit]
        parts = [exchange(values, mask) for mask in masks]
        for part in parts:
            values = values + part
    return values


def swap_total(values):
    size = lax.axis_size(AXES)
    copies = jnp.broadcast_to(values[None], (size,) + values.shape)
    return jnp.sum(lax.all_to_all(copies, AXES, 0, 0, tiled=True), 0)


def beside(run, inputs, sends, more=()):
    inputs, arrays = lax.optimization_barrier((tuple(inputs), [array for array, _ in sends]))
    came = [exchange(array, mask) for array, (_, mask) in zip(arrays, sends)]
    return lax.optimization_barrier((run(*inputs), came, tuple(more)))


def launch(run, inputs, sends):
    inputs, arrays = lax.optimization_barrier((tuple(inputs), [array for array, _ in sends]))
    came = [exchange(array, mask) for array, (_, mask) in zip(arrays, sends)]
    return lax.optimization_barrier(run(*inputs)), came


class Gather:
    def __init__(self, block):
        self.block = block

    def depth(self):
        return [(self.block, mask) for mask in (8, 16, 24)]

    def take_depth(self, came):
        self.four = join([part[None] for part in (self.block, *came)])

    def second(self):
        return [(self.four, 4)]

    def take_second(self, came):
        self.eight = join([self.four, came[0]])

    def third(self):
        return [(self.eight, 2)]

    def take_third(self, came):
        self.other = came[0]

    def core(self):
        return [(self.eight, 1), (self.other, 1)]

    def take_core(self, came):
        self.arrays = (self.eight, self.other) + tuple(came)


class Sum:
    def __init__(self, half, shape, lead):
        self.keep, self.send = half
        self.shape, self.lead, self.axes = shape, lead, "zyx"

    def core(self):
        return [(self.send, 1)]

    def take_core(self, came):
        self.values = (self.keep + came[0].astype(f32)).reshape(self.shape)

    def split(self, letter):
        place = self.lead + self.axes.index(letter)
        self.axes = self.axes.replace(letter, "")
        bit = {"x": 1, "y": 2, "z": 3}[letter]
        span = 3 if letter == "z" else 1
        mine = (lax.axis_index(AXES) >> bit) & span
        found = []
        for mask in range(1, span + 1):
            part = lax.dynamic_index_in_dim(self.values, mine ^ mask, place, keepdims=False)
            found.append((part.astype(bf16), mask << bit))
        self.values = lax.dynamic_index_in_dim(self.values, mine, place, keepdims=False)
        return found

    def split_parts(self, letter, at):
        ((send, mask),) = self.split(letter)
        return [(send[:at], mask)], [(send[at:], mask)]

    def take_parts(self, first, second):
        self.take([jnp.concatenate([first[0], second[0]])])

    def take(self, came):
        for part in came:
            self.values = self.values + part.astype(f32)

    def spread(self):
        self.part = self.values.astype(bf16)
        return [(self.part, mask) for mask in (1, 2, 3)]

    def take_spread(self, came):
        own, (core, over_x, both) = self.part, came
        odd, far = own_bit(0) == 1, own_bit(1) == 1
        near = [jnp.where(odd, core, own), jnp.where(odd, own, core)]
        away = [jnp.where(odd, both, over_x), jnp.where(odd, over_x, both)]
        self.whole = jnp.stack(
            [jnp.where(far, away[0], near[0]), jnp.where(far, away[1], near[1]),
             jnp.where(far, near[0], away[0]), jnp.where(far, near[1], away[1])]
        ).astype(f32)


def gathered(w_squeeze, w_expand, w_reduce, w_spatial, w_restore, w_class):
    def whole(weight, axis):
        return lax.all_gather(weight, "wide", axis=axis, tiled=True)

    def as_blocks(blocks):
        ordered = blocks.reshape((4, 2, 2, 2) + blocks.shape[1:])
        return [
            ordered[:, :, far, core].swapaxes(0, 1).reshape((8,) + blocks.shape[1:])
            for core in range(2)
            for far in range(2)
        ]

    squeeze = whole(w_squeeze, 0).reshape(32, -1, R)
    expand = whole(w_expand, 1).reshape(4, 2, PAIR_ROWS, 8, TILE).transpose(3, 0, 2, 1, 4)
    expand = expand.reshape(32, PAIR_ROWS, 2 * TILE)
    reduce = whole(w_reduce, 0).reshape(32, -1, B)
    spatial = whole(w_spatial, 1).reshape(9, 32, 16, B).swapaxes(0, 1).reshape(32, -1, B)
    restore = whole(w_restore, 0).reshape(8, 64, 4, B).swapaxes(1, 2).reshape(32, 64, B)
    classes = jnp.pad(whole(w_class, 0), ((0, 0), (0, TILE - CLASSES)))
    classes = classes.reshape(32, 2, CLASS_ROWS, TILE).swapaxes(1, 2).reshape(32, CLASS_ROWS, B)
    late = jnp.concatenate([restore, classes], axis=1)
    pair = jnp.concatenate([reduce, expand], axis=1)
    return as_blocks(squeeze), as_blocks(pair), as_blocks(spatial), late


def reduced(buffer, reduce_half, expand_half, squeeze_half):
    def whole(half, grain):
        keep, send = (part.astype(bf16) for part in half)
        shape = keep.shape[:1] + (-1, grain) + keep.shape[2:]
        both = jnp.stack([keep.reshape(shape), send.reshape(shape)], axis=2)
        return both.reshape(keep.shape[:1] + (-1,) + keep.shape[2:])

    def scattered(grad, axis):
        part = lax.psum_scatter(grad, "wide", scatter_dimension=axis, tiled=True)
        return lax.psum(part, "narrow").astype(f32)

    def columns(tiles):
        return tiles.swapaxes(0, 1).reshape(tiles.shape[1], -1)

    restore = buffer[:, :RESTORE_ROWS].reshape(8, 4, RESTORE_ROWS, WIDE).swapaxes(1, 2).reshape(B, C)
    spatial = buffer[:, RESTORE_ROWS:].reshape(32, 9, 16, B).swapaxes(0, 1).reshape(9, B, B)
    return (
        scattered(restore, 0),
        scattered(spatial, 1),
        scattered(columns(whole(reduce_half, 128)), 1).T,
        scattered(columns(whole(expand_half, 128)), 1),
        scattered(columns(whole(squeeze_half, 128)), 1).T,
    )


CELLS = SIDE * SIDE
HALF = 2 * PER_VIEW
PADDED = SIDE + 2
MIB = 1 << 20
LANES = 128
TILE = 256


def cell_place(cell):
    return (cell // SIDE + 1) * PADDED + cell % SIDE + 1


def tap_place(cell, tap):
    return cell_place(cell) + (tap // 3 - 1) * PADDED + tap % 3 - 1


def dot_nt(first_operand, second_operand):
    return lax.dot_general(
        first_operand, second_operand, (((1,), (1,)), ((), ())), preferred_element_type=f32
    )


def dot_tn(first_operand, second_operand):
    return lax.dot_general(
        first_operand, second_operand, (((0,), (0,)), ((), ())), preferred_element_type=f32
    )


def sigmoid(values):
    return 0.5 * jnp.tanh(0.5 * values) + 0.5


def constants(sums, affine, count):
    mean = sums[0:1] / count
    inverse = lax.rsqrt(sums[1:2] / count - mean * mean + epsilon)
    return mean, inverse, affine[0:1], affine[1:2]


def spread(row, rows=16):
    return jnp.broadcast_to(row, (rows, row.shape[1]))


def lanes(index, width):
    return pl.ds(pl.multiple_of(index * width, width), width)


def clear_border(ref):
    zero = jnp.zeros(ref.shape[1:], ref.dtype)
    for place in range(PADDED * PADDED):
        if place // PADDED in (0, PADDED - 1) or place % PADDED in (0, PADDED - 1):
            ref[place] = zero


def fold(values):
    return values[0:8] + values[8:16]


def half_spec(width):
    return pl.BlockSpec((HALF, width), lambda step, *_: (step, 0))


def whole_spec(shape):
    return pl.BlockSpec(shape, lambda *_: (0,) * len(shape), pipeline_mode=pl.Buffered(1))


def whole_out(shape):
    return pl.BlockSpec(shape, lambda *_: (0,) * len(shape))


WIDE = 512
GROUPS = C // WIDE


def group_spec():
    return pl.BlockSpec((HALF, WIDE), lambda half, group: (half, group))


def row_spec(rows):
    return pl.BlockSpec((rows, WIDE), lambda half, group: (0, group))


def view_spec(rows):
    return pl.BlockSpec((1, rows, WIDE), lambda half, group: (half, 0, group))


def first_group():
    return pl.program_id(1) == 0


def last_group():
    return pl.program_id(1) == GROUPS - 1


ANY = pl.BlockSpec(memory_space=pl.ANY)
SCALAR = pl.BlockSpec(memory_space=pltpu.SMEM)


def kernel_call(kernel, steps, in_specs, out_specs, out_shapes, scratch, flops,
                transcendentals=0, after=(), vmem=60, aliases=None):
    known = len(in_specs)
    grid = steps if isinstance(steps, tuple) else (steps,)

    def body(*refs):
        kernel(*refs[:known], *refs[known + len(after) :])

    call = pl.pallas_call(
        body,
        grid=grid,
        in_specs=list(in_specs) + [ANY] * len(after),
        out_specs=out_specs,
        out_shape=out_shapes,
        scratch_shapes=scratch,
        input_output_aliases=aliases or {},
        compiler_params=pltpu.CompilerParams(
            dimension_semantics=("arbitrary",) * len(grid), vmem_limit_bytes=vmem * MIB
        ),
        cost_estimate=pl.CostEstimate(
            flops=2 * flops, bytes_accessed=16 * MIB, transcendentals=transcendentals
        ),
    )
    return lambda *operands: call(*operands, *after)


def block_copies(me, sources, target, semaphores, rows=None, lanes_at=None, target_rows=None):
    copies = []
    for low_mask, source in zip((0, 2, 1, 3), sources):
        for entry in range(8):
            mask = low_mask | ((entry // 4) * 4) | ((entry % 4) << 3)
            taken, place = source.at[entry], target.at[me ^ mask]
            if rows is not None:
                taken = taken.at[rows] if lanes_at is None else taken.at[rows, lanes_at]
            if target_rows is not None:
                place = place.at[target_rows]
            copies.append(pltpu.make_async_copy(taken, place, semaphores.at[len(copies)]))
    return copies


PAIR_ROWS = 64


def reduce_copies(me, sources, target, semaphores):
    return block_copies(me, sources, target, semaphores, slice(0, PAIR_ROWS))


def expand_copies(me, sources, target, semaphores):
    rows = slice(PAIR_ROWS, 2 * PAIR_ROWS)
    found = []
    for part in range(2):
        found += block_copies(
            me, sources, target, semaphores.at[part], rows,
            slice(part * TILE, (part + 1) * TILE),
            slice(part * PAIR_ROWS, (part + 1) * PAIR_ROWS),
        )
    return found


def start(copies):
    for copy in copies:
        copy.start()


def wait(copies):
    for copy in copies:
        copy.wait()


def join_kernel(*refs):
    *sources, out_ref, semaphores = refs
    copies, top = [], 0
    for source in sources:
        count = source.shape[0]
        copies.append(
            pltpu.make_async_copy(
                source, out_ref.at[top : top + count], semaphores.at[len(copies)]
            )
        )
        top += count
    start(copies)
    wait(copies)


def join(arrays):
    count = sum(array.shape[0] for array in arrays)
    return kernel_call(
        join_kernel,
        1,
        [ANY] * len(arrays),
        ANY,
        jax.ShapeDtypeStruct((count,) + arrays[0].shape[1:], arrays[0].dtype),
        [pltpu.SemaphoreType.DMA((len(arrays),))],
        1000000,
        vmem=16,
    )(*arrays)


def first_step():
    return pl.program_id(0) == 0


def very_first():
    return (pl.program_id(0) == 0) & (pl.program_id(1) == 0)


def add_moments(sums_ref, where, first, second):
    sums_ref[0:1, where] += jnp.sum(first, 0, keepdims=True)
    sums_ref[1:2, where] += jnp.sum(second, 0, keepdims=True)


def mixing_kernel(
    me_ref, block_a, block_b, block_c, block_d, tokens_ref, next_ref, scale_ref,
    upcoming_ref, differ_ref, mixed_ref, natural, ahead, padded, squeeze_ref, semaphores,
):
    @pl.when(first_step())
    def _():
        copies = block_copies(
            me_ref[0], (block_a, block_b, block_c, block_d), squeeze_ref, semaphores, slice(0, 64)
        )
        start(copies)
        natural[:, HALF:] = jnp.zeros((4, natural.shape[1] - HALF, LANES), f32)
        clear_border(ahead)
        clear_border(padded)
        wait(copies)

    def squeeze_step(step, carry):
        squeezed = product(
            tokens_ref[...], squeeze_ref[:, :, lanes(step, TILE)].reshape(C, TILE)
        )
        natural[2 * step, 0:HALF] = squeezed[:, 0:LANES]
        natural[2 * step + 1, 0:HALF] = squeezed[:, LANES:TILE]
        return carry

    lax.fori_loop(0, 2, squeeze_step, 0)
    segment = lax.broadcasted_iota(jnp.int32, (16, LANES), 0) % SEG
    not_last = (segment != SEG - 1).astype(f32)

    def mixing_step(step, carry):
        where = lanes(step, LANES)
        next_rows = [spread(next_ref[tap : tap + 1, where]) for tap in range(9)]
        for cell in range(CELLS):
            upcoming = natural[step, pl.ds(cell + CELLS, 16, stride=CELLS)] * not_last
            ahead[cell_place(cell)] = upcoming
            upcoming_ref[cell * 16 : cell * 16 + 16, where] = upcoming
        mean = jnp.zeros((16, LANES), f32)
        for cell in range(CELLS):
            differ = -natural[step, pl.ds(cell, 16, stride=CELLS)]
            for tap in range(9):
                differ = differ + ahead[tap_place(cell, tap)] * next_rows[tap]
            padded[cell_place(cell)] = differ
            differ_ref[cell * 16 : cell * 16 + 16, where] = differ
            mean = mean + differ
        mean = mean * (1.0 / CELLS)
        scale_rows = [spread(scale_ref[tap : tap + 1, where]) for tap in range(9)]
        for cell in range(CELLS):
            mixed = padded[cell_place(cell)] + mean
            for tap in range(9):
                mixed = mixed + padded[tap_place(cell, tap)] * scale_rows[tap]
            natural[step, pl.ds(cell, 16, stride=CELLS)] = mixed
        mixed_ref[:, where] = natural[step, 0:HALF].astype(bf16)
        return carry

    lax.fori_loop(0, 4, mixing_step, 0)


def mixing_block(me, squeeze, tokens, next_kernel, scale_kernel, after=()):
    rows = tokens.shape[0]
    return kernel_call(
        mixing_kernel,
        rows // HALF,
        [SCALAR, ANY, ANY, ANY, ANY, half_spec(C), whole_spec((9, R)), whole_spec((9, R))],
        [half_spec(R), half_spec(R), half_spec(R)],
        [jax.ShapeDtypeStruct((rows, R), f32), jax.ShapeDtypeStruct((rows, R), f32),
         jax.ShapeDtypeStruct((rows, R), bf16)],
        [pltpu.VMEM((4, HALF + CELLS + 7, LANES), f32),
         pltpu.VMEM((PADDED * PADDED, 16, LANES), f32),
         pltpu.VMEM((PADDED * PADDED, 16, LANES), f32),
         pltpu.VMEM((32, C // 32, R), bf16), pltpu.SemaphoreType.DMA((32,))],
        2 * rows * C * R,
        after=after,
    )(me, *squeeze, tokens, next_kernel, scale_kernel)


def gate_kernel(
    me_ref, block_a, block_b, block_c, block_d, tokens_ref, mixed_ref,
    logit_ref, gated_ref, pre_ref, sums_ref,
    tile, found, expand_ref, reduce_ref, expand_semaphores, reduce_semaphores,
):
    blocks = (block_a, block_b, block_c, block_d)
    for_expand = expand_copies(me_ref[0], blocks, expand_ref, expand_semaphores)
    for_reduce = reduce_copies(me_ref[0], blocks, reduce_ref, reduce_semaphores)
    group = pl.program_id(1)

    @pl.when(very_first())
    def _():
        start(for_expand)
        start(for_reduce)
        sums_ref[...] = jnp.zeros_like(sums_ref)
        wait(for_expand)

    for part in range(2):
        columns = expand_ref[pl.ds(8 * group + 4 * part, 4)].reshape(R, TILE)
        tile[:, part * TILE : (part + 1) * TILE] = product(mixed_ref[...], columns)
    for chunk in range(HALF // 16):
        rows = slice(chunk * 16, chunk * 16 + 16)
        logit = tile[rows]
        token = tokens_ref[rows].astype(f32)
        logit_ref[rows] = logit.astype(bf16)
        gated_ref[rows] = (token + token * sigmoid(logit)).astype(bf16)

    @pl.when(very_first())
    def _():
        wait(for_reduce)

    part = product(gated_ref[...], reduce_ref[pl.ds(8 * group, 8)].reshape(WIDE, B))

    @pl.when(first_group())
    def _():
        found[...] = part

    @pl.when(group > 0)
    def _():
        found[...] += part

    @pl.when(last_group())
    def _():
        first = jnp.zeros((8, B), f32)
        second = jnp.zeros((8, B), f32)
        for chunk in range(HALF // 16):
            rows = slice(chunk * 16, chunk * 16 + 16)
            value = found[rows]
            pre_ref[rows] = value
            first = first + fold(value)
            second = second + fold(value * value)
        add_moments(sums_ref, slice(0, B), first, second)


def gate_block(me, pair, tokens, mixed):
    rows = tokens.shape[0]
    return kernel_call(
        gate_kernel,
        (rows // HALF, GROUPS),
        [SCALAR] + [ANY] * 4 + [group_spec(), half_spec(R)],
        [group_spec(), group_spec(), half_spec(B), whole_out((2, B))],
        [jax.ShapeDtypeStruct((rows, C), bf16), jax.ShapeDtypeStruct((rows, C), bf16),
         jax.ShapeDtypeStruct((rows, B), f32), jax.ShapeDtypeStruct((2, B), f32)],
        [pltpu.VMEM((HALF, WIDE), f32), pltpu.VMEM((HALF, B), f32),
         pltpu.VMEM((32, R // 4, TILE), bf16), pltpu.VMEM((32, C // 32, B), bf16),
         pltpu.SemaphoreType.DMA((2, 32)), pltpu.SemaphoreType.DMA((32,))],
        4 * rows * C * R,
        2 * rows * C,
    )(me, *pair, tokens, mixed)


SPATIAL_ROWS = 9 * 16
RESTORE_ROWS = 64
CLASS_ROWS = 32
LATE_ROWS = RESTORE_ROWS + CLASS_ROWS


def restore_copy(late_ref, target, semaphore):
    return pltpu.make_async_copy(late_ref.at[:, 0:RESTORE_ROWS], target, semaphore)


def second_kernel(count, me_ref, block_a, block_b, block_c, block_d,
                  pre_ref, in_sums_ref, affine_ref,
                  hidden_ref, out_ref, sums_ref, natural, padded, tile, spatial_ref, semaphores):
    copies = block_copies(me_ref[0], (block_a, block_b, block_c, block_d), spatial_ref, semaphores)

    @pl.when(first_step())
    def _():
        start(copies)
        sums_ref[...] = jnp.zeros_like(sums_ref)
        clear_border(padded)

    border = SIDE * 16
    hidden_ref[0, 0:border] = jnp.zeros((border, 3 * B), bf16)
    hidden_ref[0, border + HALF :] = jnp.zeros((border, 3 * B), bf16)

    def hidden_step(step, carry):
        where = lanes(step, LANES)
        mean, inverse, gain, shift = (
            spread(row) for row in constants(in_sums_ref[:, where], affine_ref[:, where], count)
        )
        for chunk in range(HALF // 16):
            rows = slice(chunk * 16, chunk * 16 + 16)
            norm = (pre_ref[rows, where] - mean) * inverse * gain + shift
            natural[rows] = norm * sigmoid(norm)
        for cell in range(CELLS):
            padded[cell_place(cell)] = natural[pl.ds(cell, 16, stride=CELLS)].astype(bf16)
        for side in range(3):
            at = lanes(side * 4 + step, LANES)
            for cell in range(CELLS):
                hidden_ref[0, border + cell * 16 : border + cell * 16 + 16, at] = padded[
                    tap_place(cell, 3 + side)
                ]
        return carry

    lax.fori_loop(0, 4, hidden_step, 0)

    @pl.when(first_step())
    def _():
        wait(copies)

    def product_step(step, carry):
        where = lanes(step, TILE)
        found = None
        for row in range(3):
            taps = [
                spatial_ref[:, tap * 16 : tap * 16 + 16, where].reshape(B, TILE)
                for tap in range(3 * row, 3 * row + 3)
            ]
            part = product(
                hidden_ref[0, row * border : row * border + HALF], jnp.concatenate(taps, axis=0)
            )
            found = part if found is None else found + part
        tile[...] = found
        first = jnp.zeros((8, TILE), f32)
        second = jnp.zeros((8, TILE), f32)
        for chunk in range(HALF // 16):
            rows = slice(chunk * 16, chunk * 16 + 16)
            value = tile[rows]
            out_ref[rows, where] = value
            first = first + fold(value)
            second = second + fold(value * value)
        add_moments(sums_ref, where, first, second)
        return carry

    lax.fori_loop(0, B // TILE, product_step, 0)


def second_block(me, spatial, pre_one, sums, affine, count):
    rows = pre_one.shape[0]
    steps = rows // HALF
    deep = HALF + 2 * SIDE * 16
    return kernel_call(
        functools.partial(second_kernel, count),
        steps,
        [SCALAR, ANY, ANY, ANY, ANY, half_spec(B), whole_spec(sums.shape), whole_spec((2, B))],
        [pl.BlockSpec((1, deep, 3 * B), lambda step: (step, 0, 0)), half_spec(B),
         whole_out((2, B))],
        [jax.ShapeDtypeStruct((steps, deep, 3 * B), bf16), jax.ShapeDtypeStruct((rows, B), f32),
         jax.ShapeDtypeStruct((2, B), f32)],
        [pltpu.VMEM((HALF, LANES), f32), pltpu.VMEM((PADDED * PADDED, 16, LANES), bf16),
         pltpu.VMEM((HALF, TILE), f32), pltpu.VMEM((32, SPATIAL_ROWS, B), bf16),
         pltpu.SemaphoreType.DMA((32,))],
        18 * rows * B * B,
        2 * rows * B,
    )(me, *spatial, pre_one, sums, affine)


def third_kernel(count, pre_ref, in_sums_ref, affine_ref, late_ref,
                 hidden_ref, out_ref, sums_ref, natural, tile, restore_ref, semaphore):
    copy = restore_copy(late_ref, restore_ref, semaphore)
    group = pl.program_id(1)

    @pl.when(very_first())
    def _():
        copy.start()
        sums_ref[...] = jnp.zeros_like(sums_ref)

    @pl.when(first_group())
    def _():
        def hidden_step(step, carry):
            where = lanes(step, LANES)
            mean, inverse, gain, shift = (
                spread(row)
                for row in constants(in_sums_ref[:, where], affine_ref[:, where], count)
            )
            for cell in range(CELLS):
                rows = slice(cell * 16, cell * 16 + 16)
                norm = (pre_ref[rows, where] - mean) * inverse * gain + shift
                natural[pl.ds(cell, 16, stride=CELLS)] = norm * sigmoid(norm)
            hidden_ref[:, where] = natural[...].astype(bf16)
            return carry

        lax.fori_loop(0, 4, hidden_step, 0)

    @pl.when(very_first())
    def _():
        copy.wait()

    columns = restore_ref.reshape(8, 4, RESTORE_ROWS, B)[:, group].reshape(B, WIDE)
    tile[...] = product(hidden_ref[...], columns)
    first = jnp.zeros((8, WIDE), f32)
    second = jnp.zeros((8, WIDE), f32)
    for chunk in range(HALF // 16):
        rows = slice(chunk * 16, chunk * 16 + 16)
        value = tile[rows]
        out_ref[rows] = value.astype(bf16)
        first = first + fold(value)
        second = second + fold(value * value)
    add_moments(sums_ref, lanes(group, WIDE), first, second)


def third_block(pre_two, sums, affine, late, count):
    rows = pre_two.shape[0]
    return kernel_call(
        functools.partial(third_kernel, count),
        (rows // HALF, GROUPS),
        [half_spec(B), whole_spec(sums.shape), whole_spec((2, B)), ANY],
        [half_spec(B), group_spec(), whole_out((2, C))],
        [jax.ShapeDtypeStruct((rows, B), bf16), jax.ShapeDtypeStruct((rows, C), bf16),
         jax.ShapeDtypeStruct((2, C), f32)],
        [pltpu.VMEM((HALF, LANES), f32), pltpu.VMEM((HALF, WIDE), f32),
         pltpu.VMEM((32, RESTORE_ROWS, B), bf16), pltpu.SemaphoreType.DMA(())],
        2 * rows * B * C,
        2 * rows * B,
    )(pre_two, sums, affine, late)


def view_rows(chunk):
    return (chunk * 16) // PER_VIEW, (chunk * 16 + 8) // PER_VIEW


def fourth_kernel(count, pre_ref, gated_ref, in_sums_ref, affine_ref,
                  out_ref, slope_ref, views_ref):
    for part in range(WIDE // TILE):
        where = slice(part * TILE, (part + 1) * TILE)
        mean, inverse, gain, shift = (
            spread(row) for row in constants(in_sums_ref[:, where], affine_ref[:, where], count)
        )
        totals = [[jnp.zeros((8, TILE), f32) for _ in range(2)] for _ in range(3)]
        for chunk in range(HALF // 16):
            rows = slice(chunk * 16, chunk * 16 + 16)
            unit = (pre_ref[rows, where].astype(f32) - mean) * inverse
            summed = unit * gain + shift + gated_ref[rows, where].astype(f32)
            sigma = sigmoid(summed)
            output = summed * sigma
            slope = sigma + output * (1.0 - sigma)
            out_ref[rows, where] = output.astype(bf16)
            slope_ref[rows, where] = slope.astype(bf16)
            low, high = view_rows(chunk)
            for kind, value in enumerate((output, slope, slope * unit)):
                if low == high:
                    totals[kind][low] = totals[kind][low] + fold(value)
                else:
                    totals[kind][low] = totals[kind][low] + value[0:8]
                    totals[kind][high] = totals[kind][high] + value[8:16]
        for kind in range(3):
            for view in range(2):
                at = 2 * kind + view
                views_ref[0, at : at + 1, where] = jnp.sum(totals[kind][view], 0, keepdims=True)
        views_ref[0, 6:8, where] = jnp.zeros((2, TILE), f32)


def fourth_block(pre_three, gated, sums, affine, count):
    rows = pre_three.shape[0]
    steps = rows // HALF
    return kernel_call(
        functools.partial(fourth_kernel, count),
        (steps, GROUPS),
        [group_spec(), group_spec(), row_spec(sums.shape[0]), row_spec(2)],
        [group_spec(), group_spec(), view_spec(8)],
        [jax.ShapeDtypeStruct((rows, C), bf16), jax.ShapeDtypeStruct((rows, C), bf16),
         jax.ShapeDtypeStruct((steps, 8, C), f32)],
        [],
        20 * rows * C,
        2 * rows * C,
    )(pre_three, gated, sums, affine)


def view_scale(pooled_ref, view, where):
    return spread(pooled_ref[0, view : view + 1, where], 8)


def view_grad_rows(slope, pooled, chunk):
    low, high = view_rows(chunk)
    return slope * jnp.concatenate([pooled[low], pooled[high]], axis=0)


def fifth_kernel(count, slope_ref, pre_three_ref, pooled_ref, sums_three_ref, affine_three_ref,
                 grads_three_ref, late_ref, pre_two_ref, sums_two_ref, affine_two_ref,
                 low_ref, out_ref, sums_ref, natural, restore_ref, semaphore):
    copy = restore_copy(late_ref, restore_ref, semaphore)

    @pl.when(first_step())
    def _():
        copy.start()
        sums_ref[...] = jnp.zeros_like(sums_ref)

    def low_step(step, carry):
        where = lanes(step, TILE)
        mean, inverse, gain, _ = constants(
            sums_three_ref[:, where], affine_three_ref[:, where], count
        )
        scale = spread(gain * inverse)
        offset = spread(grads_three_ref[0:1, where] / count)
        along = spread(grads_three_ref[1:2, where] / count * inverse)
        mean = spread(mean)
        pooled = [view_scale(pooled_ref, view, where) for view in range(2)]
        for chunk in range(HALF // 16):
            rows = slice(chunk * 16, chunk * 16 + 16)
            grad = view_grad_rows(slope_ref[rows, where].astype(f32), pooled, chunk)
            centred = pre_three_ref[rows, where].astype(f32) - mean
            low_ref[rows, where] = (scale * (grad - offset - centred * along)).astype(bf16)
        return carry

    lax.fori_loop(0, C // TILE, low_step, 0)

    @pl.when(first_step())
    def _():
        copy.wait()

    blocks = restore_ref.reshape(8, 4, RESTORE_ROWS, B)

    def product_step(step, carry):
        grad = None
        for quarter in range(4):
            rows = blocks[pl.ds(4 * step, 4), quarter].reshape(TILE, B)
            part = dot_nt(low_ref[:, quarter * B : (quarter + 1) * B], rows)
            grad = part if grad is None else grad + part
        natural[2 * step] = grad[:, 0:LANES]
        natural[2 * step + 1] = grad[:, LANES:TILE]
        return carry

    lax.fori_loop(0, B // TILE, product_step, 0)

    def slope_step(step, carry):
        where = lanes(step, LANES)
        mean, inverse, gain, shift = (
            spread(row) for row in constants(sums_two_ref[:, where], affine_two_ref[:, where], count)
        )
        first = jnp.zeros((16, LANES), f32)
        second = jnp.zeros((16, LANES), f32)
        for cell in range(CELLS):
            rows = slice(cell * 16, cell * 16 + 16)
            unit = (pre_two_ref[rows, where] - mean) * inverse
            norm = unit * gain + shift
            sigma = sigmoid(norm)
            grad = natural[step, pl.ds(cell, 16, stride=CELLS)]
            grad = grad * (sigma * (1.0 + norm * (1.0 - sigma)))
            out_ref[rows, where] = grad
            first = first + grad
            second = second + grad * unit
        add_moments(sums_ref, where, first, second)
        return carry

    lax.fori_loop(0, 4, slope_step, 0)


def fifth_block(slope, pre_three, pooled, sums_three, affine_three, grads_three, late,
                pre_two, sums_two, affine_two, count, after=()):
    rows = slope.shape[0]
    return kernel_call(
        functools.partial(fifth_kernel, count),
        rows // HALF,
        [half_spec(C), half_spec(C), pl.BlockSpec((1, 2, C), lambda step: (step, 0, 0)),
         whole_spec(sums_three.shape), whole_spec((2, C)), whole_spec(grads_three.shape), ANY,
         half_spec(B), whole_spec(sums_two.shape), whole_spec((2, B))],
        [half_spec(C), half_spec(B), whole_out((2, B))],
        [jax.ShapeDtypeStruct((rows, C), bf16), jax.ShapeDtypeStruct((rows, B), f32),
         jax.ShapeDtypeStruct((2, B), f32)],
        [pltpu.VMEM((4, HALF, LANES), f32), pltpu.VMEM((32, RESTORE_ROWS, B), bf16),
         pltpu.SemaphoreType.DMA(())],
        2 * rows * B * C,
        2 * rows * B,
        after=after,
    )(slope, pre_three, pooled, sums_three, affine_three, grads_three, late,
      pre_two, sums_two, affine_two)


def sixth_kernel(count, me_ref, block_a, block_b, block_c, block_d, grad_ref, pre_two_ref, sums_two_ref, affine_two_ref, grads_two_ref,
                 pre_one_ref, sums_one_ref, affine_one_ref,
                 low_ref, out_ref, sums_ref, padded, shifted, tile, natural, spatial_ref,
                 semaphores):
    border = SIDE * 16
    copies = block_copies(me_ref[0], (block_a, block_b, block_c, block_d), spatial_ref, semaphores)

    @pl.when(first_step())
    def _():
        start(copies)
        sums_ref[...] = jnp.zeros_like(sums_ref)
        clear_border(padded)
        shifted[0:border] = jnp.zeros((border, 3 * B), bf16)
        shifted[border + HALF :] = jnp.zeros((border, 3 * B), bf16)

    def low_step(step, carry):
        where = lanes(step, LANES)
        mean, inverse, gain, _ = constants(sums_two_ref[:, where], affine_two_ref[:, where], count)
        scale = spread(gain * inverse)
        offset = spread(grads_two_ref[0:1, where] / count)
        along = spread(grads_two_ref[1:2, where] / count * inverse)
        mean = spread(mean)
        for cell in range(CELLS):
            rows = slice(cell * 16, cell * 16 + 16)
            centred = pre_two_ref[rows, where] - mean
            low = (scale * (grad_ref[rows, where] - offset - centred * along)).astype(bf16)
            low_ref[rows, where] = low
            padded[cell_place(cell)] = low
        for side in range(3):
            at = lanes(side * 4 + step, LANES)
            for cell in range(CELLS):
                shifted[border + cell * 16 : border + cell * 16 + 16, at] = padded[
                    tap_place(cell, 3 + side)
                ]
        return carry

    lax.fori_loop(0, 4, low_step, 0)

    @pl.when(first_step())
    def _():
        wait(copies)

    def product_step(step, carry):
        grad = None
        for tap in range(9):
            top = (tap // 3) * border
            at = (tap % 3) * B
            back = (8 - tap) * 16
            rows = spatial_ref[pl.ds(16 * step, 16), back : back + 16].reshape(TILE, B)
            part = dot_nt(shifted[top : top + HALF, at : at + B], rows)
            grad = part if grad is None else grad + part
        tile[...] = grad
        for half in range(2):
            for cell in range(CELLS):
                natural[2 * step + half, pl.ds(cell, 16, stride=CELLS)] = tile[
                    cell * 16 : cell * 16 + 16, half * LANES : (half + 1) * LANES
                ]
        return carry

    lax.fori_loop(0, B // TILE, product_step, 0)

    def slope_step(step, carry):
        where = lanes(step, LANES)
        mean, inverse, gain, shift = (
            spread(row) for row in constants(sums_one_ref[:, where], affine_one_ref[:, where], count)
        )
        first = jnp.zeros((16, LANES), f32)
        second = jnp.zeros((16, LANES), f32)
        for chunk in range(HALF // 16):
            rows = slice(chunk * 16, chunk * 16 + 16)
            unit = (pre_one_ref[rows, where] - mean) * inverse
            norm = unit * gain + shift
            sigma = sigmoid(norm)
            grad = natural[step, rows] * (sigma * (1.0 + norm * (1.0 - sigma)))
            out_ref[rows, where] = grad
            first = first + grad
            second = second + grad * unit
        add_moments(sums_ref, where, first, second)
        return carry

    lax.fori_loop(0, 4, slope_step, 0)


def sixth_block(me, spatial, grad, pre_two, sums_two, affine_two, grads_two, pre_one, sums_one,
                affine_one, count):
    rows = grad.shape[0]
    deep = HALF + 2 * SIDE * 16
    return kernel_call(
        functools.partial(sixth_kernel, count),
        rows // HALF,
        [SCALAR, ANY, ANY, ANY, ANY, half_spec(B), half_spec(B), whole_spec(sums_two.shape),
         whole_spec((2, B)), whole_spec(grads_two.shape), half_spec(B), whole_spec(sums_one.shape),
         whole_spec((2, B))],
        [half_spec(B), half_spec(B), whole_out((2, B))],
        [jax.ShapeDtypeStruct((rows, B), bf16), jax.ShapeDtypeStruct((rows, B), f32),
         jax.ShapeDtypeStruct((2, B), f32)],
        [pltpu.VMEM((PADDED * PADDED, 16, LANES), bf16), pltpu.VMEM((deep, 3 * B), bf16),
         pltpu.VMEM((HALF, TILE), f32), pltpu.VMEM((4, HALF, LANES), f32),
         pltpu.VMEM((32, SPATIAL_ROWS, B), bf16), pltpu.SemaphoreType.DMA((32,))],
        18 * rows * B * B,
        2 * rows * B,
    )(me, *spatial, grad, pre_two, sums_two, affine_two, grads_two, pre_one, sums_one,
      affine_one)


def low_kernel(count, grad_ref, pre_ref, sums_ref, affine_ref, grads_ref, low_ref):
    def low_step(step, carry):
        where = lanes(step, LANES)
        mean, inverse, gain, _ = constants(sums_ref[:, where], affine_ref[:, where], count)
        scale = spread(gain * inverse)
        offset = spread(grads_ref[0:1, where] / count)
        along = spread(grads_ref[1:2, where] / count * inverse)
        mean = spread(mean)
        for chunk in range(HALF // 16):
            rows = slice(chunk * 16, chunk * 16 + 16)
            centred = pre_ref[rows, where] - mean
            low_ref[rows, where] = (
                scale * (grad_ref[rows, where] - offset - centred * along)
            ).astype(bf16)
        return carry

    lax.fori_loop(0, 4, low_step, 0)


def low_block(grad, pre, sums, affine, grads, count):
    return kernel_call(
        functools.partial(low_kernel, count),
        grad.shape[0] // HALF,
        [half_spec(B), half_spec(B), whole_spec(sums.shape), whole_spec((2, B)),
         whole_spec(grads.shape)],
        half_spec(B),
        jax.ShapeDtypeStruct(grad.shape, bf16),
        [],
        100 * grad.size,
    )(grad, pre, sums, affine, grads)


def gate_back_kernel(me_ref, block_a, block_b, block_c, block_d, low_ref,
                     slope_ref, pooled_ref, tokens_ref, logit_ref,
                     logit_grad_ref, part_ref, tile, reduce_ref, semaphores):
    copies = reduce_copies(me_ref[0], (block_a, block_b, block_c, block_d), reduce_ref, semaphores)
    group = pl.program_id(1)

    @pl.when(very_first())
    def _():
        start(copies)
        wait(copies)

    tile[...] = dot_nt(low_ref[...], reduce_ref[pl.ds(8 * group, 8)].reshape(WIDE, B))
    pooled = [view_scale(pooled_ref, view, slice(0, WIDE)) for view in range(2)]
    for chunk in range(HALF // 16):
        rows = slice(chunk * 16, chunk * 16 + 16)
        grad = tile[rows] + view_grad_rows(slope_ref[rows].astype(f32), pooled, chunk)
        gate = sigmoid(logit_ref[rows].astype(f32))
        token = tokens_ref[rows].astype(f32)
        part = grad * gate
        part_ref[rows] = (grad + part).astype(bf16)
        logit_grad_ref[rows] = (part * (1.0 - gate) * token).astype(bf16)


def gate_back_block(me, pair, low_one, slope, pooled, tokens, logit):
    rows = low_one.shape[0]
    return kernel_call(
        gate_back_kernel,
        (rows // HALF, GROUPS),
        [SCALAR, ANY, ANY, ANY, ANY, half_spec(B), group_spec(), view_spec(2),
         group_spec(), group_spec()],
        [group_spec(), group_spec()],
        [jax.ShapeDtypeStruct((rows, C), bf16), jax.ShapeDtypeStruct((rows, C), bf16)],
        [pltpu.VMEM((HALF, WIDE), f32), pltpu.VMEM((32, C // 32, B), bf16),
         pltpu.SemaphoreType.DMA((32,))],
        2 * rows * C * R,
        2 * rows * C,
    )(me, *pair, low_one, slope, pooled, tokens, logit)


def mixing_back_kernel(me_ref, block_a, block_b, block_c, block_d, logit_grad_ref,
                       upcoming_ref, differ_ref, next_ref, scale_ref, squeezed_ref, kernels_ref,
                       natural, later, ahead, padded, expand_ref, semaphores):
    @pl.when(first_step())
    def _():
        copies = expand_copies(
            me_ref[0], (block_a, block_b, block_c, block_d), expand_ref, semaphores
        )
        start(copies)
        kernels_ref[...] = jnp.zeros_like(kernels_ref)
        clear_border(ahead)
        clear_border(padded)
        later[0:CELLS] = jnp.zeros((CELLS, LANES), f32)
        wait(copies)

    quarters = expand_ref.reshape(8, 4, R // 4, TILE)

    def mixed_step(step, carry):
        grad = None
        for block in range(C // TILE):
            at = slice(block * TILE, (block + 1) * TILE)
            rows = quarters[block, pl.ds(2 * step, 2)].reshape(TILE, TILE)
            part = dot_nt(logit_grad_ref[:, at], rows)
            grad = part if grad is None else grad + part
        natural[2 * step] = grad[:, 0:LANES]
        natural[2 * step + 1] = grad[:, LANES:TILE]
        return carry

    lax.fori_loop(0, R // TILE, mixed_step, 0)
    segment = lax.broadcasted_iota(jnp.int32, (16, LANES), 0) % SEG
    not_last = (segment != SEG - 1).astype(f32)

    def mixing_step(step, carry):
        where = lanes(step, LANES)
        scale_rows = [spread(scale_ref[tap : tap + 1, where]) for tap in range(9)]
        mean = jnp.zeros((16, LANES), f32)
        for cell in range(CELLS):
            grad = natural[step, pl.ds(cell, 16, stride=CELLS)]
            padded[cell_place(cell)] = grad
            mean = mean + grad
            ahead[cell_place(cell)] = differ_ref[cell * 16 : cell * 16 + 16, where]
        mean = mean * (1.0 / CELLS)
        sums = [jnp.zeros((16, LANES), f32) for _ in range(9)]
        for cell in range(CELLS):
            grad = padded[cell_place(cell)]
            for tap in range(9):
                sums[tap] = sums[tap] + ahead[tap_place(cell, tap)] * grad
        for tap in range(9):
            kernels_ref[9 + tap : 10 + tap, where] += jnp.sum(sums[tap], 0, keepdims=True)
        for cell in range(CELLS):
            grad = padded[cell_place(cell)] + mean
            for tap in range(9):
                grad = grad + padded[tap_place(cell, tap)] * scale_rows[8 - tap]
            ahead[cell_place(cell)] = grad
        next_rows = [spread(next_ref[tap : tap + 1, where]) for tap in range(9)]
        for cell in range(CELLS):
            padded[cell_place(cell)] = upcoming_ref[cell * 16 : cell * 16 + 16, where]
        sums = [jnp.zeros((16, LANES), f32) for _ in range(9)]
        for cell in range(CELLS):
            grad = ahead[cell_place(cell)]
            for tap in range(9):
                sums[tap] = sums[tap] + padded[tap_place(cell, tap)] * grad
        for tap in range(9):
            kernels_ref[tap : tap + 1, where] += jnp.sum(sums[tap], 0, keepdims=True)
        for cell in range(CELLS):
            back = ahead[tap_place(cell, 0)] * next_rows[8]
            for tap in range(1, 9):
                back = back + ahead[tap_place(cell, tap)] * next_rows[8 - tap]
            later[pl.ds(cell + CELLS, 16, stride=CELLS)] = back * not_last
            natural[step, pl.ds(cell, 16, stride=CELLS)] = -ahead[cell_place(cell)]
        for chunk in range(HALF // 16):
            rows = slice(chunk * 16, chunk * 16 + 16)
            squeezed_ref[rows, where] = (natural[step, rows] + later[rows]).astype(bf16)
        return carry

    lax.fori_loop(0, 4, mixing_step, 0)


def mixing_back_block(me, pair, logit_grad, upcoming, differ, next_kernel, scale_kernel,
                      after=()):
    rows = logit_grad.shape[0]
    return kernel_call(
        mixing_back_kernel,
        rows // HALF,
        [SCALAR, ANY, ANY, ANY, ANY, half_spec(C), half_spec(R), half_spec(R),
         whole_spec((9, R)), whole_spec((9, R))],
        [half_spec(R), whole_out((18, R))],
        [jax.ShapeDtypeStruct((rows, R), bf16), jax.ShapeDtypeStruct((18, R), f32)],
        [pltpu.VMEM((4, HALF, LANES), f32), pltpu.VMEM((HALF + CELLS + 7, LANES), f32),
         pltpu.VMEM((PADDED * PADDED, 16, LANES), f32),
         pltpu.VMEM((PADDED * PADDED, 16, LANES), f32), pltpu.VMEM((32, R // 4, TILE), bf16),
         pltpu.SemaphoreType.DMA((2, 32))],
        2 * rows * C * R,
        after=after,
    )(me, *pair, logit_grad, upcoming, differ, next_kernel, scale_kernel)


def tokens_kernel(me_ref, block_a, block_b, block_c, block_d, part_ref, squeezed_ref, out_ref,
                  tile, squeeze_ref, semaphores):
    @pl.when(very_first())
    def _():
        copies = block_copies(
            me_ref[0], (block_a, block_b, block_c, block_d), squeeze_ref, semaphores, slice(0, 64)
        )
        start(copies)
        wait(copies)

    tile[...] = dot_nt(
        squeezed_ref[...], squeeze_ref[pl.ds(8 * pl.program_id(1), 8)].reshape(WIDE, R)
    )
    for chunk in range(HALF // 16):
        rows = slice(chunk * 16, chunk * 16 + 16)
        out_ref[rows] = (tile[rows] + part_ref[rows].astype(f32)).astype(bf16)


def tokens_block(me, squeeze, part, squeezed_grad):
    rows = part.shape[0]
    return kernel_call(
        tokens_kernel,
        (rows // HALF, GROUPS),
        [SCALAR, ANY, ANY, ANY, ANY, group_spec(), half_spec(R)],
        group_spec(),
        jax.ShapeDtypeStruct((rows, C), bf16),
        [pltpu.VMEM((HALF, WIDE), f32), pltpu.VMEM((32, C // 32, R), bf16),
         pltpu.SemaphoreType.DMA((32,))],
        2 * rows * C * R,
    )(me, *squeeze, part, squeezed_grad)


def turn(me, values, grain, plain, turned):
    core = me & 1
    plain[...] = values.T
    half = turned.shape[0] // 2
    for group in range(half // grain):
        mine = pl.multiple_of((2 * group + core) * grain, grain)
        other = pl.multiple_of((2 * group + 1 - core) * grain, grain)
        turned[group * grain : (group + 1) * grain] = plain[pl.ds(mine, grain)]
        turned[half + group * grain : half + (group + 1) * grain] = plain[pl.ds(other, grain)]


def store_tiles(found, keep_ref, send_ref):
    half = found.shape[0] // 2
    for tile in range(2):
        at = slice(tile * TILE, (tile + 1) * TILE)
        keep_ref[tile, 0:half] = found[0:half, at]
        send_ref[tile, 0:half] = found[half:, at].astype(bf16)


def outer_kernel(grain, me_ref, narrow_ref, wide_ref, keep_ref, send_ref, plain, turned):
    @pl.when(first_step())
    def _():
        turn(me_ref[0], narrow_ref[...], grain, plain, turned)

    store_tiles(product(turned[...], wide_ref[...]), keep_ref, send_ref)


def outer_block(me, narrow_values, wide_values, grain):
    rows, inner = narrow_values.shape
    blocks = wide_values.shape[1] // TILE
    half = pl.BlockSpec((2, inner // 2, TILE), lambda step: (step, 0, 0))
    return kernel_call(
        functools.partial(outer_kernel, grain),
        blocks // 2,
        [SCALAR, whole_spec((rows, inner)), pl.BlockSpec((rows, 2 * TILE), lambda step: (0, step))],
        [half, half],
        [jax.ShapeDtypeStruct((blocks, inner // 2, TILE), f32),
         jax.ShapeDtypeStruct((blocks, inner // 2, TILE), bf16)],
        [pltpu.VMEM((inner, rows), bf16), pltpu.VMEM((inner, rows), bf16)],
        2 * rows * inner * wide_values.shape[1],
    )(me, narrow_values, wide_values)


def outer_block_of(grain):
    return functools.partial(outer_block, grain=grain)


FEW_ROWS = 40


def restore_outer_kernel(narrow_ref, wide_ref, out_ref, turned):
    @pl.when(first_step())
    def _():
        turned[...] = narrow_ref[...].T

    found = product(turned[...], wide_ref[...])
    out_ref[:, 0] = found.astype(bf16).reshape(8, RESTORE_ROWS, WIDE)


def restore_outer_block(hidden, low_three):
    rows = hidden.shape[0]
    return kernel_call(
        restore_outer_kernel,
        GROUPS,
        [whole_spec((rows, B)), pl.BlockSpec((rows, WIDE), lambda step: (0, step))],
        pl.BlockSpec((8, 1, RESTORE_ROWS, WIDE), lambda step: (0, step, 0, 0)),
        jax.ShapeDtypeStruct((8, 4, RESTORE_ROWS + SPATIAL_ROWS, WIDE), bf16),
        [pltpu.VMEM((B, rows), bf16)],
        2 * rows * B * C,
    )(hidden, low_three)


def spatial_kernel(buffer_ref, hidden_ref, low_ref, out_ref, turned, padded):
    border = SIDE * 16
    halves = hidden_ref.shape[0]

    @pl.when(first_step())
    def _():
        for half in range(halves):
            padded[half, 0 : 2 * border] = jnp.zeros((2 * border, B), bf16)
            padded[half, 2 * border : 2 * border + HALF] = low_ref[half * HALF : (half + 1) * HALF]
            padded[half, 2 * border + HALF :] = jnp.zeros((2 * border, B), bf16)

    step = pl.program_id(0)

    @pl.when(step % 3 == 0)
    def _():
        for half in range(halves):
            turned[half] = hidden_ref[half].T

    top = pl.multiple_of((2 - step % 3) * border, 16)
    found = None
    for half in range(halves):
        part = product(turned[half], padded[half, pl.ds(top, HALF + 2 * border)])
        found = part if found is None else found + part
    out_ref[...] = found.astype(bf16).reshape(32, 16, B)


def spatial_block(buffer, hidden, low_two):
    halves, deep, _ = hidden.shape
    first = RESTORE_ROWS // 16
    return kernel_call(
        spatial_kernel,
        9,
        [ANY, pl.BlockSpec((halves, deep, B), lambda step: (0, 0, step // 3)),
         whole_spec(low_two.shape)],
        pl.BlockSpec((32, 16, B), lambda step: (0, first + (step % 3) * 3 + step // 3, 0)),
        jax.ShapeDtypeStruct(buffer.shape, bf16),
        [pltpu.VMEM((halves, B, deep), bf16),
         pltpu.VMEM((halves, deep + 2 * SIDE * 16, B), bf16)],
        18 * low_two.shape[0] * B * B,
        aliases={0: 0},
    )(buffer, hidden, low_two)


STEM = 64
STEM_SIDE = 16
CHANNELS = 12
SLABS = 19
STEM_LANES = STEM_SIDE * STEM
INPUT_LANES = CHANNELS * 2 * STEM_SIDE
WINDOW = 7


def frames_kernel(frames_ref, out_ref, rows):
    segments = frames_ref.shape[0]
    side = 2 * STEM_SIDE

    def segment_step(segment, carry):
        pieces = [
            frames_ref[segment, index + 1, colour].astype(f32)
            - frames_ref[segment, index, colour].astype(f32)
            for index in range(4)
            for colour in range(3)
        ]
        for group in range(3):
            rows[group, pl.ds(segment, side, stride=segments)] = jnp.concatenate(
                pieces[4 * group : 4 * group + 4], axis=1
            )
        return carry

    lax.fori_loop(0, segments, segment_step, 0)
    empty = jnp.zeros((segments, INPUT_LANES), bf16)
    for parity in range(2):
        for slab in (0, 1, SLABS - 1):
            out_ref[parity, slab] = empty
    for row in range(side):
        for group in range(3):
            out_ref[row % 2, row // 2 + 2, :, group * LANES : (group + 1) * LANES] = rows[
                group, row * segments : (row + 1) * segments
            ].astype(bf16)


def frames_block(frames):
    segments = frames.shape[0] * frames.shape[1]
    ordered = frames.transpose(0, 1, 2, 5, 3, 4).reshape(
        (segments, frames.shape[2], 3) + frames.shape[3:5]
    )
    shape = (2, SLABS, segments, INPUT_LANES)
    return kernel_call(
        frames_kernel,
        1,
        [whole_spec(ordered.shape)],
        whole_out(shape),
        jax.ShapeDtypeStruct(shape, bf16),
        [pltpu.VMEM((3, 2 * STEM_SIDE * segments, LANES), f32)],
        ordered.size * 100,
    )(ordered)


def stem_rows(input_ref, offset):
    parity = 1 - offset % 2
    top = (offset - 3) // 2 + 2 if parity == 0 else (offset - 4) // 2 + 2
    found = input_ref[parity, top : top + STEM_SIDE]
    return found.reshape(-1, INPUT_LANES)


def band_select():
    shape = (STEM_SIDE // 2, CHANNELS, 2 * STEM_SIDE, 2, LANES)
    pair, channel, place, which, entry = (
        lax.broadcasted_iota(jnp.int32, shape, axis) for axis in range(5)
    )
    met = (entry % CHANNELS == channel) & (entry < WINDOW * CHANNELS)
    met = met & (place == 2 * (2 * pair + which) + entry // CHANNELS - 3)
    return met.astype(bf16).reshape(STEM_SIDE // 2, INPUT_LANES, 2 * LANES)


def pair_weights(stem_weight):
    rows = stem_weight.reshape(WINDOW, WINDOW * CHANNELS, STEM)
    rows = jnp.pad(rows, ((0, 0), (0, LANES - WINDOW * CHANNELS), (0, 0)))
    none = jnp.zeros_like(rows)
    return jnp.concatenate(
        [jnp.concatenate([rows, none], 2), jnp.concatenate([none, rows], 2)], 1
    )


def stem_kernel(input_ref, select_ref, weights_ref, pre_ref, sums_ref, bands):
    def step_body(step, carry):
        where = lanes(step, TILE)
        for offset in range(WINDOW):
            for which in range(2):
                band = product(select_ref[2 * step + which], weights_ref[offset])
                bands[offset, :, which * LANES : (which + 1) * LANES] = band.astype(bf16)
        found = None
        for offset in range(WINDOW):
            part = product(stem_rows(input_ref, offset), bands[offset])
            found = part if found is None else found + part
        pre_ref[:, where] = found
        sums_ref[0:1, where] = jnp.sum(found, 0, keepdims=True)
        sums_ref[1:2, where] = jnp.sum(found * found, 0, keepdims=True)
        return carry

    lax.fori_loop(0, STEM_LANES // TILE, step_body, 0)


def stem_block(inputs, select, weights, after=()):
    rows = inputs.shape[2] * STEM_SIDE
    return kernel_call(
        stem_kernel,
        1,
        [whole_spec(inputs.shape), whole_spec(select.shape), whole_spec(weights.shape)],
        [whole_out((rows, STEM_LANES)), whole_out((2, STEM_LANES))],
        [jax.ShapeDtypeStruct((rows, STEM_LANES), f32),
         jax.ShapeDtypeStruct((2, STEM_LANES), f32)],
        [pltpu.VMEM((WINDOW, INPUT_LANES, TILE), bf16)],
        2 * WINDOW * rows * INPUT_LANES * STEM_LANES,
        after=after,
    )(inputs, select, weights)


def stem_norm_kernel(count, pre_ref, in_sums_ref, affine_ref, cotangent_ref,
                     out_ref, grad_ref, sums_ref):
    def step_body(step, carry):
        where = lanes(step, LANES)
        mean, inverse, gain, shift = (
            spread(row) for row in constants(in_sums_ref[:, where], affine_ref[:, where], count)
        )
        first = jnp.zeros((16, LANES), f32)
        second = jnp.zeros((16, LANES), f32)
        for chunk in range(pre_ref.shape[0] // 16):
            rows = slice(chunk * 16, chunk * 16 + 16)
            unit = (pre_ref[rows, where] - mean) * inverse
            norm = unit * gain + shift
            sigma = sigmoid(norm)
            output = norm * sigma
            out_ref[rows, where] = output.astype(bf16)
            grad = cotangent_ref[rows, where].astype(f32) * (sigma + output * (1.0 - sigma))
            grad_ref[rows, where] = grad
            first = first + grad
            second = second + grad * unit
        sums_ref[0:1, where] = jnp.sum(first, 0, keepdims=True)
        sums_ref[1:2, where] = jnp.sum(second, 0, keepdims=True)
        return carry

    lax.fori_loop(0, STEM_LANES // LANES, step_body, 0)


def stem_norm_block(pre, sums, affine, cotangent, count, after=()):
    shape = pre.shape
    return kernel_call(
        functools.partial(stem_norm_kernel, count),
        1,
        [whole_spec(shape), whole_spec(sums.shape), whole_spec(affine.shape), whole_spec(shape)],
        [whole_out(shape), whole_out(shape), whole_out((2, STEM_LANES))],
        [jax.ShapeDtypeStruct(shape, bf16), jax.ShapeDtypeStruct(shape, f32),
         jax.ShapeDtypeStruct((2, STEM_LANES), f32)],
        [],
        4000 * pre.size,
        after=after,
    )(pre, sums, affine, cotangent)


def stem_back_kernel(count, input_ref, select_ref, pre_ref, in_sums_ref, affine_ref, grad_ref,
                     grads_ref, out_ref, low, turned):
    def low_step(step, carry):
        where = lanes(step, LANES)
        mean, inverse, gain, _ = constants(in_sums_ref[:, where], affine_ref[:, where], count)
        scale = spread(gain * inverse)
        offset = spread(grads_ref[0:1, where] / count)
        along = spread(grads_ref[1:2, where] / count * inverse)
        mean = spread(mean)
        for chunk in range(pre_ref.shape[0] // 16):
            rows = slice(chunk * 16, chunk * 16 + 16)
            centred = pre_ref[rows, where] - mean
            low[rows, where] = (
                scale * (grad_ref[rows, where] - offset - centred * along)
            ).astype(bf16)
        return carry

    lax.fori_loop(0, STEM_LANES // LANES, low_step, 0)
    out_ref[...] = jnp.zeros_like(out_ref)

    for offset in range(WINDOW):
        turned[offset] = stem_rows(input_ref, offset).T

    def step_body(step, carry):
        where = lanes(step, TILE)
        for offset in range(WINDOW):
            band = product(turned[offset], low[:, where]).astype(bf16)
            found = product(select_ref[2 * step], band[:, 0:LANES]) + product(
                select_ref[2 * step + 1], band[:, LANES:TILE]
            )
            out_ref[offset] += found
        return carry

    lax.fori_loop(0, STEM_LANES // TILE, step_body, 0)


def stem_back_block(inputs, select, pre, sums, affine, grad, grads, count, after=()):
    shape = pre.shape
    out = (WINDOW, 2 * LANES, LANES)
    return kernel_call(
        functools.partial(stem_back_kernel, count),
        1,
        [whole_spec(inputs.shape), whole_spec(select.shape), whole_spec(shape),
         whole_spec(sums.shape), whole_spec(affine.shape), whole_spec(shape),
         whole_spec(grads.shape)],
        whole_out(out),
        jax.ShapeDtypeStruct(out, f32),
        [pltpu.VMEM(shape, bf16), pltpu.VMEM((WINDOW, INPUT_LANES, shape[0]), bf16)],
        2 * WINDOW * shape[0] * INPUT_LANES * STEM_LANES,
        after=after,
    )(inputs, select, pre, sums, affine, grad, grads)


SMALL_ROWS = 32
FIRST_ROWS = 64 + SMALL_ROWS


def cut_kernel(me_ref, squeeze_ref, expand_ref, reduce_ref, spatial_ref, restore_ref, class_ref,
               stem_ref, next_ref, scale_ref, outer_ref, gain_one_ref, shift_one_ref,
               gain_two_ref, shift_two_ref, stem_gain_ref, stem_shift_ref,
               first_out, pair_out, spatial_out, late_out, small):
    part = me_ref[0] & 3
    first_out[0:64] = squeeze_ref[pl.ds(pl.multiple_of(part * 64, 64), 64)]
    small[...] = jnp.zeros_like(small)
    edge = stem_ref.shape[1] - B
    small[0:8] = stem_ref[:, 0:B].astype(f32)
    small[8:16, 0:edge] = stem_ref[:, B:].astype(f32)
    small[16:25, 0 : next_ref.shape[1]] = next_ref[...].astype(f32)
    small[16:25, LANES : LANES + scale_ref.shape[1]] = scale_ref[...].astype(f32)
    small[25:26] = outer_ref[...].astype(f32)
    for place, ref in enumerate((gain_one_ref, shift_one_ref, gain_two_ref, shift_two_ref)):
        small[26:27, place * LANES : place * LANES + ref.shape[1]] = ref[...].astype(f32)
    small[27:28, 0 : stem_gain_ref.shape[1]] = stem_gain_ref[...].astype(f32)
    small[27:28, LANES : LANES + stem_shift_ref.shape[1]] = stem_shift_ref[...].astype(f32)
    first_out[64:] = small[...].astype(bf16)
    pair_out[0:PAIR_ROWS] = reduce_ref[pl.ds(pl.multiple_of(part * 64, 64), 64)]
    for half in range(2):
        pair_out[PAIR_ROWS:, half * TILE : (half + 1) * TILE] = expand_ref[
            pl.ds(pl.multiple_of(part * 128 + half * 64, 64), 64)
        ]
    for tap in range(9):
        spatial_out[tap * 16 : tap * 16 + 16] = spatial_ref[
            tap, pl.ds(pl.multiple_of(part * 16, 16), 16)
        ]
    late_out[0:RESTORE_ROWS] = restore_ref[:, pl.ds(pl.multiple_of(part * B, B), B)]
    for half in range(2):
        rows = pl.ds(pl.multiple_of(part * 64 + half * 32, 32), 32)
        late_out[RESTORE_ROWS:, half * TILE : (half + 1) * TILE] = class_ref[rows]


def cut_block(me, *weights):
    shapes = [(FIRST_ROWS, B), (2 * PAIR_ROWS, B), (SPATIAL_ROWS, B), (LATE_ROWS, B)]
    return kernel_call(
        cut_kernel,
        1,
        [SCALAR] + [whole_spec(weight.shape) for weight in weights],
        [whole_out(shape) for shape in shapes],
        [jax.ShapeDtypeStruct(shape, bf16) for shape in shapes],
        [pltpu.VMEM((SMALL_ROWS, B), f32)],
        1000000,
    )(me, *weights)


def unpack_kernel(me_ref, first_ref, weights_out, next_out, scale_out, one_out, two_out,
                  three_out, stem_out):
    wide = first_ref.shape[0]
    small = []
    for index in range(wide):
        mask = (me_ref[0] >> 2) ^ index
        entry = (mask & 1) * 4 + (mask >> 1)
        small.append(first_ref[entry, 64:].astype(f32))

    def joined(row, at, width, rows=1):
        return jnp.concatenate(
            [values[row : row + rows, at : at + width] for values in small], axis=1
        )

    own = B // wide
    next_out[...] = joined(16, 0, own, 9)
    scale_out[...] = joined(16, LANES, own, 9)
    one_out[0:1] = joined(26, 0, own)
    one_out[1:2] = joined(26, LANES, own)
    two_out[0:1] = joined(26, 2 * LANES, own)
    two_out[1:2] = joined(26, 3 * LANES, own)
    three_out[0:1] = joined(25, 0, TILE)
    three_out[1:2] = joined(25, TILE, TILE)
    for row in range(2):
        stem = joined(27, row * LANES, STEM // wide)
        stem_out[row : row + 1] = jnp.concatenate([stem] * STEM_SIDE, axis=1)
    columns = jnp.concatenate(
        [jnp.concatenate([values[0:8], values[8:16, 0:LANES]], axis=1) for values in small], axis=0
    )
    rows = columns.T
    place = lax.broadcasted_iota(jnp.int32, (LANES, STEM), 0)
    none = jnp.zeros((LANES, STEM), f32)
    for offset in range(WINDOW):
        top = offset * WINDOW * CHANNELS
        block = jnp.where(place < WINDOW * CHANNELS, rows[top : top + LANES], 0.0)
        weights_out[offset, 0:LANES] = jnp.concatenate([block, none], axis=1).astype(bf16)
        weights_out[offset, LANES:] = jnp.concatenate([none, block], axis=1).astype(bf16)


def unpack_block(me, first):
    shapes = [
        ((WINDOW, 2 * LANES, LANES), bf16), ((9, R), f32), ((9, R), f32), ((2, B), f32),
        ((2, B), f32), ((2, C), f32), ((2, STEM_LANES), f32),
    ]
    return kernel_call(
        unpack_kernel,
        1,
        [SCALAR, whole_spec(first.shape)],
        [whole_out(shape) for shape, _ in shapes],
        [jax.ShapeDtypeStruct(shape, kind) for shape, kind in shapes],
        [],
        1000000,
    )(me, first)


def shards(
    frames,
    tokens,
    stem_cotangent,
    crop_counts,
    labels,
    stem_weight,
    stem_gain,
    stem_shift,
    w_squeeze,
    next_kernel,
    scale_kernel,
    w_expand,
    w_reduce,
    gain_one,
    shift_one,
    w_spatial,
    gain_two,
    shift_two,
    w_restore,
    gain_three,
    shift_three,
    w_class,
    class_bias,
):
    view_count = frames.shape[0]
    row_count = tokens.shape[0]
    devices = lax.axis_size(AXES)
    wide = lax.axis_size("wide")
    narrow = lax.axis_size("narrow")
    count = float(row_count * devices)
    segments = view_count * SEG
    stem_rows_here = segments * STEM_SIDE
    stem_count = float(stem_rows_here * STEM_SIDE * devices)
    direct = wide == C // TILE and narrow == 4
    me = lax.axis_index(AXES)
    me_array = (me if direct else 0 * me).astype(jnp.int32).reshape(1)

    stem_width = stem_weight.shape[1]
    inner_width = gain_one.shape[0]
    outer_width = gain_three.shape[0]
    select = band_select()
    cotangent = stem_cotangent.reshape(segments, STEM_SIDE, STEM_LANES)
    cotangent = cotangent.transpose(1, 0, 2).reshape(stem_rows_here, STEM_LANES)
    if direct:
        first_own, pair_own, spatial_own, late_own = cut_block(
            me_array, w_squeeze, w_expand, w_reduce, w_spatial, w_restore,
            jnp.pad(w_class, ((0, 0), (0, TILE - CLASSES))), stem_weight.T, next_kernel,
            scale_kernel, jnp.concatenate([gain_three, shift_three])[None], gain_one[None],
            shift_one[None], gain_two[None], shift_two[None], stem_gain[None], stem_shift[None],
        )
        firsts, pairs, spatials = Gather(first_own), Gather(pair_own), Gather(spatial_own)
        (cotangent, select), came, _ = beside(
            lambda grads, band: (grads, band), [cotangent, select], firsts.depth()
        )
        firsts.take_depth(came)
        inputs, came, _ = beside(frames_block, [frames], firsts.second() + pairs.depth())
        firsts.take_second(came[:1])
        pairs.take_depth(came[1:])
        squeeze_own = firsts.eight[:, 0:64]
        (
            weights, full_next, full_scale, affine_one, affine_two, affine_three, stem_affine,
        ) = unpack_block(me_array, firsts.eight)
        (stem_pre, stem_part), came, _ = beside(
            stem_block, [inputs, select, weights],
            [(squeeze_own, 2)] + pairs.second() + spatials.depth(),
        )
        squeeze_far = came[0]
        pairs.take_second(came[1:2])
        spatials.take_depth(came[2:])
        stem_pre, came, _ = beside(
            lambda values: values, [stem_pre], [(squeeze_own, 1), (squeeze_far, 1)]
        )
        squeeze = (squeeze_own, squeeze_far) + tuple(came)
    else:
        squeeze, pair, spatial, late = gathered(
            w_squeeze, w_expand, w_reduce, w_spatial, w_restore, w_class
        )

        def whole(values):
            return lax.all_gather(values, "wide", axis=values.ndim - 1, tiled=True).astype(f32)

        weights = pair_weights(whole(stem_weight).astype(bf16))
        full_next, full_scale = whole(next_kernel), whole(scale_kernel)
        affine_one = jnp.stack([whole(gain_one), whole(shift_one)])
        affine_two = jnp.stack([whole(gain_two), whole(shift_two)])
        affine_three = jnp.stack([whole(gain_three), whole(shift_three)])
        stem_affine = jnp.tile(jnp.stack([whole(stem_gain), whole(stem_shift)]), (1, STEM_SIDE))
        inputs = frames_block(frames)
        stem_pre, stem_part = stem_block(inputs, select, weights)
    stem_part = stem_part.reshape(2, STEM_SIDE, STEM).sum(1).reshape(1, 2 * STEM)

    def stem_lanes(sums):
        return jnp.tile(sums[2, : 2 * STEM].reshape(2, STEM), (1, STEM_SIDE))

    def with_row(sums, row):
        return jnp.concatenate([sums, jnp.pad(row, ((0, 0), (0, sums.shape[1] - row.shape[1])))])

    mixing_operands = [me_array, squeeze, tokens, full_next, full_scale]
    if direct:
        (upcoming, differ, mixed_low), came, _ = beside(
            mixing_block, mixing_operands, pairs.third() + spatials.second()
        )
        pairs.take_third(came[:1])
        spatials.take_second(came[1:])
        (mixed_low, late_own), came, _ = beside(
            lambda values, mine: (values, mine), [mixed_low, late_own], pairs.core()
        )
        pairs.take_core(came)
        late = lax.all_gather(late_own, AXES)
        pair = pairs.arrays
    else:
        upcoming, differ, mixed_low = mixing_block(*mixing_operands)
    gate_operands = [me_array, pair, tokens, mixed_low]
    if direct:
        (logit, gated_low, pre_one, one_part), came, _ = beside(
            gate_block, gate_operands, spatials.third()
        )
        spatials.take_third(came)
        one_sums, came, _ = beside(swap_total, [with_row(one_part, stem_part)], spatials.core())
        spatials.take_core(came)
        spatial = spatials.arrays
    else:
        logit, gated_low, pre_one, one_part = gate_block(*gate_operands)
        one_sums = swap_total(with_row(one_part, stem_part))
    stem_sums = stem_lanes(one_sums)
    hidden_one, pre_two, two_part = second_block(
        me_array, spatial, pre_one, one_sums, affine_one, count
    )
    stem_out, stem_norm_grad, stem_part = stem_norm_block(
        stem_pre, stem_sums, stem_affine, cotangent, stem_count
    )
    stem_part = stem_part.reshape(2, STEM_SIDE, STEM).sum(1).reshape(1, 2 * STEM)
    two_sums = swap_total(two_part)
    hidden_two, pre_three, three_part = third_block(pre_two, two_sums, affine_two, late, count)
    three_sums = total(with_row(three_part, stem_part))
    stem_grads = stem_lanes(three_sums)
    activations, slope, view_sums = fourth_block(
        pre_three, gated_low, three_sums, affine_three, count
    )
    stem_features = stem_out.reshape(STEM_SIDE, segments, STEM_LANES)
    stem_features = stem_features.transpose(1, 0, 2).reshape(-1, STEM)

    def of_views(kind):
        return view_sums[:, 2 * kind : 2 * kind + 2].reshape(view_count, C)

    pooled_low = (of_views(0) / PER_VIEW).astype(bf16)

    full_class = late[:, RESTORE_ROWS:].reshape(32, CLASS_ROWS, 2, TILE)
    full_class = full_class.transpose(0, 2, 1, 3).reshape(C, TILE)[:, :CLASSES]
    view_logits = product(pooled_low, full_class) + class_bias.astype(f32)

    ends = jnp.cumsum(crop_counts)
    starts = ends - crop_counts
    positions = (me - 1) * view_count + jnp.arange(3 * view_count, dtype=jnp.int32)
    video = jnp.sum((ends[None, :] <= positions[:, None]).astype(jnp.int32), 1)
    own_video = video[view_count : 2 * view_count]
    belongs = (
        own_video[:, None] == jnp.arange(crop_counts.shape[0], dtype=jnp.int32)[None, :]
    ).astype(jnp.int32)
    own_count = jnp.sum(belongs * crop_counts[None, :], 1).astype(f32)
    own_label = jnp.sum(belongs * labels[None, :], 1)
    own_start = jnp.sum(belongs * starts[None, :], 1)
    first = (own_start == positions[view_count : 2 * view_count]).astype(f32)
    same = (own_video[:, None] == video[None, :]).astype(f32) / own_count[:, None]
    target = (own_label[:, None] == jnp.arange(CLASSES, dtype=jnp.int32)[None, :]).astype(f32)

    before = lax.ppermute(view_logits, AXES, [(i, i + 1) for i in range(devices - 1)])
    following = lax.ppermute(view_logits, AXES, [(i + 1, i) for i in range(devices - 1)])
    near = jnp.concatenate([before, view_logits, following])
    video_logits = jnp.sum(same[:, :, None] * near[None, :, :], 1)
    log_probs = jax.nn.log_softmax(video_logits, axis=-1)
    entropy_part = jnp.sum(first * -jnp.sum(target * log_probs, axis=-1))
    video_grad = loss_scale * (jnp.exp(log_probs) - target)
    bias_part = jnp.sum(first[:, None] * video_grad, 0)
    view_grad_low = (video_grad / own_count[:, None]).astype(bf16)

    factors = jnp.concatenate(
        [pooled_low, jnp.pad(view_grad_low, ((0, 0), (0, TILE - CLASSES)))], axis=1
    )
    factors = jnp.pad(factors, ((0, -view_count % 8), (0, 0)))

    pooled_grad = product_right(view_grad_low, full_class) / PER_VIEW
    part_row = jnp.concatenate([bias_part, entropy_part[None]])[None]
    three_part = jnp.stack([jnp.sum(pooled_grad * of_views(kind), 0) for kind in (1, 2)])
    three_grads = total(with_row(three_part, part_row))
    class_bias_grad = three_grads[2, :CLASSES]
    loss = three_grads[2, CLASSES] / crop_counts.shape[0]
    pooled_grad = pooled_grad.reshape(-1, 2, C)

    fifth_operands = [
        slope, pre_three, pooled_grad, three_sums, affine_three, three_grads, late,
        pre_two, two_sums, affine_two,
    ]
    run_fifth = functools.partial(fifth_block, count=count)
    run_sixth = functools.partial(sixth_block, count=count)
    run_stem_back = functools.partial(stem_back_block, count=stem_count)

    def stem_back_operands():
        return [inputs, select.swapaxes(1, 2), stem_pre, stem_sums, stem_affine, stem_norm_grad, stem_grads]
    run_low = functools.partial(low_block, count=count)
    run_outer = outer_block_of(R // 4)

    def sixth_operands():
        return [
            me_array, spatial, norm_two_grad, pre_two, two_sums, affine_two, two_grads, pre_one,
            one_sums, affine_one,
        ]

    def low_operands():
        return [norm_one_grad, pre_one, one_sums, affine_one, one_grads]

    def gate_back_operands():
        return [me_array, pair, low_one, slope, pooled_grad, tokens, logit]

    def mixing_back_operands():
        return [me_array, pair, logit_grad, upcoming, differ, full_next, full_scale]

    def few_of(stem_back, kernel_grads):
        stem_back = stem_back[:, :LANES, :STEM] + stem_back[:, LANES:, STEM:]
        stem_grad = stem_back[:, : WINDOW * CHANNELS].reshape(-1, STEM)
        stem_cut = stem_grad.T.reshape(8, 8, -1)
        stem_cut = jnp.pad(stem_cut, ((0, 0), (0, 0), (0, 3 * TILE - stem_cut.shape[2])))
        kernel_cut = kernel_grads.reshape(2, 9, 8, R // 8).transpose(2, 1, 0, 3)
        kernel_cut = jnp.pad(kernel_cut, ((0, 0), (0, 0), (0, 0), (0, LANES - R // 8)))
        few = jnp.concatenate([stem_cut.reshape(8, 24, TILE), kernel_cut.reshape(8, 9, TILE)], 1)
        return jnp.pad(few, ((0, 0), (0, FEW_ROWS - few.shape[1]), (0, 0)))

    if direct:
        views = Gather(factors)
        (low_three, norm_two_grad, two_part), came, _ = beside(
            run_fifth, fifth_operands, views.depth()
        )
        views.take_depth(came)
        (buffer, two_grads), came, _ = beside(
            lambda hidden, low, part: (restore_outer_block(hidden, low), swap_total(part)),
            [hidden_two, low_three, two_part], views.second(),
        )
        views.take_second(came)
        (low_two, norm_one_grad, one_part), came, _ = beside(
            run_sixth, sixth_operands(), views.third()
        )
        views.take_third(came)
        (buffer, one_grads), came, _ = beside(
            lambda values, hidden, low, part: (
                spatial_block(values.reshape(32, -1, WIDE), hidden, low), swap_total(part)
            ),
            [buffer, hidden_one, low_two, one_part], views.core(),
        )
        views.take_core(came)
        buffer = lax.psum_scatter(
            buffer.reshape(8, -1, WIDE), "wide", scatter_dimension=0, tiled=False
        )
        quarter = (4, 2, 2, R // 4, TILE)
        low_one = run_low(*low_operands())
        reduced_sum = Sum(run_outer(me_array, low_one, gated_low), quarter, 0)
        low_one, came, _ = beside(lambda values: values, [low_one], reduced_sum.core())
        reduced_sum.take_core(came)
        (logit_grad, tokens_part), came, _ = beside(
            gate_back_block, gate_back_operands(), reduced_sum.split("x")
        )
        reduced_sum.take(came)
        expand_half, came, _ = beside(
            run_outer, [me_array, mixed_low, logit_grad], reduced_sum.split("y")
        )
        reduced_sum.take(came)
        expand_sum = Sum(expand_half, quarter, 0)
        logit_grad, came, _ = beside(lambda values: values, [logit_grad], expand_sum.core())
        expand_sum.take_core(came)
        (low_squeezed, kernel_grads), came, _ = beside(
            mixing_back_block, mixing_back_operands(),
            expand_sum.split("x") + reduced_sum.split("z"),
        )
        expand_sum.take(came[:1])
        reduced_sum.take(came[1:])
        squeeze_half, came, _ = beside(
            run_outer, [me_array, low_squeezed, tokens],
            expand_sum.split("y") + reduced_sum.spread(),
        )
        expand_sum.take(came[:1])
        reduced_sum.take_spread(came[1:])
        squeezed = Sum(squeeze_half, quarter, 0)
        tokens_part, came, _ = beside(lambda values: values, [tokens_part], squeezed.core())
        squeezed.take_core(came)
        stem_back, came, _ = beside(
            run_stem_back, stem_back_operands(), squeezed.split("x") + expand_sum.split("z")
        )
        squeezed.take(came[:1])
        expand_sum.take(came[1:])
        few = few_of(stem_back, kernel_grads)
        (tokens_grad, few, buffer), came, _ = beside(
            lambda mine, blocks, part, low, grads, quarters: (
                tokens_block(mine, blocks, part, low),
                lax.all_to_all(grads, "wide", 0, 0, tiled=True),
                lax.all_to_all(quarters, "narrow", 0, 0, tiled=True),
            ),
            [me_array, squeeze, tokens_part, low_squeezed, few, buffer.reshape(4, -1, WIDE)],
            squeezed.split("y") + expand_sum.spread(),
        )
        buffer = jnp.sum(buffer.astype(f32), 0)
        squeezed.take(came[:1])
        expand_sum.take_spread(came[1:])
        few = jnp.sum(few, 0)
        few, came, _ = beside(
            lambda part: part + exchange(part, 1), [few], squeezed.split("z")
        )
        squeezed.take(came)
        buffers = Sum((None, None), (), 0)
        buffers.values = buffer
        few, came, _ = beside(
            lambda part: part + exchange(part, 2), [few], squeezed.spread() + buffers.spread()
        )
        squeezed.take_spread(came[:3])
        buffers.take_spread(came[3:])
        buffer = buffers.whole
        sum_stem = few[:24].reshape(8, 3 * TILE)[:, : stem_weight.shape[0]].T
        sum_next = few[24:33, :inner_width]
        sum_scale = few[24:33, LANES : LANES + inner_width]
        sum_restore = buffer[:, :RESTORE_ROWS].swapaxes(0, 1).reshape(w_restore.shape)
        sum_spatial = buffer[:, RESTORE_ROWS:].reshape(4, 9, 16, B).swapaxes(0, 1)
        sum_spatial = sum_spatial.reshape(w_spatial.shape)
        sum_reduce = reduced_sum.whole.reshape(B, TILE).T
        sum_expand = expand_sum.whole.reshape(R, TILE)
        sum_squeeze = squeezed.whole.reshape(R, TILE).T
        factors = [array.reshape(-1, C + TILE) for array in views.arrays]
    else:
        low_three, norm_two_grad, two_part = run_fifth(*fifth_operands)
        buffer = restore_outer_block(hidden_two, low_three)
        two_grads = swap_total(two_part)
        low_two, norm_one_grad, one_part = run_sixth(*sixth_operands())
        one_grads = swap_total(one_part)
        buffer = spatial_block(buffer.reshape(32, -1, WIDE), hidden_one, low_two)
        low_one = run_low(*low_operands())
        reduce_half = run_outer(me_array, low_one, gated_low)
        logit_grad, tokens_part = gate_back_block(*gate_back_operands())
        expand_half = run_outer(me_array, mixed_low, logit_grad)
        low_squeezed, kernel_grads = mixing_back_block(*mixing_back_operands())
        few = few_of(run_stem_back(*stem_back_operands()), kernel_grads)
        squeeze_half = run_outer(me_array, low_squeezed, tokens)
        tokens_grad = tokens_block(me_array, squeeze, tokens_part, low_squeezed)
        few = lax.psum(few, AXES)
        sum_stem = few[:, :24].reshape(STEM, 3 * TILE)[:, : stem_weight.shape[0]].T
        sum_next, sum_scale = (
            few[:, 24:33, at : at + R // 8].swapaxes(0, 1).reshape(9, R) for at in (0, LANES)
        )

        def own_columns(values, width):
            return lax.dynamic_slice_in_dim(values, lax.axis_index("wide") * width, width, 1)

        sum_stem = own_columns(sum_stem, stem_width)
        sum_next = own_columns(sum_next, inner_width)
        sum_scale = own_columns(sum_scale, inner_width)
        sum_restore, sum_spatial, sum_reduce, sum_expand, sum_squeeze = reduced(
            buffer, reduce_half, expand_half, squeeze_half
        )
        factors = [lax.all_gather(factors, AXES, tiled=True)]
    sum_class = sum(
        product_left(
            lax.dynamic_slice_in_dim(part, lax.axis_index("wide") * outer_width, outer_width, 1),
            part[:, C : C + CLASSES],
        )
        for part in factors
    )
    def own_slice(values, width):
        return lax.dynamic_slice_in_dim(values, lax.axis_index("wide") * width, width)

    return (
        activations,
        stem_features,
        tokens_grad,
        sum_stem,
        own_slice(stem_grads[1, :STEM], stem_width),
        own_slice(stem_grads[0, :STEM], stem_width),
        sum_squeeze,
        sum_next,
        sum_scale,
        sum_expand,
        sum_reduce,
        own_slice(one_grads[1], inner_width),
        own_slice(one_grads[0], inner_width),
        sum_spatial,
        own_slice(two_grads[1], inner_width),
        own_slice(two_grads[0], inner_width),
        sum_restore,
        own_slice(three_grads[1], outer_width),
        own_slice(three_grads[0], outer_width),
        sum_class,
        class_bias_grad,
        loss,
    )


def solution(mesh):
    in_specs = (
        P(("wide", "narrow"), None, None, None, None, None),
        P(("wide", "narrow"), None),
        P(("wide", "narrow"), None),
        P(),
        P(),
        P(None, "wide"),
        P("wide"),
        P("wide"),
        P("wide", None),
        P(None, "wide"),
        P(None, "wide"),
        P(None, "wide"),
        P("wide", None),
        P("wide"),
        P("wide"),
        P(None, "wide", None),
        P("wide"),
        P("wide"),
        P("wide", None),
        P("wide"),
        P("wide"),
        P("wide", None),
        P(),
    )
    out_specs = (
        P(("wide", "narrow"), None),
        P(("wide", "narrow"), None),
        P(("wide", "narrow"), None),
        P(None, "wide"),
        P("wide"),
        P("wide"),
        P("wide", None),
        P(None, "wide"),
        P(None, "wide"),
        P(None, "wide"),
        P("wide", None),
        P("wide"),
        P("wide"),
        P(None, "wide", None),
        P("wide"),
        P("wide"),
        P("wide", None),
        P("wide"),
        P("wide"),
        P("wide", None),
        P(),
        P(),
    )
    return jax.shard_map(shards, mesh=mesh, in_specs=in_specs, out_specs=out_specs, check_vma=False)
```

```python
import functools

import jax
import jax.numpy as jnp
from jax import lax
from jax.experimental import pallas as pl
from jax.experimental.pallas import tpu as pltpu
from jax.sharding import PartitionSpec as P

C = 2048
B = 512
R = 512
CLASSES = 174
SEG = 8
SIDE = 7
PER_VIEW = SEG * SIDE * SIDE

epsilon = 1e-05
loss_scale = 1024.0

AXES = ("wide", "narrow")
f32 = jnp.float32
bf16 = jnp.bfloat16


def product(first_operand, second_operand):
    return jnp.dot(first_operand, second_operand, preferred_element_type=f32)


def product_left(first_operand, second_operand):
    return lax.dot_general(
        first_operand, second_operand, (((0,), (0,)), ((), ())), preferred_element_type=f32
    )


def product_right(first_operand, second_operand):
    return lax.dot_general(
        first_operand, second_operand, (((1,), (1,)), ((), ())), preferred_element_type=f32
    )


def exchange(values, mask):
    size = lax.axis_size(AXES)
    return lax.ppermute(values, AXES, [(index, index ^ mask) for index in range(size)])


def own_bit(bit):
    return (lax.axis_index(AXES) >> bit) & 1


def total(values):
    bits = lax.axis_size(AXES).bit_length() - 1
    values = values + exchange(values, 1)
    for bit in range(1, bits, 2):
        masks = [1 << bit]
        if bit + 1 < bits:
            masks += [2 << bit, 3 << bit]
        parts = [exchange(values, mask) for mask in masks]
        for part in parts:
            values = values + part
    return values


def swap_total(values):
    size = lax.axis_size(AXES)
    copies = jnp.broadcast_to(values[None], (size,) + values.shape)
    return jnp.sum(lax.all_to_all(copies, AXES, 0, 0, tiled=True), 0)


def beside(run, inputs, sends, more=()):
    inputs, arrays = lax.optimization_barrier((tuple(inputs), [array for array, _ in sends]))
    came = [exchange(array, mask) for array, (_, mask) in zip(arrays, sends)]
    return lax.optimization_barrier((run(*inputs), came, tuple(more)))


def launch(run, inputs, sends):
    inputs, arrays = lax.optimization_barrier((tuple(inputs), [array for array, _ in sends]))
    came = [exchange(array, mask) for array, (_, mask) in zip(arrays, sends)]
    return lax.optimization_barrier(run(*inputs)), came


class Gather:
    def __init__(self, block):
        self.block = block

    def depth(self):
        return [(self.block, mask) for mask in (8, 16, 24)]

    def take_depth(self, came):
        self.four = join([part[None] for part in (self.block, *came)])

    def second(self):
        return [(self.four, 4)]

    def take_second(self, came):
        self.eight = join([self.four, came[0]])

    def third(self):
        return [(self.eight, 2)]

    def take_third(self, came):
        self.other = came[0]

    def core(self):
        return [(self.eight, 1), (self.other, 1)]

    def take_core(self, came):
        self.arrays = (self.eight, self.other) + tuple(came)


class HalvedGather(Gather):
    def take_second(self, came):
        self.parts = [self.four, came[0]]
        self.far = [None, None]
        self.arrays = [None] * 8

    def third_of(self, part):
        return [(self.parts[part], 2)]

    def take_third_of(self, part, came):
        self.far[part] = came[0]

    def core_of(self, part):
        return [(self.parts[part], 1), (self.far[part], 1)]

    def take_core_of(self, part, came):
        self.arrays[part::2] = [self.parts[part], self.far[part], came[0], came[1]]


class Sum:
    def __init__(self, half, shape, lead):
        self.keep, self.send = half
        self.shape, self.lead, self.axes = shape, lead, "zyx"

    def core(self):
        return [(self.send, 1)]

    def take_core(self, came):
        self.values = (self.keep + came[0].astype(f32)).reshape(self.shape)

    def split(self, letter):
        place = self.lead + self.axes.index(letter)
        self.axes = self.axes.replace(letter, "")
        bit = {"x": 1, "y": 2, "z": 3}[letter]
        span = 3 if letter == "z" else 1
        mine = (lax.axis_index(AXES) >> bit) & span
        found = []
        for mask in range(1, span + 1):
            part = lax.dynamic_index_in_dim(self.values, mine ^ mask, place, keepdims=False)
            found.append((part.astype(bf16), mask << bit))
        self.values = lax.dynamic_index_in_dim(self.values, mine, place, keepdims=False)
        return found

    def split_parts(self, letter, at):
        ((send, mask),) = self.split(letter)
        return [(send[:at], mask)], [(send[at:], mask)]

    def take_parts(self, first, second):
        self.take([jnp.concatenate([first[0], second[0]])])

    def take(self, came):
        for part in came:
            self.values = self.values + part.astype(f32)

    def spread(self):
        self.part = self.values.astype(bf16)
        return [(self.part, mask) for mask in (1, 2, 3)]

    def take_spread(self, came):
        own, (core, over_x, both) = self.part, came
        odd, far = own_bit(0) == 1, own_bit(1) == 1
        near = [jnp.where(odd, core, own), jnp.where(odd, own, core)]
        away = [jnp.where(odd, both, over_x), jnp.where(odd, over_x, both)]
        self.whole = jnp.stack(
            [jnp.where(far, away[0], near[0]), jnp.where(far, away[1], near[1]),
             jnp.where(far, near[0], away[0]), jnp.where(far, near[1], away[1])]
        ).astype(f32)


def gathered(w_squeeze, w_expand, w_reduce, w_spatial, w_restore, w_class):
    def whole(weight, axis):
        return lax.all_gather(weight, "wide", axis=axis, tiled=True)

    def as_blocks(blocks):
        ordered = blocks.reshape((4, 2, 2, 2) + blocks.shape[1:])
        return [
            ordered[:, :, far, core].swapaxes(0, 1).reshape((8,) + blocks.shape[1:])
            for core in range(2)
            for far in range(2)
        ]

    squeeze = whole(w_squeeze, 0).reshape(32, -1, R)
    expand = whole(w_expand, 1).reshape(4, 2, PAIR_ROWS, 8, TILE).transpose(3, 0, 2, 1, 4)
    expand = expand.reshape(32, PAIR_ROWS, 2 * TILE)
    reduce = whole(w_reduce, 0).reshape(32, -1, B)
    spatial = whole(w_spatial, 1).reshape(9, 32, 16, B).swapaxes(0, 1).reshape(32, -1, B)
    restore = whole(w_restore, 0).reshape(8, 64, 4, B).swapaxes(1, 2).reshape(32, 64, B)
    classes = jnp.pad(whole(w_class, 0), ((0, 0), (0, TILE - CLASSES)))
    classes = classes.reshape(32, 2, CLASS_ROWS, TILE).swapaxes(1, 2).reshape(32, CLASS_ROWS, B)
    late = jnp.concatenate([restore, classes], axis=1)
    pair = jnp.concatenate([reduce, expand], axis=1)
    spatial = [part for array in as_blocks(spatial) for part in (array[:4], array[4:])]
    return as_blocks(squeeze), as_blocks(pair), spatial, late


def reduced(buffer, reduce_half, expand_half, squeeze_half):
    def whole(half, grain):
        keep, send = (part.astype(bf16) for part in half)
        shape = keep.shape[:1] + (-1, grain) + keep.shape[2:]
        both = jnp.stack([keep.reshape(shape), send.reshape(shape)], axis=2)
        return both.reshape(keep.shape[:1] + (-1,) + keep.shape[2:])

    def scattered(grad, axis):
        part = lax.psum_scatter(grad, "wide", scatter_dimension=axis, tiled=True)
        return lax.psum(part, "narrow").astype(f32)

    def columns(tiles):
        return tiles.swapaxes(0, 1).reshape(tiles.shape[1], -1)

    restore = buffer[:, :RESTORE_ROWS].reshape(8, 4, RESTORE_ROWS, WIDE).swapaxes(1, 2).reshape(B, C)
    spatial = buffer[:, RESTORE_ROWS:].reshape(32, 9, 16, B).swapaxes(0, 1).reshape(9, B, B)
    return (
        scattered(restore, 0),
        scattered(spatial, 1),
        scattered(columns(whole(reduce_half, 128)), 1).T,
        scattered(columns(whole(expand_half, 128)), 1),
        scattered(columns(whole(squeeze_half, 128)), 1).T,
    )


CELLS = SIDE * SIDE
HALF = 2 * PER_VIEW
PADDED = SIDE + 2
MIB = 1 << 20
VMEM = 60
LANES = 128
TILE = 256


def cell_place(cell):
    return (cell // SIDE + 1) * PADDED + cell % SIDE + 1


def tap_place(cell, tap):
    return cell_place(cell) + (tap // 3 - 1) * PADDED + tap % 3 - 1


def dot_nt(first_operand, second_operand):
    return lax.dot_general(
        first_operand, second_operand, (((1,), (1,)), ((), ())), preferred_element_type=f32
    )


def dot_tn(first_operand, second_operand):
    return lax.dot_general(
        first_operand, second_operand, (((0,), (0,)), ((), ())), preferred_element_type=f32
    )


def sigmoid(values):
    return 0.5 * jnp.tanh(0.5 * values) + 0.5


def constants(sums, affine, count):
    mean = sums[0:1] / count
    inverse = lax.rsqrt(sums[1:2] / count - mean * mean + epsilon)
    return mean, inverse, affine[0:1], affine[1:2]


def spread(row, rows=16):
    return jnp.broadcast_to(row, (rows, row.shape[1]))


def lanes(index, width):
    return pl.ds(pl.multiple_of(index * width, width), width)


def clear_border(ref):
    zero = jnp.zeros(ref.shape[1:], ref.dtype)
    for place in range(PADDED * PADDED):
        if place // PADDED in (0, PADDED - 1) or place % PADDED in (0, PADDED - 1):
            ref[place] = zero


def fold(values):
    return values[0:8] + values[8:16]


def half_spec(width):
    return pl.BlockSpec((HALF, width), lambda step, *_: (step, 0))


def whole_spec(shape):
    return pl.BlockSpec(shape, lambda *_: (0,) * len(shape), pipeline_mode=pl.Buffered(1))


def whole_out(shape):
    return pl.BlockSpec(shape, lambda *_: (0,) * len(shape))


WIDE = 512
GROUPS = C // WIDE


def group_at(group):
    return slice(group * WIDE, (group + 1) * WIDE)


def chunks():
    for chunk in range(HALF // 16):
        yield chunk, slice(chunk * 16, chunk * 16 + 16)


ANY = pl.BlockSpec(memory_space=pl.ANY)
SCALAR = pl.BlockSpec(memory_space=pltpu.SMEM)


def kernel_call(kernel, steps, in_specs, out_specs, out_shapes, scratch, flops,
                transcendentals=0, after=(), vmem=VMEM, aliases=None):
    known = len(in_specs)
    grid = steps if isinstance(steps, tuple) else (steps,)

    def body(*refs):
        kernel(*refs[:known], *refs[known + len(after) :])

    call = pl.pallas_call(
        body,
        grid=grid,
        in_specs=list(in_specs) + [ANY] * len(after),
        out_specs=out_specs,
        out_shape=out_shapes,
        scratch_shapes=scratch,
        input_output_aliases=aliases or {},
        compiler_params=pltpu.CompilerParams(
            dimension_semantics=("arbitrary",) * len(grid), vmem_limit_bytes=vmem * MIB
        ),
        cost_estimate=pl.CostEstimate(
            flops=2 * flops, bytes_accessed=16 * MIB, transcendentals=transcendentals
        ),
    )
    return lambda *operands: call(*operands, *after)


def block_copies(me, sources, target, semaphores, rows=None, lanes_at=None, target_rows=None):
    copies = []
    split = len(sources) // 4
    for which, low_mask in enumerate((0, 2, 1, 3)):
        for entry in range(8):
            mask = low_mask | ((entry // 4) * 4) | ((entry % 4) << 3)
            if split == 1:
                taken = sources[which].at[entry]
            else:
                taken = sources[2 * which + entry // 4].at[entry % 4]
            place = target.at[me ^ mask]
            if rows is not None:
                taken = taken.at[rows] if lanes_at is None else taken.at[rows, lanes_at]
            if target_rows is not None:
                place = place.at[target_rows]
            copies.append(pltpu.make_async_copy(taken, place, semaphores.at[len(copies)]))
    return copies


PAIR_ROWS = 64


def reduce_copies(me, sources, target, semaphores):
    return block_copies(me, sources, target, semaphores, slice(0, PAIR_ROWS))


def expand_copies(me, sources, target, semaphores):
    rows = slice(PAIR_ROWS, 2 * PAIR_ROWS)
    found = []
    for part in range(2):
        found += block_copies(
            me, sources, target, semaphores.at[part], rows,
            slice(part * TILE, (part + 1) * TILE),
            slice(part * PAIR_ROWS, (part + 1) * PAIR_ROWS),
        )
    return found


def start(copies):
    for copy in copies:
        copy.start()


def wait(copies):
    for copy in copies:
        copy.wait()


def join_kernel(*refs):
    *sources, out_ref, semaphores = refs
    copies, top = [], 0
    for source in sources:
        count = source.shape[0]
        copies.append(
            pltpu.make_async_copy(
                source, out_ref.at[top : top + count], semaphores.at[len(copies)]
            )
        )
        top += count
    start(copies)
    wait(copies)


def join(arrays):
    count = sum(array.shape[0] for array in arrays)
    return kernel_call(
        join_kernel,
        1,
        [ANY] * len(arrays),
        ANY,
        jax.ShapeDtypeStruct((count,) + arrays[0].shape[1:], arrays[0].dtype),
        [pltpu.SemaphoreType.DMA((len(arrays),))],
        1000000,
        vmem=16,
    )(*arrays)


def first_step():
    return pl.program_id(0) == 0


def add_moments(sums_ref, where, first, second):
    sums_ref[0:1, where] += jnp.sum(first, 0, keepdims=True)
    sums_ref[1:2, where] += jnp.sum(second, 0, keepdims=True)


def mixing_kernel(
    me_ref, block_a, block_b, block_c, block_d, tokens_ref, next_ref, scale_ref,
    upcoming_ref, differ_ref, mixed_ref, natural, ahead, padded, squeeze_ref, semaphores,
):
    @pl.when(first_step())
    def _():
        copies = block_copies(
            me_ref[0], (block_a, block_b, block_c, block_d), squeeze_ref, semaphores, slice(0, 64)
        )
        start(copies)
        natural[:, HALF:] = jnp.zeros((4, natural.shape[1] - HALF, LANES), f32)
        clear_border(ahead)
        clear_border(padded)
        wait(copies)

    def squeeze_step(step, carry):
        squeezed = product(
            tokens_ref[...], squeeze_ref[:, :, lanes(step, TILE)].reshape(C, TILE)
        )
        natural[2 * step, 0:HALF] = squeezed[:, 0:LANES]
        natural[2 * step + 1, 0:HALF] = squeezed[:, LANES:TILE]
        return carry

    lax.fori_loop(0, 2, squeeze_step, 0)
    segment = lax.broadcasted_iota(jnp.int32, (16, LANES), 0) % SEG
    not_last = (segment != SEG - 1).astype(f32)

    def mixing_step(step, carry):
        where = lanes(step, LANES)
        next_rows = [spread(next_ref[tap : tap + 1, where]) for tap in range(9)]
        for cell in range(CELLS):
            upcoming = natural[step, pl.ds(cell + CELLS, 16, stride=CELLS)] * not_last
            ahead[cell_place(cell)] = upcoming
            upcoming_ref[cell * 16 : cell * 16 + 16, where] = upcoming
        mean = jnp.zeros((16, LANES), f32)
        for cell in range(CELLS):
            differ = -natural[step, pl.ds(cell, 16, stride=CELLS)]
            for tap in range(9):
                differ = differ + ahead[tap_place(cell, tap)] * next_rows[tap]
            padded[cell_place(cell)] = differ
            differ_ref[cell * 16 : cell * 16 + 16, where] = differ
            mean = mean + differ
        mean = mean * (1.0 / CELLS)
        scale_rows = [spread(scale_ref[tap : tap + 1, where]) for tap in range(9)]
        for cell in range(CELLS):
            mixed = padded[cell_place(cell)] + mean
            for tap in range(9):
                mixed = mixed + padded[tap_place(cell, tap)] * scale_rows[tap]
            natural[step, pl.ds(cell, 16, stride=CELLS)] = mixed
        mixed_ref[:, where] = natural[step, 0:HALF].astype(bf16)
        return carry

    lax.fori_loop(0, 4, mixing_step, 0)


def mixing_block(me, squeeze, tokens, next_kernel, scale_kernel, after=()):
    rows = tokens.shape[0]
    return kernel_call(
        mixing_kernel,
        rows // HALF,
        [SCALAR, ANY, ANY, ANY, ANY, half_spec(C), whole_spec((9, R)), whole_spec((9, R))],
        [half_spec(R), half_spec(R), half_spec(R)],
        [jax.ShapeDtypeStruct((rows, R), f32), jax.ShapeDtypeStruct((rows, R), f32),
         jax.ShapeDtypeStruct((rows, R), bf16)],
        [pltpu.VMEM((4, HALF + CELLS + 7, LANES), f32),
         pltpu.VMEM((PADDED * PADDED, 16, LANES), f32),
         pltpu.VMEM((PADDED * PADDED, 16, LANES), f32),
         pltpu.VMEM((32, C // 32, R), bf16), pltpu.SemaphoreType.DMA((32,))],
        2 * rows * C * R,
        after=after,
    )(me, *squeeze, tokens, next_kernel, scale_kernel)


def gate_kernel(
    me_ref, block_a, block_b, block_c, block_d, tokens_ref, mixed_ref,
    logit_ref, gated_ref, pre_ref, sums_ref,
    tile, expand_ref, reduce_ref, expand_semaphores, reduce_semaphores,
):
    blocks = (block_a, block_b, block_c, block_d)
    for_expand = expand_copies(me_ref[0], blocks, expand_ref, expand_semaphores)
    for_reduce = reduce_copies(me_ref[0], blocks, reduce_ref, reduce_semaphores)

    @pl.when(first_step())
    def _():
        start(for_expand)
        start(for_reduce)
        sums_ref[...] = jnp.zeros_like(sums_ref)
        wait(for_expand)
        wait(for_reduce)

    for group in range(GROUPS):
        where, found = group_at(group), tile.at[group % 2]
        columns = [
            expand_ref[top : top + 4].reshape(R, TILE) for top in (8 * group, 8 * group + 4)
        ]
        found[...] = product(mixed_ref[...], jnp.concatenate(columns, axis=1))
        for _, rows in chunks():
            logit = found[rows]
            token = tokens_ref[rows, where].astype(f32)
            logit_ref[rows, where] = logit.astype(bf16)
            gated_ref[rows, where] = (token + token * sigmoid(logit)).astype(bf16)
    found = tile.at[0]
    found[...] = product(gated_ref[...], reduce_ref[...].reshape(C, B))
    first = jnp.zeros((8, B), f32)
    second = jnp.zeros((8, B), f32)
    for _, rows in chunks():
        value = found[rows]
        pre_ref[rows] = value
        first = first + fold(value)
        second = second + fold(value * value)
    add_moments(sums_ref, slice(0, B), first, second)


def gate_block(me, pair, tokens, mixed):
    rows = tokens.shape[0]
    return kernel_call(
        gate_kernel,
        rows // HALF,
        [SCALAR] + [ANY] * 4 + [half_spec(C), half_spec(R)],
        [half_spec(C), half_spec(C), half_spec(B), whole_out((2, B))],
        [jax.ShapeDtypeStruct((rows, C), bf16), jax.ShapeDtypeStruct((rows, C), bf16),
         jax.ShapeDtypeStruct((rows, B), f32), jax.ShapeDtypeStruct((2, B), f32)],
        [pltpu.VMEM((2, HALF, WIDE), f32),
         pltpu.VMEM((32, R // 4, TILE), bf16), pltpu.VMEM((32, C // 32, B), bf16),
         pltpu.SemaphoreType.DMA((2, 32)), pltpu.SemaphoreType.DMA((32,))],
        4 * rows * C * R,
        2 * rows * C,
    )(me, *pair, tokens, mixed)


SPATIAL_ROWS = 9 * 16
RESTORE_ROWS = 64
CLASS_ROWS = 32
LATE_ROWS = RESTORE_ROWS + CLASS_ROWS


def restore_copy(late_ref, target, semaphore):
    return pltpu.make_async_copy(late_ref.at[:, 0:RESTORE_ROWS], target, semaphore)


def second_kernel(count, me_ref, *refs):
    blocks, refs = refs[:8], refs[8:]
    pre_ref, in_sums_ref, affine_ref, hidden_ref, out_ref, sums_ref, *refs = refs
    natural, padded, tile, spatial_ref, semaphores = refs
    copies = block_copies(me_ref[0], blocks, spatial_ref, semaphores)

    @pl.when(first_step())
    def _():
        start(copies)
        sums_ref[...] = jnp.zeros_like(sums_ref)
        clear_border(padded)

    border = SIDE * 16
    hidden_ref[0, 0:border] = jnp.zeros((border, 3 * B), bf16)
    hidden_ref[0, border + HALF :] = jnp.zeros((border, 3 * B), bf16)

    def hidden_step(step, carry):
        where = lanes(step, LANES)
        mean, inverse, gain, shift = (
            spread(row) for row in constants(in_sums_ref[:, where], affine_ref[:, where], count)
        )
        for chunk in range(HALF // 16):
            rows = slice(chunk * 16, chunk * 16 + 16)
            norm = (pre_ref[rows, where] - mean) * inverse * gain + shift
            natural[rows] = norm * sigmoid(norm)
        for cell in range(CELLS):
            padded[cell_place(cell)] = natural[pl.ds(cell, 16, stride=CELLS)].astype(bf16)
        for side in range(3):
            at = lanes(side * 4 + step, LANES)
            for cell in range(CELLS):
                hidden_ref[0, border + cell * 16 : border + cell * 16 + 16, at] = padded[
                    tap_place(cell, 3 + side)
                ]
        return carry

    lax.fori_loop(0, 4, hidden_step, 0)

    @pl.when(first_step())
    def _():
        wait(copies)

    found = None
    for row in range(3):
        taps = [
            spatial_ref[:, tap * 16 : tap * 16 + 16].reshape(B, B)
            for tap in range(3 * row, 3 * row + 3)
        ]
        part = product(
            hidden_ref[0, row * border : row * border + HALF], jnp.concatenate(taps, axis=0)
        )
        found = part if found is None else found + part
    tile[...] = found
    first = jnp.zeros((8, B), f32)
    second = jnp.zeros((8, B), f32)
    for chunk in range(HALF // 16):
        rows = slice(chunk * 16, chunk * 16 + 16)
        value = tile[rows]
        out_ref[rows] = value
        first = first + fold(value)
        second = second + fold(value * value)
    add_moments(sums_ref, slice(0, B), first, second)


def second_block(me, spatial, pre_one, sums, affine, count):
    rows = pre_one.shape[0]
    steps = rows // HALF
    deep = HALF + 2 * SIDE * 16
    return kernel_call(
        functools.partial(second_kernel, count),
        steps,
        [SCALAR] + [ANY] * 8 + [half_spec(B), whole_spec(sums.shape), whole_spec((2, B))],
        [pl.BlockSpec((1, deep, 3 * B), lambda step: (step, 0, 0)), half_spec(B),
         whole_out((2, B))],
        [jax.ShapeDtypeStruct((steps, deep, 3 * B), bf16), jax.ShapeDtypeStruct((rows, B), f32),
         jax.ShapeDtypeStruct((2, B), f32)],
        [pltpu.VMEM((HALF, LANES), f32), pltpu.VMEM((PADDED * PADDED, 16, LANES), bf16),
         pltpu.VMEM((HALF, B), f32), pltpu.VMEM((32, SPATIAL_ROWS, B), bf16),
         pltpu.SemaphoreType.DMA((32,))],
        18 * rows * B * B,
        2 * rows * B,
    )(me, *spatial, pre_one, sums, affine)


def third_kernel(count, pre_ref, in_sums_ref, affine_ref, late_ref,
                 hidden_ref, out_ref, centre_ref, sums_ref, natural, tile, middle, restore_ref,
                 semaphore):
    copy = restore_copy(late_ref, restore_ref, semaphore)

    @pl.when(first_step())
    def _():
        copy.start()
        sums_ref[...] = jnp.zeros_like(sums_ref)

    def hidden_step(step, carry):
        where = lanes(step, LANES)
        mean, inverse, gain, shift = (
            spread(row) for row in constants(in_sums_ref[:, where], affine_ref[:, where], count)
        )
        for cell in range(CELLS):
            rows = slice(cell * 16, cell * 16 + 16)
            norm = (pre_ref[rows, where] - mean) * inverse * gain + shift
            natural[pl.ds(cell, 16, stride=CELLS)] = norm * sigmoid(norm)
        hidden_ref[:, where] = natural[...].astype(bf16)
        middle[:, where] = spread(jnp.mean(natural[...], 0, keepdims=True)).astype(bf16)
        return carry

    lax.fori_loop(0, 4, hidden_step, 0)

    @pl.when(first_step())
    def _():
        copy.wait()

    blocks = restore_ref.reshape(8, 4, RESTORE_ROWS, B)
    for group in range(GROUPS):
        where, found = group_at(group), tile.at[group % 2]
        columns = blocks[:, group].reshape(B, WIDE)
        found[...] = product(hidden_ref[...], columns)
        centre = product(middle[...], columns)
        centre_ref[0, :, where] = centre[0:1]
        first = jnp.zeros((8, WIDE), f32)
        second = jnp.zeros((8, WIDE), f32)
        for _, rows in chunks():
            value = found[rows]
            out_ref[rows, where] = (value - centre).astype(bf16)
            first = first + fold(value)
            second = second + fold(value * value)
        add_moments(sums_ref, where, first, second)


def third_block(pre_two, sums, affine, late, count):
    rows = pre_two.shape[0]
    return kernel_call(
        functools.partial(third_kernel, count),
        rows // HALF,
        [half_spec(B), whole_spec(sums.shape), whole_spec((2, B)), ANY],
        [half_spec(B), half_spec(C), pl.BlockSpec((1, 1, C), lambda step: (step, 0, 0)),
         whole_out((2, C))],
        [jax.ShapeDtypeStruct((rows, B), bf16), jax.ShapeDtypeStruct((rows, C), bf16),
         jax.ShapeDtypeStruct((rows // HALF, 1, C), f32), jax.ShapeDtypeStruct((2, C), f32)],
        [pltpu.VMEM((HALF, LANES), f32), pltpu.VMEM((2, HALF, WIDE), f32),
         pltpu.VMEM((16, B), bf16),
         pltpu.VMEM((32, RESTORE_ROWS, B), bf16), pltpu.SemaphoreType.DMA(())],
        2 * rows * B * C,
        2 * rows * B,
    )(pre_two, sums, affine, late)


def view_rows(chunk):
    return (chunk * 16) // PER_VIEW, (chunk * 16 + 8) // PER_VIEW


def class_copy(late_ref, target, semaphore):
    return pltpu.make_async_copy(late_ref.at[:, RESTORE_ROWS:], target, semaphore)


def order_classes(late, classes):
    for block in range(32):
        for half in range(2):
            top = (2 * block + half) * CLASS_ROWS
            classes[top : top + CLASS_ROWS] = late[block, :, half * TILE : (half + 1) * TILE]


def fourth_kernel(count, pre_ref, centre_ref, gated_ref, in_sums_ref, affine_ref,
                  late_ref, bias_ref, out_ref, slope_ref, views_ref, logits_ref, pooled_ref,
                  classes, late, sums, semaphore):
    copy = class_copy(late_ref, late, semaphore)
    step = pl.program_id(0)

    @pl.when(first_step())
    def _():
        copy.start()
        sums[...] = jnp.zeros_like(sums)

    for part in range(C // TILE):
        where = slice(part * TILE, (part + 1) * TILE)
        mean, inverse, gain, shift = (
            spread(row) for row in constants(in_sums_ref[:, where], affine_ref[:, where], count)
        )
        mean = mean - spread(centre_ref[0, :, where])
        totals = [[jnp.zeros((8, TILE), f32) for _ in range(2)] for _ in range(3)]
        for chunk in range(HALF // 16):
            rows = slice(chunk * 16, chunk * 16 + 16)
            unit = (pre_ref[rows, where].astype(f32) - mean) * inverse
            summed = unit * gain + shift + gated_ref[rows, where].astype(f32)
            sigma = sigmoid(summed)
            output = summed * sigma
            slope = sigma + output * (1.0 - sigma)
            out_ref[rows, where] = output.astype(bf16)
            slope_ref[rows, where] = slope.astype(bf16)
            low, high = view_rows(chunk)
            for kind, value in enumerate((output, slope, slope * unit)):
                if low == high:
                    totals[kind][low] = totals[kind][low] + fold(value)
                else:
                    totals[kind][low] = totals[kind][low] + value[0:8]
                    totals[kind][high] = totals[kind][high] + value[8:16]
        for kind in range(3):
            for view in range(2):
                at = 2 * kind + view
                row = jnp.sum(totals[kind][view], 0, keepdims=True)
                views_ref[0, at : at + 1, where] = row
                if kind == 0:
                    sums[pl.ds(2 * step + view, 1), where] = row
        views_ref[0, 6:8, where] = jnp.zeros((2, TILE), f32)

    @pl.when(step == pl.num_programs(0) - 1)
    def _():
        copy.wait()
        order_classes(late, classes)
        pooled = (sums[...] / PER_VIEW).astype(bf16)
        pooled_ref[...] = pooled
        logits_ref[...] = product(pooled, classes[...]) + bias_ref[...]


def fourth_block(pre_three, centres, gated, sums, affine, late, bias, count):
    rows = pre_three.shape[0]
    steps = rows // HALF
    return kernel_call(
        functools.partial(fourth_kernel, count),
        steps,
        [half_spec(C), pl.BlockSpec((1, 1, C), lambda step: (step, 0, 0)), half_spec(C),
         whole_spec(sums.shape), whole_spec((2, C)), ANY, whole_spec((1, TILE))],
        [half_spec(C), half_spec(C), pl.BlockSpec((1, 8, C), lambda step: (step, 0, 0)),
         whole_out((16, TILE)), whole_out((16, C))],
        [jax.ShapeDtypeStruct((rows, C), bf16), jax.ShapeDtypeStruct((rows, C), bf16),
         jax.ShapeDtypeStruct((steps, 8, C), f32), jax.ShapeDtypeStruct((16, TILE), f32),
         jax.ShapeDtypeStruct((16, C), bf16)],
        [pltpu.VMEM((C, TILE), bf16), pltpu.VMEM((32, CLASS_ROWS, B), bf16),
         pltpu.VMEM((16, C), f32), pltpu.SemaphoreType.DMA(())],
        20 * rows * C,
        2 * rows * C,
    )(pre_three, centres, gated, sums, affine, late, bias)


def video_kernel(view_count, before_ref, own_ref, after_ref, marks_ref, target_ref, views_ref,
                 late_ref, part_ref, pooled_ref, grad_ref, classes, late, semaphore):
    copy = class_copy(late_ref, late, semaphore)
    copy.start()
    marks = marks_ref[...]
    video_logits = jnp.zeros((8, TILE), f32)
    near = (before_ref, own_ref, after_ref)
    for index in range(3 * view_count):
        row = near[index // view_count][index % view_count : index % view_count + 1]
        video_logits = video_logits + marks[:, index : index + 1] * row
    known = lax.broadcasted_iota(jnp.int32, (8, TILE), 1) < CLASSES
    top = jnp.max(jnp.where(known, video_logits, -jnp.inf), 1, keepdims=True)
    weights = jnp.where(known, jnp.exp(jnp.minimum(video_logits - top, 0.0)), 0.0)
    total_weight = jnp.sum(weights, 1, keepdims=True)
    target = target_ref[...]
    entropy = jnp.log(total_weight) + top - jnp.sum(target * video_logits, 1, keepdims=True)
    video_grad = loss_scale * (weights / total_weight - target)
    first = marks[:, 3 * view_count + 1 : 3 * view_count + 2]
    view_grad = (video_grad * marks[:, 3 * view_count : 3 * view_count + 1]).astype(bf16)
    grad_ref[...] = view_grad
    place = lax.broadcasted_iota(jnp.int32, (8, TILE), 1)
    row = jnp.sum(first * jnp.where(place == CLASSES, entropy, video_grad), 0, keepdims=True)
    copy.wait()
    order_classes(late, classes)
    pooled = dot_nt(view_grad, classes[...]) * (1.0 / PER_VIEW)
    parts = [jnp.zeros((1, C), f32), jnp.zeros((1, C), f32)]
    for view in range(view_count):
        half, place = view // 2, view % 2
        pooled_ref[half, place : place + 1] = pooled[view : view + 1]
        for kind in range(2):
            at = 2 * (kind + 1) + place
            parts[kind] = parts[kind] + pooled[view : view + 1] * views_ref[half, at : at + 1]
    part_ref[0:1] = parts[0]
    part_ref[1:2] = parts[1]
    part_ref[2:3] = jnp.zeros((1, C), f32)
    part_ref[2:3, 0:TILE] = row


def video_block(before, own, following, marks, target, views, late, view_count):
    outs = [((3, C), f32), ((view_count // 2, 2, C), f32), ((8, TILE), bf16)]
    operands = (before, own, following, marks, target, views)
    return kernel_call(
        functools.partial(video_kernel, view_count),
        1,
        [whole_spec(operand.shape) for operand in operands] + [ANY],
        [whole_out(shape) for shape, _ in outs],
        [jax.ShapeDtypeStruct(shape, kind) for shape, kind in outs],
        [pltpu.VMEM((C, TILE), bf16), pltpu.VMEM((32, CLASS_ROWS, B), bf16),
         pltpu.SemaphoreType.DMA(())],
        1000000,
    )(*operands, late)


def view_scale(pooled_ref, view, where):
    return spread(pooled_ref[0, view : view + 1, where], 8)


def view_grad_rows(slope, pooled, chunk):
    low, high = view_rows(chunk)
    return slope * jnp.concatenate([pooled[low], pooled[high]], axis=0)


def fifth_kernel(count, slope_ref, pre_three_ref, centre_ref, pooled_ref, sums_three_ref, affine_three_ref,
                 grads_three_ref, late_ref, pre_two_ref, sums_two_ref, affine_two_ref,
                 low_ref, out_ref, sums_ref, natural, restore_ref, semaphore):
    copy = restore_copy(late_ref, restore_ref, semaphore)

    @pl.when(first_step())
    def _():
        copy.start()
        sums_ref[...] = jnp.zeros_like(sums_ref)

    for group in range(GROUPS):
        where = group_at(group)
        mean, inverse, gain, _ = constants(
            sums_three_ref[:, where], affine_three_ref[:, where], count
        )
        scale = spread(gain * inverse)
        offset = spread(grads_three_ref[0:1, where] / count)
        along = spread(grads_three_ref[1:2, where] / count * inverse)
        mean = spread(mean - centre_ref[0, :, where])
        pooled = [view_scale(pooled_ref, view, where) for view in range(2)]
        for chunk, rows in chunks():
            grad = view_grad_rows(slope_ref[rows, where].astype(f32), pooled, chunk)
            centred = pre_three_ref[rows, where].astype(f32) - mean
            low_ref[rows, where] = (scale * (grad - offset - centred * along)).astype(bf16)

    @pl.when(first_step())
    def _():
        copy.wait()

    blocks = restore_ref.reshape(8, 4, RESTORE_ROWS, B)
    grad = None
    for group in range(GROUPS):
        part = dot_nt(low_ref[:, group_at(group)], blocks[:, group].reshape(B, WIDE))
        grad = part if grad is None else grad + part
    for step in range(4):
        natural[step] = grad[:, step * LANES : (step + 1) * LANES]

    def slope_step(step, carry):
        where = lanes(step, LANES)
        mean, inverse, gain, shift = (
            spread(row) for row in constants(sums_two_ref[:, where], affine_two_ref[:, where], count)
        )
        first = jnp.zeros((16, LANES), f32)
        second = jnp.zeros((16, LANES), f32)
        for cell in range(CELLS):
            rows = slice(cell * 16, cell * 16 + 16)
            unit = (pre_two_ref[rows, where] - mean) * inverse
            norm = unit * gain + shift
            sigma = sigmoid(norm)
            grad = natural[step, pl.ds(cell, 16, stride=CELLS)]
            grad = grad * (sigma * (1.0 + norm * (1.0 - sigma)))
            out_ref[rows, where] = grad
            first = first + grad
            second = second + grad * unit
        add_moments(sums_ref, where, first, second)
        return carry

    lax.fori_loop(0, 4, slope_step, 0)


def fifth_block(slope, pre_three, centres, pooled, sums_three, affine_three, grads_three, late,
                pre_two, sums_two, affine_two, count, after=()):
    rows = slope.shape[0]
    return kernel_call(
        functools.partial(fifth_kernel, count),
        rows // HALF,
        [half_spec(C), half_spec(C), pl.BlockSpec((1, 1, C), lambda step: (step, 0, 0)),
         pl.BlockSpec((1, 2, C), lambda step: (step, 0, 0)),
         whole_spec(sums_three.shape), whole_spec((2, C)), whole_spec(grads_three.shape), ANY,
         half_spec(B), whole_spec(sums_two.shape), whole_spec((2, B))],
        [half_spec(C), half_spec(B), whole_out((2, B))],
        [jax.ShapeDtypeStruct((rows, C), bf16), jax.ShapeDtypeStruct((rows, B), f32),
         jax.ShapeDtypeStruct((2, B), f32)],
        [pltpu.VMEM((4, HALF, LANES), f32), pltpu.VMEM((32, RESTORE_ROWS, B), bf16),
         pltpu.SemaphoreType.DMA(())],
        2 * rows * B * C,
        2 * rows * B,
        after=after,
    )(slope, pre_three, centres, pooled, sums_three, affine_three, grads_three, late,
      pre_two, sums_two, affine_two)


def sixth_kernel(count, me_ref, *refs):
    blocks, refs = refs[:8], refs[8:]
    grad_ref, pre_two_ref, sums_two_ref, affine_two_ref, grads_two_ref, *refs = refs
    pre_one_ref, sums_one_ref, affine_one_ref, low_ref, out_ref, sums_ref, *refs = refs
    padded, shifted, tile, natural, spatial_ref, semaphores = refs
    border = SIDE * 16
    copies = block_copies(me_ref[0], blocks, spatial_ref, semaphores)

    @pl.when(first_step())
    def _():
        start(copies)
        sums_ref[...] = jnp.zeros_like(sums_ref)
        clear_border(padded)
        shifted[0:border] = jnp.zeros((border, 3 * B), bf16)
        shifted[border + HALF :] = jnp.zeros((border, 3 * B), bf16)

    def low_step(step, carry):
        where = lanes(step, LANES)
        mean, inverse, gain, _ = constants(sums_two_ref[:, where], affine_two_ref[:, where], count)
        scale = spread(gain * inverse)
        offset = spread(grads_two_ref[0:1, where] / count)
        along = spread(grads_two_ref[1:2, where] / count * inverse)
        mean = spread(mean)
        for cell in range(CELLS):
            rows = slice(cell * 16, cell * 16 + 16)
            centred = pre_two_ref[rows, where] - mean
            low = (scale * (grad_ref[rows, where] - offset - centred * along)).astype(bf16)
            low_ref[rows, where] = low
            padded[cell_place(cell)] = low
        for side in range(3):
            at = lanes(side * 4 + step, LANES)
            for cell in range(CELLS):
                shifted[border + cell * 16 : border + cell * 16 + 16, at] = padded[
                    tap_place(cell, 3 + side)
                ]
        return carry

    lax.fori_loop(0, 4, low_step, 0)

    @pl.when(first_step())
    def _():
        wait(copies)

    grad = None
    for tap in range(9):
        top = (tap // 3) * border
        at = (tap % 3) * B
        back = (8 - tap) * 16
        part = dot_nt(
            shifted[top : top + HALF, at : at + B],
            spatial_ref[:, back : back + 16].reshape(B, B),
        )
        grad = part if grad is None else grad + part
    tile[...] = grad
    for group in range(4):
        for cell in range(CELLS):
            natural[group, pl.ds(cell, 16, stride=CELLS)] = tile[
                cell * 16 : cell * 16 + 16, group * LANES : (group + 1) * LANES
            ]

    def slope_step(step, carry):
        where = lanes(step, LANES)
        mean, inverse, gain, shift = (
            spread(row) for row in constants(sums_one_ref[:, where], affine_one_ref[:, where], count)
        )
        first = jnp.zeros((16, LANES), f32)
        second = jnp.zeros((16, LANES), f32)
        for chunk in range(HALF // 16):
            rows = slice(chunk * 16, chunk * 16 + 16)
            unit = (pre_one_ref[rows, where] - mean) * inverse
            norm = unit * gain + shift
            sigma = sigmoid(norm)
            grad = natural[step, rows] * (sigma * (1.0 + norm * (1.0 - sigma)))
            out_ref[rows, where] = grad
            first = first + grad
            second = second + grad * unit
        add_moments(sums_ref, where, first, second)
        return carry

    lax.fori_loop(0, 4, slope_step, 0)


def sixth_block(me, spatial, grad, pre_two, sums_two, affine_two, grads_two, pre_one, sums_one,
                affine_one, count):
    rows = grad.shape[0]
    deep = HALF + 2 * SIDE * 16
    return kernel_call(
        functools.partial(sixth_kernel, count),
        rows // HALF,
        [SCALAR] + [ANY] * 8 + [half_spec(B), half_spec(B), whole_spec(sums_two.shape),
         whole_spec((2, B)), whole_spec(grads_two.shape), half_spec(B), whole_spec(sums_one.shape),
         whole_spec((2, B))],
        [half_spec(B), half_spec(B), whole_out((2, B))],
        [jax.ShapeDtypeStruct((rows, B), bf16), jax.ShapeDtypeStruct((rows, B), f32),
         jax.ShapeDtypeStruct((2, B), f32)],
        [pltpu.VMEM((PADDED * PADDED, 16, LANES), bf16), pltpu.VMEM((deep, 3 * B), bf16),
         pltpu.VMEM((HALF, B), f32), pltpu.VMEM((4, HALF, LANES), f32),
         pltpu.VMEM((32, SPATIAL_ROWS, B), bf16), pltpu.SemaphoreType.DMA((32,))],
        18 * rows * B * B,
        2 * rows * B,
    )(me, *spatial, grad, pre_two, sums_two, affine_two, grads_two, pre_one, sums_one,
      affine_one)


def low_kernel(count, grad_ref, pre_ref, sums_ref, affine_ref, grads_ref, low_ref):
    def low_step(step, carry):
        where = lanes(step, LANES)
        mean, inverse, gain, _ = constants(sums_ref[:, where], affine_ref[:, where], count)
        scale = spread(gain * inverse)
        offset = spread(grads_ref[0:1, where] / count)
        along = spread(grads_ref[1:2, where] / count * inverse)
        mean = spread(mean)
        for chunk in range(HALF // 16):
            rows = slice(chunk * 16, chunk * 16 + 16)
            centred = pre_ref[rows, where] - mean
            low_ref[rows, where] = (
                scale * (grad_ref[rows, where] - offset - centred * along)
            ).astype(bf16)
        return carry

    lax.fori_loop(0, 4, low_step, 0)


def low_outer_kernel(count, grain, me_ref, grad_ref, pre_ref, sums_ref, affine_ref, grads_ref,
                     wide_ref, low_ref, keep_ref, send_ref, plain, turned):
    @pl.when(first_step())
    def _():
        for half in range(low_ref.shape[0] // HALF):
            rows = pl.ds(half * HALF, HALF)
            low_kernel(
                count, grad_ref.at[rows], pre_ref.at[rows], sums_ref, affine_ref, grads_ref,
                low_ref.at[rows],
            )
        turn(me_ref[0], low_ref[...], grain, plain, turned)

    store_tiles(product(turned[...], wide_ref[...]), keep_ref, send_ref)


def low_outer_block(me, grad, pre, sums, affine, grads, wide_values, count):
    rows, inner = grad.shape
    blocks = wide_values.shape[1] // TILE
    half = pl.BlockSpec((2, inner // 2, TILE), lambda step: (step, 0, 0))
    low, keep, send = kernel_call(
        functools.partial(low_outer_kernel, count, inner // 4),
        blocks // 2,
        [SCALAR, whole_spec(grad.shape), whole_spec(grad.shape), whole_spec(sums.shape),
         whole_spec((2, B)), whole_spec(grads.shape),
         pl.BlockSpec((rows, 2 * TILE), lambda step: (0, step))],
        [whole_out(grad.shape), half, half],
        [jax.ShapeDtypeStruct(grad.shape, bf16),
         jax.ShapeDtypeStruct((blocks, inner // 2, TILE), f32),
         jax.ShapeDtypeStruct((blocks, inner // 2, TILE), bf16)],
        [pltpu.VMEM((inner, rows), bf16), pltpu.VMEM((inner, rows), bf16)],
        2 * rows * inner * wide_values.shape[1],
    )(me, grad, pre, sums, affine, grads, wide_values)
    return low, (keep, send)


def gate_back_kernel(me_ref, block_a, block_b, block_c, block_d, low_ref,
                     slope_ref, pooled_ref, tokens_ref, logit_ref,
                     logit_grad_ref, part_ref, tile, reduce_ref, semaphores):
    copies = reduce_copies(me_ref[0], (block_a, block_b, block_c, block_d), reduce_ref, semaphores)

    @pl.when(first_step())
    def _():
        start(copies)
        wait(copies)

    for group in range(GROUPS):
        where, found = group_at(group), tile.at[group % 2]
        found[...] = dot_nt(low_ref[...], reduce_ref[8 * group : 8 * group + 8].reshape(WIDE, B))
        pooled = [view_scale(pooled_ref, view, where) for view in range(2)]
        for chunk, rows in chunks():
            slope = slope_ref[rows, where].astype(f32)
            grad = found[rows] + view_grad_rows(slope, pooled, chunk)
            gate = sigmoid(logit_ref[rows, where].astype(f32))
            part = grad * gate
            part_ref[rows, where] = (grad + part).astype(bf16)
            token = tokens_ref[rows, where].astype(f32)
            logit_grad_ref[rows, where] = (part * (1.0 - gate) * token).astype(bf16)


def gate_back_block(me, pair, low_one, slope, pooled, tokens, logit):
    rows = low_one.shape[0]
    return kernel_call(
        gate_back_kernel,
        rows // HALF,
        [SCALAR, ANY, ANY, ANY, ANY, half_spec(B), half_spec(C),
         pl.BlockSpec((1, 2, C), lambda step: (step, 0, 0)), half_spec(C), half_spec(C)],
        [half_spec(C), half_spec(C)],
        [jax.ShapeDtypeStruct((rows, C), bf16), jax.ShapeDtypeStruct((rows, C), bf16)],
        [pltpu.VMEM((2, HALF, WIDE), f32), pltpu.VMEM((32, C // 32, B), bf16),
         pltpu.SemaphoreType.DMA((32,))],
        2 * rows * C * R,
        2 * rows * C,
    )(me, *pair, low_one, slope, pooled, tokens, logit)


def mixing_back_kernel(me_ref, block_a, block_b, block_c, block_d, logit_grad_ref,
                       upcoming_ref, differ_ref, next_ref, scale_ref, squeezed_ref, kernels_ref,
                       natural, later, ahead, padded, expand_ref, semaphores):
    @pl.when(first_step())
    def _():
        copies = expand_copies(
            me_ref[0], (block_a, block_b, block_c, block_d), expand_ref, semaphores
        )
        start(copies)
        kernels_ref[...] = jnp.zeros_like(kernels_ref)
        clear_border(ahead)
        clear_border(padded)
        later[0:CELLS] = jnp.zeros((CELLS, LANES), f32)
        wait(copies)

    grad = None
    for group in range(GROUPS):
        columns = [
            expand_ref[top : top + 4].reshape(R, TILE) for top in (8 * group, 8 * group + 4)
        ]
        part = dot_nt(logit_grad_ref[:, group_at(group)], jnp.concatenate(columns, axis=1))
        grad = part if grad is None else grad + part
    for step in range(4):
        natural[step] = grad[:, step * LANES : (step + 1) * LANES]
    segment = lax.broadcasted_iota(jnp.int32, (16, LANES), 0) % SEG
    not_last = (segment != SEG - 1).astype(f32)

    def mixing_step(step, carry):
        where = lanes(step, LANES)
        scale_rows = [spread(scale_ref[tap : tap + 1, where]) for tap in range(9)]
        mean = jnp.zeros((16, LANES), f32)
        for cell in range(CELLS):
            grad = natural[step, pl.ds(cell, 16, stride=CELLS)]
            padded[cell_place(cell)] = grad
            mean = mean + grad
            ahead[cell_place(cell)] = differ_ref[cell * 16 : cell * 16 + 16, where]
        mean = mean * (1.0 / CELLS)
        sums = [jnp.zeros((16, LANES), f32) for _ in range(9)]
        for cell in range(CELLS):
            grad = padded[cell_place(cell)]
            for tap in range(9):
                sums[tap] = sums[tap] + ahead[tap_place(cell, tap)] * grad
        for tap in range(9):
            kernels_ref[9 + tap : 10 + tap, where] += jnp.sum(sums[tap], 0, keepdims=True)
        for cell in range(CELLS):
            grad = padded[cell_place(cell)] + mean
            for tap in range(9):
                grad = grad + padded[tap_place(cell, tap)] * scale_rows[8 - tap]
            ahead[cell_place(cell)] = grad
        next_rows = [spread(next_ref[tap : tap + 1, where]) for tap in range(9)]
        for cell in range(CELLS):
            padded[cell_place(cell)] = upcoming_ref[cell * 16 : cell * 16 + 16, where]
        sums = [jnp.zeros((16, LANES), f32) for _ in range(9)]
        for cell in range(CELLS):
            grad = ahead[cell_place(cell)]
            for tap in range(9):
                sums[tap] = sums[tap] + padded[tap_place(cell, tap)] * grad
        for tap in range(9):
            kernels_ref[tap : tap + 1, where] += jnp.sum(sums[tap], 0, keepdims=True)
        for cell in range(CELLS):
            back = ahead[tap_place(cell, 0)] * next_rows[8]
            for tap in range(1, 9):
                back = back + ahead[tap_place(cell, tap)] * next_rows[8 - tap]
            later[pl.ds(cell + CELLS, 16, stride=CELLS)] = back * not_last
            natural[step, pl.ds(cell, 16, stride=CELLS)] = -ahead[cell_place(cell)]
        for chunk in range(HALF // 16):
            rows = slice(chunk * 16, chunk * 16 + 16)
            squeezed_ref[rows, where] = (natural[step, rows] + later[rows]).astype(bf16)
        return carry

    lax.fori_loop(0, 4, mixing_step, 0)


def mixing_back_block(me, pair, logit_grad, upcoming, differ, next_kernel, scale_kernel,
                      after=()):
    rows = logit_grad.shape[0]
    return kernel_call(
        mixing_back_kernel,
        rows // HALF,
        [SCALAR, ANY, ANY, ANY, ANY, half_spec(C), half_spec(R), half_spec(R),
         whole_spec((9, R)), whole_spec((9, R))],
        [half_spec(R), whole_out((18, R))],
        [jax.ShapeDtypeStruct((rows, R), bf16), jax.ShapeDtypeStruct((18, R), f32)],
        [pltpu.VMEM((4, HALF, LANES), f32), pltpu.VMEM((HALF + CELLS + 7, LANES), f32),
         pltpu.VMEM((PADDED * PADDED, 16, LANES), f32),
         pltpu.VMEM((PADDED * PADDED, 16, LANES), f32), pltpu.VMEM((32, R // 4, TILE), bf16),
         pltpu.SemaphoreType.DMA((2, 32))],
        2 * rows * C * R,
        after=after,
    )(me, *pair, logit_grad, upcoming, differ, next_kernel, scale_kernel)


def tokens_kernel(me_ref, block_a, block_b, block_c, block_d, part_ref, squeezed_ref, out_ref,
                  squeeze_ref, semaphores):
    @pl.when(first_step())
    def _():
        copies = block_copies(
            me_ref[0], (block_a, block_b, block_c, block_d), squeeze_ref, semaphores, slice(0, 64)
        )
        start(copies)
        wait(copies)

    found = dot_nt(squeezed_ref[...], squeeze_ref[...].reshape(C, R))
    out_ref[...] = (found + part_ref[...].astype(f32)).astype(bf16)


def tokens_block(me, squeeze, part, squeezed_grad):
    rows = part.shape[0]
    return kernel_call(
        tokens_kernel,
        rows // HALF,
        [SCALAR, ANY, ANY, ANY, ANY, half_spec(C), half_spec(R)],
        half_spec(C),
        jax.ShapeDtypeStruct((rows, C), bf16),
        [pltpu.VMEM((32, C // 32, R), bf16), pltpu.SemaphoreType.DMA((32,))],
        2 * rows * C * R,
    )(me, *squeeze, part, squeezed_grad)


def turn(me, values, grain, plain, turned):
    core = me & 1
    plain[...] = values.T
    half = turned.shape[0] // 2
    for group in range(half // grain):
        mine = pl.multiple_of((2 * group + core) * grain, grain)
        other = pl.multiple_of((2 * group + 1 - core) * grain, grain)
        turned[group * grain : (group + 1) * grain] = plain[pl.ds(mine, grain)]
        turned[half + group * grain : half + (group + 1) * grain] = plain[pl.ds(other, grain)]


def store_tiles(found, keep_ref, send_ref):
    half = found.shape[0] // 2
    for tile in range(2):
        at = slice(tile * TILE, (tile + 1) * TILE)
        keep_ref[tile, 0:half] = found[0:half, at]
        send_ref[tile, 0:half] = found[half:, at].astype(bf16)


def outer_kernel(grain, me_ref, narrow_ref, wide_ref, keep_ref, send_ref, plain, turned):
    @pl.when(first_step())
    def _():
        turn(me_ref[0], narrow_ref[...], grain, plain, turned)

    store_tiles(product(turned[...], wide_ref[...]), keep_ref, send_ref)


def outer_block(me, narrow_values, wide_values, grain):
    rows, inner = narrow_values.shape
    blocks = wide_values.shape[1] // TILE
    half = pl.BlockSpec((2, inner // 2, TILE), lambda step: (step, 0, 0))
    return kernel_call(
        functools.partial(outer_kernel, grain),
        blocks // 2,
        [SCALAR, whole_spec((rows, inner)), pl.BlockSpec((rows, 2 * TILE), lambda step: (0, step))],
        [half, half],
        [jax.ShapeDtypeStruct((blocks, inner // 2, TILE), f32),
         jax.ShapeDtypeStruct((blocks, inner // 2, TILE), bf16)],
        [pltpu.VMEM((inner, rows), bf16), pltpu.VMEM((inner, rows), bf16)],
        2 * rows * inner * wide_values.shape[1],
    )(me, narrow_values, wide_values)


def outer_block_of(grain):
    return functools.partial(outer_block, grain=grain)


FEW_ROWS = 40


def restore_outer_kernel(narrow_ref, wide_ref, out_ref, turned):
    @pl.when(first_step())
    def _():
        turned[...] = narrow_ref[...].T

    found = product(turned[...], wide_ref[...])
    out_ref[:, 0] = found.astype(bf16).reshape(8, RESTORE_ROWS, WIDE)


def restore_outer_block(hidden, low_three):
    rows = hidden.shape[0]
    return kernel_call(
        restore_outer_kernel,
        GROUPS,
        [whole_spec((rows, B)), pl.BlockSpec((rows, WIDE), lambda step: (0, step))],
        pl.BlockSpec((8, 1, RESTORE_ROWS, WIDE), lambda step: (0, step, 0, 0)),
        jax.ShapeDtypeStruct((8, 4, RESTORE_ROWS + SPATIAL_ROWS, WIDE), bf16),
        [pltpu.VMEM((B, rows), bf16)],
        2 * rows * B * C,
    )(hidden, low_three)


def spatial_kernel(buffer_ref, hidden_ref, low_ref, out_ref, turned, padded):
    border = SIDE * 16
    halves = hidden_ref.shape[0]

    @pl.when(first_step())
    def _():
        for half in range(halves):
            padded[half, 0 : 2 * border] = jnp.zeros((2 * border, B), bf16)
            padded[half, 2 * border : 2 * border + HALF] = low_ref[half * HALF : (half + 1) * HALF]
            padded[half, 2 * border + HALF :] = jnp.zeros((2 * border, B), bf16)

    step = pl.program_id(0)

    @pl.when(step % 3 == 0)
    def _():
        for half in range(halves):
            turned[half] = hidden_ref[half].T

    top = pl.multiple_of((2 - step % 3) * border, 16)
    found = None
    for half in range(halves):
        part = product(turned[half], padded[half, pl.ds(top, HALF + 2 * border)])
        found = part if found is None else found + part
    out_ref[...] = found.astype(bf16).reshape(32, 16, B)


def spatial_block(buffer, hidden, low_two):
    halves, deep, _ = hidden.shape
    first = RESTORE_ROWS // 16
    return kernel_call(
        spatial_kernel,
        9,
        [ANY, pl.BlockSpec((halves, deep, B), lambda step: (0, 0, step // 3)),
         whole_spec(low_two.shape)],
        pl.BlockSpec((32, 16, B), lambda step: (0, first + (step % 3) * 3 + step // 3, 0)),
        jax.ShapeDtypeStruct(buffer.shape, bf16),
        [pltpu.VMEM((halves, B, deep), bf16),
         pltpu.VMEM((halves, deep + 2 * SIDE * 16, B), bf16)],
        18 * low_two.shape[0] * B * B,
        aliases={0: 0},
    )(buffer, hidden, low_two)


STEM = 64
STEM_SIDE = 16
CHANNELS = 12
SLABS = 19
STEM_LANES = STEM_SIDE * STEM
INPUT_LANES = CHANNELS * 2 * STEM_SIDE
WINDOW = 7


def frames_kernel(frames_ref, out_ref, rows):
    segments = frames_ref.shape[0]
    side = 2 * STEM_SIDE

    def segment_step(segment, carry):
        pieces = [
            frames_ref[segment, index + 1, colour].astype(f32)
            - frames_ref[segment, index, colour].astype(f32)
            for index in range(4)
            for colour in range(3)
        ]
        for group in range(3):
            rows[group, pl.ds(segment, side, stride=segments)] = jnp.concatenate(
                pieces[4 * group : 4 * group + 4], axis=1
            )
        return carry

    lax.fori_loop(0, segments, segment_step, 0)
    empty = jnp.zeros((segments, INPUT_LANES), bf16)
    for parity in range(2):
        for slab in (0, 1, SLABS - 1):
            out_ref[parity, slab] = empty
    for row in range(side):
        for group in range(3):
            out_ref[row % 2, row // 2 + 2, :, group * LANES : (group + 1) * LANES] = rows[
                group, row * segments : (row + 1) * segments
            ].astype(bf16)


def frames_block(frames):
    segments = frames.shape[0] * frames.shape[1]
    ordered = frames.transpose(0, 1, 2, 5, 3, 4).reshape(
        (segments, frames.shape[2], 3) + frames.shape[3:5]
    )
    shape = (2, SLABS, segments, INPUT_LANES)
    return kernel_call(
        frames_kernel,
        1,
        [whole_spec(ordered.shape)],
        whole_out(shape),
        jax.ShapeDtypeStruct(shape, bf16),
        [pltpu.VMEM((3, 2 * STEM_SIDE * segments, LANES), f32)],
        ordered.size * 100,
    )(ordered)


def stem_rows(input_ref, offset):
    parity = 1 - offset % 2
    top = (offset - 3) // 2 + 2 if parity == 0 else (offset - 4) // 2 + 2
    found = input_ref[parity, top : top + STEM_SIDE]
    return found.reshape(-1, INPUT_LANES)


def band_select(turned=False):
    shape = [STEM_SIDE // 2, CHANNELS, 2 * STEM_SIDE, 2, LANES]
    axes = [0, 1, 2, 3, 4]
    if turned:
        shape, axes = [shape[axis] for axis in (0, 3, 4, 1, 2)], [0, 3, 4, 1, 2]
    pair, channel, place, which, entry = (
        lax.broadcasted_iota(jnp.int32, shape, axis) for axis in axes
    )
    met = (entry % CHANNELS == channel) & (entry < WINDOW * CHANNELS)
    met = met & (place == 2 * (2 * pair + which) + entry // CHANNELS - 3)
    ends = (2 * LANES, INPUT_LANES) if turned else (INPUT_LANES, 2 * LANES)
    return met.astype(bf16).reshape((STEM_SIDE // 2,) + ends)


def pair_weights(stem_weight):
    rows = stem_weight.reshape(WINDOW, WINDOW * CHANNELS, STEM)
    rows = jnp.pad(rows, ((0, 0), (0, LANES - WINDOW * CHANNELS), (0, 0)))
    none = jnp.zeros_like(rows)
    return jnp.concatenate(
        [jnp.concatenate([rows, none], 2), jnp.concatenate([none, rows], 2)], 1
    )


PAIRS = STEM_SIDE // 2


def stem_kernel(input_ref, select_ref, weights_ref, pre_ref, sums_ref, bands):
    selects = select_ref[...].reshape(PAIRS * INPUT_LANES, 2 * LANES)
    for offset in range(WINDOW):
        band = product(selects, weights_ref[offset]).astype(bf16)
        top = offset * INPUT_LANES
        for pair in range(PAIRS):
            bands[top : top + INPUT_LANES, pair * LANES : (pair + 1) * LANES] = band[
                pair * INPUT_LANES : (pair + 1) * INPUT_LANES
            ]
    rows = jnp.concatenate([stem_rows(input_ref, offset) for offset in range(WINDOW)], axis=1)
    for half in range(2):
        where = slice(half * WIDE, (half + 1) * WIDE)
        found = product(rows, bands[:, where])
        pre_ref[:, where] = found
        sums_ref[0:1, where] = jnp.sum(found, 0, keepdims=True)
        sums_ref[1:2, where] = jnp.sum(found * found, 0, keepdims=True)


def stem_block(inputs, select, weights, after=()):
    rows = inputs.shape[2] * STEM_SIDE
    return kernel_call(
        stem_kernel,
        1,
        [whole_spec(inputs.shape), whole_spec(select.shape), whole_spec(weights.shape)],
        [whole_out((rows, STEM_LANES)), whole_out((2, STEM_LANES))],
        [jax.ShapeDtypeStruct((rows, STEM_LANES), f32),
         jax.ShapeDtypeStruct((2, STEM_LANES), f32)],
        [pltpu.VMEM((WINDOW * INPUT_LANES, STEM_LANES), bf16)],
        2 * WINDOW * rows * INPUT_LANES * STEM_LANES,
        after=after,
    )(inputs, select, weights)


def stem_norm_kernel(count, pre_ref, in_sums_ref, affine_ref, cotangent_ref,
                     out_ref, grad_ref, sums_ref):
    def step_body(step, carry):
        where = lanes(step, LANES)
        mean, inverse, gain, shift = (
            spread(row) for row in constants(in_sums_ref[:, where], affine_ref[:, where], count)
        )
        first = jnp.zeros((16, LANES), f32)
        second = jnp.zeros((16, LANES), f32)
        for chunk in range(pre_ref.shape[0] // 16):
            rows = slice(chunk * 16, chunk * 16 + 16)
            unit = (pre_ref[rows, where] - mean) * inverse
            norm = unit * gain + shift
            sigma = sigmoid(norm)
            output = norm * sigma
            out_ref[rows, where] = output.astype(bf16)
            grad = cotangent_ref[rows, where].astype(f32) * (sigma + output * (1.0 - sigma))
            grad_ref[rows, where] = grad
            first = first + grad
            second = second + grad * unit
        sums_ref[0:1, where] = jnp.sum(first, 0, keepdims=True)
        sums_ref[1:2, where] = jnp.sum(second, 0, keepdims=True)
        return carry

    lax.fori_loop(0, STEM_LANES // LANES, step_body, 0)


def stem_norm_block(pre, sums, affine, cotangent, count, after=()):
    shape = pre.shape
    return kernel_call(
        functools.partial(stem_norm_kernel, count),
        1,
        [whole_spec(shape), whole_spec(sums.shape), whole_spec(affine.shape), whole_spec(shape)],
        [whole_out(shape), whole_out(shape), whole_out((2, STEM_LANES))],
        [jax.ShapeDtypeStruct(shape, bf16), jax.ShapeDtypeStruct(shape, f32),
         jax.ShapeDtypeStruct((2, STEM_LANES), f32)],
        [],
        4000 * pre.size,
        after=after,
    )(pre, sums, affine, cotangent)


def stem_back_kernel(count, input_ref, select_ref, pre_ref, in_sums_ref, affine_ref, grad_ref,
                     grads_ref, out_ref, low):
    def low_step(step, carry):
        where = lanes(step, LANES)
        mean, inverse, gain, _ = constants(in_sums_ref[:, where], affine_ref[:, where], count)
        scale = spread(gain * inverse)
        offset = spread(grads_ref[0:1, where] / count)
        along = spread(grads_ref[1:2, where] / count * inverse)
        mean = spread(mean)
        for chunk in range(pre_ref.shape[0] // 16):
            rows = slice(chunk * 16, chunk * 16 + 16)
            centred = pre_ref[rows, where] - mean
            low[rows, where] = (
                scale * (grad_ref[rows, where] - offset - centred * along)
            ).astype(bf16)
        return carry

    lax.fori_loop(0, STEM_LANES // LANES, low_step, 0)
    selects = jnp.concatenate([select_ref[pair] for pair in range(PAIRS)], axis=1)
    for offset in range(WINDOW):
        band = product(stem_rows(input_ref, offset).T, low[...]).astype(bf16)
        lined = [band[:, pair * LANES : (pair + 1) * LANES] for pair in range(PAIRS)]
        out_ref[offset] = product(selects, jnp.concatenate(lined, axis=0))


def stem_back_block(inputs, select, pre, sums, affine, grad, grads, count, after=()):
    shape = pre.shape
    out = (WINDOW, 2 * LANES, LANES)
    return kernel_call(
        functools.partial(stem_back_kernel, count),
        1,
        [whole_spec(inputs.shape), whole_spec(select.shape), whole_spec(shape),
         whole_spec(sums.shape), whole_spec(affine.shape), whole_spec(shape),
         whole_spec(grads.shape)],
        whole_out(out),
        jax.ShapeDtypeStruct(out, f32),
        [pltpu.VMEM(shape, bf16)],
        2 * WINDOW * shape[0] * INPUT_LANES * STEM_LANES,
        after=after,
    )(inputs, select, pre, sums, affine, grad, grads)


SMALL_ROWS = 32
FIRST_ROWS = 64 + SMALL_ROWS


def cut_kernel(me_ref, squeeze_ref, expand_ref, reduce_ref, spatial_ref, restore_ref, class_ref,
               stem_ref, next_ref, scale_ref, outer_ref, gain_one_ref, shift_one_ref,
               gain_two_ref, shift_two_ref, stem_gain_ref, stem_shift_ref,
               first_out, pair_out, spatial_out, late_out, small):
    part = me_ref[0] & 3
    first_out[0:64] = squeeze_ref[pl.ds(pl.multiple_of(part * 64, 64), 64)]
    small[...] = jnp.zeros_like(small)
    edge = stem_ref.shape[1] - B
    small[0:8] = stem_ref[:, 0:B].astype(f32)
    small[8:16, 0:edge] = stem_ref[:, B:].astype(f32)
    small[16:25, 0 : next_ref.shape[1]] = next_ref[...].astype(f32)
    small[16:25, LANES : LANES + scale_ref.shape[1]] = scale_ref[...].astype(f32)
    small[25:26] = outer_ref[...].astype(f32)
    for place, ref in enumerate((gain_one_ref, shift_one_ref, gain_two_ref, shift_two_ref)):
        small[26:27, place * LANES : place * LANES + ref.shape[1]] = ref[...].astype(f32)
    small[27:28, 0 : stem_gain_ref.shape[1]] = stem_gain_ref[...].astype(f32)
    small[27:28, LANES : LANES + stem_shift_ref.shape[1]] = stem_shift_ref[...].astype(f32)
    first_out[64:] = small[...].astype(bf16)
    pair_out[0:PAIR_ROWS] = reduce_ref[pl.ds(pl.multiple_of(part * 64, 64), 64)]
    for half in range(2):
        pair_out[PAIR_ROWS:, half * TILE : (half + 1) * TILE] = expand_ref[
            pl.ds(pl.multiple_of(part * 128 + half * 64, 64), 64)
        ]
    for tap in range(9):
        spatial_out[tap * 16 : tap * 16 + 16] = spatial_ref[
            tap, pl.ds(pl.multiple_of(part * 16, 16), 16)
        ]
    late_out[0:RESTORE_ROWS] = restore_ref[:, pl.ds(pl.multiple_of(part * B, B), B)]
    for half in range(2):
        rows = pl.ds(pl.multiple_of(part * 64 + half * 32, 32), 32)
        late_out[RESTORE_ROWS:, half * TILE : (half + 1) * TILE] = class_ref[rows]


def cut_block(me, *weights):
    shapes = [(FIRST_ROWS, B), (2 * PAIR_ROWS, B), (SPATIAL_ROWS, B), (LATE_ROWS, B)]
    return kernel_call(
        cut_kernel,
        1,
        [SCALAR] + [whole_spec(weight.shape) for weight in weights],
        [whole_out(shape) for shape in shapes],
        [jax.ShapeDtypeStruct(shape, bf16) for shape in shapes],
        [pltpu.VMEM((SMALL_ROWS, B), f32)],
        1000000,
    )(me, *weights)


def unpack_kernel(me_ref, first_ref, squeeze_out, weights_out, next_out, scale_out,
                  one_out, two_out, three_out, stem_out):
    squeeze_out[...] = first_ref[:, 0:64]
    wide = first_ref.shape[0]
    small = []
    for index in range(wide):
        mask = (me_ref[0] >> 2) ^ index
        entry = (mask & 1) * 4 + (mask >> 1)
        small.append(first_ref[entry, 64:].astype(f32))

    def joined(row, at, width, rows=1):
        return jnp.concatenate(
            [values[row : row + rows, at : at + width] for values in small], axis=1
        )

    own = B // wide
    next_out[...] = joined(16, 0, own, 9)
    scale_out[...] = joined(16, LANES, own, 9)
    one_out[0:1] = joined(26, 0, own)
    one_out[1:2] = joined(26, LANES, own)
    two_out[0:1] = joined(26, 2 * LANES, own)
    two_out[1:2] = joined(26, 3 * LANES, own)
    three_out[0:1] = joined(25, 0, TILE)
    three_out[1:2] = joined(25, TILE, TILE)
    for row in range(2):
        stem = joined(27, row * LANES, STEM // wide)
        stem_out[row : row + 1] = jnp.concatenate([stem] * STEM_SIDE, axis=1)
    columns = jnp.concatenate(
        [jnp.concatenate([values[0:8], values[8:16, 0:LANES]], axis=1) for values in small], axis=0
    )
    rows = columns.T
    place = lax.broadcasted_iota(jnp.int32, (LANES, STEM), 0)
    none = jnp.zeros((LANES, STEM), f32)
    for offset in range(WINDOW):
        top = offset * WINDOW * CHANNELS
        block = jnp.where(place < WINDOW * CHANNELS, rows[top : top + LANES], 0.0)
        weights_out[offset, 0:LANES] = jnp.concatenate([block, none], axis=1).astype(bf16)
        weights_out[offset, LANES:] = jnp.concatenate([none, block], axis=1).astype(bf16)


def unpack_block(me, first):
    shapes = [
        ((first.shape[0], 64, B), bf16), ((WINDOW, 2 * LANES, LANES), bf16), ((9, R), f32), ((9, R), f32), ((2, B), f32),
        ((2, B), f32), ((2, C), f32), ((2, STEM_LANES), f32),
    ]
    return kernel_call(
        unpack_kernel,
        1,
        [SCALAR, whole_spec(first.shape)],
        [whole_out(shape) for shape, _ in shapes],
        [jax.ShapeDtypeStruct(shape, kind) for shape, kind in shapes],
        [],
        1000000,
    )(me, first)


def shards(
    frames,
    tokens,
    stem_cotangent,
    crop_counts,
    labels,
    stem_weight,
    stem_gain,
    stem_shift,
    w_squeeze,
    next_kernel,
    scale_kernel,
    w_expand,
    w_reduce,
    gain_one,
    shift_one,
    w_spatial,
    gain_two,
    shift_two,
    w_restore,
    gain_three,
    shift_three,
    w_class,
    class_bias,
):
    view_count = frames.shape[0]
    row_count = tokens.shape[0]
    devices = lax.axis_size(AXES)
    wide = lax.axis_size("wide")
    narrow = lax.axis_size("narrow")
    count = float(row_count * devices)
    segments = view_count * SEG
    stem_rows_here = segments * STEM_SIDE
    stem_count = float(stem_rows_here * STEM_SIDE * devices)
    direct = wide == C // TILE and narrow == 4
    me = lax.axis_index(AXES)
    me_array = (me if direct else 0 * me).astype(jnp.int32).reshape(1)

    stem_width = stem_weight.shape[1]
    inner_width = gain_one.shape[0]
    outer_width = gain_three.shape[0]

    def by_output_row(values):
        values = values.reshape(segments, STEM_SIDE, STEM_LANES)
        return values.transpose(1, 0, 2).reshape(stem_rows_here, STEM_LANES)

    if direct:
        first_own, pair_own, spatial_own, late_own = cut_block(
            me_array, w_squeeze, w_expand, w_reduce, w_spatial, w_restore,
            jnp.pad(w_class, ((0, 0), (0, TILE - CLASSES))), stem_weight.T, next_kernel,
            scale_kernel, jnp.concatenate([gain_three, shift_three])[None], gain_one[None],
            shift_one[None], gain_two[None], shift_two[None], stem_gain[None], stem_shift[None],
        )
        firsts, pairs, spatials = Gather(first_own), Gather(pair_own), HalvedGather(spatial_own)
        (cotangent, select), came, _ = beside(
            lambda grads: (by_output_row(grads), band_select()), [stem_cotangent], firsts.depth()
        )
        firsts.take_depth(came)
        inputs, came, _ = beside(frames_block, [frames], firsts.second() + pairs.depth())
        firsts.take_second(came[:1])
        pairs.take_depth(came[1:])
        (
            squeeze_own, weights, full_next, full_scale, affine_one, affine_two, affine_three, stem_affine,
        ) = unpack_block(me_array, firsts.eight)
        (stem_pre, stem_part), came, _ = beside(
            stem_block, [inputs, select, weights],
            [(squeeze_own, 2)] + pairs.second() + spatials.depth(),
        )
        squeeze_far = came[0]
        pairs.take_second(came[1:2])
        spatials.take_depth(came[2:])
        stem_pre, came, _ = beside(
            lambda values: values, [stem_pre], [(squeeze_own, 1), (squeeze_far, 1)]
        )
        squeeze = (squeeze_own, squeeze_far) + tuple(came)
    else:
        squeeze, pair, spatial, late = gathered(
            w_squeeze, w_expand, w_reduce, w_spatial, w_restore, w_class
        )

        def whole(values):
            return lax.all_gather(values, "wide", axis=values.ndim - 1, tiled=True).astype(f32)

        weights = pair_weights(whole(stem_weight).astype(bf16))
        full_next, full_scale = whole(next_kernel), whole(scale_kernel)
        affine_one = jnp.stack([whole(gain_one), whole(shift_one)])
        affine_two = jnp.stack([whole(gain_two), whole(shift_two)])
        affine_three = jnp.stack([whole(gain_three), whole(shift_three)])
        stem_affine = jnp.tile(jnp.stack([whole(stem_gain), whole(stem_shift)]), (1, STEM_SIDE))
        inputs, select, cotangent = frames_block(frames), band_select(), by_output_row(stem_cotangent)
        stem_pre, stem_part = stem_block(inputs, select, weights)
    stem_part = stem_part.reshape(2, STEM_SIDE, STEM).sum(1).reshape(1, 2 * STEM)

    def stem_lanes(sums):
        return jnp.tile(sums[2, : 2 * STEM].reshape(2, STEM), (1, STEM_SIDE))

    def with_row(sums, row):
        return jnp.concatenate([sums, jnp.pad(row, ((0, 0), (0, sums.shape[1] - row.shape[1])))])

    mixing_operands = [me_array, squeeze, tokens, full_next, full_scale]
    if direct:
        (upcoming, differ, mixed_low), came, _ = beside(
            mixing_block, mixing_operands, pairs.third() + spatials.second()
        )
        pairs.take_third(came[:1])
        spatials.take_second(came[1:])
        (mixed_low, late_own), came, _ = beside(
            lambda values, mine: (values, mine), [mixed_low, late_own], pairs.core()
        )
        pairs.take_core(came)
        late = lax.all_gather(late_own, AXES)
        pair = pairs.arrays
    else:
        upcoming, differ, mixed_low = mixing_block(*mixing_operands)
    gate_operands = [me_array, pair, tokens, mixed_low]
    if direct:
        (logit, gated_low, pre_one, one_part), came, _ = beside(
            gate_block, gate_operands, spatials.third_of(0)
        )
        spatials.take_third_of(0, came)
        one_sums, came, _ = beside(
            swap_total, [with_row(one_part, stem_part)],
            spatials.third_of(1) + spatials.core_of(0),
        )
        spatials.take_third_of(1, came[:1])
        spatials.take_core_of(0, came[1:])
        one_sums, came, _ = beside(lambda values: values, [one_sums], spatials.core_of(1))
        spatials.take_core_of(1, came)
        spatial = spatials.arrays
    else:
        logit, gated_low, pre_one, one_part = gate_block(*gate_operands)
        one_sums = swap_total(with_row(one_part, stem_part))
    stem_sums = stem_lanes(one_sums)
    hidden_one, pre_two, two_part = second_block(
        me_array, spatial, pre_one, one_sums, affine_one, count
    )
    stem_out, stem_norm_grad, stem_part = stem_norm_block(
        stem_pre, stem_sums, stem_affine, cotangent, stem_count
    )
    stem_part = stem_part.reshape(2, STEM_SIDE, STEM).sum(1).reshape(1, 2 * STEM)
    two_sums = swap_total(two_part)
    hidden_two, pre_three, centres, three_part = third_block(pre_two, two_sums, affine_two, late, count)
    three_sums = total(with_row(three_part, stem_part))
    stem_grads = stem_lanes(three_sums)
    bias = jnp.pad(class_bias.astype(f32), (0, TILE - CLASSES))[None]
    activations, slope, view_sums, view_logits, pooled_low = fourth_block(
        pre_three, centres, gated_low, three_sums, affine_three, late, bias, count
    )
    pooled_low = pooled_low[:view_count]

    ends = jnp.cumsum(crop_counts)
    starts = ends - crop_counts
    positions = (me - 1) * view_count + jnp.arange(3 * view_count, dtype=jnp.int32)
    video = jnp.sum((ends[None, :] <= positions[:, None]).astype(jnp.int32), 1)
    own_video = video[view_count : 2 * view_count]
    belongs = (
        own_video[:, None] == jnp.arange(crop_counts.shape[0], dtype=jnp.int32)[None, :]
    ).astype(jnp.int32)
    own_count = jnp.sum(belongs * crop_counts[None, :], 1).astype(f32)
    own_label = jnp.sum(belongs * labels[None, :], 1)
    own_start = jnp.sum(belongs * starts[None, :], 1)
    first = (own_start == positions[view_count : 2 * view_count]).astype(f32)
    same = (own_video[:, None] == video[None, :]).astype(f32) / own_count[:, None]
    target = (own_label[:, None] == jnp.arange(TILE, dtype=jnp.int32)[None, :]).astype(f32)
    marks = jnp.concatenate([same, 1.0 / own_count[:, None], first[:, None]], axis=1)
    marks = jnp.pad(marks, ((0, 8 - view_count), (0, LANES - marks.shape[1])))
    target = jnp.pad(target, ((0, 8 - view_count), (0, 0)))

    before = lax.ppermute(view_logits, AXES, [(i, i + 1) for i in range(devices - 1)])
    following = lax.ppermute(view_logits, AXES, [(i + 1, i) for i in range(devices - 1)])
    three_part, pooled_grad, view_grad_low = video_block(
        before, view_logits, following, marks, target, view_sums, late, view_count
    )
    view_grad_low = view_grad_low[:view_count]

    own_parts = pooled_low.reshape(view_count, wide, outer_width).swapaxes(0, 1)
    grad_parts = jnp.broadcast_to(
        view_grad_low, (wide, view_count, TILE)
    )
    factors = jnp.concatenate([own_parts, grad_parts], axis=2)
    factors = jnp.broadcast_to(factors[:, None], (wide, narrow) + factors.shape[1:])
    factors = factors.reshape((devices,) + factors.shape[2:])

    def send_factors(parts):
        return lax.all_to_all(parts, AXES, 0, 0, tiled=True)

    three_grads = total(three_part)
    class_bias_grad = three_grads[2, :CLASSES]
    loss = three_grads[2, CLASSES] / crop_counts.shape[0]

    fifth_operands = [
        slope, pre_three, centres, pooled_grad, three_sums, affine_three, three_grads, late,
        pre_two, two_sums, affine_two,
    ]
    run_fifth = functools.partial(fifth_block, count=count)
    run_sixth = functools.partial(sixth_block, count=count)
    run_stem_back = functools.partial(stem_back_block, count=stem_count)

    def stem_back_operands():
        return [inputs, band_select(True), stem_pre, stem_sums, stem_affine, stem_norm_grad, stem_grads]
    run_outer = outer_block_of(R // 4)

    def sixth_operands():
        return [
            me_array, spatial, norm_two_grad, pre_two, two_sums, affine_two, two_grads, pre_one,
            one_sums, affine_one,
        ]

    def low_operands():
        return [me_array, norm_one_grad, pre_one, one_sums, affine_one, one_grads, gated_low]

    def gate_back_operands():
        return [me_array, pair, low_one, slope, pooled_grad, tokens, logit]

    def mixing_back_operands():
        return [me_array, pair, logit_grad, upcoming, differ, full_next, full_scale]

    def few_of(stem_back, kernel_grads):
        stem_back = stem_back[:, :LANES, :STEM] + stem_back[:, LANES:, STEM:]
        stem_grad = stem_back[:, : WINDOW * CHANNELS].reshape(-1, STEM)
        stem_cut = stem_grad.T.reshape(8, 8, -1)
        stem_cut = jnp.pad(stem_cut, ((0, 0), (0, 0), (0, 3 * TILE - stem_cut.shape[2])))
        kernel_cut = kernel_grads.reshape(2, 9, 8, R // 8).transpose(2, 1, 0, 3)
        kernel_cut = jnp.pad(kernel_cut, ((0, 0), (0, 0), (0, 0), (0, LANES - R // 8)))
        few = jnp.concatenate([stem_cut.reshape(8, 24, TILE), kernel_cut.reshape(8, 9, TILE)], 1)
        return jnp.pad(few, ((0, 0), (0, FEW_ROWS - few.shape[1]), (0, 0)))

    if direct:
        low_three, norm_two_grad, two_part = run_fifth(*fifth_operands)
        (buffer, two_grads), _, _ = beside(
            lambda hidden, low, part: (restore_outer_block(hidden, low), swap_total(part)),
            [hidden_two, low_three, two_part], [],
        )
        (low_two, norm_one_grad, one_part, factors), _, _ = beside(
            lambda parts, *operands: (*run_sixth(*operands), send_factors(parts)),
            [factors] + sixth_operands(), [],
        )
        (buffer, one_grads), _, _ = beside(
            lambda values, hidden, low, part: (
                spatial_block(values.reshape(32, -1, WIDE), hidden, low), swap_total(part)
            ),
            [buffer, hidden_one, low_two, one_part], [],
        )
        buffer = lax.psum_scatter(
            buffer.reshape(8, -1, WIDE), "wide", scatter_dimension=0, tiled=False
        )
        quarter = (4, 2, 2, R // 4, TILE)
        low_one, reduce_half = low_outer_block(*low_operands(), count)
        reduced_sum = Sum(reduce_half, quarter, 0)
        low_one, came, _ = beside(lambda values: values, [low_one], reduced_sum.core())
        reduced_sum.take_core(came)
        (logit_grad, tokens_part), came, _ = beside(
            gate_back_block, gate_back_operands(), reduced_sum.split("x")
        )
        reduced_sum.take(came)
        expand_half, came, _ = beside(
            run_outer, [me_array, mixed_low, logit_grad], reduced_sum.split("y")
        )
        reduced_sum.take(came)
        expand_sum = Sum(expand_half, quarter, 0)
        logit_grad, came, _ = beside(lambda values: values, [logit_grad], expand_sum.core())
        expand_sum.take_core(came)
        (low_squeezed, kernel_grads), came, _ = beside(
            mixing_back_block, mixing_back_operands(),
            expand_sum.split("x") + reduced_sum.split("z"),
        )
        expand_sum.take(came[:1])
        reduced_sum.take(came[1:])
        squeeze_half, came, _ = beside(
            run_outer, [me_array, low_squeezed, tokens],
            expand_sum.split("y") + reduced_sum.spread(),
        )
        expand_sum.take(came[:1])
        reduced_sum.take_spread(came[1:])
        squeezed = Sum(squeeze_half, quarter, 0)
        tokens_part, came, _ = beside(lambda values: values, [tokens_part], squeezed.core())
        squeezed.take_core(came)
        stem_back, came, _ = beside(
            run_stem_back, stem_back_operands(), squeezed.split("x") + expand_sum.split("z")
        )
        squeezed.take(came[:1])
        expand_sum.take(came[1:])
        (tokens_grad, few), came, _ = beside(
            lambda grads, *operands: (
                tokens_block(*operands), lax.all_to_all(grads, "wide", 0, 0, tiled=True)
            ),
            [few_of(stem_back, kernel_grads), me_array, squeeze, tokens_part, low_squeezed],
            squeezed.split("y") + expand_sum.spread(),
        )
        squeezed.take(came[:1])
        expand_sum.take_spread(came[1:])
        few = jnp.sum(few, 0)
        buffer = buffer.reshape(4, -1, WIDE)
        near_place = lax.axis_index("narrow")
        (few, stem_out, own), came, _ = beside(
            lambda part, *kept: (
                part + exchange(part, 1) + exchange(part, 2) + exchange(part, 3), *kept
            ),
            [few, stem_out, lax.dynamic_index_in_dim(buffer, near_place, 0, keepdims=False)],
            squeezed.split("z") + [
                (lax.dynamic_index_in_dim(buffer, near_place ^ mask, 0, keepdims=False), mask)
                for mask in (1, 2, 3)
            ],
        )
        squeezed.take(came[:3])
        own = own.astype(f32)
        for part in came[3:]:
            own = own + part.astype(f32)
        buffers = Sum((None, None), (), 0)
        buffers.values = own
        _, came, _ = beside(lambda: None, [], squeezed.spread() + buffers.spread())
        squeezed.take_spread(came[:3])
        buffers.take_spread(came[3:])
        buffer = buffers.whole
        sum_stem = few[:24].reshape(8, 3 * TILE)[:, : stem_weight.shape[0]].T
        sum_next = few[24:33, :inner_width]
        sum_scale = few[24:33, LANES : LANES + inner_width]
        sum_restore = buffer[:, :RESTORE_ROWS].swapaxes(0, 1).reshape(w_restore.shape)
        sum_spatial = buffer[:, RESTORE_ROWS:].reshape(4, 9, 16, B).swapaxes(0, 1)
        sum_spatial = sum_spatial.reshape(w_spatial.shape)
        sum_reduce = reduced_sum.whole.reshape(B, TILE).T
        sum_expand = expand_sum.whole.reshape(R, TILE)
        sum_squeeze = squeezed.whole.reshape(R, TILE).T
    else:
        low_three, norm_two_grad, two_part = run_fifth(*fifth_operands)
        buffer = restore_outer_block(hidden_two, low_three)
        two_grads = swap_total(two_part)
        low_two, norm_one_grad, one_part = run_sixth(*sixth_operands())
        factors = send_factors(factors)
        one_grads = swap_total(one_part)
        buffer = spatial_block(buffer.reshape(32, -1, WIDE), hidden_one, low_two)
        low_one, reduce_half = low_outer_block(*low_operands(), count)
        logit_grad, tokens_part = gate_back_block(*gate_back_operands())
        expand_half = run_outer(me_array, mixed_low, logit_grad)
        low_squeezed, kernel_grads = mixing_back_block(*mixing_back_operands())
        few = few_of(run_stem_back(*stem_back_operands()), kernel_grads)
        squeeze_half = run_outer(me_array, low_squeezed, tokens)
        tokens_grad = tokens_block(me_array, squeeze, tokens_part, low_squeezed)
        few = lax.psum(few, AXES)
        sum_stem = few[:, :24].reshape(STEM, 3 * TILE)[:, : stem_weight.shape[0]].T
        sum_next, sum_scale = (
            few[:, 24:33, at : at + R // 8].swapaxes(0, 1).reshape(9, R) for at in (0, LANES)
        )

        def own_columns(values, width):
            return lax.dynamic_slice_in_dim(values, lax.axis_index("wide") * width, width, 1)

        sum_stem = own_columns(sum_stem, stem_width)
        sum_next = own_columns(sum_next, inner_width)
        sum_scale = own_columns(sum_scale, inner_width)
        sum_restore, sum_spatial, sum_reduce, sum_expand, sum_squeeze = reduced(
            buffer, reduce_half, expand_half, squeeze_half
        )
    factors = factors.reshape(devices * view_count, outer_width + TILE)
    sum_class = product_left(
        factors[:, :outer_width], factors[:, outer_width : outer_width + CLASSES]
    )

    stem_features = stem_out.reshape(STEM_SIDE, segments, STEM_LANES)
    stem_features = stem_features.transpose(1, 0, 2).reshape(-1, STEM)

    def own_slice(values, width):
        return lax.dynamic_slice_in_dim(values, lax.axis_index("wide") * width, width)

    return (
        activations,
        stem_features,
        tokens_grad,
        sum_stem,
        own_slice(stem_grads[1, :STEM], stem_width),
        own_slice(stem_grads[0, :STEM], stem_width),
        sum_squeeze,
        sum_next,
        sum_scale,
        sum_expand,
        sum_reduce,
        own_slice(one_grads[1], inner_width),
        own_slice(one_grads[0], inner_width),
        sum_spatial,
        own_slice(two_grads[1], inner_width),
        own_slice(two_grads[0], inner_width),
        sum_restore,
        own_slice(three_grads[1], outer_width),
        own_slice(three_grads[0], outer_width),
        sum_class,
        class_bias_grad,
        loss,
    )


def solution(mesh):
    in_specs = (
        P(("wide", "narrow"), None, None, None, None, None),
        P(("wide", "narrow"), None),
        P(("wide", "narrow"), None),
        P(),
        P(),
        P(None, "wide"),
        P("wide"),
        P("wide"),
        P("wide", None),
        P(None, "wide"),
        P(None, "wide"),
        P(None, "wide"),
        P("wide", None),
        P("wide"),
        P("wide"),
        P(None, "wide", None),
        P("wide"),
        P("wide"),
        P("wide", None),
        P("wide"),
        P("wide"),
        P("wide", None),
        P(),
    )
    out_specs = (
        P(("wide", "narrow"), None),
        P(("wide", "narrow"), None),
        P(("wide", "narrow"), None),
        P(None, "wide"),
        P("wide"),
        P("wide"),
        P("wide", None),
        P(None, "wide"),
        P(None, "wide"),
        P(None, "wide"),
        P("wide", None),
        P("wide"),
        P("wide"),
        P(None, "wide", None),
        P("wide"),
        P("wide"),
        P("wide", None),
        P("wide"),
        P("wide"),
        P("wide", None),
        P(),
        P(),
    )
    return jax.shard_map(shards, mesh=mesh, in_specs=in_specs, out_specs=out_specs, check_vma=False)
```

```python
import functools

import jax
import jax.numpy as jnp
from jax import lax
from jax.experimental import pallas as pl
from jax.experimental.pallas import tpu as pltpu
from jax.sharding import PartitionSpec as P

C = 2048
B = 512
R = 512
CLASSES = 174
SEG = 8
SIDE = 7
PER_VIEW = SEG * SIDE * SIDE

epsilon = 1e-05
loss_scale = 1024.0

AXES = ("wide", "narrow")
f32 = jnp.float32
bf16 = jnp.bfloat16


def product(first_operand, second_operand):
    return jnp.dot(first_operand, second_operand, preferred_element_type=f32)


def product_left(first_operand, second_operand):
    return lax.dot_general(
        first_operand, second_operand, (((0,), (0,)), ((), ())), preferred_element_type=f32
    )


def product_right(first_operand, second_operand):
    return lax.dot_general(
        first_operand, second_operand, (((1,), (1,)), ((), ())), preferred_element_type=f32
    )


def exchange(values, mask):
    size = lax.axis_size(AXES)
    return lax.ppermute(values, AXES, [(index, index ^ mask) for index in range(size)])


def own_bit(bit):
    return (lax.axis_index(AXES) >> bit) & 1


def total(values):
    bits = lax.axis_size(AXES).bit_length() - 1
    values = values + exchange(values, 1)
    for bit in range(1, bits, 2):
        masks = [1 << bit]
        if bit + 1 < bits:
            masks += [2 << bit, 3 << bit]
        parts = [exchange(values, mask) for mask in masks]
        for part in parts:
            values = values + part
    return values


def total_beside(values, run, inputs):
    bits = lax.axis_size(AXES).bit_length() - 1
    values = values + exchange(values, 1)
    for bit in range(1, bits, 2):
        masks = [1 << bit] + ([2 << bit, 3 << bit] if bit + 1 < bits else [])
        if bit == 3:
            out, parts, _ = beside(run, inputs, [(values, mask) for mask in masks])
        else:
            parts = [exchange(values, mask) for mask in masks]
        for part in parts:
            values = values + part
    return values, out


def swap_total(copies):
    return jnp.sum(lax.all_to_all(copies, AXES, 0, 0, tiled=True), 0)


def to_all(values):
    return jnp.broadcast_to(values[None], (lax.axis_size(AXES),) + values.shape)


def beside(run, inputs, sends, more=()):
    inputs, arrays = lax.optimization_barrier((tuple(inputs), [array for array, _ in sends]))
    came = [exchange(array, mask) for array, (_, mask) in zip(arrays, sends)]
    return lax.optimization_barrier((run(*inputs), came, tuple(more)))


def launch(run, inputs, sends):
    inputs, arrays = lax.optimization_barrier((tuple(inputs), [array for array, _ in sends]))
    came = [exchange(array, mask) for array, (_, mask) in zip(arrays, sends)]
    return lax.optimization_barrier(run(*inputs)), came


class Gather:
    def __init__(self, block):
        self.block = block

    def depth(self):
        return [(self.block, mask) for mask in (8, 16, 24)]

    def take_depth(self, came):
        self.four = join([part[None] for part in (self.block, *came)])

    def second(self):
        return [(self.four, 4)]

    def take_second(self, came):
        self.eight = join([self.four, came[0]])

    def third(self):
        return [(self.eight, 2)]

    def take_third(self, came):
        self.other = came[0]

    def core(self):
        return [(self.eight, 1), (self.other, 1)]

    def take_core(self, came):
        self.arrays = (self.eight, self.other) + tuple(came)


class HalvedGather(Gather):
    def take_second(self, came):
        self.parts = [self.four, came[0]]
        self.far = [None, None]
        self.arrays = [None] * 8

    def third_of(self, part):
        return [(self.parts[part], 2)]

    def take_third_of(self, part, came):
        self.far[part] = came[0]

    def core_of(self, part):
        return [(self.parts[part], 1), (self.far[part], 1)]

    def take_core_of(self, part, came):
        self.arrays[part::2] = [self.parts[part], self.far[part], came[0], came[1]]


class Sum:
    def __init__(self, half, shape, lead):
        self.keep, self.send = half
        self.shape, self.lead, self.axes = shape, lead, "zyx"

    def core(self):
        return [(self.send, 1)]

    def take_core(self, came):
        self.values = (self.keep.astype(f32) + came[0].astype(f32)).reshape(self.shape)

    def split(self, letter):
        place = self.lead + self.axes.index(letter)
        self.axes = self.axes.replace(letter, "")
        bit = {"x": 1, "y": 2, "z": 3}[letter]
        span = 3 if letter == "z" else 1
        mine = (lax.axis_index(AXES) >> bit) & span
        found = []
        for mask in range(1, span + 1):
            part = lax.dynamic_index_in_dim(self.values, mine ^ mask, place, keepdims=False)
            found.append((part.astype(bf16), mask << bit))
        self.values = lax.dynamic_index_in_dim(self.values, mine, place, keepdims=False)
        return found

    def split_parts(self, letter, at):
        ((send, mask),) = self.split(letter)
        return [(send[:at], mask)], [(send[at:], mask)]

    def take_parts(self, first, second):
        self.take([jnp.concatenate([first[0], second[0]])])

    def take(self, came):
        for part in came:
            self.values = self.values + part.astype(f32)

    def spread(self):
        self.part = self.values.astype(bf16)
        return [(self.part, mask) for mask in (1, 2, 3)]

    def take_spread(self, came):
        own, (core, over_x, both) = self.part, came
        odd, far = own_bit(0) == 1, own_bit(1) == 1
        near = [jnp.where(odd, core, own), jnp.where(odd, own, core)]
        away = [jnp.where(odd, both, over_x), jnp.where(odd, over_x, both)]
        self.whole = jnp.stack(
            [jnp.where(far, away[0], near[0]), jnp.where(far, away[1], near[1]),
             jnp.where(far, near[0], away[0]), jnp.where(far, near[1], away[1])]
        ).astype(f32)


def gathered(w_squeeze, w_expand, w_reduce, w_spatial, w_restore, w_class):
    def whole(weight, axis):
        return lax.all_gather(weight, "wide", axis=axis, tiled=True)

    def as_blocks(blocks):
        ordered = blocks.reshape((4, 2, 2, 2) + blocks.shape[1:])
        return [
            ordered[:, :, far, core].swapaxes(0, 1).reshape((8,) + blocks.shape[1:])
            for core in range(2)
            for far in range(2)
        ]

    squeeze = whole(w_squeeze, 0).reshape(32, -1, R)
    expand = whole(w_expand, 1).reshape(4, 2, PAIR_ROWS, 8, TILE).transpose(3, 0, 2, 1, 4)
    expand = expand.reshape(32, PAIR_ROWS, 2 * TILE)
    reduce = whole(w_reduce, 0).reshape(32, -1, B)
    spatial = whole(w_spatial, 1).reshape(9, 32, 16, B).swapaxes(0, 1).reshape(32, -1, B)
    restore = whole(w_restore, 0).reshape(8, 64, 4, B).swapaxes(1, 2).reshape(32, 64, B)
    classes = jnp.pad(whole(w_class, 0), ((0, 0), (0, TILE - CLASSES)))
    classes = classes.reshape(32, 2, CLASS_ROWS, TILE).swapaxes(1, 2).reshape(32, CLASS_ROWS, B)
    late = jnp.concatenate([restore, classes], axis=1)
    pair = jnp.concatenate([reduce, expand], axis=1)
    spatial = [part for array in as_blocks(spatial) for part in (array[:4], array[4:])]
    return as_blocks(squeeze), as_blocks(pair), spatial, late


def reduced(buffers, reduce_half, expand_half, squeeze_half):
    def whole(half, grain):
        keep, send = (part.astype(bf16) for part in half)
        shape = keep.shape[:1] + (-1, grain) + keep.shape[2:]
        both = jnp.stack([keep.reshape(shape), send.reshape(shape)], axis=2)
        return both.reshape(keep.shape[:1] + (-1,) + keep.shape[2:])

    def scattered(grad, axis):
        part = lax.psum_scatter(grad, "wide", scatter_dimension=axis, tiled=True)
        return lax.psum(part, "narrow").astype(f32)

    def columns(tiles):
        return tiles.swapaxes(0, 1).reshape(tiles.shape[1], -1)

    shared = jnp.stack([part.reshape(16, SHARED, 16, WIDE) for part in buffers], axis=1)
    shared = shared.transpose(2, 0, 1, 3, 4).reshape(SHARED, B, WIDE)
    restore = shared[:GROUPS].swapaxes(0, 1).reshape(B, C)
    spatial = shared[GROUPS:]
    return (
        scattered(restore, 0),
        scattered(spatial, 1),
        scattered(columns(whole(reduce_half, 128)), 1).T,
        scattered(columns(whole(expand_half, 128)), 1),
        scattered(columns(whole(squeeze_half, 128)), 1).T,
    )


CELLS = SIDE * SIDE
HALF = 2 * PER_VIEW
PADDED = SIDE + 2
MIB = 1 << 20
VMEM = 60
LANES = 128
TILE = 256


def cell_place(cell):
    return (cell // SIDE + 1) * PADDED + cell % SIDE + 1


def tap_place(cell, tap):
    return cell_place(cell) + (tap // 3 - 1) * PADDED + tap % 3 - 1


def dot_nt(first_operand, second_operand):
    return lax.dot_general(
        first_operand, second_operand, (((1,), (1,)), ((), ())), preferred_element_type=f32
    )


def dot_tn(first_operand, second_operand):
    return lax.dot_general(
        first_operand, second_operand, (((0,), (0,)), ((), ())), preferred_element_type=f32
    )


def sigmoid(values):
    return 0.5 * jnp.tanh(0.5 * values) + 0.5


def constants(sums, affine, count):
    mean = sums[0:1] / count
    inverse = lax.rsqrt(sums[1:2] / count - mean * mean + epsilon)
    return mean, inverse, affine[0:1], affine[1:2]


def spread(row, rows=16):
    return jnp.broadcast_to(row, (rows, row.shape[1]))


def lanes(index, width):
    return pl.ds(pl.multiple_of(index * width, width), width)


def clear_border(ref):
    zero = jnp.zeros(ref.shape[1:], ref.dtype)
    for place in range(PADDED * PADDED):
        if place // PADDED in (0, PADDED - 1) or place % PADDED in (0, PADDED - 1):
            ref[place] = zero


def fold(values):
    return values[0:8] + values[8:16]


def half_spec(width):
    return pl.BlockSpec((HALF, width), lambda step, *_: (step, 0))


def whole_spec(shape):
    return pl.BlockSpec(shape, lambda *_: (0,) * len(shape), pipeline_mode=pl.Buffered(1))


def whole_out(shape):
    return pl.BlockSpec(shape, lambda *_: (0,) * len(shape))


WIDE = 512
GROUPS = C // WIDE


def group_at(group):
    return slice(group * WIDE, (group + 1) * WIDE)


def chunks():
    for chunk in range(HALF // 16):
        yield chunk, slice(chunk * 16, chunk * 16 + 16)


ANY = pl.BlockSpec(memory_space=pl.ANY)
SCALAR = pl.BlockSpec(memory_space=pltpu.SMEM)


def kernel_call(kernel, steps, in_specs, out_specs, out_shapes, scratch, flops,
                transcendentals=0, after=(), vmem=VMEM, aliases=None):
    known = len(in_specs)
    grid = steps if isinstance(steps, tuple) else (steps,)

    def body(*refs):
        kernel(*refs[:known], *refs[known + len(after) :])

    call = pl.pallas_call(
        body,
        grid=grid,
        in_specs=list(in_specs) + [ANY] * len(after),
        out_specs=out_specs,
        out_shape=out_shapes,
        scratch_shapes=scratch,
        input_output_aliases=aliases or {},
        compiler_params=pltpu.CompilerParams(
            dimension_semantics=("arbitrary",) * len(grid), vmem_limit_bytes=vmem * MIB
        ),
        cost_estimate=pl.CostEstimate(
            flops=2 * flops, bytes_accessed=16 * MIB, transcendentals=transcendentals
        ),
    )
    return lambda *operands: call(*operands, *after)


def block_copies(me, sources, target, semaphores, rows=None, lanes_at=None, target_rows=None):
    copies = []
    split = len(sources) // 4
    for which, low_mask in enumerate((0, 2, 1, 3)):
        for entry in range(8):
            mask = low_mask | ((entry // 4) * 4) | ((entry % 4) << 3)
            if split == 1:
                taken = sources[which].at[entry]
            else:
                taken = sources[2 * which + entry // 4].at[entry % 4]
            place = target.at[me ^ mask]
            if rows is not None:
                taken = taken.at[rows] if lanes_at is None else taken.at[rows, lanes_at]
            if target_rows is not None:
                place = place.at[target_rows]
            copies.append(pltpu.make_async_copy(taken, place, semaphores.at[len(copies)]))
    return copies


PAIR_ROWS = 64


def reduce_copies(me, sources, target, semaphores):
    return block_copies(me, sources, target, semaphores, slice(0, PAIR_ROWS))


def expand_copies(me, sources, target, semaphores):
    rows = slice(PAIR_ROWS, 2 * PAIR_ROWS)
    found = []
    for part in range(2):
        found += block_copies(
            me, sources, target, semaphores.at[part], rows,
            slice(part * TILE, (part + 1) * TILE),
            slice(part * PAIR_ROWS, (part + 1) * PAIR_ROWS),
        )
    return found


def start(copies):
    for copy in copies:
        copy.start()


def wait(copies):
    for copy in copies:
        copy.wait()


def join_kernel(*refs):
    *sources, out_ref, semaphores = refs
    copies, top = [], 0
    for source in sources:
        count = source.shape[0]
        copies.append(
            pltpu.make_async_copy(
                source, out_ref.at[top : top + count], semaphores.at[len(copies)]
            )
        )
        top += count
    start(copies)
    wait(copies)


def join(arrays):
    count = sum(array.shape[0] for array in arrays)
    return kernel_call(
        join_kernel,
        1,
        [ANY] * len(arrays),
        ANY,
        jax.ShapeDtypeStruct((count,) + arrays[0].shape[1:], arrays[0].dtype),
        [pltpu.SemaphoreType.DMA((len(arrays),))],
        1000000,
        vmem=16,
    )(*arrays)


def first_step():
    return pl.program_id(0) == 0


def store_copies(copies_ref, sums):
    @pl.when(pl.program_id(0) == pl.num_programs(0) - 1)
    def _():
        values = sums[...]
        for index in range(copies_ref.shape[0]):
            copies_ref[index] = values


def add_moments(sums_ref, where, first, second):
    sums_ref[0:1, where] += jnp.sum(first, 0, keepdims=True)
    sums_ref[1:2, where] += jnp.sum(second, 0, keepdims=True)


def mixing_kernel(
    me_ref, block_a, block_b, block_c, block_d, tokens_ref, next_ref, scale_ref,
    upcoming_ref, differ_ref, mixed_ref, natural, ahead, padded, squeeze_ref, semaphores,
):
    @pl.when(first_step())
    def _():
        copies = block_copies(
            me_ref[0], (block_a, block_b, block_c, block_d), squeeze_ref, semaphores, slice(0, 64)
        )
        start(copies)
        natural[:, HALF:] = jnp.zeros((4, natural.shape[1] - HALF, LANES), f32)
        clear_border(ahead)
        clear_border(padded)
        wait(copies)

    def squeeze_step(step, carry):
        squeezed = product(
            tokens_ref[...], squeeze_ref[:, :, lanes(step, TILE)].reshape(C, TILE)
        )
        natural[2 * step, 0:HALF] = squeezed[:, 0:LANES]
        natural[2 * step + 1, 0:HALF] = squeezed[:, LANES:TILE]
        return carry

    lax.fori_loop(0, 2, squeeze_step, 0)
    segment = lax.broadcasted_iota(jnp.int32, (16, LANES), 0) % SEG
    not_last = (segment != SEG - 1).astype(f32)

    def mixing_step(step, carry):
        where = lanes(step, LANES)
        next_rows = [spread(next_ref[tap : tap + 1, where]) for tap in range(9)]
        for cell in range(CELLS):
            upcoming = natural[step, pl.ds(cell + CELLS, 16, stride=CELLS)] * not_last
            ahead[cell_place(cell)] = upcoming
            upcoming_ref[cell * 16 : cell * 16 + 16, where] = upcoming
        mean = jnp.zeros((16, LANES), f32)
        for cell in range(CELLS):
            differ = -natural[step, pl.ds(cell, 16, stride=CELLS)]
            for tap in range(9):
                differ = differ + ahead[tap_place(cell, tap)] * next_rows[tap]
            padded[cell_place(cell)] = differ
            differ_ref[cell * 16 : cell * 16 + 16, where] = differ
            mean = mean + differ
        mean = mean * (1.0 / CELLS)
        scale_rows = [spread(scale_ref[tap : tap + 1, where]) for tap in range(9)]
        for cell in range(CELLS):
            mixed = padded[cell_place(cell)] + mean
            for tap in range(9):
                mixed = mixed + padded[tap_place(cell, tap)] * scale_rows[tap]
            natural[step, pl.ds(cell, 16, stride=CELLS)] = mixed
        mixed_ref[:, where] = natural[step, 0:HALF].astype(bf16)
        return carry

    lax.fori_loop(0, 4, mixing_step, 0)


def mixing_block(me, squeeze, tokens, next_kernel, scale_kernel, after=()):
    rows = tokens.shape[0]
    return kernel_call(
        mixing_kernel,
        rows // HALF,
        [SCALAR, ANY, ANY, ANY, ANY, half_spec(C), whole_spec((9, R)), whole_spec((9, R))],
        [half_spec(R), half_spec(R), half_spec(R)],
        [jax.ShapeDtypeStruct((rows, R), f32), jax.ShapeDtypeStruct((rows, R), f32),
         jax.ShapeDtypeStruct((rows, R), bf16)],
        [pltpu.VMEM((4, HALF + CELLS + 7, LANES), f32),
         pltpu.VMEM((PADDED * PADDED, 16, LANES), f32),
         pltpu.VMEM((PADDED * PADDED, 16, LANES), f32),
         pltpu.VMEM((32, C // 32, R), bf16), pltpu.SemaphoreType.DMA((32,))],
        2 * rows * C * R,
        after=after,
    )(me, *squeeze, tokens, next_kernel, scale_kernel)


def gate_kernel(
    me_ref, block_a, block_b, block_c, block_d, tokens_ref, mixed_ref,
    logit_ref, gated_ref, pre_ref, sums_ref,
    tile, expand_ref, reduce_ref, expand_semaphores, reduce_semaphores,
):
    blocks = (block_a, block_b, block_c, block_d)
    for_expand = expand_copies(me_ref[0], blocks, expand_ref, expand_semaphores)
    for_reduce = reduce_copies(me_ref[0], blocks, reduce_ref, reduce_semaphores)

    @pl.when(first_step())
    def _():
        start(for_expand)
        start(for_reduce)
        sums_ref[...] = jnp.zeros_like(sums_ref)
        wait(for_expand)
        wait(for_reduce)

    for group in range(GROUPS):
        where, found = group_at(group), tile.at[group % 2]
        columns = [
            expand_ref[top : top + 4].reshape(R, TILE) for top in (8 * group, 8 * group + 4)
        ]
        found[...] = product(mixed_ref[...], jnp.concatenate(columns, axis=1))
        for _, rows in chunks():
            logit = found[rows]
            token = tokens_ref[rows, where].astype(f32)
            logit_ref[rows, where] = logit.astype(bf16)
            gated_ref[rows, where] = (token + token * sigmoid(logit)).astype(bf16)
    found = tile.at[0]
    found[...] = product(gated_ref[...], reduce_ref[...].reshape(C, B))
    first = jnp.zeros((8, B), f32)
    second = jnp.zeros((8, B), f32)
    for _, rows in chunks():
        value = found[rows]
        pre_ref[rows] = value
        first = first + fold(value)
        second = second + fold(value * value)
    add_moments(sums_ref, slice(0, B), first, second)


def gate_block(me, pair, tokens, mixed):
    rows = tokens.shape[0]
    return kernel_call(
        gate_kernel,
        rows // HALF,
        [SCALAR] + [ANY] * 4 + [half_spec(C), half_spec(R)],
        [half_spec(C), half_spec(C), half_spec(B), whole_out((2, B))],
        [jax.ShapeDtypeStruct((rows, C), bf16), jax.ShapeDtypeStruct((rows, C), bf16),
         jax.ShapeDtypeStruct((rows, B), f32), jax.ShapeDtypeStruct((2, B), f32)],
        [pltpu.VMEM((2, HALF, WIDE), f32),
         pltpu.VMEM((32, R // 4, TILE), bf16), pltpu.VMEM((32, C // 32, B), bf16),
         pltpu.SemaphoreType.DMA((2, 32)), pltpu.SemaphoreType.DMA((32,))],
        4 * rows * C * R,
        2 * rows * C,
    )(me, *pair, tokens, mixed)


SPATIAL_ROWS = 9 * 16
RESTORE_ROWS = 64
CLASS_ROWS = 32
LATE_ROWS = RESTORE_ROWS + CLASS_ROWS


def restore_copy(late_ref, target, semaphore):
    return pltpu.make_async_copy(late_ref.at[:, 0:RESTORE_ROWS], target, semaphore)


def second_kernel(count, me_ref, *refs):
    blocks, refs = refs[:8], refs[8:]
    pre_ref, in_sums_ref, affine_ref, hidden_ref, out_ref, copies_ref, *refs = refs
    natural, padded, tile, spatial_ref, sums_ref, semaphores = refs
    copies = block_copies(me_ref[0], blocks, spatial_ref, semaphores)

    @pl.when(first_step())
    def _():
        start(copies)
        sums_ref[...] = jnp.zeros_like(sums_ref)
        clear_border(padded)

    border = SIDE * 16
    hidden_ref[0, 0:border] = jnp.zeros((border, 3 * B), bf16)
    hidden_ref[0, border + HALF :] = jnp.zeros((border, 3 * B), bf16)

    def hidden_step(step, carry):
        where = lanes(step, LANES)
        mean, inverse, gain, shift = (
            spread(row) for row in constants(in_sums_ref[:, where], affine_ref[:, where], count)
        )
        for chunk in range(HALF // 16):
            rows = slice(chunk * 16, chunk * 16 + 16)
            norm = (pre_ref[rows, where] - mean) * inverse * gain + shift
            natural[rows] = norm * sigmoid(norm)
        for cell in range(CELLS):
            padded[cell_place(cell)] = natural[pl.ds(cell, 16, stride=CELLS)].astype(bf16)
        for side in range(3):
            at = lanes(side * 4 + step, LANES)
            for cell in range(CELLS):
                hidden_ref[0, border + cell * 16 : border + cell * 16 + 16, at] = padded[
                    tap_place(cell, 3 + side)
                ]
        return carry

    lax.fori_loop(0, 4, hidden_step, 0)

    @pl.when(first_step())
    def _():
        wait(copies)

    found = None
    for row in range(3):
        taps = [
            spatial_ref[:, tap * 16 : tap * 16 + 16].reshape(B, B)
            for tap in range(3 * row, 3 * row + 3)
        ]
        part = product(
            hidden_ref[0, row * border : row * border + HALF], jnp.concatenate(taps, axis=0)
        )
        found = part if found is None else found + part
    tile[...] = found
    first = jnp.zeros((8, B), f32)
    second = jnp.zeros((8, B), f32)
    for chunk in range(HALF // 16):
        rows = slice(chunk * 16, chunk * 16 + 16)
        value = tile[rows]
        out_ref[rows] = value
        first = first + fold(value)
        second = second + fold(value * value)
    add_moments(sums_ref, slice(0, B), first, second)
    store_copies(copies_ref, sums_ref)


def second_block(me, spatial, pre_one, sums, affine, count):
    rows = pre_one.shape[0]
    devices = lax.axis_size(AXES)
    steps = rows // HALF
    deep = HALF + 2 * SIDE * 16
    return kernel_call(
        functools.partial(second_kernel, count),
        steps,
        [SCALAR] + [ANY] * 8 + [half_spec(B), whole_spec(sums.shape), whole_spec((2, B))],
        [pl.BlockSpec((1, deep, 3 * B), lambda step: (step, 0, 0)), half_spec(B),
         whole_out((devices, 2, B))],
        [jax.ShapeDtypeStruct((steps, deep, 3 * B), bf16), jax.ShapeDtypeStruct((rows, B), f32),
         jax.ShapeDtypeStruct((devices, 2, B), f32)],
        [pltpu.VMEM((HALF, LANES), f32), pltpu.VMEM((PADDED * PADDED, 16, LANES), bf16),
         pltpu.VMEM((HALF, B), f32), pltpu.VMEM((32, SPATIAL_ROWS, B), bf16),
         pltpu.VMEM((2, B), f32),
         pltpu.SemaphoreType.DMA((32,))],
        18 * rows * B * B,
        2 * rows * B,
    )(me, *spatial, pre_one, sums, affine)


def third_kernel(count, pre_ref, in_sums_ref, affine_ref, late_ref,
                 hidden_ref, out_ref, centre_ref, sums_ref, natural, tile, middle, restore_ref,
                 semaphore):
    copy = restore_copy(late_ref, restore_ref, semaphore)

    @pl.when(first_step())
    def _():
        copy.start()
        sums_ref[...] = jnp.zeros_like(sums_ref)

    def hidden_step(step, carry):
        where = lanes(step, LANES)
        mean, inverse, gain, shift = (
            spread(row) for row in constants(in_sums_ref[:, where], affine_ref[:, where], count)
        )
        for cell in range(CELLS):
            rows = slice(cell * 16, cell * 16 + 16)
            norm = (pre_ref[rows, where] - mean) * inverse * gain + shift
            natural[pl.ds(cell, 16, stride=CELLS)] = norm * sigmoid(norm)
        hidden_ref[:, where] = natural[...].astype(bf16)
        middle[:, where] = spread(jnp.mean(natural[...], 0, keepdims=True)).astype(bf16)
        return carry

    lax.fori_loop(0, 4, hidden_step, 0)

    @pl.when(first_step())
    def _():
        copy.wait()

    blocks = restore_ref.reshape(8, 4, RESTORE_ROWS, B)
    for group in range(GROUPS):
        where, found = group_at(group), tile.at[group % 2]
        columns = blocks[:, group].reshape(B, WIDE)
        found[...] = product(hidden_ref[...], columns)
        centre = product(middle[...], columns)
        centre_ref[0, :, where] = centre[0:1]
        first = jnp.zeros((8, WIDE), f32)
        second = jnp.zeros((8, WIDE), f32)
        for _, rows in chunks():
            value = found[rows]
            out_ref[rows, where] = (value - centre).astype(bf16)
            first = first + fold(value)
            second = second + fold(value * value)
        add_moments(sums_ref, where, first, second)


def third_block(pre_two, sums, affine, late, count):
    rows = pre_two.shape[0]
    return kernel_call(
        functools.partial(third_kernel, count),
        rows // HALF,
        [half_spec(B), whole_spec(sums.shape), whole_spec((2, B)), ANY],
        [half_spec(B), half_spec(C), pl.BlockSpec((1, 1, C), lambda step: (step, 0, 0)),
         whole_out((2, C))],
        [jax.ShapeDtypeStruct((rows, B), bf16), jax.ShapeDtypeStruct((rows, C), bf16),
         jax.ShapeDtypeStruct((rows // HALF, 1, C), f32), jax.ShapeDtypeStruct((2, C), f32)],
        [pltpu.VMEM((HALF, LANES), f32), pltpu.VMEM((2, HALF, WIDE), f32),
         pltpu.VMEM((16, B), bf16),
         pltpu.VMEM((32, RESTORE_ROWS, B), bf16), pltpu.SemaphoreType.DMA(())],
        2 * rows * B * C,
        2 * rows * B,
    )(pre_two, sums, affine, late)


def view_rows(chunk):
    return (chunk * 16) // PER_VIEW, (chunk * 16 + 8) // PER_VIEW


def class_copy(late_ref, target, semaphore):
    return pltpu.make_async_copy(late_ref.at[:, RESTORE_ROWS:], target, semaphore)


def order_classes(late, classes):
    for block in range(32):
        for half in range(2):
            top = (2 * block + half) * CLASS_ROWS
            classes[top : top + CLASS_ROWS] = late[block, :, half * TILE : (half + 1) * TILE]


def fourth_kernel(count, pre_ref, centre_ref, gated_ref, in_sums_ref, affine_ref,
                  late_ref, bias_ref, out_ref, slope_ref, views_ref, logits_ref, pooled_ref,
                  classes, late, sums, semaphore):
    copy = class_copy(late_ref, late, semaphore)
    step = pl.program_id(0)

    @pl.when(first_step())
    def _():
        copy.start()
        sums[...] = jnp.zeros_like(sums)

    for part in range(C // TILE):
        where = slice(part * TILE, (part + 1) * TILE)
        mean, inverse, gain, shift = (
            spread(row) for row in constants(in_sums_ref[:, where], affine_ref[:, where], count)
        )
        mean = mean - spread(centre_ref[0, :, where])
        totals = [[jnp.zeros((8, TILE), f32) for _ in range(2)] for _ in range(3)]
        for chunk in range(HALF // 16):
            rows = slice(chunk * 16, chunk * 16 + 16)
            unit = (pre_ref[rows, where].astype(f32) - mean) * inverse
            summed = unit * gain + shift + gated_ref[rows, where].astype(f32)
            sigma = sigmoid(summed)
            output = summed * sigma
            slope = sigma + output * (1.0 - sigma)
            out_ref[rows, where] = output.astype(bf16)
            slope_ref[rows, where] = slope.astype(bf16)
            low, high = view_rows(chunk)
            for kind, value in enumerate((output, slope, slope * unit)):
                if low == high:
                    totals[kind][low] = totals[kind][low] + fold(value)
                else:
                    totals[kind][low] = totals[kind][low] + value[0:8]
                    totals[kind][high] = totals[kind][high] + value[8:16]
        for kind in range(3):
            for view in range(2):
                at = 2 * kind + view
                row = jnp.sum(totals[kind][view], 0, keepdims=True)
                views_ref[0, at : at + 1, where] = row
                if kind == 0:
                    sums[pl.ds(2 * step + view, 1), where] = row
        views_ref[0, 6:8, where] = jnp.zeros((2, TILE), f32)

    @pl.when(step == pl.num_programs(0) - 1)
    def _():
        copy.wait()
        order_classes(late, classes)
        pooled = (sums[...] / PER_VIEW).astype(bf16)
        pooled_ref[...] = pooled
        logits_ref[...] = product(pooled, classes[...]) + bias_ref[...]


def fourth_block(pre_three, centres, gated, sums, affine, late, bias, count):
    rows = pre_three.shape[0]
    steps = rows // HALF
    return kernel_call(
        functools.partial(fourth_kernel, count),
        steps,
        [half_spec(C), pl.BlockSpec((1, 1, C), lambda step: (step, 0, 0)), half_spec(C),
         whole_spec(sums.shape), whole_spec((2, C)), ANY, whole_spec((1, TILE))],
        [half_spec(C), half_spec(C), pl.BlockSpec((1, 8, C), lambda step: (step, 0, 0)),
         whole_out((16, TILE)), whole_out((16, C))],
        [jax.ShapeDtypeStruct((rows, C), bf16), jax.ShapeDtypeStruct((rows, C), bf16),
         jax.ShapeDtypeStruct((steps, 8, C), f32), jax.ShapeDtypeStruct((16, TILE), f32),
         jax.ShapeDtypeStruct((16, C), bf16)],
        [pltpu.VMEM((C, TILE), bf16), pltpu.VMEM((32, CLASS_ROWS, B), bf16),
         pltpu.VMEM((16, C), f32), pltpu.SemaphoreType.DMA(())],
        20 * rows * C,
        2 * rows * C,
    )(pre_three, centres, gated, sums, affine, late, bias)


def video_kernel(view_count, before_ref, own_ref, after_ref, marks_ref, target_ref, views_ref,
                 late_ref, part_ref, pooled_ref, grad_ref, classes, late, semaphore):
    copy = class_copy(late_ref, late, semaphore)
    copy.start()
    marks = marks_ref[...]
    video_logits = jnp.zeros((8, TILE), f32)
    near = (before_ref, own_ref, after_ref)
    for index in range(3 * view_count):
        row = near[index // view_count][index % view_count : index % view_count + 1]
        video_logits = video_logits + marks[:, index : index + 1] * row
    known = lax.broadcasted_iota(jnp.int32, (8, TILE), 1) < CLASSES
    top = jnp.max(jnp.where(known, video_logits, -jnp.inf), 1, keepdims=True)
    weights = jnp.where(known, jnp.exp(jnp.minimum(video_logits - top, 0.0)), 0.0)
    total_weight = jnp.sum(weights, 1, keepdims=True)
    target = target_ref[...]
    entropy = jnp.log(total_weight) + top - jnp.sum(target * video_logits, 1, keepdims=True)
    video_grad = loss_scale * (weights / total_weight - target)
    first = marks[:, 3 * view_count + 1 : 3 * view_count + 2]
    view_grad = (video_grad * marks[:, 3 * view_count : 3 * view_count + 1]).astype(bf16)
    grad_ref[...] = view_grad
    place = lax.broadcasted_iota(jnp.int32, (8, TILE), 1)
    row = jnp.sum(first * jnp.where(place == CLASSES, entropy, video_grad), 0, keepdims=True)
    copy.wait()
    order_classes(late, classes)
    pooled = dot_nt(view_grad, classes[...]) * (1.0 / PER_VIEW)
    parts = [jnp.zeros((1, C), f32), jnp.zeros((1, C), f32)]
    for view in range(view_count):
        half, place = view // 2, view % 2
        pooled_ref[half, place : place + 1] = pooled[view : view + 1]
        for kind in range(2):
            at = 2 * (kind + 1) + place
            parts[kind] = parts[kind] + pooled[view : view + 1] * views_ref[half, at : at + 1]
    part_ref[0:1] = parts[0]
    part_ref[1:2] = parts[1]
    part_ref[2:3] = jnp.zeros((1, C), f32)
    part_ref[2:3, 0:TILE] = row


def video_block(before, own, following, marks, target, views, late, view_count):
    outs = [((3, C), f32), ((view_count // 2, 2, C), f32), ((8, TILE), bf16)]
    operands = (before, own, following, marks, target, views)
    return kernel_call(
        functools.partial(video_kernel, view_count),
        1,
        [whole_spec(operand.shape) for operand in operands] + [ANY],
        [whole_out(shape) for shape, _ in outs],
        [jax.ShapeDtypeStruct(shape, kind) for shape, kind in outs],
        [pltpu.VMEM((C, TILE), bf16), pltpu.VMEM((32, CLASS_ROWS, B), bf16),
         pltpu.SemaphoreType.DMA(())],
        1000000,
    )(*operands, late)


def view_scale(pooled_ref, view, where):
    return spread(pooled_ref[0, view : view + 1, where], 8)


def view_grad_rows(slope, pooled, chunk):
    low, high = view_rows(chunk)
    return slope * jnp.concatenate([pooled[low], pooled[high]], axis=0)


def fifth_kernel(count, slope_ref, pre_three_ref, centre_ref, pooled_ref, sums_three_ref, affine_three_ref,
                 grads_three_ref, late_ref, pre_two_ref, sums_two_ref, affine_two_ref,
                 low_ref, out_ref, copies_ref, natural, restore_ref, sums_ref, semaphore):
    copy = restore_copy(late_ref, restore_ref, semaphore)

    @pl.when(first_step())
    def _():
        copy.start()
        sums_ref[...] = jnp.zeros_like(sums_ref)

    for group in range(GROUPS):
        where = group_at(group)
        mean, inverse, gain, _ = constants(
            sums_three_ref[:, where], affine_three_ref[:, where], count
        )
        scale = spread(gain * inverse)
        offset = spread(grads_three_ref[0:1, where] / count)
        along = spread(grads_three_ref[1:2, where] / count * inverse)
        mean = spread(mean - centre_ref[0, :, where])
        pooled = [view_scale(pooled_ref, view, where) for view in range(2)]
        for chunk, rows in chunks():
            grad = view_grad_rows(slope_ref[rows, where].astype(f32), pooled, chunk)
            centred = pre_three_ref[rows, where].astype(f32) - mean
            low_ref[rows, where] = (scale * (grad - offset - centred * along)).astype(bf16)

    @pl.when(first_step())
    def _():
        copy.wait()

    blocks = restore_ref.reshape(8, 4, RESTORE_ROWS, B)
    grad = None
    for group in range(GROUPS):
        part = dot_nt(low_ref[:, group_at(group)], blocks[:, group].reshape(B, WIDE))
        grad = part if grad is None else grad + part
    for step in range(4):
        natural[step] = grad[:, step * LANES : (step + 1) * LANES]

    def slope_step(step, carry):
        where = lanes(step, LANES)
        mean, inverse, gain, shift = (
            spread(row) for row in constants(sums_two_ref[:, where], affine_two_ref[:, where], count)
        )
        first = jnp.zeros((16, LANES), f32)
        second = jnp.zeros((16, LANES), f32)
        for cell in range(CELLS):
            rows = slice(cell * 16, cell * 16 + 16)
            unit = (pre_two_ref[rows, where] - mean) * inverse
            norm = unit * gain + shift
            sigma = sigmoid(norm)
            grad = natural[step, pl.ds(cell, 16, stride=CELLS)]
            grad = grad * (sigma * (1.0 + norm * (1.0 - sigma)))
            out_ref[rows, where] = grad
            first = first + grad
            second = second + grad * unit
        add_moments(sums_ref, where, first, second)
        return carry

    lax.fori_loop(0, 4, slope_step, 0)
    store_copies(copies_ref, sums_ref)


def fifth_block(slope, pre_three, centres, pooled, sums_three, affine_three, grads_three, late,
                pre_two, sums_two, affine_two, count, after=()):
    rows = slope.shape[0]
    devices = lax.axis_size(AXES)
    return kernel_call(
        functools.partial(fifth_kernel, count),
        rows // HALF,
        [half_spec(C), half_spec(C), pl.BlockSpec((1, 1, C), lambda step: (step, 0, 0)),
         pl.BlockSpec((1, 2, C), lambda step: (step, 0, 0)),
         whole_spec(sums_three.shape), whole_spec((2, C)), whole_spec(grads_three.shape), ANY,
         half_spec(B), whole_spec(sums_two.shape), whole_spec((2, B))],
        [half_spec(C), half_spec(B), whole_out((devices, 2, B))],
        [jax.ShapeDtypeStruct((rows, C), bf16), jax.ShapeDtypeStruct((rows, B), f32),
         jax.ShapeDtypeStruct((devices, 2, B), f32)],
        [pltpu.VMEM((4, HALF, LANES), f32), pltpu.VMEM((32, RESTORE_ROWS, B), bf16),
         pltpu.VMEM((2, B), f32),
         pltpu.SemaphoreType.DMA(())],
        2 * rows * B * C,
        2 * rows * B,
        after=after,
    )(slope, pre_three, centres, pooled, sums_three, affine_three, grads_three, late,
      pre_two, sums_two, affine_two)


def sixth_kernel(count, me_ref, *refs):
    blocks, refs = refs[:8], refs[8:]
    grad_ref, pre_two_ref, sums_two_ref, affine_two_ref, grads_two_ref, *refs = refs
    pre_one_ref, sums_one_ref, affine_one_ref, low_ref, out_ref, copies_ref, *refs = refs
    padded, shifted, tile, natural, spatial_ref, sums_ref, semaphores = refs
    border = SIDE * 16
    copies = block_copies(me_ref[0], blocks, spatial_ref, semaphores)

    @pl.when(first_step())
    def _():
        start(copies)
        sums_ref[...] = jnp.zeros_like(sums_ref)
        clear_border(padded)
        shifted[0:border] = jnp.zeros((border, 3 * B), bf16)
        shifted[border + HALF :] = jnp.zeros((border, 3 * B), bf16)

    def low_step(step, carry):
        where = lanes(step, LANES)
        mean, inverse, gain, _ = constants(sums_two_ref[:, where], affine_two_ref[:, where], count)
        scale = spread(gain * inverse)
        offset = spread(grads_two_ref[0:1, where] / count)
        along = spread(grads_two_ref[1:2, where] / count * inverse)
        mean = spread(mean)
        for cell in range(CELLS):
            rows = slice(cell * 16, cell * 16 + 16)
            centred = pre_two_ref[rows, where] - mean
            low = (scale * (grad_ref[rows, where] - offset - centred * along)).astype(bf16)
            low_ref[rows, where] = low
            padded[cell_place(cell)] = low
        for side in range(3):
            at = lanes(side * 4 + step, LANES)
            for cell in range(CELLS):
                shifted[border + cell * 16 : border + cell * 16 + 16, at] = padded[
                    tap_place(cell, 3 + side)
                ]
        return carry

    lax.fori_loop(0, 4, low_step, 0)

    @pl.when(first_step())
    def _():
        wait(copies)

    grad = None
    for tap in range(9):
        top = (tap // 3) * border
        at = (tap % 3) * B
        back = (8 - tap) * 16
        part = dot_nt(
            shifted[top : top + HALF, at : at + B],
            spatial_ref[:, back : back + 16].reshape(B, B),
        )
        grad = part if grad is None else grad + part
    tile[...] = grad
    for group in range(4):
        for cell in range(CELLS):
            natural[group, pl.ds(cell, 16, stride=CELLS)] = tile[
                cell * 16 : cell * 16 + 16, group * LANES : (group + 1) * LANES
            ]

    def slope_step(step, carry):
        where = lanes(step, LANES)
        mean, inverse, gain, shift = (
            spread(row) for row in constants(sums_one_ref[:, where], affine_one_ref[:, where], count)
        )
        first = jnp.zeros((16, LANES), f32)
        second = jnp.zeros((16, LANES), f32)
        for chunk in range(HALF // 16):
            rows = slice(chunk * 16, chunk * 16 + 16)
            unit = (pre_one_ref[rows, where] - mean) * inverse
            norm = unit * gain + shift
            sigma = sigmoid(norm)
            grad = natural[step, rows] * (sigma * (1.0 + norm * (1.0 - sigma)))
            out_ref[rows, where] = grad
            first = first + grad
            second = second + grad * unit
        add_moments(sums_ref, where, first, second)
        return carry

    lax.fori_loop(0, 4, slope_step, 0)
    store_copies(copies_ref, sums_ref)


def sixth_block(me, spatial, grad, pre_two, sums_two, affine_two, grads_two, pre_one, sums_one,
                affine_one, count):
    rows = grad.shape[0]
    devices = lax.axis_size(AXES)
    deep = HALF + 2 * SIDE * 16
    return kernel_call(
        functools.partial(sixth_kernel, count),
        rows // HALF,
        [SCALAR] + [ANY] * 8 + [half_spec(B), half_spec(B), whole_spec(sums_two.shape),
         whole_spec((2, B)), whole_spec(grads_two.shape), half_spec(B), whole_spec(sums_one.shape),
         whole_spec((2, B))],
        [half_spec(B), half_spec(B), whole_out((devices, 2, B))],
        [jax.ShapeDtypeStruct((rows, B), bf16), jax.ShapeDtypeStruct((rows, B), f32),
         jax.ShapeDtypeStruct((devices, 2, B), f32)],
        [pltpu.VMEM((PADDED * PADDED, 16, LANES), bf16), pltpu.VMEM((deep, 3 * B), bf16),
         pltpu.VMEM((HALF, B), f32), pltpu.VMEM((4, HALF, LANES), f32),
         pltpu.VMEM((32, SPATIAL_ROWS, B), bf16),
         pltpu.VMEM((2, B), f32), pltpu.SemaphoreType.DMA((32,))],
        18 * rows * B * B,
        2 * rows * B,
    )(me, *spatial, grad, pre_two, sums_two, affine_two, grads_two, pre_one, sums_one,
      affine_one)


def low_kernel(count, grad_ref, pre_ref, sums_ref, affine_ref, grads_ref, low_ref):
    def low_step(step, carry):
        where = lanes(step, LANES)
        mean, inverse, gain, _ = constants(sums_ref[:, where], affine_ref[:, where], count)
        scale = spread(gain * inverse)
        offset = spread(grads_ref[0:1, where] / count)
        along = spread(grads_ref[1:2, where] / count * inverse)
        mean = spread(mean)
        for chunk in range(HALF // 16):
            rows = slice(chunk * 16, chunk * 16 + 16)
            centred = pre_ref[rows, where] - mean
            low_ref[rows, where] = (
                scale * (grad_ref[rows, where] - offset - centred * along)
            ).astype(bf16)
        return carry

    lax.fori_loop(0, 4, low_step, 0)


def low_outer_kernel(count, grain, me_ref, grad_ref, pre_ref, sums_ref, affine_ref, grads_ref,
                     wide_ref, low_ref, keep_ref, send_ref, plain, turned):
    @pl.when(first_step())
    def _():
        for half in range(low_ref.shape[0] // HALF):
            rows = pl.ds(half * HALF, HALF)
            low_kernel(
                count, grad_ref.at[rows], pre_ref.at[rows], sums_ref, affine_ref, grads_ref,
                low_ref.at[rows],
            )
        turn(me_ref[0], low_ref[...], grain, plain, turned)

    store_tiles(product(turned[...], wide_ref[...]), keep_ref, send_ref)


def low_outer_block(me, grad, pre, sums, affine, grads, wide_values, count):
    rows, inner = grad.shape
    blocks = wide_values.shape[1] // TILE
    half = pl.BlockSpec((2, inner // 2, TILE), lambda step: (step, 0, 0))
    low, keep, send = kernel_call(
        functools.partial(low_outer_kernel, count, inner // 4),
        blocks // 2,
        [SCALAR, whole_spec(grad.shape), whole_spec(grad.shape), whole_spec(sums.shape),
         whole_spec((2, B)), whole_spec(grads.shape),
         pl.BlockSpec((rows, 2 * TILE), lambda step: (0, step))],
        [whole_out(grad.shape), half, half],
        [jax.ShapeDtypeStruct(grad.shape, bf16),
         jax.ShapeDtypeStruct((blocks, inner // 2, TILE), bf16),
         jax.ShapeDtypeStruct((blocks, inner // 2, TILE), bf16)],
        [pltpu.VMEM((inner, rows), bf16), pltpu.VMEM((inner, rows), bf16)],
        2 * rows * inner * wide_values.shape[1],
    )(me, grad, pre, sums, affine, grads, wide_values)
    return low, (keep, send)


def gate_back_kernel(me_ref, block_a, block_b, block_c, block_d, low_ref,
                     slope_ref, pooled_ref, tokens_ref, logit_ref,
                     logit_grad_ref, part_ref, tile, reduce_ref, semaphores):
    copies = reduce_copies(me_ref[0], (block_a, block_b, block_c, block_d), reduce_ref, semaphores)

    @pl.when(first_step())
    def _():
        start(copies)
        wait(copies)

    for group in range(GROUPS):
        where, found = group_at(group), tile.at[group % 2]
        found[...] = dot_nt(low_ref[...], reduce_ref[8 * group : 8 * group + 8].reshape(WIDE, B))
        pooled = [view_scale(pooled_ref, view, where) for view in range(2)]
        for chunk, rows in chunks():
            slope = slope_ref[rows, where].astype(f32)
            grad = found[rows] + view_grad_rows(slope, pooled, chunk)
            gate = sigmoid(logit_ref[rows, where].astype(f32))
            part = grad * gate
            part_ref[rows, where] = (grad + part).astype(bf16)
            token = tokens_ref[rows, where].astype(f32)
            logit_grad_ref[rows, where] = (part * (1.0 - gate) * token).astype(bf16)


def gate_back_block(me, pair, low_one, slope, pooled, tokens, logit):
    rows = low_one.shape[0]
    return kernel_call(
        gate_back_kernel,
        rows // HALF,
        [SCALAR, ANY, ANY, ANY, ANY, half_spec(B), half_spec(C),
         pl.BlockSpec((1, 2, C), lambda step: (step, 0, 0)), half_spec(C), half_spec(C)],
        [half_spec(C), half_spec(C)],
        [jax.ShapeDtypeStruct((rows, C), bf16), jax.ShapeDtypeStruct((rows, C), bf16)],
        [pltpu.VMEM((2, HALF, WIDE), f32), pltpu.VMEM((32, C // 32, B), bf16),
         pltpu.SemaphoreType.DMA((32,))],
        2 * rows * C * R,
        2 * rows * C,
    )(me, *pair, low_one, slope, pooled, tokens, logit)


def mixing_back_kernel(me_ref, block_a, block_b, block_c, block_d, logit_grad_ref,
                       upcoming_ref, differ_ref, next_ref, scale_ref, squeezed_ref, kernels_ref,
                       natural, later, ahead, padded, expand_ref, semaphores):
    @pl.when(first_step())
    def _():
        copies = expand_copies(
            me_ref[0], (block_a, block_b, block_c, block_d), expand_ref, semaphores
        )
        start(copies)
        kernels_ref[...] = jnp.zeros_like(kernels_ref)
        clear_border(ahead)
        clear_border(padded)
        later[0:CELLS] = jnp.zeros((CELLS, LANES), f32)
        wait(copies)

    grad = None
    for group in range(GROUPS):
        columns = [
            expand_ref[top : top + 4].reshape(R, TILE) for top in (8 * group, 8 * group + 4)
        ]
        part = dot_nt(logit_grad_ref[:, group_at(group)], jnp.concatenate(columns, axis=1))
        grad = part if grad is None else grad + part
    for step in range(4):
        natural[step] = grad[:, step * LANES : (step + 1) * LANES]
    segment = lax.broadcasted_iota(jnp.int32, (16, LANES), 0) % SEG
    not_last = (segment != SEG - 1).astype(f32)

    def mixing_step(step, carry):
        where = lanes(step, LANES)
        scale_rows = [spread(scale_ref[tap : tap + 1, where]) for tap in range(9)]
        mean = jnp.zeros((16, LANES), f32)
        for cell in range(CELLS):
            grad = natural[step, pl.ds(cell, 16, stride=CELLS)]
            padded[cell_place(cell)] = grad
            mean = mean + grad
            ahead[cell_place(cell)] = differ_ref[cell * 16 : cell * 16 + 16, where]
        mean = mean * (1.0 / CELLS)
        sums = [jnp.zeros((16, LANES), f32) for _ in range(9)]
        for cell in range(CELLS):
            grad = padded[cell_place(cell)]
            for tap in range(9):
                sums[tap] = sums[tap] + ahead[tap_place(cell, tap)] * grad
        for tap in range(9):
            kernels_ref[9 + tap : 10 + tap, where] += jnp.sum(sums[tap], 0, keepdims=True)
        for cell in range(CELLS):
            grad = padded[cell_place(cell)] + mean
            for tap in range(9):
                grad = grad + padded[tap_place(cell, tap)] * scale_rows[8 - tap]
            ahead[cell_place(cell)] = grad
        next_rows = [spread(next_ref[tap : tap + 1, where]) for tap in range(9)]
        for cell in range(CELLS):
            padded[cell_place(cell)] = upcoming_ref[cell * 16 : cell * 16 + 16, where]
        sums = [jnp.zeros((16, LANES), f32) for _ in range(9)]
        for cell in range(CELLS):
            grad = ahead[cell_place(cell)]
            for tap in range(9):
                sums[tap] = sums[tap] + padded[tap_place(cell, tap)] * grad
        for tap in range(9):
            kernels_ref[tap : tap + 1, where] += jnp.sum(sums[tap], 0, keepdims=True)
        for cell in range(CELLS):
            back = ahead[tap_place(cell, 0)] * next_rows[8]
            for tap in range(1, 9):
                back = back + ahead[tap_place(cell, tap)] * next_rows[8 - tap]
            later[pl.ds(cell + CELLS, 16, stride=CELLS)] = back * not_last
            natural[step, pl.ds(cell, 16, stride=CELLS)] = -ahead[cell_place(cell)]
        for chunk in range(HALF // 16):
            rows = slice(chunk * 16, chunk * 16 + 16)
            squeezed_ref[rows, where] = (natural[step, rows] + later[rows]).astype(bf16)
        return carry

    lax.fori_loop(0, 4, mixing_step, 0)


def mixing_back_block(me, pair, logit_grad, upcoming, differ, next_kernel, scale_kernel,
                      after=()):
    rows = logit_grad.shape[0]
    return kernel_call(
        mixing_back_kernel,
        rows // HALF,
        [SCALAR, ANY, ANY, ANY, ANY, half_spec(C), half_spec(R), half_spec(R),
         whole_spec((9, R)), whole_spec((9, R))],
        [half_spec(R), whole_out((18, R))],
        [jax.ShapeDtypeStruct((rows, R), bf16), jax.ShapeDtypeStruct((18, R), f32)],
        [pltpu.VMEM((4, HALF, LANES), f32), pltpu.VMEM((HALF + CELLS + 7, LANES), f32),
         pltpu.VMEM((PADDED * PADDED, 16, LANES), f32),
         pltpu.VMEM((PADDED * PADDED, 16, LANES), f32), pltpu.VMEM((32, R // 4, TILE), bf16),
         pltpu.SemaphoreType.DMA((2, 32))],
        2 * rows * C * R,
        after=after,
    )(me, *pair, logit_grad, upcoming, differ, next_kernel, scale_kernel)


def tokens_kernel(me_ref, block_a, block_b, block_c, block_d, part_ref, squeezed_ref, out_ref,
                  squeeze_ref, semaphores):
    @pl.when(first_step())
    def _():
        copies = block_copies(
            me_ref[0], (block_a, block_b, block_c, block_d), squeeze_ref, semaphores, slice(0, 64)
        )
        start(copies)
        wait(copies)

    found = dot_nt(squeezed_ref[...], squeeze_ref[...].reshape(C, R))
    out_ref[...] = (found + part_ref[...].astype(f32)).astype(bf16)


def tokens_block(me, squeeze, part, squeezed_grad):
    rows = part.shape[0]
    return kernel_call(
        tokens_kernel,
        rows // HALF,
        [SCALAR, ANY, ANY, ANY, ANY, half_spec(C), half_spec(R)],
        half_spec(C),
        jax.ShapeDtypeStruct((rows, C), bf16),
        [pltpu.VMEM((32, C // 32, R), bf16), pltpu.SemaphoreType.DMA((32,))],
        2 * rows * C * R,
    )(me, *squeeze, part, squeezed_grad)


def turn(me, values, grain, plain, turned):
    core = me & 1
    plain[...] = values.T
    half = turned.shape[0] // 2
    for group in range(half // grain):
        mine = pl.multiple_of((2 * group + core) * grain, grain)
        other = pl.multiple_of((2 * group + 1 - core) * grain, grain)
        turned[group * grain : (group + 1) * grain] = plain[pl.ds(mine, grain)]
        turned[half + group * grain : half + (group + 1) * grain] = plain[pl.ds(other, grain)]


def store_tiles(found, keep_ref, send_ref):
    half = found.shape[0] // 2
    for tile in range(2):
        at = slice(tile * TILE, (tile + 1) * TILE)
        keep_ref[tile, 0:half] = found[0:half, at].astype(bf16)
        send_ref[tile, 0:half] = found[half:, at].astype(bf16)


def outer_kernel(grain, me_ref, narrow_ref, wide_ref, keep_ref, send_ref, plain, turned):
    @pl.when(first_step())
    def _():
        turn(me_ref[0], narrow_ref[...], grain, plain, turned)

    store_tiles(product(turned[...], wide_ref[...]), keep_ref, send_ref)


def outer_block(me, narrow_values, wide_values, grain):
    rows, inner = narrow_values.shape
    blocks = wide_values.shape[1] // TILE
    half = pl.BlockSpec((2, inner // 2, TILE), lambda step: (step, 0, 0))
    return kernel_call(
        functools.partial(outer_kernel, grain),
        blocks // 2,
        [SCALAR, whole_spec((rows, inner)), pl.BlockSpec((rows, 2 * TILE), lambda step: (0, step))],
        [half, half],
        [jax.ShapeDtypeStruct((blocks, inner // 2, TILE), bf16)] * 2,
        [pltpu.VMEM((inner, rows), bf16), pltpu.VMEM((inner, rows), bf16)],
        2 * rows * inner * wide_values.shape[1],
    )(me, narrow_values, wide_values)


def outer_block_of(grain):
    return functools.partial(outer_block, grain=grain)


FEW_ROWS = 40


SHARED = GROUPS + 9


def store_shared(found, keep_ref, send_ref):
    half = found.shape[0] // 2
    keep_ref[...] = found[:half].astype(bf16).reshape(16, 16, WIDE)
    send_ref[...] = found[half:].astype(bf16).reshape(16, 16, WIDE)


def restore_outer_kernel(me_ref, narrow_ref, wide_ref, keep_ref, send_ref, plain, turned):
    @pl.when(first_step())
    def _():
        turn(me_ref[0], narrow_ref[...], 16, plain, turned)

    store_shared(product(turned[...], wide_ref[...]), keep_ref, send_ref)


def restore_outer_block(me, hidden, low_three):
    rows = hidden.shape[0]
    out = pl.BlockSpec((16, 16, WIDE), lambda step: (0, step, 0))
    return kernel_call(
        restore_outer_kernel,
        GROUPS,
        [SCALAR, whole_spec((rows, B)), pl.BlockSpec((rows, WIDE), lambda step: (0, step))],
        [out, out],
        [jax.ShapeDtypeStruct((16, 16 * SHARED, WIDE), bf16)] * 2,
        [pltpu.VMEM((B, rows), bf16), pltpu.VMEM((B, rows), bf16)],
        2 * rows * B * C,
    )(me, hidden, low_three)


def spatial_kernel(me_ref, kept_ref, sent_ref, hidden_ref, low_ref, keep_ref, send_ref, plain,
                   turned, padded):
    border = SIDE * 16
    halves = hidden_ref.shape[0]

    @pl.when(first_step())
    def _():
        for half in range(halves):
            padded[half, 0 : 2 * border] = jnp.zeros((2 * border, B), bf16)
            padded[half, 2 * border : 2 * border + HALF] = low_ref[half * HALF : (half + 1) * HALF]
            padded[half, 2 * border + HALF :] = jnp.zeros((2 * border, B), bf16)

    step = pl.program_id(0)

    @pl.when(step % 3 == 0)
    def _():
        for half in range(halves):
            turn(me_ref[0], hidden_ref[half], 16, plain, turned.at[half])

    top = pl.multiple_of((2 - step % 3) * border, 16)
    found = None
    for half in range(halves):
        part = product(turned[half], padded[half, pl.ds(top, HALF + 2 * border)])
        found = part if found is None else found + part
    store_shared(found, keep_ref, send_ref)


def spatial_block(me, buffers, hidden, low_two):
    halves, deep, _ = hidden.shape
    out = pl.BlockSpec((16, 16, B), lambda step: (0, GROUPS + (step % 3) * 3 + step // 3, 0))
    return kernel_call(
        spatial_kernel,
        9,
        [SCALAR, ANY, ANY, pl.BlockSpec((halves, deep, B), lambda step: (0, 0, step // 3)),
         whole_spec(low_two.shape)],
        [out, out],
        [jax.ShapeDtypeStruct(buffers[0].shape, bf16)] * 2,
        [pltpu.VMEM((B, deep), bf16), pltpu.VMEM((halves, B, deep), bf16),
         pltpu.VMEM((halves, deep + 2 * SIDE * 16, B), bf16)],
        18 * low_two.shape[0] * B * B,
        aliases={1: 0, 2: 1},
    )(me, *buffers, hidden, low_two)


STEM = 64
STEM_SIDE = 16
CHANNELS = 12
SLABS = 19
STEM_LANES = STEM_SIDE * STEM
INPUT_LANES = CHANNELS * 2 * STEM_SIDE
WINDOW = 7


def frames_kernel(frames_ref, out_ref, rows):
    segments = frames_ref.shape[0]
    side = 2 * STEM_SIDE

    def segment_step(segment, carry):
        pieces = [
            frames_ref[segment, index + 1, colour].astype(f32)
            - frames_ref[segment, index, colour].astype(f32)
            for index in range(4)
            for colour in range(3)
        ]
        for group in range(3):
            rows[group, pl.ds(segment, side, stride=segments)] = jnp.concatenate(
                pieces[4 * group : 4 * group + 4], axis=1
            )
        return carry

    lax.fori_loop(0, segments, segment_step, 0)
    empty = jnp.zeros((segments, INPUT_LANES), bf16)
    for parity in range(2):
        for slab in (0, 1, SLABS - 1):
            out_ref[parity, slab] = empty
    for row in range(side):
        for group in range(3):
            out_ref[row % 2, row // 2 + 2, :, group * LANES : (group + 1) * LANES] = rows[
                group, row * segments : (row + 1) * segments
            ].astype(bf16)


def frames_block(frames):
    segments = frames.shape[0] * frames.shape[1]
    ordered = frames.transpose(0, 1, 2, 5, 3, 4).reshape(
        (segments, frames.shape[2], 3) + frames.shape[3:5]
    )
    shape = (2, SLABS, segments, INPUT_LANES)
    return kernel_call(
        frames_kernel,
        1,
        [whole_spec(ordered.shape)],
        whole_out(shape),
        jax.ShapeDtypeStruct(shape, bf16),
        [pltpu.VMEM((3, 2 * STEM_SIDE * segments, LANES), f32)],
        ordered.size * 100,
    )(ordered)


def stem_rows(input_ref, offset):
    parity = 1 - offset % 2
    top = (offset - 3) // 2 + 2 if parity == 0 else (offset - 4) // 2 + 2
    found = input_ref[parity, top : top + STEM_SIDE]
    return found.reshape(-1, INPUT_LANES)


def band_select(turned=False):
    shape = [STEM_SIDE // 2, CHANNELS, 2 * STEM_SIDE, 2, LANES]
    axes = [0, 1, 2, 3, 4]
    if turned:
        shape, axes = [shape[axis] for axis in (0, 3, 4, 1, 2)], [0, 3, 4, 1, 2]
    pair, channel, place, which, entry = (
        lax.broadcasted_iota(jnp.int32, shape, axis) for axis in axes
    )
    met = (entry % CHANNELS == channel) & (entry < WINDOW * CHANNELS)
    met = met & (place == 2 * (2 * pair + which) + entry // CHANNELS - 3)
    ends = (2 * LANES, INPUT_LANES) if turned else (INPUT_LANES, 2 * LANES)
    return met.astype(bf16).reshape((STEM_SIDE // 2,) + ends)


def pair_weights(stem_weight):
    rows = stem_weight.reshape(WINDOW, WINDOW * CHANNELS, STEM)
    rows = jnp.pad(rows, ((0, 0), (0, LANES - WINDOW * CHANNELS), (0, 0)))
    none = jnp.zeros_like(rows)
    return jnp.concatenate(
        [jnp.concatenate([rows, none], 2), jnp.concatenate([none, rows], 2)], 1
    )


PAIRS = STEM_SIDE // 2


def stem_kernel(input_ref, select_ref, weights_ref, pre_ref, sums_ref, bands):
    selects = select_ref[...].reshape(PAIRS * INPUT_LANES, 2 * LANES)
    for offset in range(WINDOW):
        band = product(selects, weights_ref[offset]).astype(bf16)
        top = offset * INPUT_LANES
        for pair in range(PAIRS):
            bands[top : top + INPUT_LANES, pair * LANES : (pair + 1) * LANES] = band[
                pair * INPUT_LANES : (pair + 1) * INPUT_LANES
            ]
    rows = jnp.concatenate([stem_rows(input_ref, offset) for offset in range(WINDOW)], axis=1)
    for half in range(2):
        where = slice(half * WIDE, (half + 1) * WIDE)
        found = product(rows, bands[:, where])
        pre_ref[:, where] = found
        sums_ref[0:1, where] = jnp.sum(found, 0, keepdims=True)
        sums_ref[1:2, where] = jnp.sum(found * found, 0, keepdims=True)


def stem_block(inputs, select, weights, after=()):
    rows = inputs.shape[2] * STEM_SIDE
    return kernel_call(
        stem_kernel,
        1,
        [whole_spec(inputs.shape), whole_spec(select.shape), whole_spec(weights.shape)],
        [whole_out((rows, STEM_LANES)), whole_out((2, STEM_LANES))],
        [jax.ShapeDtypeStruct((rows, STEM_LANES), f32),
         jax.ShapeDtypeStruct((2, STEM_LANES), f32)],
        [pltpu.VMEM((WINDOW * INPUT_LANES, STEM_LANES), bf16)],
        2 * WINDOW * rows * INPUT_LANES * STEM_LANES,
        after=after,
    )(inputs, select, weights)


def stem_norm_kernel(count, pre_ref, in_sums_ref, affine_ref, cotangent_ref,
                     out_ref, grad_ref, sums_ref):
    def step_body(step, carry):
        where = lanes(step, LANES)
        mean, inverse, gain, shift = (
            spread(row) for row in constants(in_sums_ref[:, where], affine_ref[:, where], count)
        )
        first = jnp.zeros((16, LANES), f32)
        second = jnp.zeros((16, LANES), f32)
        for chunk in range(pre_ref.shape[0] // 16):
            rows = slice(chunk * 16, chunk * 16 + 16)
            unit = (pre_ref[rows, where] - mean) * inverse
            norm = unit * gain + shift
            sigma = sigmoid(norm)
            output = norm * sigma
            out_ref[rows, where] = output.astype(bf16)
            grad = cotangent_ref[rows, where].astype(f32) * (sigma + output * (1.0 - sigma))
            grad_ref[rows, where] = grad
            first = first + grad
            second = second + grad * unit
        sums_ref[0:1, where] = jnp.sum(first, 0, keepdims=True)
        sums_ref[1:2, where] = jnp.sum(second, 0, keepdims=True)
        return carry

    lax.fori_loop(0, STEM_LANES // LANES, step_body, 0)


def stem_norm_block(pre, sums, affine, cotangent, count, after=()):
    shape = pre.shape
    return kernel_call(
        functools.partial(stem_norm_kernel, count),
        1,
        [whole_spec(shape), whole_spec(sums.shape), whole_spec(affine.shape), whole_spec(shape)],
        [whole_out(shape), whole_out(shape), whole_out((2, STEM_LANES))],
        [jax.ShapeDtypeStruct(shape, bf16), jax.ShapeDtypeStruct(shape, f32),
         jax.ShapeDtypeStruct((2, STEM_LANES), f32)],
        [],
        4000 * pre.size,
        after=after,
    )(pre, sums, affine, cotangent)


def stem_back_kernel(count, input_ref, select_ref, pre_ref, in_sums_ref, affine_ref, grad_ref,
                     grads_ref, kernels_ref, out_ref, low):
    def low_step(step, carry):
        where = lanes(step, LANES)
        mean, inverse, gain, _ = constants(in_sums_ref[:, where], affine_ref[:, where], count)
        scale = spread(gain * inverse)
        offset = spread(grads_ref[0:1, where] / count)
        along = spread(grads_ref[1:2, where] / count * inverse)
        mean = spread(mean)
        for chunk in range(pre_ref.shape[0] // 16):
            rows = slice(chunk * 16, chunk * 16 + 16)
            centred = pre_ref[rows, where] - mean
            low[rows, where] = (
                scale * (grad_ref[rows, where] - offset - centred * along)
            ).astype(bf16)
        return carry

    lax.fori_loop(0, STEM_LANES // LANES, low_step, 0)
    selects = jnp.concatenate([select_ref[pair] for pair in range(PAIRS)], axis=1)
    pieces = []
    for offset in range(WINDOW):
        band = product(stem_rows(input_ref, offset).T, low[...]).astype(bf16)
        lined = [band[:, pair * LANES : (pair + 1) * LANES] for pair in range(PAIRS)]
        found = product(selects, jnp.concatenate(lined, axis=0))
        found = found[:LANES, :STEM] + found[LANES:, STEM:]
        pieces.append(found[: WINDOW * CHANNELS])
    pieces.append(jnp.zeros((3 * TILE - WINDOW * WINDOW * CHANNELS, STEM), f32))
    turned = jnp.concatenate(pieces, axis=0).T
    out_ref[...] = jnp.zeros_like(out_ref)
    own = R // 8
    for index in range(8):
        for piece in range(3):
            out_ref[index, piece * 8 : piece * 8 + 8] = turned[
                index * 8 : index * 8 + 8, piece * TILE : (piece + 1) * TILE
            ]
        for kind in range(2):
            out_ref[index, 24:33, kind * LANES : kind * LANES + own] = kernels_ref[
                9 * kind : 9 * kind + 9, index * own : (index + 1) * own
            ]


def stem_back_block(inputs, select, pre, sums, affine, grad, grads, kernel_grads, count):
    shape = pre.shape
    out = (8, FEW_ROWS, TILE)
    return kernel_call(
        functools.partial(stem_back_kernel, count),
        1,
        [whole_spec(inputs.shape), whole_spec(select.shape), whole_spec(shape),
         whole_spec(sums.shape), whole_spec(affine.shape), whole_spec(shape),
         whole_spec(grads.shape), whole_spec(kernel_grads.shape)],
        whole_out(out),
        jax.ShapeDtypeStruct(out, f32),
        [pltpu.VMEM(shape, bf16)],
        2 * WINDOW * shape[0] * INPUT_LANES * STEM_LANES,
    )(inputs, select, pre, sums, affine, grad, grads, kernel_grads)


SMALL_ROWS = 32
FIRST_ROWS = 64 + SMALL_ROWS


def cut_kernel(me_ref, squeeze_ref, expand_ref, reduce_ref, spatial_ref,
               stem_ref, next_ref, scale_ref, outer_ref, gain_one_ref, shift_one_ref,
               gain_two_ref, shift_two_ref, stem_gain_ref, stem_shift_ref,
               first_out, pair_out, spatial_out, small):
    part = me_ref[0] & 3
    first_out[0:64] = squeeze_ref[pl.ds(pl.multiple_of(part * 64, 64), 64)]
    small[...] = jnp.zeros_like(small)
    edge = stem_ref.shape[1] - B
    small[0:8] = stem_ref[:, 0:B].astype(f32)
    small[8:16, 0:edge] = stem_ref[:, B:].astype(f32)
    small[16:25, 0 : next_ref.shape[1]] = next_ref[...].astype(f32)
    small[16:25, LANES : LANES + scale_ref.shape[1]] = scale_ref[...].astype(f32)
    small[25:26] = outer_ref[...].astype(f32)
    for place, ref in enumerate((gain_one_ref, shift_one_ref, gain_two_ref, shift_two_ref)):
        small[26:27, place * LANES : place * LANES + ref.shape[1]] = ref[...].astype(f32)
    small[27:28, 0 : stem_gain_ref.shape[1]] = stem_gain_ref[...].astype(f32)
    small[27:28, LANES : LANES + stem_shift_ref.shape[1]] = stem_shift_ref[...].astype(f32)
    first_out[64:] = small[...].astype(bf16)
    pair_out[0:PAIR_ROWS] = reduce_ref[pl.ds(pl.multiple_of(part * 64, 64), 64)]
    for half in range(2):
        pair_out[PAIR_ROWS:, half * TILE : (half + 1) * TILE] = expand_ref[
            pl.ds(pl.multiple_of(part * 128 + half * 64, 64), 64)
        ]
    for tap in range(9):
        spatial_out[tap * 16 : tap * 16 + 16] = spatial_ref[
            tap, pl.ds(pl.multiple_of(part * 16, 16), 16)
        ]


def late_cut_kernel(me_ref, restore_ref, class_ref, late_out):
    part = me_ref[0] & 3
    late_out[0:RESTORE_ROWS] = restore_ref[:, pl.ds(pl.multiple_of(part * B, B), B)]
    for half in range(2):
        rows = pl.ds(pl.multiple_of(part * 64 + half * 32, 32), 32)
        late_out[RESTORE_ROWS:, half * TILE : (half + 1) * TILE] = class_ref[rows]


def late_cut_block(me, restore, classes):
    return kernel_call(
        late_cut_kernel,
        1,
        [SCALAR, whole_spec(restore.shape), whole_spec(classes.shape)],
        whole_out((LATE_ROWS, B)),
        jax.ShapeDtypeStruct((LATE_ROWS, B), bf16),
        [],
        1000000,
    )(me, restore, classes)


def cut_block(me, *weights):
    shapes = [(FIRST_ROWS, B), (2 * PAIR_ROWS, B), (SPATIAL_ROWS, B)]
    return kernel_call(
        cut_kernel,
        1,
        [SCALAR] + [whole_spec(weight.shape) for weight in weights],
        [whole_out(shape) for shape in shapes],
        [jax.ShapeDtypeStruct(shape, bf16) for shape in shapes],
        [pltpu.VMEM((SMALL_ROWS, B), f32)],
        1000000,
    )(me, *weights)


def unpack_kernel(me_ref, first_ref, squeeze_out, weights_out, next_out, scale_out,
                  one_out, two_out, three_out, stem_out):
    squeeze_out[...] = first_ref[:, 0:64]
    wide = first_ref.shape[0]
    small = []
    for index in range(wide):
        mask = (me_ref[0] >> 2) ^ index
        entry = (mask & 1) * 4 + (mask >> 1)
        small.append(first_ref[entry, 64:].astype(f32))

    def joined(row, at, width, rows=1):
        return jnp.concatenate(
            [values[row : row + rows, at : at + width] for values in small], axis=1
        )

    own = B // wide
    next_out[...] = joined(16, 0, own, 9)
    scale_out[...] = joined(16, LANES, own, 9)
    one_out[0:1] = joined(26, 0, own)
    one_out[1:2] = joined(26, LANES, own)
    two_out[0:1] = joined(26, 2 * LANES, own)
    two_out[1:2] = joined(26, 3 * LANES, own)
    three_out[0:1] = joined(25, 0, TILE)
    three_out[1:2] = joined(25, TILE, TILE)
    for row in range(2):
        stem = joined(27, row * LANES, STEM // wide)
        stem_out[row : row + 1] = jnp.concatenate([stem] * STEM_SIDE, axis=1)
    columns = jnp.concatenate(
        [jnp.concatenate([values[0:8], values[8:16, 0:LANES]], axis=1) for values in small], axis=0
    )
    rows = columns.T
    place = lax.broadcasted_iota(jnp.int32, (LANES, STEM), 0)
    none = jnp.zeros((LANES, STEM), f32)
    for offset in range(WINDOW):
        top = offset * WINDOW * CHANNELS
        block = jnp.where(place < WINDOW * CHANNELS, rows[top : top + LANES], 0.0)
        weights_out[offset, 0:LANES] = jnp.concatenate([block, none], axis=1).astype(bf16)
        weights_out[offset, LANES:] = jnp.concatenate([none, block], axis=1).astype(bf16)


def unpack_block(me, first):
    shapes = [
        ((first.shape[0], 64, B), bf16), ((WINDOW, 2 * LANES, LANES), bf16), ((9, R), f32), ((9, R), f32), ((2, B), f32),
        ((2, B), f32), ((2, C), f32), ((2, STEM_LANES), f32),
    ]
    return kernel_call(
        unpack_kernel,
        1,
        [SCALAR, whole_spec(first.shape)],
        [whole_out(shape) for shape, _ in shapes],
        [jax.ShapeDtypeStruct(shape, kind) for shape, kind in shapes],
        [],
        1000000,
    )(me, first)


def shards(
    frames,
    tokens,
    stem_cotangent,
    crop_counts,
    labels,
    stem_weight,
    stem_gain,
    stem_shift,
    w_squeeze,
    next_kernel,
    scale_kernel,
    w_expand,
    w_reduce,
    gain_one,
    shift_one,
    w_spatial,
    gain_two,
    shift_two,
    w_restore,
    gain_three,
    shift_three,
    w_class,
    class_bias,
):
    view_count = frames.shape[0]
    row_count = tokens.shape[0]
    devices = lax.axis_size(AXES)
    wide = lax.axis_size("wide")
    narrow = lax.axis_size("narrow")
    count = float(row_count * devices)
    segments = view_count * SEG
    stem_rows_here = segments * STEM_SIDE
    stem_count = float(stem_rows_here * STEM_SIDE * devices)
    direct = wide == C // TILE and narrow == 4
    me = lax.axis_index(AXES)
    me_array = (me if direct else 0 * me).astype(jnp.int32).reshape(1)

    stem_width = stem_weight.shape[1]
    inner_width = gain_one.shape[0]
    outer_width = gain_three.shape[0]

    def by_segment(values):
        values = values.reshape(STEM_SIDE, segments, STEM_LANES)
        return values.transpose(1, 0, 2).reshape(-1, STEM)

    def by_output_row(values):
        values = values.reshape(segments, STEM_SIDE, STEM_LANES)
        return values.transpose(1, 0, 2).reshape(stem_rows_here, STEM_LANES)

    if direct:
        first_own, pair_own, spatial_own = cut_block(
            me_array, w_squeeze, w_expand, w_reduce, w_spatial, stem_weight.T, next_kernel,
            scale_kernel, jnp.concatenate([gain_three, shift_three])[None], gain_one[None],
            shift_one[None], gain_two[None], shift_two[None], stem_gain[None], stem_shift[None],
        )
        firsts, pairs, spatials = Gather(first_own), Gather(pair_own), HalvedGather(spatial_own)
        (cotangent, select), came, _ = beside(
            lambda grads: (by_output_row(grads), band_select()), [stem_cotangent], firsts.depth()
        )
        firsts.take_depth(came)
        (inputs, late_own), came, _ = beside(
            lambda images, mine, restore, classes: (
                frames_block(images),
                late_cut_block(
                    mine, restore, jnp.pad(classes, ((0, 0), (0, TILE - CLASSES)))
                ),
            ),
            [frames, me_array, w_restore, w_class], firsts.second() + pairs.depth(),
        )
        firsts.take_second(came[:1])
        pairs.take_depth(came[1:])
        (
            squeeze_own, weights, full_next, full_scale, affine_one, affine_two, affine_three, stem_affine,
        ) = unpack_block(me_array, firsts.eight)
        (stem_pre, stem_part), came, _ = beside(
            stem_block, [inputs, select, weights],
            [(squeeze_own, 2)] + pairs.second() + spatials.depth(),
        )
        squeeze_far = came[0]
        pairs.take_second(came[1:2])
        spatials.take_depth(came[2:])
        stem_pre, came, _ = beside(
            lambda values: values, [stem_pre], [(squeeze_own, 1), (squeeze_far, 1)]
        )
        squeeze = (squeeze_own, squeeze_far) + tuple(came)
    else:
        squeeze, pair, spatial, late = gathered(
            w_squeeze, w_expand, w_reduce, w_spatial, w_restore, w_class
        )

        def whole(values):
            return lax.all_gather(values, "wide", axis=values.ndim - 1, tiled=True).astype(f32)

        weights = pair_weights(whole(stem_weight).astype(bf16))
        full_next, full_scale = whole(next_kernel), whole(scale_kernel)
        affine_one = jnp.stack([whole(gain_one), whole(shift_one)])
        affine_two = jnp.stack([whole(gain_two), whole(shift_two)])
        affine_three = jnp.stack([whole(gain_three), whole(shift_three)])
        stem_affine = jnp.tile(jnp.stack([whole(stem_gain), whole(stem_shift)]), (1, STEM_SIDE))
        inputs, select, cotangent = frames_block(frames), band_select(), by_output_row(stem_cotangent)
        stem_pre, stem_part = stem_block(inputs, select, weights)
    stem_part = stem_part.reshape(2, STEM_SIDE, STEM).sum(1).reshape(1, 2 * STEM)

    def stem_lanes(sums):
        return jnp.tile(sums[2, : 2 * STEM].reshape(2, STEM), (1, STEM_SIDE))

    def with_row(sums, row):
        return jnp.concatenate([sums, jnp.pad(row, ((0, 0), (0, sums.shape[1] - row.shape[1])))])

    mixing_operands = [me_array, squeeze, tokens, full_next, full_scale]
    if direct:
        (upcoming, differ, mixed_low), came, _ = beside(
            mixing_block, mixing_operands, pairs.third() + spatials.second()
        )
        pairs.take_third(came[:1])
        spatials.take_second(came[1:])
        (mixed_low, late_own), came, _ = beside(
            lambda values, mine: (values, mine), [mixed_low, late_own], pairs.core()
        )
        pairs.take_core(came)
        late = lax.all_gather(late_own, AXES)
        pair = pairs.arrays
    else:
        upcoming, differ, mixed_low = mixing_block(*mixing_operands)
    gate_operands = [me_array, pair, tokens, mixed_low]
    if direct:
        (logit, gated_low, pre_one, one_part), came, _ = beside(
            gate_block, gate_operands, spatials.third_of(0)
        )
        spatials.take_third_of(0, came)
        one_sums, came, _ = beside(
            swap_total, [to_all(with_row(one_part, stem_part))],
            spatials.third_of(1) + spatials.core_of(0),
        )
        spatials.take_third_of(1, came[:1])
        spatials.take_core_of(0, came[1:])
        one_sums, came, _ = beside(lambda values: values, [one_sums], spatials.core_of(1))
        spatials.take_core_of(1, came)
        spatial = spatials.arrays
    else:
        logit, gated_low, pre_one, one_part = gate_block(*gate_operands)
        one_sums = swap_total(to_all(with_row(one_part, stem_part)))
    stem_sums = stem_lanes(one_sums)
    hidden_one, pre_two, two_part = second_block(
        me_array, spatial, pre_one, one_sums, affine_one, count
    )
    stem_out, stem_norm_grad, stem_part = stem_norm_block(
        stem_pre, stem_sums, stem_affine, cotangent, stem_count
    )
    stem_part = stem_part.reshape(2, STEM_SIDE, STEM).sum(1).reshape(1, 2 * STEM)
    two_sums = swap_total(two_part)
    hidden_two, pre_three, centres, three_part = third_block(pre_two, two_sums, affine_two, late, count)
    three_sums, stem_features = total_beside(
        with_row(three_part, stem_part), by_segment, [stem_out]
    )
    stem_grads = stem_lanes(three_sums)
    bias = jnp.pad(class_bias.astype(f32), (0, TILE - CLASSES))[None]
    activations, slope, view_sums, view_logits, pooled_low = fourth_block(
        pre_three, centres, gated_low, three_sums, affine_three, late, bias, count
    )
    pooled_low = pooled_low[:view_count]

    ends = jnp.cumsum(crop_counts)
    starts = ends - crop_counts
    positions = (me - 1) * view_count + jnp.arange(3 * view_count, dtype=jnp.int32)
    video = jnp.sum((ends[None, :] <= positions[:, None]).astype(jnp.int32), 1)
    own_video = video[view_count : 2 * view_count]
    belongs = (
        own_video[:, None] == jnp.arange(crop_counts.shape[0], dtype=jnp.int32)[None, :]
    ).astype(jnp.int32)
    own_count = jnp.sum(belongs * crop_counts[None, :], 1).astype(f32)
    own_label = jnp.sum(belongs * labels[None, :], 1)
    own_start = jnp.sum(belongs * starts[None, :], 1)
    first = (own_start == positions[view_count : 2 * view_count]).astype(f32)
    same = (own_video[:, None] == video[None, :]).astype(f32) / own_count[:, None]
    target = (own_label[:, None] == jnp.arange(TILE, dtype=jnp.int32)[None, :]).astype(f32)
    marks = jnp.concatenate([same, 1.0 / own_count[:, None], first[:, None]], axis=1)
    marks = jnp.pad(marks, ((0, 8 - view_count), (0, LANES - marks.shape[1])))
    target = jnp.pad(target, ((0, 8 - view_count), (0, 0)))

    before = lax.ppermute(view_logits, AXES, [(i, i + 1) for i in range(devices - 1)])
    following = lax.ppermute(view_logits, AXES, [(i + 1, i) for i in range(devices - 1)])
    three_part, pooled_grad, view_grad_low = video_block(
        before, view_logits, following, marks, target, view_sums, late, view_count
    )
    view_grad_low = view_grad_low[:view_count]

    own_parts = pooled_low.reshape(view_count, wide, outer_width).swapaxes(0, 1)
    grad_parts = jnp.broadcast_to(
        view_grad_low, (wide, view_count, TILE)
    )
    factors = jnp.concatenate([own_parts, grad_parts], axis=2)
    factors = jnp.broadcast_to(factors[:, None], (wide, narrow) + factors.shape[1:])
    factors = factors.reshape((devices,) + factors.shape[2:])

    def send_factors(parts):
        return lax.all_to_all(parts, AXES, 0, 0, tiled=True)

    three_grads = total(three_part)
    class_bias_grad = three_grads[2, :CLASSES]
    loss = three_grads[2, CLASSES] / crop_counts.shape[0]

    fifth_operands = [
        slope, pre_three, centres, pooled_grad, three_sums, affine_three, three_grads, late,
        pre_two, two_sums, affine_two,
    ]
    run_fifth = functools.partial(fifth_block, count=count)
    run_sixth = functools.partial(sixth_block, count=count)
    run_stem_back = functools.partial(stem_back_block, count=stem_count)

    def stem_back_operands():
        return [
            inputs, band_select(True), stem_pre, stem_sums, stem_affine, stem_norm_grad, stem_grads,
            kernel_grads,
        ]
    run_outer = outer_block_of(R // 4)

    def sixth_operands():
        return [
            me_array, spatial, norm_two_grad, pre_two, two_sums, affine_two, two_grads, pre_one,
            one_sums, affine_one,
        ]

    def low_operands():
        return [me_array, norm_one_grad, pre_one, one_sums, affine_one, one_grads, gated_low]

    def gate_back_operands():
        return [me_array, pair, low_one, slope, pooled_grad, tokens, logit]

    def mixing_back_operands():
        return [me_array, pair, logit_grad, upcoming, differ, full_next, full_scale]

    if direct:
        low_three, norm_two_grad, two_part = run_fifth(*fifth_operands)
        (buffers, two_grads), _, _ = beside(
            lambda mine, hidden, low, part: (
                restore_outer_block(mine, hidden, low), swap_total(part)
            ),
            [me_array, hidden_two, low_three, two_part], [],
        )
        (low_two, norm_one_grad, one_part, factors), _, _ = beside(
            lambda parts, *operands: (*run_sixth(*operands), send_factors(parts)),
            [factors] + sixth_operands(), [],
        )
        ((keep, send), one_grads), _, _ = beside(
            lambda mine, shared, hidden, low, part: (
                spatial_block(mine, shared, hidden, low), swap_total(part)
            ),
            [me_array, buffers, hidden_one, low_two, one_part], [],
        )
        quarter = (4, 2, 2, R // 4, TILE)
        (low_one, reduce_half), came, _ = beside(
            functools.partial(low_outer_block, count=count), low_operands(), [(send, 1)]
        )
        buffer = (keep.astype(f32) + came[0].astype(f32)).astype(bf16)
        reduced_sum = Sum(reduce_half, quarter, 0)
        (low_one, buffer), came, _ = beside(
            lambda *values: values, [low_one, buffer], reduced_sum.core()
        )
        buffer = lax.psum_scatter(
            buffer.reshape(8, -1, WIDE), "wide", scatter_dimension=0, tiled=False
        )
        reduced_sum.take_core(came)
        (logit_grad, tokens_part), came, _ = beside(
            gate_back_block, gate_back_operands(), reduced_sum.split("x")
        )
        reduced_sum.take(came)
        expand_half, came, _ = beside(
            run_outer, [me_array, mixed_low, logit_grad], reduced_sum.split("y")
        )
        reduced_sum.take(came)
        expand_sum = Sum(expand_half, quarter, 0)
        logit_grad, came, _ = beside(lambda values: values, [logit_grad], expand_sum.core())
        expand_sum.take_core(came)
        (low_squeezed, kernel_grads), came, _ = beside(
            mixing_back_block, mixing_back_operands(),
            expand_sum.split("x"),
        )
        expand_sum.take(came)
        squeeze_half, came, _ = beside(
            run_outer, [me_array, low_squeezed, tokens],
            expand_sum.split("y"),
        )
        expand_sum.take(came)
        both_sum = Sum((None, None), (), 1)
        both_sum.axes = "z"
        both_sum.values = jnp.stack([reduced_sum.values, expand_sum.values])
        shared = Sum((None, None), (), 0)
        shared.axes = "x"
        shared.values = buffer.reshape(2, -1, WIDE)
        squeezed = Sum(squeeze_half, quarter, 0)
        tokens_part, came, _ = beside(lambda values: values, [tokens_part], squeezed.core())
        squeezed.take_core(came)
        stem_back, came, _ = beside(
            run_stem_back, stem_back_operands(),
            squeezed.split("x") + both_sum.split("z") + shared.split("x"),
        )
        squeezed.take(came[:1])
        both_sum.take(came[1:4])
        shared.take(came[4:])
        few = Sum((None, None), (), 0)
        few.axes = "zy"
        few.values = stem_back.reshape(4, 2, FEW_ROWS, TILE)
        tokens_grad, came, _ = beside(
            tokens_block, [me_array, squeeze, tokens_part, low_squeezed],
            squeezed.split("y") + few.split("y") + both_sum.spread(),
        )
        squeezed.take(came[:1])
        few.take(came[1:2])
        both_sum.take_spread(came[2:])
        squeezed.values = jnp.concatenate([squeezed.values, few.values], axis=1)
        _, came, _ = beside(lambda: None, [], squeezed.split("z") + shared.spread())
        squeezed.take(came[:3])
        shared.take_spread(came[3:])
        last = Sum((None, None), (), 0)
        last.values = squeezed.values.astype(bf16)
        _, came, _ = beside(lambda: None, [], last.spread())
        last.take_spread(came)
        squeezed.whole = last.whole[:, : R // 4]
        few = jnp.sum(last.whole[:, R // 4 :], 0)
        buffer = shared.whole
        sum_stem = few[:24].reshape(3, 8, TILE).swapaxes(0, 1).reshape(8, 3 * TILE)
        sum_stem = sum_stem[:, : stem_weight.shape[0]].T
        sum_next = few[24:33, :inner_width]
        sum_scale = few[24:33, LANES : LANES + inner_width]
        buffer = buffer.reshape(4, SHARED, 16, WIDE)
        sum_restore = buffer[:, :GROUPS].swapaxes(1, 2).reshape(w_restore.shape)
        sum_spatial = buffer[:, GROUPS:].swapaxes(0, 1)
        sum_spatial = sum_spatial.reshape(w_spatial.shape)
        sum_reduce = both_sum.whole[:, 0].reshape(B, TILE).T
        sum_expand = both_sum.whole[:, 1].reshape(R, TILE)
        sum_squeeze = squeezed.whole.reshape(R, TILE).T
    else:
        low_three, norm_two_grad, two_part = run_fifth(*fifth_operands)
        buffers = restore_outer_block(me_array, hidden_two, low_three)
        two_grads = swap_total(two_part)
        low_two, norm_one_grad, one_part = run_sixth(*sixth_operands())
        factors = send_factors(factors)
        one_grads = swap_total(one_part)
        buffers = spatial_block(me_array, buffers, hidden_one, low_two)
        low_one, reduce_half = low_outer_block(*low_operands(), count)
        logit_grad, tokens_part = gate_back_block(*gate_back_operands())
        expand_half = run_outer(me_array, mixed_low, logit_grad)
        low_squeezed, kernel_grads = mixing_back_block(*mixing_back_operands())
        few = run_stem_back(*stem_back_operands())
        squeeze_half = run_outer(me_array, low_squeezed, tokens)
        tokens_grad = tokens_block(me_array, squeeze, tokens_part, low_squeezed)
        few = lax.psum(few, AXES)
        sum_stem = few[:, :24].reshape(8, 3, 8, TILE).swapaxes(1, 2).reshape(STEM, 3 * TILE)
        sum_stem = sum_stem[:, : stem_weight.shape[0]].T
        sum_next, sum_scale = (
            few[:, 24:33, at : at + R // 8].swapaxes(0, 1).reshape(9, R) for at in (0, LANES)
        )

        def own_columns(values, width):
            return lax.dynamic_slice_in_dim(values, lax.axis_index("wide") * width, width, 1)

        sum_stem = own_columns(sum_stem, stem_width)
        sum_next = own_columns(sum_next, inner_width)
        sum_scale = own_columns(sum_scale, inner_width)
        sum_restore, sum_spatial, sum_reduce, sum_expand, sum_squeeze = reduced(
            buffers, reduce_half, expand_half, squeeze_half
        )
    factors = factors.reshape(devices * view_count, outer_width + TILE)
    sum_class = product_left(
        factors[:, :outer_width], factors[:, outer_width : outer_width + CLASSES]
    )

    def own_slice(values, width):
        return lax.dynamic_slice_in_dim(values, lax.axis_index("wide") * width, width)

    return (
        activations,
        stem_features,
        tokens_grad,
        sum_stem,
        own_slice(stem_grads[1, :STEM], stem_width),
        own_slice(stem_grads[0, :STEM], stem_width),
        sum_squeeze,
        sum_next,
        sum_scale,
        sum_expand,
        sum_reduce,
        own_slice(one_grads[1], inner_width),
        own_slice(one_grads[0], inner_width),
        sum_spatial,
        own_slice(two_grads[1], inner_width),
        own_slice(two_grads[0], inner_width),
        sum_restore,
        own_slice(three_grads[1], outer_width),
        own_slice(three_grads[0], outer_width),
        sum_class,
        class_bias_grad,
        loss,
    )


def solution(mesh):
    in_specs = (
        P(("wide", "narrow"), None, None, None, None, None),
        P(("wide", "narrow"), None),
        P(("wide", "narrow"), None),
        P(),
        P(),
        P(None, "wide"),
        P("wide"),
        P("wide"),
        P("wide", None),
        P(None, "wide"),
        P(None, "wide"),
        P(None, "wide"),
        P("wide", None),
        P("wide"),
        P("wide"),
        P(None, "wide", None),
        P("wide"),
        P("wide"),
        P("wide", None),
        P("wide"),
        P("wide"),
        P("wide", None),
        P(),
    )
    out_specs = (
        P(("wide", "narrow"), None),
        P(("wide", "narrow"), None),
        P(("wide", "narrow"), None),
        P(None, "wide"),
        P("wide"),
        P("wide"),
        P("wide", None),
        P(None, "wide"),
        P(None, "wide"),
        P(None, "wide"),
        P("wide", None),
        P("wide"),
        P("wide"),
        P(None, "wide", None),
        P("wide"),
        P("wide"),
        P("wide", None),
        P("wide"),
        P("wide"),
        P("wide", None),
        P(),
        P(),
    )
    return jax.shard_map(shards, mesh=mesh, in_specs=in_specs, out_specs=out_specs, check_vma=False)
```

```python
import functools

import jax
import jax.numpy as jnp
from jax import lax
from jax.experimental import pallas as pl
from jax.experimental.pallas import tpu as pltpu
from jax.sharding import PartitionSpec as P

C = 2048
B = 512
R = 512
CLASSES = 174
SEG = 8
SIDE = 7
PER_VIEW = SEG * SIDE * SIDE

epsilon = 1e-05
loss_scale = 1024.0

AXES = ("wide", "narrow")
f32 = jnp.float32
bf16 = jnp.bfloat16


def product(first_operand, second_operand):
    return jnp.dot(first_operand, second_operand, preferred_element_type=f32)


def product_left(first_operand, second_operand):
    return lax.dot_general(
        first_operand, second_operand, (((0,), (0,)), ((), ())), preferred_element_type=f32
    )


def product_right(first_operand, second_operand):
    return lax.dot_general(
        first_operand, second_operand, (((1,), (1,)), ((), ())), preferred_element_type=f32
    )


def exchange(values, mask):
    size = lax.axis_size(AXES)
    return lax.ppermute(values, AXES, [(index, index ^ mask) for index in range(size)])


def own_bit(bit):
    return (lax.axis_index(AXES) >> bit) & 1


def total(values):
    bits = lax.axis_size(AXES).bit_length() - 1
    values = values + exchange(values, 1)
    for bit in range(1, bits, 2):
        masks = [1 << bit]
        if bit + 1 < bits:
            masks += [2 << bit, 3 << bit]
        parts = [exchange(values, mask) for mask in masks]
        for part in parts:
            values = values + part
    return values


def total_beside(values, run, inputs):
    bits = lax.axis_size(AXES).bit_length() - 1
    values = values + exchange(values, 1)
    for bit in range(1, bits, 2):
        masks = [1 << bit] + ([2 << bit, 3 << bit] if bit + 1 < bits else [])
        if bit == 3:
            out, parts, _ = beside(run, inputs, [(values, mask) for mask in masks])
        else:
            parts = [exchange(values, mask) for mask in masks]
        for part in parts:
            values = values + part
    return values, out


def swap_total(copies):
    return jnp.sum(lax.all_to_all(copies, AXES, 0, 0, tiled=True), 0)


def swap(parts):
    return lax.all_to_all(parts, AXES, 0, 0, tiled=True)


def apart(came):
    return jnp.sum(came[:, 0:2], 0), came[:, 2:].astype(bf16)


def to_all(values):
    return jnp.broadcast_to(values[None], (lax.axis_size(AXES),) + values.shape)


def beside(run, inputs, sends, more=()):
    inputs, arrays = lax.optimization_barrier((tuple(inputs), [array for array, _ in sends]))
    came = [exchange(array, mask) for array, (_, mask) in zip(arrays, sends)]
    return lax.optimization_barrier((run(*inputs), came, tuple(more)))


def launch(run, inputs, sends):
    inputs, arrays = lax.optimization_barrier((tuple(inputs), [array for array, _ in sends]))
    came = [exchange(array, mask) for array, (_, mask) in zip(arrays, sends)]
    return lax.optimization_barrier(run(*inputs)), came


class Gather:
    def __init__(self, block):
        self.block = block

    def depth(self):
        return [(self.block, mask) for mask in (8, 16, 24)]

    def take_depth(self, came):
        self.four = join([part[None] for part in (self.block, *came)])

    def second(self):
        return [(self.four, 4)]

    def take_second(self, came):
        self.eight = join([self.four, came[0]])

    def third(self):
        return [(self.eight, 2)]

    def take_third(self, came):
        self.other = came[0]

    def core(self):
        return [(self.eight, 1), (self.other, 1)]

    def take_core(self, came):
        self.arrays = (self.eight, self.other) + tuple(came)


class HalvedGather(Gather):
    def take_second(self, came):
        self.parts = [self.four, came[0]]
        self.far = [None, None]
        self.arrays = [None] * 8

    def third_of(self, part):
        return [(self.parts[part], 2)]

    def take_third_of(self, part, came):
        self.far[part] = came[0]

    def core_of(self, part):
        return [(self.parts[part], 1), (self.far[part], 1)]

    def take_core_of(self, part, came):
        self.arrays[part::2] = [self.parts[part], self.far[part], came[0], came[1]]


class Sum:
    def __init__(self, half, shape, lead):
        self.keep, self.send = half
        self.shape, self.lead, self.axes = shape, lead, "zyx"

    def core(self):
        return [(self.send, 1)]

    def take_core(self, came):
        self.values = (self.keep.astype(f32) + came[0].astype(f32)).reshape(self.shape)

    def split(self, letter):
        place = self.lead + self.axes.index(letter)
        self.axes = self.axes.replace(letter, "")
        bit = {"x": 1, "y": 2, "z": 3}[letter]
        span = 3 if letter == "z" else 1
        mine = (lax.axis_index(AXES) >> bit) & span
        found = []
        for mask in range(1, span + 1):
            part = lax.dynamic_index_in_dim(self.values, mine ^ mask, place, keepdims=False)
            found.append((part.astype(bf16), mask << bit))
        self.values = lax.dynamic_index_in_dim(self.values, mine, place, keepdims=False)
        return found

    def split_parts(self, letter, at):
        ((send, mask),) = self.split(letter)
        return [(send[:at], mask)], [(send[at:], mask)]

    def take_parts(self, first, second):
        self.take([jnp.concatenate([first[0], second[0]])])

    def take(self, came):
        for part in came:
            self.values = self.values + part.astype(f32)

    def spread(self):
        self.part = self.values.astype(bf16)
        return [(self.part, mask) for mask in (1, 2, 3)]

    def take_spread(self, came):
        own, (core, over_x, both) = self.part, came
        odd, far = own_bit(0) == 1, own_bit(1) == 1
        near = [jnp.where(odd, core, own), jnp.where(odd, own, core)]
        away = [jnp.where(odd, both, over_x), jnp.where(odd, over_x, both)]
        self.whole = jnp.stack(
            [jnp.where(far, away[0], near[0]), jnp.where(far, away[1], near[1]),
             jnp.where(far, near[0], away[0]), jnp.where(far, near[1], away[1])]
        ).astype(f32)


def gathered(w_squeeze, w_expand, w_reduce, w_spatial, w_restore, w_class):
    def whole(weight, axis):
        return lax.all_gather(weight, "wide", axis=axis, tiled=True)

    def as_blocks(blocks):
        ordered = blocks.reshape((4, 2, 2, 2) + blocks.shape[1:])
        return [
            ordered[:, :, far, core].swapaxes(0, 1).reshape((8,) + blocks.shape[1:])
            for core in range(2)
            for far in range(2)
        ]

    squeeze = whole(w_squeeze, 0).reshape(32, -1, R)
    expand = whole(w_expand, 1).reshape(4, 2, PAIR_ROWS, 8, TILE).transpose(3, 0, 2, 1, 4)
    expand = expand.reshape(32, PAIR_ROWS, 2 * TILE)
    reduce = whole(w_reduce, 0).reshape(32, -1, B)
    spatial = whole(w_spatial, 1).reshape(9, 32, 16, B).swapaxes(0, 1).reshape(32, -1, B)
    restore = whole(w_restore, 0).reshape(8, 64, 4, B).swapaxes(1, 2).reshape(32, 64, B)
    classes = jnp.pad(whole(w_class, 0), ((0, 0), (0, TILE - CLASSES)))
    classes = classes.reshape(32, 2, CLASS_ROWS, TILE).swapaxes(1, 2).reshape(32, CLASS_ROWS, B)
    late = jnp.concatenate([restore, classes], axis=1)
    pair = jnp.concatenate([reduce, expand], axis=1)
    spatial = [part for array in as_blocks(spatial) for part in (array[:4], array[4:])]
    return as_blocks(squeeze), as_blocks(pair), spatial, late


def reduced(buffers, reduce_half, expand_half, squeeze_half):
    def whole(half, grain):
        keep, send = (part.astype(bf16) for part in half)
        shape = keep.shape[:1] + (-1, grain) + keep.shape[2:]
        both = jnp.stack([keep.reshape(shape), send.reshape(shape)], axis=2)
        return both.reshape(keep.shape[:1] + (-1,) + keep.shape[2:])

    def scattered(grad, axis):
        part = lax.psum_scatter(grad, "wide", scatter_dimension=axis, tiled=True)
        return lax.psum(part, "narrow").astype(f32)

    def columns(tiles):
        return tiles.swapaxes(0, 1).reshape(tiles.shape[1], -1)

    shared = jnp.stack([part.reshape(16, SHARED, 16, WIDE) for part in buffers], axis=1)
    shared = shared.transpose(2, 0, 1, 3, 4).reshape(SHARED, B, WIDE)
    restore = shared[:GROUPS].swapaxes(0, 1).reshape(B, C)
    spatial = shared[GROUPS:]
    return (
        scattered(restore, 0),
        scattered(spatial, 1),
        scattered(columns(whole(reduce_half, 128)), 1).T,
        scattered(columns(whole(expand_half, 128)), 1),
        scattered(columns(whole(squeeze_half, 128)), 1).T,
    )


CELLS = SIDE * SIDE
HALF = 2 * PER_VIEW
PADDED = SIDE + 2
MIB = 1 << 20
VMEM = 60
LANES = 128
TILE = 256


def cell_place(cell):
    return (cell // SIDE + 1) * PADDED + cell % SIDE + 1


def tap_place(cell, tap):
    return cell_place(cell) + (tap // 3 - 1) * PADDED + tap % 3 - 1


def dot_nt(first_operand, second_operand):
    return lax.dot_general(
        first_operand, second_operand, (((1,), (1,)), ((), ())), preferred_element_type=f32
    )


def dot_tn(first_operand, second_operand):
    return lax.dot_general(
        first_operand, second_operand, (((0,), (0,)), ((), ())), preferred_element_type=f32
    )


def sigmoid(values):
    return 0.5 * jnp.tanh(0.5 * values) + 0.5


def constants(sums, affine, count):
    mean = sums[0:1] / count
    inverse = lax.rsqrt(sums[1:2] / count - mean * mean + epsilon)
    return mean, inverse, affine[0:1], affine[1:2]


def spread(row, rows=16):
    return jnp.broadcast_to(row, (rows, row.shape[1]))


def lanes(index, width):
    return pl.ds(pl.multiple_of(index * width, width), width)


def clear_border(ref):
    zero = jnp.zeros(ref.shape[1:], ref.dtype)
    for place in range(PADDED * PADDED):
        if place // PADDED in (0, PADDED - 1) or place % PADDED in (0, PADDED - 1):
            ref[place] = zero


def fold(values):
    return values[0:8] + values[8:16]


def half_spec(width):
    return pl.BlockSpec((HALF, width), lambda step, *_: (step, 0))


def whole_spec(shape):
    return pl.BlockSpec(shape, lambda *_: (0,) * len(shape), pipeline_mode=pl.Buffered(1))


def whole_out(shape):
    return pl.BlockSpec(shape, lambda *_: (0,) * len(shape))


WIDE = 512
GROUPS = C // WIDE


def group_at(group):
    return slice(group * WIDE, (group + 1) * WIDE)


def chunks():
    for chunk in range(HALF // 16):
        yield chunk, slice(chunk * 16, chunk * 16 + 16)


ANY = pl.BlockSpec(memory_space=pl.ANY)
SCALAR = pl.BlockSpec(memory_space=pltpu.SMEM)


def kernel_call(kernel, steps, in_specs, out_specs, out_shapes, scratch, flops,
                transcendentals=0, after=(), vmem=VMEM, aliases=None):
    known = len(in_specs)
    grid = steps if isinstance(steps, tuple) else (steps,)

    def body(*refs):
        kernel(*refs[:known], *refs[known + len(after) :])

    call = pl.pallas_call(
        body,
        grid=grid,
        in_specs=list(in_specs) + [ANY] * len(after),
        out_specs=out_specs,
        out_shape=out_shapes,
        scratch_shapes=scratch,
        input_output_aliases=aliases or {},
        compiler_params=pltpu.CompilerParams(
            dimension_semantics=("arbitrary",) * len(grid), vmem_limit_bytes=vmem * MIB
        ),
        cost_estimate=pl.CostEstimate(
            flops=2 * flops, bytes_accessed=16 * MIB, transcendentals=transcendentals
        ),
    )
    return lambda *operands: call(*operands, *after)


def block_copies(me, sources, target, semaphores, rows=None, lanes_at=None, target_rows=None):
    copies = []
    split = len(sources) // 4
    for which, low_mask in enumerate((0, 2, 1, 3)):
        for entry in range(8):
            mask = low_mask | ((entry // 4) * 4) | ((entry % 4) << 3)
            if split == 1:
                taken = sources[which].at[entry]
            else:
                taken = sources[2 * which + entry // 4].at[entry % 4]
            place = target.at[me ^ mask]
            if rows is not None:
                taken = taken.at[rows] if lanes_at is None else taken.at[rows, lanes_at]
            if target_rows is not None:
                place = place.at[target_rows]
            copies.append(pltpu.make_async_copy(taken, place, semaphores.at[len(copies)]))
    return copies


PAIR_ROWS = 64


def reduce_copies(me, sources, target, semaphores):
    return block_copies(me, sources, target, semaphores, slice(0, PAIR_ROWS))


def expand_copies(me, sources, target, semaphores):
    rows = slice(PAIR_ROWS, 2 * PAIR_ROWS)
    found = []
    for part in range(2):
        found += block_copies(
            me, sources, target, semaphores.at[part], rows,
            slice(part * TILE, (part + 1) * TILE),
            slice(part * PAIR_ROWS, (part + 1) * PAIR_ROWS),
        )
    return found


def start(copies):
    for copy in copies:
        copy.start()


def wait(copies):
    for copy in copies:
        copy.wait()


def join_kernel(*refs):
    *sources, out_ref, semaphores = refs
    copies, top = [], 0
    for source in sources:
        count = source.shape[0]
        copies.append(
            pltpu.make_async_copy(
                source, out_ref.at[top : top + count], semaphores.at[len(copies)]
            )
        )
        top += count
    start(copies)
    wait(copies)


def join(arrays):
    count = sum(array.shape[0] for array in arrays)
    return kernel_call(
        join_kernel,
        1,
        [ANY] * len(arrays),
        ANY,
        jax.ShapeDtypeStruct((count,) + arrays[0].shape[1:], arrays[0].dtype),
        [pltpu.SemaphoreType.DMA((len(arrays),))],
        1000000,
        vmem=16,
    )(*arrays)


def first_step():
    return pl.program_id(0) == 0


def store_copies(copies_ref, sums, others_ref=None):
    @pl.when(pl.program_id(0) == pl.num_programs(0) - 1)
    def _():
        values = sums[...]
        for index in range(copies_ref.shape[0]):
            copies_ref[index, 0 : values.shape[0]] = values
            if others_ref is not None:
                copies_ref[index, values.shape[0] :] = others_ref[index].astype(f32)


def add_moments(sums_ref, where, first, second):
    sums_ref[0:1, where] += jnp.sum(first, 0, keepdims=True)
    sums_ref[1:2, where] += jnp.sum(second, 0, keepdims=True)


def mixing_kernel(
    me_ref, block_a, block_b, block_c, block_d, tokens_ref, next_ref, scale_ref,
    upcoming_ref, differ_ref, mixed_ref, natural, ahead, padded, squeeze_ref, semaphores,
):
    @pl.when(first_step())
    def _():
        copies = block_copies(
            me_ref[0], (block_a, block_b, block_c, block_d), squeeze_ref, semaphores, slice(0, 64)
        )
        start(copies)
        natural[:, HALF:] = jnp.zeros((4, natural.shape[1] - HALF, LANES), f32)
        clear_border(ahead)
        clear_border(padded)
        wait(copies)

    def squeeze_step(step, carry):
        squeezed = product(
            tokens_ref[...], squeeze_ref[:, :, lanes(step, TILE)].reshape(C, TILE)
        )
        natural[2 * step, 0:HALF] = squeezed[:, 0:LANES]
        natural[2 * step + 1, 0:HALF] = squeezed[:, LANES:TILE]
        return carry

    lax.fori_loop(0, 2, squeeze_step, 0)
    segment = lax.broadcasted_iota(jnp.int32, (16, LANES), 0) % SEG
    not_last = (segment != SEG - 1).astype(f32)

    def mixing_step(step, carry):
        where = lanes(step, LANES)
        next_rows = [spread(next_ref[tap : tap + 1, where]) for tap in range(9)]
        for cell in range(CELLS):
            upcoming = natural[step, pl.ds(cell + CELLS, 16, stride=CELLS)] * not_last
            ahead[cell_place(cell)] = upcoming
            upcoming_ref[cell * 16 : cell * 16 + 16, where] = upcoming
        mean = jnp.zeros((16, LANES), f32)
        for cell in range(CELLS):
            differ = -natural[step, pl.ds(cell, 16, stride=CELLS)]
            for tap in range(9):
                differ = differ + ahead[tap_place(cell, tap)] * next_rows[tap]
            padded[cell_place(cell)] = differ
            differ_ref[cell * 16 : cell * 16 + 16, where] = differ
            mean = mean + differ
        mean = mean * (1.0 / CELLS)
        scale_rows = [spread(scale_ref[tap : tap + 1, where]) for tap in range(9)]
        for cell in range(CELLS):
            mixed = padded[cell_place(cell)] + mean
            for tap in range(9):
                mixed = mixed + padded[tap_place(cell, tap)] * scale_rows[tap]
            natural[step, pl.ds(cell, 16, stride=CELLS)] = mixed
        mixed_ref[:, where] = natural[step, 0:HALF].astype(bf16)
        return carry

    lax.fori_loop(0, 4, mixing_step, 0)


def mixing_block(me, squeeze, tokens, next_kernel, scale_kernel, after=()):
    rows = tokens.shape[0]
    return kernel_call(
        mixing_kernel,
        rows // HALF,
        [SCALAR, ANY, ANY, ANY, ANY, half_spec(C), whole_spec((9, R)), whole_spec((9, R))],
        [half_spec(R), half_spec(R), half_spec(R)],
        [jax.ShapeDtypeStruct((rows, R), f32), jax.ShapeDtypeStruct((rows, R), f32),
         jax.ShapeDtypeStruct((rows, R), bf16)],
        [pltpu.VMEM((4, HALF + CELLS + 7, LANES), f32),
         pltpu.VMEM((PADDED * PADDED, 16, LANES), f32),
         pltpu.VMEM((PADDED * PADDED, 16, LANES), f32),
         pltpu.VMEM((32, C // 32, R), bf16), pltpu.SemaphoreType.DMA((32,))],
        2 * rows * C * R,
        after=after,
    )(me, *squeeze, tokens, next_kernel, scale_kernel)


def gate_kernel(
    me_ref, block_a, block_b, block_c, block_d, tokens_ref, mixed_ref,
    logit_ref, gated_ref, pre_ref, sums_ref,
    tile, expand_ref, reduce_ref, expand_semaphores, reduce_semaphores,
):
    blocks = (block_a, block_b, block_c, block_d)
    for_expand = expand_copies(me_ref[0], blocks, expand_ref, expand_semaphores)
    for_reduce = reduce_copies(me_ref[0], blocks, reduce_ref, reduce_semaphores)

    @pl.when(first_step())
    def _():
        start(for_expand)
        start(for_reduce)
        sums_ref[...] = jnp.zeros_like(sums_ref)
        wait(for_expand)
        wait(for_reduce)

    for group in range(GROUPS):
        where, found = group_at(group), tile.at[group % 2]
        columns = [
            expand_ref[top : top + 4].reshape(R, TILE) for top in (8 * group, 8 * group + 4)
        ]
        found[...] = product(mixed_ref[...], jnp.concatenate(columns, axis=1))
        for _, rows in chunks():
            logit = found[rows]
            token = tokens_ref[rows, where].astype(f32)
            logit_ref[rows, where] = logit.astype(bf16)
            gated_ref[rows, where] = (token + token * sigmoid(logit)).astype(bf16)
    found = tile.at[0]
    found[...] = product(gated_ref[...], reduce_ref[...].reshape(C, B))
    first = jnp.zeros((8, B), f32)
    second = jnp.zeros((8, B), f32)
    for _, rows in chunks():
        value = found[rows]
        pre_ref[rows] = value
        first = first + fold(value)
        second = second + fold(value * value)
    add_moments(sums_ref, slice(0, B), first, second)


def gate_block(me, pair, tokens, mixed):
    rows = tokens.shape[0]
    return kernel_call(
        gate_kernel,
        rows // HALF,
        [SCALAR] + [ANY] * 4 + [half_spec(C), half_spec(R)],
        [half_spec(C), half_spec(C), half_spec(B), whole_out((2, B))],
        [jax.ShapeDtypeStruct((rows, C), bf16), jax.ShapeDtypeStruct((rows, C), bf16),
         jax.ShapeDtypeStruct((rows, B), f32), jax.ShapeDtypeStruct((2, B), f32)],
        [pltpu.VMEM((2, HALF, WIDE), f32),
         pltpu.VMEM((32, R // 4, TILE), bf16), pltpu.VMEM((32, C // 32, B), bf16),
         pltpu.SemaphoreType.DMA((2, 32)), pltpu.SemaphoreType.DMA((32,))],
        4 * rows * C * R,
        2 * rows * C,
    )(me, *pair, tokens, mixed)


SPATIAL_ROWS = 9 * 16
RESTORE_ROWS = 64
CLASS_ROWS = 32
LATE_ROWS = RESTORE_ROWS + CLASS_ROWS


def restore_copy(late_ref, target, semaphore):
    return pltpu.make_async_copy(late_ref.at[:, 0:RESTORE_ROWS], target, semaphore)


def second_kernel(count, me_ref, *refs):
    blocks, refs = refs[:8], refs[8:]
    pre_ref, in_sums_ref, affine_ref, hidden_ref, out_ref, copies_ref, *refs = refs
    natural, padded, tile, spatial_ref, sums_ref, semaphores = refs
    copies = block_copies(me_ref[0], blocks, spatial_ref, semaphores)

    @pl.when(first_step())
    def _():
        start(copies)
        sums_ref[...] = jnp.zeros_like(sums_ref)
        clear_border(padded)

    border = SIDE * 16
    hidden_ref[0, 0:border] = jnp.zeros((border, 3 * B), bf16)
    hidden_ref[0, border + HALF :] = jnp.zeros((border, 3 * B), bf16)

    def hidden_step(step, carry):
        where = lanes(step, LANES)
        mean, inverse, gain, shift = (
            spread(row) for row in constants(in_sums_ref[:, where], affine_ref[:, where], count)
        )
        for chunk in range(HALF // 16):
            rows = slice(chunk * 16, chunk * 16 + 16)
            norm = (pre_ref[rows, where] - mean) * inverse * gain + shift
            natural[rows] = norm * sigmoid(norm)
        for cell in range(CELLS):
            padded[cell_place(cell)] = natural[pl.ds(cell, 16, stride=CELLS)].astype(bf16)
        for side in range(3):
            at = lanes(side * 4 + step, LANES)
            for cell in range(CELLS):
                hidden_ref[0, border + cell * 16 : border + cell * 16 + 16, at] = padded[
                    tap_place(cell, 3 + side)
                ]
        return carry

    lax.fori_loop(0, 4, hidden_step, 0)

    @pl.when(first_step())
    def _():
        wait(copies)

    found = None
    for row in range(3):
        taps = [
            spatial_ref[:, tap * 16 : tap * 16 + 16].reshape(B, B)
            for tap in range(3 * row, 3 * row + 3)
        ]
        part = product(
            hidden_ref[0, row * border : row * border + HALF], jnp.concatenate(taps, axis=0)
        )
        found = part if found is None else found + part
    tile[...] = found
    first = jnp.zeros((8, B), f32)
    second = jnp.zeros((8, B), f32)
    for chunk in range(HALF // 16):
        rows = slice(chunk * 16, chunk * 16 + 16)
        value = tile[rows]
        out_ref[rows] = value
        first = first + fold(value)
        second = second + fold(value * value)
    add_moments(sums_ref, slice(0, B), first, second)
    store_copies(copies_ref, sums_ref)


def second_block(me, spatial, pre_one, sums, affine, count):
    rows = pre_one.shape[0]
    devices = lax.axis_size(AXES)
    steps = rows // HALF
    deep = HALF + 2 * SIDE * 16
    return kernel_call(
        functools.partial(second_kernel, count),
        steps,
        [SCALAR] + [ANY] * 8 + [half_spec(B), whole_spec(sums.shape), whole_spec((2, B))],
        [pl.BlockSpec((1, deep, 3 * B), lambda step: (step, 0, 0)), half_spec(B),
         whole_out((devices, 2, B))],
        [jax.ShapeDtypeStruct((steps, deep, 3 * B), bf16), jax.ShapeDtypeStruct((rows, B), f32),
         jax.ShapeDtypeStruct((devices, 2, B), f32)],
        [pltpu.VMEM((HALF, LANES), f32), pltpu.VMEM((PADDED * PADDED, 16, LANES), bf16),
         pltpu.VMEM((HALF, B), f32), pltpu.VMEM((32, SPATIAL_ROWS, B), bf16),
         pltpu.VMEM((2, B), f32),
         pltpu.SemaphoreType.DMA((32,))],
        18 * rows * B * B,
        2 * rows * B,
    )(me, *spatial, pre_one, sums, affine)


def third_kernel(count, pre_ref, in_sums_ref, affine_ref, late_ref,
                 hidden_ref, out_ref, centre_ref, sums_ref, natural, tile, middle, restore_ref,
                 semaphore):
    copy = restore_copy(late_ref, restore_ref, semaphore)

    @pl.when(first_step())
    def _():
        copy.start()
        sums_ref[...] = jnp.zeros_like(sums_ref)

    def hidden_step(step, carry):
        where = lanes(step, LANES)
        mean, inverse, gain, shift = (
            spread(row) for row in constants(in_sums_ref[:, where], affine_ref[:, where], count)
        )
        for cell in range(CELLS):
            rows = slice(cell * 16, cell * 16 + 16)
            norm = (pre_ref[rows, where] - mean) * inverse * gain + shift
            natural[pl.ds(cell, 16, stride=CELLS)] = norm * sigmoid(norm)
        hidden_ref[:, where] = natural[...].astype(bf16)
        middle[:, where] = spread(jnp.mean(natural[...], 0, keepdims=True)).astype(bf16)
        return carry

    lax.fori_loop(0, 4, hidden_step, 0)

    @pl.when(first_step())
    def _():
        copy.wait()

    blocks = restore_ref.reshape(8, 4, RESTORE_ROWS, B)
    for group in range(GROUPS):
        where, found = group_at(group), tile.at[group % 2]
        columns = blocks[:, group].reshape(B, WIDE)
        found[...] = product(hidden_ref[...], columns)
        centre = product(middle[...], columns)
        centre_ref[0, :, where] = centre[0:1]
        first = jnp.zeros((8, WIDE), f32)
        second = jnp.zeros((8, WIDE), f32)
        for _, rows in chunks():
            value = found[rows]
            out_ref[rows, where] = (value - centre).astype(bf16)
            first = first + fold(value)
            second = second + fold(value * value)
        add_moments(sums_ref, where, first, second)


def third_block(pre_two, sums, affine, late, count):
    rows = pre_two.shape[0]
    return kernel_call(
        functools.partial(third_kernel, count),
        rows // HALF,
        [half_spec(B), whole_spec(sums.shape), whole_spec((2, B)), ANY],
        [half_spec(B), half_spec(C), pl.BlockSpec((1, 1, C), lambda step: (step, 0, 0)),
         whole_out((2, C))],
        [jax.ShapeDtypeStruct((rows, B), bf16), jax.ShapeDtypeStruct((rows, C), bf16),
         jax.ShapeDtypeStruct((rows // HALF, 1, C), f32), jax.ShapeDtypeStruct((2, C), f32)],
        [pltpu.VMEM((HALF, LANES), f32), pltpu.VMEM((2, HALF, WIDE), f32),
         pltpu.VMEM((16, B), bf16),
         pltpu.VMEM((32, RESTORE_ROWS, B), bf16), pltpu.SemaphoreType.DMA(())],
        2 * rows * B * C,
        2 * rows * B,
    )(pre_two, sums, affine, late)


def view_rows(chunk):
    return (chunk * 16) // PER_VIEW, (chunk * 16 + 8) // PER_VIEW


def class_copy(late_ref, target, semaphore):
    return pltpu.make_async_copy(late_ref.at[:, RESTORE_ROWS:], target, semaphore)


def order_classes(late, classes):
    for block in range(32):
        for half in range(2):
            top = (2 * block + half) * CLASS_ROWS
            classes[top : top + CLASS_ROWS] = late[block, :, half * TILE : (half + 1) * TILE]


def fourth_kernel(count, pre_ref, centre_ref, gated_ref, in_sums_ref, affine_ref,
                  late_ref, bias_ref, out_ref, slope_ref, views_ref, logits_ref, pooled_ref,
                  classes, late, sums, semaphore):
    copy = class_copy(late_ref, late, semaphore)
    step = pl.program_id(0)

    @pl.when(first_step())
    def _():
        copy.start()
        sums[...] = jnp.zeros_like(sums)

    for part in range(C // TILE):
        where = slice(part * TILE, (part + 1) * TILE)
        mean, inverse, gain, shift = (
            spread(row) for row in constants(in_sums_ref[:, where], affine_ref[:, where], count)
        )
        mean = mean - spread(centre_ref[0, :, where])
        totals = [[jnp.zeros((8, TILE), f32) for _ in range(2)] for _ in range(3)]
        for chunk in range(HALF // 16):
            rows = slice(chunk * 16, chunk * 16 + 16)
            unit = (pre_ref[rows, where].astype(f32) - mean) * inverse
            summed = unit * gain + shift + gated_ref[rows, where].astype(f32)
            sigma = sigmoid(summed)
            output = summed * sigma
            slope = sigma + output * (1.0 - sigma)
            out_ref[rows, where] = output.astype(bf16)
            slope_ref[rows, where] = slope.astype(bf16)
            low, high = view_rows(chunk)
            for kind, value in enumerate((output, slope, slope * unit)):
                if low == high:
                    totals[kind][low] = totals[kind][low] + fold(value)
                else:
                    totals[kind][low] = totals[kind][low] + value[0:8]
                    totals[kind][high] = totals[kind][high] + value[8:16]
        for kind in range(3):
            for view in range(2):
                at = 2 * kind + view
                row = jnp.sum(totals[kind][view], 0, keepdims=True)
                views_ref[0, at : at + 1, where] = row
                if kind == 0:
                    sums[pl.ds(2 * step + view, 1), where] = row
        views_ref[0, 6:8, where] = jnp.zeros((2, TILE), f32)

    @pl.when(step == pl.num_programs(0) - 1)
    def _():
        copy.wait()
        order_classes(late, classes)
        pooled = (sums[...] / PER_VIEW).astype(bf16)
        pooled_ref[...] = pooled
        logits_ref[...] = product(pooled, classes[...]) + bias_ref[...]


def fourth_block(pre_three, centres, gated, sums, affine, late, bias, count):
    rows = pre_three.shape[0]
    steps = rows // HALF
    return kernel_call(
        functools.partial(fourth_kernel, count),
        steps,
        [half_spec(C), pl.BlockSpec((1, 1, C), lambda step: (step, 0, 0)), half_spec(C),
         whole_spec(sums.shape), whole_spec((2, C)), ANY, whole_spec((1, TILE))],
        [half_spec(C), half_spec(C), pl.BlockSpec((1, 8, C), lambda step: (step, 0, 0)),
         whole_out((16, TILE)), whole_out((16, C))],
        [jax.ShapeDtypeStruct((rows, C), bf16), jax.ShapeDtypeStruct((rows, C), bf16),
         jax.ShapeDtypeStruct((steps, 8, C), f32), jax.ShapeDtypeStruct((16, TILE), f32),
         jax.ShapeDtypeStruct((16, C), bf16)],
        [pltpu.VMEM((C, TILE), bf16), pltpu.VMEM((32, CLASS_ROWS, B), bf16),
         pltpu.VMEM((16, C), f32), pltpu.SemaphoreType.DMA(())],
        20 * rows * C,
        2 * rows * C,
    )(pre_three, centres, gated, sums, affine, late, bias)


def video_kernel(view_count, before_ref, own_ref, after_ref, marks_ref, target_ref, views_ref,
                 late_ref, part_ref, pooled_ref, grad_ref, classes, late, semaphore):
    copy = class_copy(late_ref, late, semaphore)
    copy.start()
    marks = marks_ref[...]
    video_logits = jnp.zeros((8, TILE), f32)
    near = (before_ref, own_ref, after_ref)
    for index in range(3 * view_count):
        row = near[index // view_count][index % view_count : index % view_count + 1]
        video_logits = video_logits + marks[:, index : index + 1] * row
    known = lax.broadcasted_iota(jnp.int32, (8, TILE), 1) < CLASSES
    top = jnp.max(jnp.where(known, video_logits, -jnp.inf), 1, keepdims=True)
    weights = jnp.where(known, jnp.exp(jnp.minimum(video_logits - top, 0.0)), 0.0)
    total_weight = jnp.sum(weights, 1, keepdims=True)
    target = target_ref[...]
    entropy = jnp.log(total_weight) + top - jnp.sum(target * video_logits, 1, keepdims=True)
    video_grad = loss_scale * (weights / total_weight - target)
    first = marks[:, 3 * view_count + 1 : 3 * view_count + 2]
    view_grad = (video_grad * marks[:, 3 * view_count : 3 * view_count + 1]).astype(bf16)
    grad_ref[...] = view_grad
    place = lax.broadcasted_iota(jnp.int32, (8, TILE), 1)
    row = jnp.sum(first * jnp.where(place == CLASSES, entropy, video_grad), 0, keepdims=True)
    copy.wait()
    order_classes(late, classes)
    pooled = dot_nt(view_grad, classes[...]) * (1.0 / PER_VIEW)
    parts = [jnp.zeros((1, C), f32), jnp.zeros((1, C), f32)]
    for view in range(view_count):
        half, place = view // 2, view % 2
        pooled_ref[half, place : place + 1] = pooled[view : view + 1]
        for kind in range(2):
            at = 2 * (kind + 1) + place
            parts[kind] = parts[kind] + pooled[view : view + 1] * views_ref[half, at : at + 1]
    part_ref[0:1] = parts[0]
    part_ref[1:2] = parts[1]
    part_ref[2:3] = jnp.zeros((1, C), f32)
    part_ref[2:3, 0:TILE] = row


def video_block(before, own, following, marks, target, views, late, view_count):
    outs = [((3, C), f32), ((view_count // 2, 2, C), f32), ((8, TILE), bf16)]
    operands = (before, own, following, marks, target, views)
    return kernel_call(
        functools.partial(video_kernel, view_count),
        1,
        [whole_spec(operand.shape) for operand in operands] + [ANY],
        [whole_out(shape) for shape, _ in outs],
        [jax.ShapeDtypeStruct(shape, kind) for shape, kind in outs],
        [pltpu.VMEM((C, TILE), bf16), pltpu.VMEM((32, CLASS_ROWS, B), bf16),
         pltpu.SemaphoreType.DMA(())],
        1000000,
    )(*operands, late)


def view_scale(pooled_ref, view, where):
    return spread(pooled_ref[0, view : view + 1, where], 8)


def view_grad_rows(slope, pooled, chunk):
    low, high = view_rows(chunk)
    return slope * jnp.concatenate([pooled[low], pooled[high]], axis=0)


def fifth_kernel(count, slope_ref, pre_three_ref, centre_ref, pooled_ref, sums_three_ref, affine_three_ref,
                 grads_three_ref, late_ref, pre_two_ref, sums_two_ref, affine_two_ref,
                 low_ref, out_ref, copies_ref, natural, restore_ref, sums_ref, semaphore):
    copy = restore_copy(late_ref, restore_ref, semaphore)

    @pl.when(first_step())
    def _():
        copy.start()
        sums_ref[...] = jnp.zeros_like(sums_ref)

    for group in range(GROUPS):
        where = group_at(group)
        mean, inverse, gain, _ = constants(
            sums_three_ref[:, where], affine_three_ref[:, where], count
        )
        scale = spread(gain * inverse)
        offset = spread(grads_three_ref[0:1, where] / count)
        along = spread(grads_three_ref[1:2, where] / count * inverse)
        mean = spread(mean - centre_ref[0, :, where])
        pooled = [view_scale(pooled_ref, view, where) for view in range(2)]
        for chunk, rows in chunks():
            grad = view_grad_rows(slope_ref[rows, where].astype(f32), pooled, chunk)
            centred = pre_three_ref[rows, where].astype(f32) - mean
            low_ref[rows, where] = (scale * (grad - offset - centred * along)).astype(bf16)

    @pl.when(first_step())
    def _():
        copy.wait()

    blocks = restore_ref.reshape(8, 4, RESTORE_ROWS, B)
    grad = None
    for group in range(GROUPS):
        part = dot_nt(low_ref[:, group_at(group)], blocks[:, group].reshape(B, WIDE))
        grad = part if grad is None else grad + part
    for step in range(4):
        natural[step] = grad[:, step * LANES : (step + 1) * LANES]

    def slope_step(step, carry):
        where = lanes(step, LANES)
        mean, inverse, gain, shift = (
            spread(row) for row in constants(sums_two_ref[:, where], affine_two_ref[:, where], count)
        )
        first = jnp.zeros((16, LANES), f32)
        second = jnp.zeros((16, LANES), f32)
        for cell in range(CELLS):
            rows = slice(cell * 16, cell * 16 + 16)
            unit = (pre_two_ref[rows, where] - mean) * inverse
            norm = unit * gain + shift
            sigma = sigmoid(norm)
            grad = natural[step, pl.ds(cell, 16, stride=CELLS)]
            grad = grad * (sigma * (1.0 + norm * (1.0 - sigma)))
            out_ref[rows, where] = grad
            first = first + grad
            second = second + grad * unit
        add_moments(sums_ref, where, first, second)
        return carry

    lax.fori_loop(0, 4, slope_step, 0)
    store_copies(copies_ref, sums_ref)


def fifth_block(slope, pre_three, centres, pooled, sums_three, affine_three, grads_three, late,
                pre_two, sums_two, affine_two, count, after=()):
    rows = slope.shape[0]
    devices = lax.axis_size(AXES)
    return kernel_call(
        functools.partial(fifth_kernel, count),
        rows // HALF,
        [half_spec(C), half_spec(C), pl.BlockSpec((1, 1, C), lambda step: (step, 0, 0)),
         pl.BlockSpec((1, 2, C), lambda step: (step, 0, 0)),
         whole_spec(sums_three.shape), whole_spec((2, C)), whole_spec(grads_three.shape), ANY,
         half_spec(B), whole_spec(sums_two.shape), whole_spec((2, B))],
        [half_spec(C), half_spec(B), whole_out((devices, 2, B))],
        [jax.ShapeDtypeStruct((rows, C), bf16), jax.ShapeDtypeStruct((rows, B), f32),
         jax.ShapeDtypeStruct((devices, 2, B), f32)],
        [pltpu.VMEM((4, HALF, LANES), f32), pltpu.VMEM((32, RESTORE_ROWS, B), bf16),
         pltpu.VMEM((2, B), f32),
         pltpu.SemaphoreType.DMA(())],
        2 * rows * B * C,
        2 * rows * B,
        after=after,
    )(slope, pre_three, centres, pooled, sums_three, affine_three, grads_three, late,
      pre_two, sums_two, affine_two)


def sixth_kernel(count, me_ref, *refs):
    blocks, refs = refs[:8], refs[8:]
    grad_ref, pre_two_ref, sums_two_ref, affine_two_ref, grads_two_ref, *refs = refs
    pre_one_ref, sums_one_ref, affine_one_ref, factors_ref, *refs = refs
    low_ref, out_ref, copies_ref, *refs = refs
    padded, shifted, tile, natural, spatial_ref, sums_ref, semaphores = refs
    border = SIDE * 16
    copies = block_copies(me_ref[0], blocks, spatial_ref, semaphores)

    @pl.when(first_step())
    def _():
        start(copies)
        sums_ref[...] = jnp.zeros_like(sums_ref)
        clear_border(padded)
        shifted[0:border] = jnp.zeros((border, 3 * B), bf16)
        shifted[border + HALF :] = jnp.zeros((border, 3 * B), bf16)

    def low_step(step, carry):
        where = lanes(step, LANES)
        mean, inverse, gain, _ = constants(sums_two_ref[:, where], affine_two_ref[:, where], count)
        scale = spread(gain * inverse)
        offset = spread(grads_two_ref[0:1, where] / count)
        along = spread(grads_two_ref[1:2, where] / count * inverse)
        mean = spread(mean)
        for cell in range(CELLS):
            rows = slice(cell * 16, cell * 16 + 16)
            centred = pre_two_ref[rows, where] - mean
            low = (scale * (grad_ref[rows, where] - offset - centred * along)).astype(bf16)
            low_ref[rows, where] = low
            padded[cell_place(cell)] = low
        for side in range(3):
            at = lanes(side * 4 + step, LANES)
            for cell in range(CELLS):
                shifted[border + cell * 16 : border + cell * 16 + 16, at] = padded[
                    tap_place(cell, 3 + side)
                ]
        return carry

    lax.fori_loop(0, 4, low_step, 0)

    @pl.when(first_step())
    def _():
        wait(copies)

    grad = None
    for tap in range(9):
        top = (tap // 3) * border
        at = (tap % 3) * B
        back = (8 - tap) * 16
        part = dot_nt(
            shifted[top : top + HALF, at : at + B],
            spatial_ref[:, back : back + 16].reshape(B, B),
        )
        grad = part if grad is None else grad + part
    tile[...] = grad
    for group in range(4):
        for cell in range(CELLS):
            natural[group, pl.ds(cell, 16, stride=CELLS)] = tile[
                cell * 16 : cell * 16 + 16, group * LANES : (group + 1) * LANES
            ]

    def slope_step(step, carry):
        where = lanes(step, LANES)
        mean, inverse, gain, shift = (
            spread(row) for row in constants(sums_one_ref[:, where], affine_one_ref[:, where], count)
        )
        first = jnp.zeros((16, LANES), f32)
        second = jnp.zeros((16, LANES), f32)
        for chunk in range(HALF // 16):
            rows = slice(chunk * 16, chunk * 16 + 16)
            unit = (pre_one_ref[rows, where] - mean) * inverse
            norm = unit * gain + shift
            sigma = sigmoid(norm)
            grad = natural[step, rows] * (sigma * (1.0 + norm * (1.0 - sigma)))
            out_ref[rows, where] = grad
            first = first + grad
            second = second + grad * unit
        add_moments(sums_ref, where, first, second)
        return carry

    lax.fori_loop(0, 4, slope_step, 0)
    store_copies(copies_ref, sums_ref, factors_ref)


def sixth_block(me, spatial, grad, pre_two, sums_two, affine_two, grads_two, pre_one, sums_one,
                affine_one, factors, count):
    rows = grad.shape[0]
    devices = lax.axis_size(AXES)
    deep = HALF + 2 * SIDE * 16
    return kernel_call(
        functools.partial(sixth_kernel, count),
        rows // HALF,
        [SCALAR] + [ANY] * 8 + [half_spec(B), half_spec(B), whole_spec(sums_two.shape),
         whole_spec((2, B)), whole_spec(grads_two.shape), half_spec(B), whole_spec(sums_one.shape),
         whole_spec((2, B)), whole_spec(factors.shape)],
        [half_spec(B), half_spec(B), whole_out((devices, 2 + factors.shape[1], B))],
        [jax.ShapeDtypeStruct((rows, B), bf16), jax.ShapeDtypeStruct((rows, B), f32),
         jax.ShapeDtypeStruct((devices, 2 + factors.shape[1], B), f32)],
        [pltpu.VMEM((PADDED * PADDED, 16, LANES), bf16), pltpu.VMEM((deep, 3 * B), bf16),
         pltpu.VMEM((HALF, B), f32), pltpu.VMEM((4, HALF, LANES), f32),
         pltpu.VMEM((32, SPATIAL_ROWS, B), bf16),
         pltpu.VMEM((2, B), f32), pltpu.SemaphoreType.DMA((32,))],
        18 * rows * B * B,
        2 * rows * B,
    )(me, *spatial, grad, pre_two, sums_two, affine_two, grads_two, pre_one, sums_one,
      affine_one, factors)


def low_kernel(count, grad_ref, pre_ref, sums_ref, affine_ref, grads_ref, low_ref):
    def low_step(step, carry):
        where = lanes(step, LANES)
        mean, inverse, gain, _ = constants(sums_ref[:, where], affine_ref[:, where], count)
        scale = spread(gain * inverse)
        offset = spread(grads_ref[0:1, where] / count)
        along = spread(grads_ref[1:2, where] / count * inverse)
        mean = spread(mean)
        for chunk in range(HALF // 16):
            rows = slice(chunk * 16, chunk * 16 + 16)
            centred = pre_ref[rows, where] - mean
            low_ref[rows, where] = (
                scale * (grad_ref[rows, where] - offset - centred * along)
            ).astype(bf16)
        return carry

    lax.fori_loop(0, 4, low_step, 0)


def low_outer_kernel(count, grain, me_ref, grad_ref, pre_ref, sums_ref, affine_ref, grads_ref,
                     wide_ref, low_ref, keep_ref, send_ref, plain, turned):
    @pl.when(first_step())
    def _():
        for half in range(low_ref.shape[0] // HALF):
            rows = pl.ds(half * HALF, HALF)
            low_kernel(
                count, grad_ref.at[rows], pre_ref.at[rows], sums_ref, affine_ref, grads_ref,
                low_ref.at[rows],
            )
        turn(me_ref[0], low_ref[...], grain, plain, turned)

    store_tiles(product(turned[...], wide_ref[...]), keep_ref, send_ref)


def low_outer_block(me, grad, pre, sums, affine, grads, wide_values, count):
    rows, inner = grad.shape
    blocks = wide_values.shape[1] // TILE
    half = pl.BlockSpec((2, inner // 2, TILE), lambda step: (step, 0, 0))
    low, keep, send = kernel_call(
        functools.partial(low_outer_kernel, count, inner // 4),
        blocks // 2,
        [SCALAR, whole_spec(grad.shape), whole_spec(grad.shape), whole_spec(sums.shape),
         whole_spec((2, B)), whole_spec(grads.shape),
         pl.BlockSpec((rows, 2 * TILE), lambda step: (0, step))],
        [whole_out(grad.shape), half, half],
        [jax.ShapeDtypeStruct(grad.shape, bf16),
         jax.ShapeDtypeStruct((blocks, inner // 2, TILE), bf16),
         jax.ShapeDtypeStruct((blocks, inner // 2, TILE), bf16)],
        [pltpu.VMEM((inner, rows), bf16), pltpu.VMEM((inner, rows), bf16)],
        2 * rows * inner * wide_values.shape[1],
    )(me, grad, pre, sums, affine, grads, wide_values)
    return low, (keep, send)


def gate_back_kernel(me_ref, block_a, block_b, block_c, block_d, low_ref,
                     slope_ref, pooled_ref, tokens_ref, logit_ref,
                     logit_grad_ref, part_ref, tile, reduce_ref, semaphores):
    copies = reduce_copies(me_ref[0], (block_a, block_b, block_c, block_d), reduce_ref, semaphores)

    @pl.when(first_step())
    def _():
        start(copies)
        wait(copies)

    for group in range(GROUPS):
        where, found = group_at(group), tile.at[group % 2]
        found[...] = dot_nt(low_ref[...], reduce_ref[8 * group : 8 * group + 8].reshape(WIDE, B))
        pooled = [view_scale(pooled_ref, view, where) for view in range(2)]
        for chunk, rows in chunks():
            slope = slope_ref[rows, where].astype(f32)
            grad = found[rows] + view_grad_rows(slope, pooled, chunk)
            gate = sigmoid(logit_ref[rows, where].astype(f32))
            part = grad * gate
            part_ref[rows, where] = (grad + part).astype(bf16)
            token = tokens_ref[rows, where].astype(f32)
            logit_grad_ref[rows, where] = (part * (1.0 - gate) * token).astype(bf16)


def gate_back_block(me, pair, low_one, slope, pooled, tokens, logit):
    rows = low_one.shape[0]
    return kernel_call(
        gate_back_kernel,
        rows // HALF,
        [SCALAR, ANY, ANY, ANY, ANY, half_spec(B), half_spec(C),
         pl.BlockSpec((1, 2, C), lambda step: (step, 0, 0)), half_spec(C), half_spec(C)],
        [half_spec(C), half_spec(C)],
        [jax.ShapeDtypeStruct((rows, C), bf16), jax.ShapeDtypeStruct((rows, C), bf16)],
        [pltpu.VMEM((2, HALF, WIDE), f32), pltpu.VMEM((32, C // 32, B), bf16),
         pltpu.SemaphoreType.DMA((32,))],
        2 * rows * C * R,
        2 * rows * C,
    )(me, *pair, low_one, slope, pooled, tokens, logit)


def mixing_back_kernel(me_ref, block_a, block_b, block_c, block_d, logit_grad_ref,
                       upcoming_ref, differ_ref, next_ref, scale_ref, squeezed_ref, kernels_ref,
                       natural, later, ahead, padded, expand_ref, semaphores):
    @pl.when(first_step())
    def _():
        copies = expand_copies(
            me_ref[0], (block_a, block_b, block_c, block_d), expand_ref, semaphores
        )
        start(copies)
        kernels_ref[...] = jnp.zeros_like(kernels_ref)
        clear_border(ahead)
        clear_border(padded)
        later[0:CELLS] = jnp.zeros((CELLS, LANES), f32)
        wait(copies)

    grad = None
    for group in range(GROUPS):
        columns = [
            expand_ref[top : top + 4].reshape(R, TILE) for top in (8 * group, 8 * group + 4)
        ]
        part = dot_nt(logit_grad_ref[:, group_at(group)], jnp.concatenate(columns, axis=1))
        grad = part if grad is None else grad + part
    for step in range(4):
        natural[step] = grad[:, step * LANES : (step + 1) * LANES]
    segment = lax.broadcasted_iota(jnp.int32, (16, LANES), 0) % SEG
    not_last = (segment != SEG - 1).astype(f32)

    def mixing_step(step, carry):
        where = lanes(step, LANES)
        scale_rows = [spread(scale_ref[tap : tap + 1, where]) for tap in range(9)]
        mean = jnp.zeros((16, LANES), f32)
        for cell in range(CELLS):
            grad = natural[step, pl.ds(cell, 16, stride=CELLS)]
            padded[cell_place(cell)] = grad
            mean = mean + grad
            ahead[cell_place(cell)] = differ_ref[cell * 16 : cell * 16 + 16, where]
        mean = mean * (1.0 / CELLS)
        sums = [jnp.zeros((16, LANES), f32) for _ in range(9)]
        for cell in range(CELLS):
            grad = padded[cell_place(cell)]
            for tap in range(9):
                sums[tap] = sums[tap] + ahead[tap_place(cell, tap)] * grad
        for tap in range(9):
            kernels_ref[9 + tap : 10 + tap, where] += jnp.sum(sums[tap], 0, keepdims=True)
        for cell in range(CELLS):
            grad = padded[cell_place(cell)] + mean
            for tap in range(9):
                grad = grad + padded[tap_place(cell, tap)] * scale_rows[8 - tap]
            ahead[cell_place(cell)] = grad
        next_rows = [spread(next_ref[tap : tap + 1, where]) for tap in range(9)]
        for cell in range(CELLS):
            padded[cell_place(cell)] = upcoming_ref[cell * 16 : cell * 16 + 16, where]
        sums = [jnp.zeros((16, LANES), f32) for _ in range(9)]
        for cell in range(CELLS):
            grad = ahead[cell_place(cell)]
            for tap in range(9):
                sums[tap] = sums[tap] + padded[tap_place(cell, tap)] * grad
        for tap in range(9):
            kernels_ref[tap : tap + 1, where] += jnp.sum(sums[tap], 0, keepdims=True)
        for cell in range(CELLS):
            back = ahead[tap_place(cell, 0)] * next_rows[8]
            for tap in range(1, 9):
                back = back + ahead[tap_place(cell, tap)] * next_rows[8 - tap]
            later[pl.ds(cell + CELLS, 16, stride=CELLS)] = back * not_last
            natural[step, pl.ds(cell, 16, stride=CELLS)] = -ahead[cell_place(cell)]
        for chunk in range(HALF // 16):
            rows = slice(chunk * 16, chunk * 16 + 16)
            squeezed_ref[rows, where] = (natural[step, rows] + later[rows]).astype(bf16)
        return carry

    lax.fori_loop(0, 4, mixing_step, 0)


def mixing_back_block(me, pair, logit_grad, upcoming, differ, next_kernel, scale_kernel,
                      after=()):
    rows = logit_grad.shape[0]
    return kernel_call(
        mixing_back_kernel,
        rows // HALF,
        [SCALAR, ANY, ANY, ANY, ANY, half_spec(C), half_spec(R), half_spec(R),
         whole_spec((9, R)), whole_spec((9, R))],
        [half_spec(R), whole_out((18, R))],
        [jax.ShapeDtypeStruct((rows, R), bf16), jax.ShapeDtypeStruct((18, R), f32)],
        [pltpu.VMEM((4, HALF, LANES), f32), pltpu.VMEM((HALF + CELLS + 7, LANES), f32),
         pltpu.VMEM((PADDED * PADDED, 16, LANES), f32),
         pltpu.VMEM((PADDED * PADDED, 16, LANES), f32), pltpu.VMEM((32, R // 4, TILE), bf16),
         pltpu.SemaphoreType.DMA((2, 32))],
        2 * rows * C * R,
        after=after,
    )(me, *pair, logit_grad, upcoming, differ, next_kernel, scale_kernel)


def tokens_kernel(me_ref, block_a, block_b, block_c, block_d, part_ref, squeezed_ref, out_ref,
                  squeeze_ref, semaphores):
    @pl.when(first_step())
    def _():
        copies = block_copies(
            me_ref[0], (block_a, block_b, block_c, block_d), squeeze_ref, semaphores, slice(0, 64)
        )
        start(copies)
        wait(copies)

    found = dot_nt(squeezed_ref[...], squeeze_ref[...].reshape(C, R))
    out_ref[...] = (found + part_ref[...].astype(f32)).astype(bf16)


def tokens_block(me, squeeze, part, squeezed_grad):
    rows = part.shape[0]
    return kernel_call(
        tokens_kernel,
        rows // HALF,
        [SCALAR, ANY, ANY, ANY, ANY, half_spec(C), half_spec(R)],
        half_spec(C),
        jax.ShapeDtypeStruct((rows, C), bf16),
        [pltpu.VMEM((32, C // 32, R), bf16), pltpu.SemaphoreType.DMA((32,))],
        2 * rows * C * R,
    )(me, *squeeze, part, squeezed_grad)


def turn(me, values, grain, plain, turned):
    core = me & 1
    plain[...] = values.T
    half = turned.shape[0] // 2
    for group in range(half // grain):
        mine = pl.multiple_of((2 * group + core) * grain, grain)
        other = pl.multiple_of((2 * group + 1 - core) * grain, grain)
        turned[group * grain : (group + 1) * grain] = plain[pl.ds(mine, grain)]
        turned[half + group * grain : half + (group + 1) * grain] = plain[pl.ds(other, grain)]


def store_tiles(found, keep_ref, send_ref):
    half = found.shape[0] // 2
    for tile in range(2):
        at = slice(tile * TILE, (tile + 1) * TILE)
        keep_ref[tile, 0:half] = found[0:half, at].astype(bf16)
        send_ref[tile, 0:half] = found[half:, at].astype(bf16)


def outer_kernel(grain, me_ref, narrow_ref, wide_ref, keep_ref, send_ref, plain, turned):
    @pl.when(first_step())
    def _():
        turn(me_ref[0], narrow_ref[...], grain, plain, turned)

    store_tiles(product(turned[...], wide_ref[...]), keep_ref, send_ref)


def outer_block(me, narrow_values, wide_values, grain):
    rows, inner = narrow_values.shape
    blocks = wide_values.shape[1] // TILE
    half = pl.BlockSpec((2, inner // 2, TILE), lambda step: (step, 0, 0))
    return kernel_call(
        functools.partial(outer_kernel, grain),
        blocks // 2,
        [SCALAR, whole_spec((rows, inner)), pl.BlockSpec((rows, 2 * TILE), lambda step: (0, step))],
        [half, half],
        [jax.ShapeDtypeStruct((blocks, inner // 2, TILE), bf16)] * 2,
        [pltpu.VMEM((inner, rows), bf16), pltpu.VMEM((inner, rows), bf16)],
        2 * rows * inner * wide_values.shape[1],
    )(me, narrow_values, wide_values)


def outer_block_of(grain):
    return functools.partial(outer_block, grain=grain)


FEW_ROWS = 40


SHARED = GROUPS + 9


def store_shared(found, keep_ref, send_ref):
    half = found.shape[0] // 2
    keep_ref[...] = found[:half].astype(bf16).reshape(16, 16, WIDE)
    send_ref[...] = found[half:].astype(bf16).reshape(16, 16, WIDE)


def add_kernel(first_ref, second_ref, out_ref):
    out_ref[...] = (first_ref[...].astype(f32) + second_ref[...].astype(f32)).astype(bf16)


def add_block(first, second):
    part = pl.BlockSpec((first.shape[0] // 4,) + first.shape[1:], lambda step: (step, 0, 0))
    return kernel_call(
        add_kernel,
        4,
        [part, part],
        part,
        jax.ShapeDtypeStruct(first.shape, bf16),
        [],
        first.size,
    )(first, second)


def restore_outer_kernel(me_ref, narrow_ref, wide_ref, keep_ref, send_ref, plain, turned):
    @pl.when(first_step())
    def _():
        turn(me_ref[0], narrow_ref[...], 16, plain, turned)

    store_shared(product(turned[...], wide_ref[...]), keep_ref, send_ref)


def restore_outer_block(me, hidden, low_three):
    rows = hidden.shape[0]
    out = pl.BlockSpec((16, 16, WIDE), lambda step: (0, step, 0))
    return kernel_call(
        restore_outer_kernel,
        GROUPS,
        [SCALAR, whole_spec((rows, B)), pl.BlockSpec((rows, WIDE), lambda step: (0, step))],
        [out, out],
        [jax.ShapeDtypeStruct((16, 16 * SHARED, WIDE), bf16)] * 2,
        [pltpu.VMEM((B, rows), bf16), pltpu.VMEM((B, rows), bf16)],
        2 * rows * B * C,
    )(me, hidden, low_three)


def spatial_kernel(me_ref, kept_ref, sent_ref, hidden_ref, low_ref, keep_ref, send_ref, plain,
                   turned, padded):
    border = SIDE * 16
    halves = hidden_ref.shape[0]

    @pl.when(first_step())
    def _():
        for half in range(halves):
            padded[half, 0 : 2 * border] = jnp.zeros((2 * border, B), bf16)
            padded[half, 2 * border : 2 * border + HALF] = low_ref[half * HALF : (half + 1) * HALF]
            padded[half, 2 * border + HALF :] = jnp.zeros((2 * border, B), bf16)

    step = pl.program_id(0)

    @pl.when(step % 3 == 0)
    def _():
        for half in range(halves):
            turn(me_ref[0], hidden_ref[half], 16, plain, turned.at[half])

    top = pl.multiple_of((2 - step % 3) * border, 16)
    found = None
    for half in range(halves):
        part = product(turned[half], padded[half, pl.ds(top, HALF + 2 * border)])
        found = part if found is None else found + part
    store_shared(found, keep_ref, send_ref)


def spatial_block(me, buffers, hidden, low_two):
    halves, deep, _ = hidden.shape
    out = pl.BlockSpec((16, 16, B), lambda step: (0, GROUPS + (step % 3) * 3 + step // 3, 0))
    return kernel_call(
        spatial_kernel,
        9,
        [SCALAR, ANY, ANY, pl.BlockSpec((halves, deep, B), lambda step: (0, 0, step // 3)),
         whole_spec(low_two.shape)],
        [out, out],
        [jax.ShapeDtypeStruct(buffers[0].shape, bf16)] * 2,
        [pltpu.VMEM((B, deep), bf16), pltpu.VMEM((halves, B, deep), bf16),
         pltpu.VMEM((halves, deep + 2 * SIDE * 16, B), bf16)],
        18 * low_two.shape[0] * B * B,
        aliases={1: 0, 2: 1},
    )(me, *buffers, hidden, low_two)


STEM = 64
STEM_SIDE = 16
CHANNELS = 12
SLABS = 19
STEM_LANES = STEM_SIDE * STEM
INPUT_LANES = CHANNELS * 2 * STEM_SIDE
WINDOW = 7


def frames_kernel(frames_ref, out_ref, rows):
    segments = frames_ref.shape[0]
    side = 2 * STEM_SIDE

    def segment_step(segment, carry):
        pieces = [
            frames_ref[segment, index + 1, colour].astype(f32)
            - frames_ref[segment, index, colour].astype(f32)
            for index in range(4)
            for colour in range(3)
        ]
        for group in range(3):
            rows[group, pl.ds(segment, side, stride=segments)] = jnp.concatenate(
                pieces[4 * group : 4 * group + 4], axis=1
            )
        return carry

    lax.fori_loop(0, segments, segment_step, 0)
    empty = jnp.zeros((segments, INPUT_LANES), bf16)
    for parity in range(2):
        for slab in (0, 1, SLABS - 1):
            out_ref[parity, slab] = empty
    for row in range(side):
        for group in range(3):
            out_ref[row % 2, row // 2 + 2, :, group * LANES : (group + 1) * LANES] = rows[
                group, row * segments : (row + 1) * segments
            ].astype(bf16)


def frames_block(frames):
    segments = frames.shape[0] * frames.shape[1]
    ordered = frames.transpose(0, 1, 2, 5, 3, 4).reshape(
        (segments, frames.shape[2], 3) + frames.shape[3:5]
    )
    shape = (2, SLABS, segments, INPUT_LANES)
    return kernel_call(
        frames_kernel,
        1,
        [whole_spec(ordered.shape)],
        whole_out(shape),
        jax.ShapeDtypeStruct(shape, bf16),
        [pltpu.VMEM((3, 2 * STEM_SIDE * segments, LANES), f32)],
        ordered.size * 100,
    )(ordered)


def stem_rows(input_ref, offset):
    parity = 1 - offset % 2
    top = (offset - 3) // 2 + 2 if parity == 0 else (offset - 4) // 2 + 2
    found = input_ref[parity, top : top + STEM_SIDE]
    return found.reshape(-1, INPUT_LANES)


def band_select(turned=False):
    shape = [STEM_SIDE // 2, CHANNELS, 2 * STEM_SIDE, 2, LANES]
    axes = [0, 1, 2, 3, 4]
    if turned:
        shape, axes = [shape[axis] for axis in (0, 3, 4, 1, 2)], [0, 3, 4, 1, 2]
    pair, channel, place, which, entry = (
        lax.broadcasted_iota(jnp.int32, shape, axis) for axis in axes
    )
    met = (entry % CHANNELS == channel) & (entry < WINDOW * CHANNELS)
    met = met & (place == 2 * (2 * pair + which) + entry // CHANNELS - 3)
    ends = (2 * LANES, INPUT_LANES) if turned else (INPUT_LANES, 2 * LANES)
    return met.astype(bf16).reshape((STEM_SIDE // 2,) + ends)


def pair_weights(stem_weight):
    rows = stem_weight.reshape(WINDOW, WINDOW * CHANNELS, STEM)
    rows = jnp.pad(rows, ((0, 0), (0, LANES - WINDOW * CHANNELS), (0, 0)))
    none = jnp.zeros_like(rows)
    return jnp.concatenate(
        [jnp.concatenate([rows, none], 2), jnp.concatenate([none, rows], 2)], 1
    )


PAIRS = STEM_SIDE // 2


def stem_kernel(input_ref, select_ref, weights_ref, pre_ref, sums_ref, bands):
    selects = select_ref[...].reshape(PAIRS * INPUT_LANES, 2 * LANES)
    for offset in range(WINDOW):
        band = product(selects, weights_ref[offset]).astype(bf16)
        top = offset * INPUT_LANES
        for pair in range(PAIRS):
            bands[top : top + INPUT_LANES, pair * LANES : (pair + 1) * LANES] = band[
                pair * INPUT_LANES : (pair + 1) * INPUT_LANES
            ]
    rows = jnp.concatenate([stem_rows(input_ref, offset) for offset in range(WINDOW)], axis=1)
    for half in range(2):
        where = slice(half * WIDE, (half + 1) * WIDE)
        found = product(rows, bands[:, where])
        pre_ref[:, where] = found
        sums_ref[0:1, where] = jnp.sum(found, 0, keepdims=True)
        sums_ref[1:2, where] = jnp.sum(found * found, 0, keepdims=True)


def stem_block(inputs, select, weights, after=()):
    rows = inputs.shape[2] * STEM_SIDE
    return kernel_call(
        stem_kernel,
        1,
        [whole_spec(inputs.shape), whole_spec(select.shape), whole_spec(weights.shape)],
        [whole_out((rows, STEM_LANES)), whole_out((2, STEM_LANES))],
        [jax.ShapeDtypeStruct((rows, STEM_LANES), f32),
         jax.ShapeDtypeStruct((2, STEM_LANES), f32)],
        [pltpu.VMEM((WINDOW * INPUT_LANES, STEM_LANES), bf16)],
        2 * WINDOW * rows * INPUT_LANES * STEM_LANES,
        after=after,
    )(inputs, select, weights)


def stem_norm_kernel(count, pre_ref, in_sums_ref, affine_ref, cotangent_ref,
                     out_ref, grad_ref, sums_ref):
    def step_body(step, carry):
        where = lanes(step, LANES)
        mean, inverse, gain, shift = (
            spread(row) for row in constants(in_sums_ref[:, where], affine_ref[:, where], count)
        )
        first = jnp.zeros((16, LANES), f32)
        second = jnp.zeros((16, LANES), f32)
        for chunk in range(pre_ref.shape[0] // 16):
            rows = slice(chunk * 16, chunk * 16 + 16)
            unit = (pre_ref[rows, where] - mean) * inverse
            norm = unit * gain + shift
            sigma = sigmoid(norm)
            output = norm * sigma
            out_ref[rows, where] = output.astype(bf16)
            grad = cotangent_ref[rows, where].astype(f32) * (sigma + output * (1.0 - sigma))
            grad_ref[rows, where] = grad
            first = first + grad
            second = second + grad * unit
        sums_ref[0:1, where] = jnp.sum(first, 0, keepdims=True)
        sums_ref[1:2, where] = jnp.sum(second, 0, keepdims=True)
        return carry

    lax.fori_loop(0, STEM_LANES // LANES, step_body, 0)


def stem_norm_block(pre, sums, affine, cotangent, count, after=()):
    shape = pre.shape
    return kernel_call(
        functools.partial(stem_norm_kernel, count),
        1,
        [whole_spec(shape), whole_spec(sums.shape), whole_spec(affine.shape), whole_spec(shape)],
        [whole_out(shape), whole_out(shape), whole_out((2, STEM_LANES))],
        [jax.ShapeDtypeStruct(shape, bf16), jax.ShapeDtypeStruct(shape, f32),
         jax.ShapeDtypeStruct((2, STEM_LANES), f32)],
        [],
        4000 * pre.size,
        after=after,
    )(pre, sums, affine, cotangent)


def stem_back_kernel(count, input_ref, select_ref, pre_ref, in_sums_ref, affine_ref, grad_ref,
                     grads_ref, kernels_ref, out_ref, low):
    def low_step(step, carry):
        where = lanes(step, LANES)
        mean, inverse, gain, _ = constants(in_sums_ref[:, where], affine_ref[:, where], count)
        scale = spread(gain * inverse)
        offset = spread(grads_ref[0:1, where] / count)
        along = spread(grads_ref[1:2, where] / count * inverse)
        mean = spread(mean)
        for chunk in range(pre_ref.shape[0] // 16):
            rows = slice(chunk * 16, chunk * 16 + 16)
            centred = pre_ref[rows, where] - mean
            low[rows, where] = (
                scale * (grad_ref[rows, where] - offset - centred * along)
            ).astype(bf16)
        return carry

    lax.fori_loop(0, STEM_LANES // LANES, low_step, 0)
    selects = jnp.concatenate([select_ref[pair] for pair in range(PAIRS)], axis=1)
    pieces = []
    for offset in range(WINDOW):
        band = product(stem_rows(input_ref, offset).T, low[...]).astype(bf16)
        lined = [band[:, pair * LANES : (pair + 1) * LANES] for pair in range(PAIRS)]
        found = product(selects, jnp.concatenate(lined, axis=0))
        found = found[:LANES, :STEM] + found[LANES:, STEM:]
        pieces.append(found[: WINDOW * CHANNELS])
    pieces.append(jnp.zeros((3 * TILE - WINDOW * WINDOW * CHANNELS, STEM), f32))
    turned = jnp.concatenate(pieces, axis=0).T
    out_ref[...] = jnp.zeros_like(out_ref)
    own = R // 8
    for index in range(8):
        for piece in range(3):
            out_ref[index, piece * 8 : piece * 8 + 8] = turned[
                index * 8 : index * 8 + 8, piece * TILE : (piece + 1) * TILE
            ]
        for kind in range(2):
            out_ref[index, 24:33, kind * LANES : kind * LANES + own] = kernels_ref[
                9 * kind : 9 * kind + 9, index * own : (index + 1) * own
            ]


def stem_back_block(inputs, select, pre, sums, affine, grad, grads, kernel_grads, count):
    shape = pre.shape
    out = (8, FEW_ROWS, TILE)
    return kernel_call(
        functools.partial(stem_back_kernel, count),
        1,
        [whole_spec(inputs.shape), whole_spec(select.shape), whole_spec(shape),
         whole_spec(sums.shape), whole_spec(affine.shape), whole_spec(shape),
         whole_spec(grads.shape), whole_spec(kernel_grads.shape)],
        whole_out(out),
        jax.ShapeDtypeStruct(out, f32),
        [pltpu.VMEM(shape, bf16)],
        2 * WINDOW * shape[0] * INPUT_LANES * STEM_LANES,
    )(inputs, select, pre, sums, affine, grad, grads, kernel_grads)


SMALL_ROWS = 32
FIRST_ROWS = 64 + SMALL_ROWS


def cut_kernel(me_ref, squeeze_ref, expand_ref, reduce_ref, spatial_ref,
               stem_ref, next_ref, scale_ref, outer_ref, gain_one_ref, shift_one_ref,
               gain_two_ref, shift_two_ref, stem_gain_ref, stem_shift_ref,
               first_out, pair_out, spatial_out, small):
    part = me_ref[0] & 3
    first_out[0:64] = squeeze_ref[pl.ds(pl.multiple_of(part * 64, 64), 64)]
    small[...] = jnp.zeros_like(small)
    edge = stem_ref.shape[1] - B
    small[0:8] = stem_ref[:, 0:B].astype(f32)
    small[8:16, 0:edge] = stem_ref[:, B:].astype(f32)
    small[16:25, 0 : next_ref.shape[1]] = next_ref[...].astype(f32)
    small[16:25, LANES : LANES + scale_ref.shape[1]] = scale_ref[...].astype(f32)
    small[25:26] = outer_ref[...].astype(f32)
    for place, ref in enumerate((gain_one_ref, shift_one_ref, gain_two_ref, shift_two_ref)):
        small[26:27, place * LANES : place * LANES + ref.shape[1]] = ref[...].astype(f32)
    small[27:28, 0 : stem_gain_ref.shape[1]] = stem_gain_ref[...].astype(f32)
    small[27:28, LANES : LANES + stem_shift_ref.shape[1]] = stem_shift_ref[...].astype(f32)
    first_out[64:] = small[...].astype(bf16)
    pair_out[0:PAIR_ROWS] = reduce_ref[pl.ds(pl.multiple_of(part * 64, 64), 64)]
    for half in range(2):
        pair_out[PAIR_ROWS:, half * TILE : (half + 1) * TILE] = expand_ref[
            pl.ds(pl.multiple_of(part * 128 + half * 64, 64), 64)
        ]
    for tap in range(9):
        spatial_out[tap * 16 : tap * 16 + 16] = spatial_ref[
            tap, pl.ds(pl.multiple_of(part * 16, 16), 16)
        ]


def late_cut_kernel(me_ref, restore_ref, class_ref, late_out):
    part = me_ref[0] & 3
    late_out[0:RESTORE_ROWS] = restore_ref[:, pl.ds(pl.multiple_of(part * B, B), B)]
    for half in range(2):
        rows = pl.ds(pl.multiple_of(part * 64 + half * 32, 32), 32)
        late_out[RESTORE_ROWS:, half * TILE : (half + 1) * TILE] = class_ref[rows]


def late_cut_block(me, restore, classes):
    return kernel_call(
        late_cut_kernel,
        1,
        [SCALAR, whole_spec(restore.shape), whole_spec(classes.shape)],
        whole_out((LATE_ROWS, B)),
        jax.ShapeDtypeStruct((LATE_ROWS, B), bf16),
        [],
        1000000,
    )(me, restore, classes)


def cut_block(me, *weights):
    shapes = [(FIRST_ROWS, B), (2 * PAIR_ROWS, B), (SPATIAL_ROWS, B)]
    return kernel_call(
        cut_kernel,
        1,
        [SCALAR] + [whole_spec(weight.shape) for weight in weights],
        [whole_out(shape) for shape in shapes],
        [jax.ShapeDtypeStruct(shape, bf16) for shape in shapes],
        [pltpu.VMEM((SMALL_ROWS, B), f32)],
        1000000,
    )(me, *weights)


def unpack_kernel(me_ref, first_ref, squeeze_out, weights_out, next_out, scale_out,
                  one_out, two_out, three_out, stem_out):
    squeeze_out[...] = first_ref[:, 0:64]
    wide = first_ref.shape[0]
    small = []
    for index in range(wide):
        mask = (me_ref[0] >> 2) ^ index
        entry = (mask & 1) * 4 + (mask >> 1)
        small.append(first_ref[entry, 64:].astype(f32))

    def joined(row, at, width, rows=1):
        return jnp.concatenate(
            [values[row : row + rows, at : at + width] for values in small], axis=1
        )

    own = B // wide
    next_out[...] = joined(16, 0, own, 9)
    scale_out[...] = joined(16, LANES, own, 9)
    one_out[0:1] = joined(26, 0, own)
    one_out[1:2] = joined(26, LANES, own)
    two_out[0:1] = joined(26, 2 * LANES, own)
    two_out[1:2] = joined(26, 3 * LANES, own)
    three_out[0:1] = joined(25, 0, TILE)
    three_out[1:2] = joined(25, TILE, TILE)
    for row in range(2):
        stem = joined(27, row * LANES, STEM // wide)
        stem_out[row : row + 1] = jnp.concatenate([stem] * STEM_SIDE, axis=1)
    columns = jnp.concatenate(
        [jnp.concatenate([values[0:8], values[8:16, 0:LANES]], axis=1) for values in small], axis=0
    )
    rows = columns.T
    place = lax.broadcasted_iota(jnp.int32, (LANES, STEM), 0)
    none = jnp.zeros((LANES, STEM), f32)
    for offset in range(WINDOW):
        top = offset * WINDOW * CHANNELS
        block = jnp.where(place < WINDOW * CHANNELS, rows[top : top + LANES], 0.0)
        weights_out[offset, 0:LANES] = jnp.concatenate([block, none], axis=1).astype(bf16)
        weights_out[offset, LANES:] = jnp.concatenate([none, block], axis=1).astype(bf16)


def unpack_block(me, first):
    shapes = [
        ((first.shape[0], 64, B), bf16), ((WINDOW, 2 * LANES, LANES), bf16), ((9, R), f32), ((9, R), f32), ((2, B), f32),
        ((2, B), f32), ((2, C), f32), ((2, STEM_LANES), f32),
    ]
    return kernel_call(
        unpack_kernel,
        1,
        [SCALAR, whole_spec(first.shape)],
        [whole_out(shape) for shape, _ in shapes],
        [jax.ShapeDtypeStruct(shape, kind) for shape, kind in shapes],
        [],
        1000000,
    )(me, first)


def shards(
    frames,
    tokens,
    stem_cotangent,
    crop_counts,
    labels,
    stem_weight,
    stem_gain,
    stem_shift,
    w_squeeze,
    next_kernel,
    scale_kernel,
    w_expand,
    w_reduce,
    gain_one,
    shift_one,
    w_spatial,
    gain_two,
    shift_two,
    w_restore,
    gain_three,
    shift_three,
    w_class,
    class_bias,
):
    view_count = frames.shape[0]
    row_count = tokens.shape[0]
    devices = lax.axis_size(AXES)
    wide = lax.axis_size("wide")
    narrow = lax.axis_size("narrow")
    count = float(row_count * devices)
    segments = view_count * SEG
    stem_rows_here = segments * STEM_SIDE
    stem_count = float(stem_rows_here * STEM_SIDE * devices)
    direct = wide == C // TILE and narrow == 4
    me = lax.axis_index(AXES)
    me_array = (me if direct else 0 * me).astype(jnp.int32).reshape(1)

    stem_width = stem_weight.shape[1]
    inner_width = gain_one.shape[0]
    outer_width = gain_three.shape[0]

    def by_segment(values):
        values = values.reshape(STEM_SIDE, segments, STEM_LANES)
        return values.transpose(1, 0, 2).reshape(-1, STEM)

    def by_output_row(values):
        values = values.reshape(segments, STEM_SIDE, STEM_LANES)
        return values.transpose(1, 0, 2).reshape(stem_rows_here, STEM_LANES)

    if direct:
        first_own, pair_own, spatial_own = cut_block(
            me_array, w_squeeze, w_expand, w_reduce, w_spatial, stem_weight.T, next_kernel,
            scale_kernel, jnp.concatenate([gain_three, shift_three])[None], gain_one[None],
            shift_one[None], gain_two[None], shift_two[None], stem_gain[None], stem_shift[None],
        )
        firsts, pairs, spatials = Gather(first_own), Gather(pair_own), HalvedGather(spatial_own)
        (inputs, select), came, _ = beside(
            lambda images: (frames_block(images), band_select()), [frames], firsts.depth()
        )
        firsts.take_depth(came)
        late_own, came, _ = beside(
            lambda mine, restore, classes: late_cut_block(
                mine, restore, jnp.pad(classes, ((0, 0), (0, TILE - CLASSES)))
            ),
            [me_array, w_restore, w_class], firsts.second() + pairs.depth(),
        )
        firsts.take_second(came[:1])
        pairs.take_depth(came[1:])
        (
            squeeze_own, weights, full_next, full_scale, affine_one, affine_two, affine_three, stem_affine,
        ) = unpack_block(me_array, firsts.eight)
        (stem_pre, stem_part), came, _ = beside(
            stem_block, [inputs, select, weights],
            [(squeeze_own, 2)] + pairs.second() + spatials.depth(),
        )
        squeeze_far = came[0]
        pairs.take_second(came[1:2])
        spatials.take_depth(came[2:])
        (stem_pre, late_own), came, _ = beside(
            lambda *values: values, [stem_pre, late_own], [(squeeze_own, 1), (squeeze_far, 1)]
        )
        late = lax.all_gather(late_own, AXES)
        squeeze = (squeeze_own, squeeze_far) + tuple(came)
    else:
        squeeze, pair, spatial, late = gathered(
            w_squeeze, w_expand, w_reduce, w_spatial, w_restore, w_class
        )

        def whole(values):
            return lax.all_gather(values, "wide", axis=values.ndim - 1, tiled=True).astype(f32)

        weights = pair_weights(whole(stem_weight).astype(bf16))
        full_next, full_scale = whole(next_kernel), whole(scale_kernel)
        affine_one = jnp.stack([whole(gain_one), whole(shift_one)])
        affine_two = jnp.stack([whole(gain_two), whole(shift_two)])
        affine_three = jnp.stack([whole(gain_three), whole(shift_three)])
        stem_affine = jnp.tile(jnp.stack([whole(stem_gain), whole(stem_shift)]), (1, STEM_SIDE))
        inputs, select, cotangent = frames_block(frames), band_select(), by_output_row(stem_cotangent)
        stem_pre, stem_part = stem_block(inputs, select, weights)
    stem_part = stem_part.reshape(2, STEM_SIDE, STEM).sum(1).reshape(1, 2 * STEM)

    def stem_lanes(sums):
        return jnp.tile(sums[2, : 2 * STEM].reshape(2, STEM), (1, STEM_SIDE))

    def with_row(sums, row):
        return jnp.concatenate([sums, jnp.pad(row, ((0, 0), (0, sums.shape[1] - row.shape[1])))])

    mixing_operands = [me_array, squeeze, tokens, full_next, full_scale]
    if direct:
        (upcoming, differ, mixed_low), came, _ = beside(
            mixing_block, mixing_operands, pairs.third() + spatials.second()
        )
        pairs.take_third(came[:1])
        spatials.take_second(came[1:])
        mixed_low, came, _ = beside(lambda values: values, [mixed_low], pairs.core())
        pairs.take_core(came)
        pair = pairs.arrays
    else:
        upcoming, differ, mixed_low = mixing_block(*mixing_operands)
    gate_operands = [me_array, pair, tokens, mixed_low]
    if direct:
        (logit, gated_low, pre_one, one_part), came, _ = beside(
            gate_block, gate_operands, spatials.third_of(0)
        )
        spatials.take_third_of(0, came)
        (one_sums, cotangent), came, _ = beside(
            lambda copies, grads: (swap_total(copies), by_output_row(grads)),
            [to_all(with_row(one_part, stem_part)), stem_cotangent],
            spatials.third_of(1) + spatials.core_of(0),
        )
        spatials.take_third_of(1, came[:1])
        spatials.take_core_of(0, came[1:])
        one_sums, came, _ = beside(lambda values: values, [one_sums], spatials.core_of(1))
        spatials.take_core_of(1, came)
        spatial = spatials.arrays
    else:
        logit, gated_low, pre_one, one_part = gate_block(*gate_operands)
        one_sums = swap_total(to_all(with_row(one_part, stem_part)))
    stem_sums = stem_lanes(one_sums)
    hidden_one, pre_two, two_part = second_block(
        me_array, spatial, pre_one, one_sums, affine_one, count
    )
    stem_out, stem_norm_grad, stem_part = stem_norm_block(
        stem_pre, stem_sums, stem_affine, cotangent, stem_count
    )
    stem_part = stem_part.reshape(2, STEM_SIDE, STEM).sum(1).reshape(1, 2 * STEM)
    two_sums = swap_total(two_part)
    hidden_two, pre_three, centres, three_part = third_block(pre_two, two_sums, affine_two, late, count)
    three_sums, (stem_features, select_turned) = total_beside(
        with_row(three_part, stem_part),
        lambda values: (by_segment(values).T, band_select(True)), [stem_out],
    )
    stem_features = stem_features.T
    stem_grads = stem_lanes(three_sums)
    bias = jnp.pad(class_bias.astype(f32), (0, TILE - CLASSES))[None]
    activations, slope, view_sums, view_logits, pooled_low = fourth_block(
        pre_three, centres, gated_low, three_sums, affine_three, late, bias, count
    )
    pooled_low = pooled_low[:view_count]

    ends = jnp.cumsum(crop_counts)
    starts = ends - crop_counts
    positions = (me - 1) * view_count + jnp.arange(3 * view_count, dtype=jnp.int32)
    video = jnp.sum((ends[None, :] <= positions[:, None]).astype(jnp.int32), 1)
    own_video = video[view_count : 2 * view_count]
    belongs = (
        own_video[:, None] == jnp.arange(crop_counts.shape[0], dtype=jnp.int32)[None, :]
    ).astype(jnp.int32)
    own_count = jnp.sum(belongs * crop_counts[None, :], 1).astype(f32)
    own_label = jnp.sum(belongs * labels[None, :], 1)
    own_start = jnp.sum(belongs * starts[None, :], 1)
    first = (own_start == positions[view_count : 2 * view_count]).astype(f32)
    same = (own_video[:, None] == video[None, :]).astype(f32) / own_count[:, None]
    target = (own_label[:, None] == jnp.arange(TILE, dtype=jnp.int32)[None, :]).astype(f32)
    marks = jnp.concatenate([same, 1.0 / own_count[:, None], first[:, None]], axis=1)
    marks = jnp.pad(marks, ((0, 8 - view_count), (0, LANES - marks.shape[1])))
    target = jnp.pad(target, ((0, 8 - view_count), (0, 0)))

    before = lax.ppermute(view_logits, AXES, [(i, i + 1) for i in range(devices - 1)])
    following = lax.ppermute(view_logits, AXES, [(i + 1, i) for i in range(devices - 1)])
    three_part, pooled_grad, view_grad_low = video_block(
        before, view_logits, following, marks, target, view_sums, late, view_count
    )
    view_grad_low = view_grad_low[:view_count]

    own_parts = pooled_low.reshape(view_count, wide, outer_width).swapaxes(0, 1)
    grad_parts = jnp.broadcast_to(
        view_grad_low, (wide, view_count, TILE)
    )
    factors = jnp.concatenate([own_parts, grad_parts], axis=2)
    factors = jnp.broadcast_to(factors[:, None], (wide, narrow) + factors.shape[1:])
    factors = factors.reshape((devices,) + factors.shape[2:])
    factors = jnp.pad(factors, ((0, 0), (0, 0), (0, B - factors.shape[2])))

    three_grads = total(three_part)
    class_bias_grad = three_grads[2, :CLASSES]
    loss = three_grads[2, CLASSES] / crop_counts.shape[0]

    fifth_operands = [
        slope, pre_three, centres, pooled_grad, three_sums, affine_three, three_grads, late,
        pre_two, two_sums, affine_two,
    ]
    run_fifth = functools.partial(fifth_block, count=count)
    run_sixth = functools.partial(sixth_block, count=count)
    run_stem_back = functools.partial(stem_back_block, count=stem_count)

    def stem_back_operands():
        return [
            inputs, select_turned, stem_pre, stem_sums, stem_affine, stem_norm_grad, stem_grads,
            kernel_grads,
        ]
    run_outer = outer_block_of(R // 4)

    def sixth_operands():
        return [
            me_array, spatial, norm_two_grad, pre_two, two_sums, affine_two, two_grads, pre_one,
            one_sums, affine_one, factors,
        ]

    def low_operands():
        return [me_array, norm_one_grad, pre_one, one_sums, affine_one, one_grads, gated_low]

    def gate_back_operands():
        return [me_array, pair, low_one, slope, pooled_grad, tokens, logit]

    def mixing_back_operands():
        return [me_array, pair, logit_grad, upcoming, differ, full_next, full_scale]

    if direct:
        low_three, norm_two_grad, two_part = run_fifth(*fifth_operands)
        (buffers, two_grads), _, _ = beside(
            lambda mine, hidden, low, part: (
                restore_outer_block(mine, hidden, low), swap_total(part)
            ),
            [me_array, hidden_two, low_three, two_part], [],
        )
        low_two, norm_one_grad, one_part = run_sixth(*sixth_operands())
        ((keep, send), one_grads), _, _ = beside(
            lambda mine, shared, hidden, low, part: (
                spatial_block(mine, shared, hidden, low), swap(part)
            ),
            [me_array, buffers, hidden_one, low_two, one_part], [],
        )
        one_grads, factors = apart(one_grads)
        quarter = (4, 2, 2, R // 4, TILE)
        (low_one, reduce_half), came, _ = beside(
            functools.partial(low_outer_block, count=count), low_operands(), [(send, 1)]
        )
        buffer = add_block(keep, came[0])
        reduced_sum = Sum(reduce_half, quarter, 0)
        (low_one, buffer), came, _ = beside(
            lambda *values: values, [low_one, buffer], reduced_sum.core()
        )
        buffer = lax.psum_scatter(
            buffer.reshape(8, -1, WIDE), "wide", scatter_dimension=0, tiled=False
        )
        reduced_sum.take_core(came)
        (logit_grad, tokens_part), came, _ = beside(
            gate_back_block, gate_back_operands(), reduced_sum.split("x")
        )
        reduced_sum.take(came)
        expand_half, came, _ = beside(
            run_outer, [me_array, mixed_low, logit_grad], reduced_sum.split("y")
        )
        reduced_sum.take(came)
        expand_sum = Sum(expand_half, quarter, 0)
        logit_grad, came, _ = beside(lambda values: values, [logit_grad], expand_sum.core())
        expand_sum.take_core(came)
        (low_squeezed, kernel_grads), came, _ = beside(
            mixing_back_block, mixing_back_operands(),
            expand_sum.split("x"),
        )
        expand_sum.take(came)
        squeeze_half, came, _ = beside(
            run_outer, [me_array, low_squeezed, tokens],
            expand_sum.split("y"),
        )
        expand_sum.take(came)
        both_sum = Sum((None, None), (), 1)
        both_sum.axes = "z"
        both_sum.values = jnp.stack([reduced_sum.values, expand_sum.values])
        shared = Sum((None, None), (), 0)
        shared.axes = "x"
        shared.values = buffer.reshape(2, -1, WIDE)
        squeezed = Sum(squeeze_half, quarter, 0)
        tokens_part, came, _ = beside(lambda values: values, [tokens_part], squeezed.core())
        squeezed.take_core(came)
        stem_back, came, _ = beside(
            run_stem_back, stem_back_operands(),
            squeezed.split("x") + both_sum.split("z") + shared.split("x"),
        )
        squeezed.take(came[:1])
        both_sum.take(came[1:4])
        shared.take(came[4:])
        few = Sum((None, None), (), 0)
        few.axes = "zy"
        few.values = stem_back.reshape(4, 2, FEW_ROWS, TILE)
        tokens_grad, came, _ = beside(
            tokens_block, [me_array, squeeze, tokens_part, low_squeezed],
            squeezed.split("y") + few.split("y") + both_sum.spread(),
        )
        squeezed.take(came[:1])
        few.take(came[1:2])
        both_sum.take_spread(came[2:])
        squeezed.values = jnp.concatenate([squeezed.values, few.values], axis=1)
        _, came, _ = beside(lambda: None, [], squeezed.split("z") + shared.spread())
        squeezed.take(came[:3])
        shared.take_spread(came[3:])
        last = Sum((None, None), (), 0)
        last.values = squeezed.values.astype(bf16)
        _, came, _ = beside(lambda: None, [], last.spread())
        last.take_spread(came)
        squeezed.whole = last.whole[:, : R // 4]
        few = jnp.sum(last.whole[:, R // 4 :], 0)
        buffer = shared.whole
        sum_stem = few[:24].reshape(3, 8, TILE).swapaxes(0, 1).reshape(8, 3 * TILE)
        sum_stem = sum_stem[:, : stem_weight.shape[0]].T
        sum_next = few[24:33, :inner_width]
        sum_scale = few[24:33, LANES : LANES + inner_width]
        buffer = buffer.reshape(4, SHARED, 16, WIDE)
        sum_restore = buffer[:, :GROUPS].swapaxes(1, 2).reshape(w_restore.shape)
        sum_spatial = buffer[:, GROUPS:].swapaxes(0, 1)
        sum_spatial = sum_spatial.reshape(w_spatial.shape)
        sum_reduce = both_sum.whole[:, 0].reshape(B, TILE).T
        sum_expand = both_sum.whole[:, 1].reshape(R, TILE)
        sum_squeeze = squeezed.whole.reshape(R, TILE).T
    else:
        low_three, norm_two_grad, two_part = run_fifth(*fifth_operands)
        buffers = restore_outer_block(me_array, hidden_two, low_three)
        two_grads = swap_total(two_part)
        low_two, norm_one_grad, one_part = run_sixth(*sixth_operands())
        one_grads, factors = apart(swap(one_part))
        buffers = spatial_block(me_array, buffers, hidden_one, low_two)
        low_one, reduce_half = low_outer_block(*low_operands(), count)
        logit_grad, tokens_part = gate_back_block(*gate_back_operands())
        expand_half = run_outer(me_array, mixed_low, logit_grad)
        low_squeezed, kernel_grads = mixing_back_block(*mixing_back_operands())
        few = run_stem_back(*stem_back_operands())
        squeeze_half = run_outer(me_array, low_squeezed, tokens)
        tokens_grad = tokens_block(me_array, squeeze, tokens_part, low_squeezed)
        few = lax.psum(few, AXES)
        sum_stem = few[:, :24].reshape(8, 3, 8, TILE).swapaxes(1, 2).reshape(STEM, 3 * TILE)
        sum_stem = sum_stem[:, : stem_weight.shape[0]].T
        sum_next, sum_scale = (
            few[:, 24:33, at : at + R // 8].swapaxes(0, 1).reshape(9, R) for at in (0, LANES)
        )

        def own_columns(values, width):
            return lax.dynamic_slice_in_dim(values, lax.axis_index("wide") * width, width, 1)

        sum_stem = own_columns(sum_stem, stem_width)
        sum_next = own_columns(sum_next, inner_width)
        sum_scale = own_columns(sum_scale, inner_width)
        sum_restore, sum_spatial, sum_reduce, sum_expand, sum_squeeze = reduced(
            buffers, reduce_half, expand_half, squeeze_half
        )
    factors = factors.reshape(devices * view_count, B)
    sum_class = product_left(
        factors[:, :outer_width], factors[:, outer_width : outer_width + CLASSES]
    )

    def own_slice(values, width):
        return lax.dynamic_slice_in_dim(values, lax.axis_index("wide") * width, width)

    return (
        activations,
        stem_features,
        tokens_grad,
        sum_stem,
        own_slice(stem_grads[1, :STEM], stem_width),
        own_slice(stem_grads[0, :STEM], stem_width),
        sum_squeeze,
        sum_next,
        sum_scale,
        sum_expand,
        sum_reduce,
        own_slice(one_grads[1], inner_width),
        own_slice(one_grads[0], inner_width),
        sum_spatial,
        own_slice(two_grads[1], inner_width),
        own_slice(two_grads[0], inner_width),
        sum_restore,
        own_slice(three_grads[1], outer_width),
        own_slice(three_grads[0], outer_width),
        sum_class,
        class_bias_grad,
        loss,
    )


def solution(mesh):
    in_specs = (
        P(("wide", "narrow"), None, None, None, None, None),
        P(("wide", "narrow"), None),
        P(("wide", "narrow"), None),
        P(),
        P(),
        P(None, "wide"),
        P("wide"),
        P("wide"),
        P("wide", None),
        P(None, "wide"),
        P(None, "wide"),
        P(None, "wide"),
        P("wide", None),
        P("wide"),
        P("wide"),
        P(None, "wide", None),
        P("wide"),
        P("wide"),
        P("wide", None),
        P("wide"),
        P("wide"),
        P("wide", None),
        P(),
    )
    out_specs = (
        P(("wide", "narrow"), None),
        P(("wide", "narrow"), None),
        P(("wide", "narrow"), None),
        P(None, "wide"),
        P("wide"),
        P("wide"),
        P("wide", None),
        P(None, "wide"),
        P(None, "wide"),
        P(None, "wide"),
        P("wide", None),
        P("wide"),
        P("wide"),
        P(None, "wide", None),
        P("wide"),
        P("wide"),
        P("wide", None),
        P("wide"),
        P("wide"),
        P("wide", None),
        P(),
        P(),
    )
    return jax.shard_map(shards, mesh=mesh, in_specs=in_specs, out_specs=out_specs, check_vma=False)
```

```python
import functools

import jax
import jax.numpy as jnp
from jax import lax
from jax.experimental import pallas as pl
from jax.experimental.pallas import tpu as pltpu
from jax.sharding import PartitionSpec as P

C = 2048
B = 512
R = 512
CLASSES = 174
SEG = 8
SIDE = 7
PER_VIEW = SEG * SIDE * SIDE

epsilon = 1e-05
loss_scale = 1024.0

AXES = ("wide", "narrow")
f32 = jnp.float32
bf16 = jnp.bfloat16


def product(first_operand, second_operand):
    return jnp.dot(first_operand, second_operand, preferred_element_type=f32)


def product_left(first_operand, second_operand):
    return lax.dot_general(
        first_operand, second_operand, (((0,), (0,)), ((), ())), preferred_element_type=f32
    )


def product_right(first_operand, second_operand):
    return lax.dot_general(
        first_operand, second_operand, (((1,), (1,)), ((), ())), preferred_element_type=f32
    )


def exchange(values, mask):
    size = lax.axis_size(AXES)
    return lax.ppermute(values, AXES, [(index, index ^ mask) for index in range(size)])


def own_bit(bit):
    return (lax.axis_index(AXES) >> bit) & 1


def total(values):
    bits = lax.axis_size(AXES).bit_length() - 1
    values = values + exchange(values, 1)
    for bit in range(1, bits, 2):
        masks = [1 << bit]
        if bit + 1 < bits:
            masks += [2 << bit, 3 << bit]
        parts = [exchange(values, mask) for mask in masks]
        for part in parts:
            values = values + part
    return values


def total_beside(values, run, inputs):
    bits = lax.axis_size(AXES).bit_length() - 1
    values = values + exchange(values, 1)
    for bit in range(1, bits, 2):
        masks = [1 << bit] + ([2 << bit, 3 << bit] if bit + 1 < bits else [])
        if bit == 3:
            out, parts, _ = beside(run, inputs, [(values, mask) for mask in masks])
        else:
            parts = [exchange(values, mask) for mask in masks]
        for part in parts:
            values = values + part
    return values, out


def swap_total(copies):
    return jnp.sum(lax.all_to_all(copies, AXES, 0, 0, tiled=True), 0)


def swap(parts):
    return lax.all_to_all(parts, AXES, 0, 0, tiled=True)


def apart(came):
    return jnp.sum(came[:, 0:2], 0), came[:, 2:].astype(bf16)


def to_all(values):
    return jnp.broadcast_to(values[None], (lax.axis_size(AXES),) + values.shape)


def beside(run, inputs, sends, more=()):
    inputs, arrays = lax.optimization_barrier((tuple(inputs), [array for array, _ in sends]))
    came = [exchange(array, mask) for array, (_, mask) in zip(arrays, sends)]
    return lax.optimization_barrier((run(*inputs), came, tuple(more)))


def launch(run, inputs, sends):
    inputs, arrays = lax.optimization_barrier((tuple(inputs), [array for array, _ in sends]))
    came = [exchange(array, mask) for array, (_, mask) in zip(arrays, sends)]
    return lax.optimization_barrier(run(*inputs)), came


class Gather:
    def __init__(self, block):
        self.block = block

    def depth(self):
        return [(self.block, mask) for mask in (8, 16, 24)]

    def take_depth(self, came):
        self.four = join([part[None] for part in (self.block, *came)])

    def second(self):
        return [(self.four, 4)]

    def take_second(self, came):
        self.eight = join([self.four, came[0]])

    def third(self):
        return [(self.eight, 2)]

    def take_third(self, came):
        self.other = came[0]

    def core(self):
        return [(self.eight, 1), (self.other, 1)]

    def take_core(self, came):
        self.arrays = (self.eight, self.other) + tuple(came)


class HalvedGather(Gather):
    def take_second(self, came):
        self.parts = [self.four, came[0]]
        self.far = [None, None]
        self.arrays = [None] * 8

    def third_of(self, part):
        return [(self.parts[part], 2)]

    def take_third_of(self, part, came):
        self.far[part] = came[0]

    def core_of(self, part):
        return [(self.parts[part], 1), (self.far[part], 1)]

    def take_core_of(self, part, came):
        self.arrays[part::2] = [self.parts[part], self.far[part], came[0], came[1]]


class Sum:
    def __init__(self, half, shape, lead):
        self.keep, self.send = half
        self.shape, self.lead, self.axes = shape, lead, "zyx"

    def core(self):
        return [(self.send, 1)]

    def take_core(self, came):
        self.values = (self.keep.astype(f32) + came[0].astype(f32)).reshape(self.shape)

    def split(self, letter):
        place = self.lead + self.axes.index(letter)
        self.axes = self.axes.replace(letter, "")
        bit = {"x": 1, "y": 2, "z": 3}[letter]
        span = 3 if letter == "z" else 1
        mine = (lax.axis_index(AXES) >> bit) & span
        found = []
        for mask in range(1, span + 1):
            part = lax.dynamic_index_in_dim(self.values, mine ^ mask, place, keepdims=False)
            found.append((part.astype(bf16), mask << bit))
        self.values = lax.dynamic_index_in_dim(self.values, mine, place, keepdims=False)
        return found

    def split_parts(self, letter, at):
        ((send, mask),) = self.split(letter)
        return [(send[:at], mask)], [(send[at:], mask)]

    def take_parts(self, first, second):
        self.take([jnp.concatenate([first[0], second[0]])])

    def take(self, came):
        for part in came:
            self.values = self.values + part.astype(f32)

    def spread(self):
        self.part = self.values.astype(bf16)
        return [(self.part, mask) for mask in (1, 2, 3)]

    def take_spread(self, came):
        own, (core, over_x, both) = self.part, came
        odd, far = own_bit(0) == 1, own_bit(1) == 1
        near = [jnp.where(odd, core, own), jnp.where(odd, own, core)]
        away = [jnp.where(odd, both, over_x), jnp.where(odd, over_x, both)]
        self.whole = jnp.stack(
            [jnp.where(far, away[0], near[0]), jnp.where(far, away[1], near[1]),
             jnp.where(far, near[0], away[0]), jnp.where(far, near[1], away[1])]
        ).astype(f32)


def gathered(w_squeeze, w_expand, w_reduce, w_spatial, w_restore, w_class):
    def whole(weight, axis):
        return lax.all_gather(weight, "wide", axis=axis, tiled=True)

    def as_blocks(blocks):
        ordered = blocks.reshape((4, 2, 2, 2) + blocks.shape[1:])
        return [
            ordered[:, :, far, core].swapaxes(0, 1).reshape((8,) + blocks.shape[1:])
            for core in range(2)
            for far in range(2)
        ]

    squeeze = whole(w_squeeze, 0).reshape(32, -1, R)
    expand = whole(w_expand, 1).reshape(4, 2, PAIR_ROWS, 8, TILE).transpose(3, 0, 2, 1, 4)
    expand = expand.reshape(32, PAIR_ROWS, 2 * TILE)
    reduce = whole(w_reduce, 0).reshape(32, -1, B)
    spatial = whole(w_spatial, 1).reshape(9, 32, 16, B).swapaxes(0, 1).reshape(32, -1, B)
    restore = whole(w_restore, 0).reshape(8, 64, 4, B).swapaxes(1, 2).reshape(32, 64, B)
    classes = jnp.pad(whole(w_class, 0), ((0, 0), (0, TILE - CLASSES)))
    classes = classes.reshape(32, 2, CLASS_ROWS, TILE).swapaxes(1, 2).reshape(32, CLASS_ROWS, B)
    late = jnp.concatenate([restore, classes], axis=1)
    pair = jnp.concatenate([reduce, expand], axis=1)
    spatial = [part for array in as_blocks(spatial) for part in (array[:4], array[4:])]
    return as_blocks(squeeze), as_blocks(pair), spatial, late


def reduced(buffers, reduce_half, expand_half, squeeze_half):
    def whole(half, grain):
        keep, send = (part.astype(bf16) for part in half)
        shape = keep.shape[:1] + (-1, grain) + keep.shape[2:]
        both = jnp.stack([keep.reshape(shape), send.reshape(shape)], axis=2)
        return both.reshape(keep.shape[:1] + (-1,) + keep.shape[2:])

    def scattered(grad, axis):
        part = lax.psum_scatter(grad, "wide", scatter_dimension=axis, tiled=True)
        return lax.psum(part, "narrow").astype(f32)

    def columns(tiles):
        return tiles.swapaxes(0, 1).reshape(tiles.shape[1], -1)

    shared = jnp.stack([part.reshape(16, SHARED, 16, WIDE) for part in buffers], axis=1)
    shared = shared.transpose(2, 0, 1, 3, 4).reshape(SHARED, B, WIDE)
    restore = shared[:GROUPS].swapaxes(0, 1).reshape(B, C)
    spatial = shared[GROUPS:]
    return (
        scattered(restore, 0),
        scattered(spatial, 1),
        scattered(columns(whole(reduce_half, 128)), 1).T,
        scattered(columns(whole(expand_half, 128)), 1),
        scattered(columns(whole(squeeze_half, 128)), 1).T,
    )


CELLS = SIDE * SIDE
HALF = 2 * PER_VIEW
PADDED = SIDE + 2
STRIDED = HALF + 112
MIB = 1 << 20
VMEM = 60
LANES = 128
TILE = 256


def cell_place(cell):
    return (cell // SIDE + 1) * PADDED + cell % SIDE + 1


def tap_place(cell, tap):
    return cell_place(cell) + (tap // 3 - 1) * PADDED + tap % 3 - 1


def dot_nt(first_operand, second_operand):
    return lax.dot_general(
        first_operand, second_operand, (((1,), (1,)), ((), ())), preferred_element_type=f32
    )


def dot_tn(first_operand, second_operand):
    return lax.dot_general(
        first_operand, second_operand, (((0,), (0,)), ((), ())), preferred_element_type=f32
    )


def sigmoid(values):
    return 0.5 * jnp.tanh(0.5 * values) + 0.5


def constants(sums, affine, count):
    mean = sums[0:1] / count
    inverse = lax.rsqrt(sums[1:2] / count - mean * mean + epsilon)
    return mean, inverse, affine[0:1], affine[1:2]


def spread(row, rows=16):
    return jnp.broadcast_to(row, (rows, row.shape[1]))


def lanes(index, width):
    return pl.ds(pl.multiple_of(index * width, width), width)


def clear_border(ref):
    zero = jnp.zeros(ref.shape[1:], ref.dtype)
    for place in range(PADDED * PADDED):
        if place // PADDED in (0, PADDED - 1) or place % PADDED in (0, PADDED - 1):
            ref[place] = zero


def fold(values):
    return values[0:8] + values[8:16]


def half_spec(width):
    return pl.BlockSpec((HALF, width), lambda step, *_: (step, 0))


def whole_spec(shape):
    return pl.BlockSpec(shape, lambda *_: (0,) * len(shape), pipeline_mode=pl.Buffered(1))


def whole_out(shape):
    return pl.BlockSpec(shape, lambda *_: (0,) * len(shape))


WIDE = 512
GROUPS = C // WIDE


def group_at(group):
    return slice(group * WIDE, (group + 1) * WIDE)


def chunks():
    for chunk in range(HALF // 16):
        yield chunk, slice(chunk * 16, chunk * 16 + 16)


ANY = pl.BlockSpec(memory_space=pl.ANY)
SCALAR = pl.BlockSpec(memory_space=pltpu.SMEM)


def kernel_call(kernel, steps, in_specs, out_specs, out_shapes, scratch, flops,
                transcendentals=0, after=(), vmem=VMEM, aliases=None):
    known = len(in_specs)
    grid = steps if isinstance(steps, tuple) else (steps,)

    def body(*refs):
        kernel(*refs[:known], *refs[known + len(after) :])

    call = pl.pallas_call(
        body,
        grid=grid,
        in_specs=list(in_specs) + [ANY] * len(after),
        out_specs=out_specs,
        out_shape=out_shapes,
        scratch_shapes=scratch,
        input_output_aliases=aliases or {},
        compiler_params=pltpu.CompilerParams(
            dimension_semantics=("arbitrary",) * len(grid), vmem_limit_bytes=vmem * MIB
        ),
        cost_estimate=pl.CostEstimate(
            flops=2 * flops, bytes_accessed=16 * MIB, transcendentals=transcendentals
        ),
    )
    return lambda *operands: call(*operands, *after)


def block_copies(me, sources, target, semaphores, rows=None, lanes_at=None, target_rows=None):
    copies = []
    split = len(sources) // 4
    for which, low_mask in enumerate((0, 2, 1, 3)):
        for entry in range(8):
            mask = low_mask | ((entry // 4) * 4) | ((entry % 4) << 3)
            if split == 1:
                taken = sources[which].at[entry]
            else:
                taken = sources[2 * which + entry // 4].at[entry % 4]
            place = target.at[me ^ mask]
            if rows is not None:
                taken = taken.at[rows] if lanes_at is None else taken.at[rows, lanes_at]
            if target_rows is not None:
                place = place.at[target_rows]
            copies.append(pltpu.make_async_copy(taken, place, semaphores.at[len(copies)]))
    return copies


PAIR_ROWS = 64


def reduce_copies(me, sources, target, semaphores):
    return block_copies(me, sources, target, semaphores, slice(0, PAIR_ROWS))


def expand_copies(me, sources, target, semaphores):
    rows = slice(PAIR_ROWS, 2 * PAIR_ROWS)
    found = []
    for part in range(2):
        found += block_copies(
            me, sources, target, semaphores.at[part], rows,
            slice(part * TILE, (part + 1) * TILE),
            slice(part * PAIR_ROWS, (part + 1) * PAIR_ROWS),
        )
    return found


def start(copies):
    for copy in copies:
        copy.start()


def wait(copies):
    for copy in copies:
        copy.wait()


def join_kernel(*refs):
    *sources, out_ref, semaphores = refs
    copies, top = [], 0
    for source in sources:
        count = source.shape[0]
        copies.append(
            pltpu.make_async_copy(
                source, out_ref.at[top : top + count], semaphores.at[len(copies)]
            )
        )
        top += count
    start(copies)
    wait(copies)


def join(arrays):
    count = sum(array.shape[0] for array in arrays)
    return kernel_call(
        join_kernel,
        1,
        [ANY] * len(arrays),
        ANY,
        jax.ShapeDtypeStruct((count,) + arrays[0].shape[1:], arrays[0].dtype),
        [pltpu.SemaphoreType.DMA((len(arrays),))],
        1000000,
        vmem=16,
    )(*arrays)


def first_step():
    return pl.program_id(0) == 0


def store_copies(copies_ref, sums, others_ref=None):
    @pl.when(pl.program_id(0) == pl.num_programs(0) - 1)
    def _():
        values = sums[...]
        for index in range(copies_ref.shape[0]):
            copies_ref[index, 0 : values.shape[0]] = values
            if others_ref is not None:
                copies_ref[index, values.shape[0] :] = others_ref[index].astype(f32)


def add_moments(sums_ref, where, first, second):
    sums_ref[0:1, where] += jnp.sum(first, 0, keepdims=True)
    sums_ref[1:2, where] += jnp.sum(second, 0, keepdims=True)


def mixing_kernel(
    me_ref, block_a, block_b, block_c, block_d, tokens_ref, next_ref, scale_ref,
    upcoming_ref, differ_ref, mixed_ref, natural, ahead, padded, squeeze_ref, semaphores,
):
    @pl.when(first_step())
    def _():
        copies = block_copies(
            me_ref[0], (block_a, block_b, block_c, block_d), squeeze_ref, semaphores, slice(0, 64)
        )
        start(copies)
        natural[:, HALF:] = jnp.zeros((4, natural.shape[1] - HALF, LANES), f32)
        clear_border(ahead)
        clear_border(padded)
        wait(copies)

    def squeeze_step(step, carry):
        squeezed = product(
            tokens_ref[...], squeeze_ref[:, :, lanes(step, TILE)].reshape(C, TILE)
        )
        natural[2 * step, 0:HALF] = squeezed[:, 0:LANES]
        natural[2 * step + 1, 0:HALF] = squeezed[:, LANES:TILE]
        return carry

    lax.fori_loop(0, 2, squeeze_step, 0)
    segment = lax.broadcasted_iota(jnp.int32, (16, LANES), 0) % SEG
    not_last = (segment != SEG - 1).astype(f32)

    def mixing_step(step, carry):
        where = lanes(step, LANES)
        next_rows = [spread(next_ref[tap : tap + 1, where]) for tap in range(9)]
        for cell in range(CELLS):
            upcoming = natural[step, pl.ds(cell + CELLS, 16, stride=CELLS)] * not_last
            ahead[cell_place(cell)] = upcoming
            upcoming_ref[cell * 16 : cell * 16 + 16, where] = upcoming
        mean = jnp.zeros((16, LANES), f32)
        for cell in range(CELLS):
            differ = -natural[step, pl.ds(cell, 16, stride=CELLS)]
            for tap in range(9):
                differ = differ + ahead[tap_place(cell, tap)] * next_rows[tap]
            padded[cell_place(cell)] = differ
            differ_ref[cell * 16 : cell * 16 + 16, where] = differ
            mean = mean + differ
        mean = mean * (1.0 / CELLS)
        scale_rows = [spread(scale_ref[tap : tap + 1, where]) for tap in range(9)]
        for cell in range(CELLS):
            mixed = padded[cell_place(cell)] + mean
            for tap in range(9):
                mixed = mixed + padded[tap_place(cell, tap)] * scale_rows[tap]
            natural[step, pl.ds(cell, 16, stride=CELLS)] = mixed
        mixed_ref[:, where] = natural[step, 0:HALF].astype(bf16)
        return carry

    lax.fori_loop(0, 4, mixing_step, 0)


def mixing_block(me, squeeze, tokens, next_kernel, scale_kernel, after=()):
    rows = tokens.shape[0]
    return kernel_call(
        mixing_kernel,
        rows // HALF,
        [SCALAR, ANY, ANY, ANY, ANY, half_spec(C), whole_spec((9, R)), whole_spec((9, R))],
        [half_spec(R), half_spec(R), half_spec(R)],
        [jax.ShapeDtypeStruct((rows, R), f32), jax.ShapeDtypeStruct((rows, R), f32),
         jax.ShapeDtypeStruct((rows, R), bf16)],
        [pltpu.VMEM((4, STRIDED, LANES), f32),
         pltpu.VMEM((PADDED * PADDED, 16, LANES), f32),
         pltpu.VMEM((PADDED * PADDED, 16, LANES), f32),
         pltpu.VMEM((32, C // 32, R), bf16), pltpu.SemaphoreType.DMA((32,))],
        2 * rows * C * R,
        after=after,
    )(me, *squeeze, tokens, next_kernel, scale_kernel)


def gate_kernel(
    me_ref, block_a, block_b, block_c, block_d, tokens_ref, mixed_ref,
    logit_ref, gated_ref, pre_ref, sums_ref,
    tile, expand_ref, reduce_ref, expand_semaphores, reduce_semaphores,
):
    blocks = (block_a, block_b, block_c, block_d)
    for_expand = expand_copies(me_ref[0], blocks, expand_ref, expand_semaphores)
    for_reduce = reduce_copies(me_ref[0], blocks, reduce_ref, reduce_semaphores)

    @pl.when(first_step())
    def _():
        start(for_expand)
        start(for_reduce)
        sums_ref[...] = jnp.zeros_like(sums_ref)
        wait(for_expand)
        wait(for_reduce)

    for group in range(GROUPS):
        where, found = group_at(group), tile.at[group % 2]
        columns = [
            expand_ref[top : top + 4].reshape(R, TILE) for top in (8 * group, 8 * group + 4)
        ]
        found[...] = product(mixed_ref[...], jnp.concatenate(columns, axis=1))
        for _, rows in chunks():
            logit = found[rows]
            token = tokens_ref[rows, where].astype(f32)
            logit_ref[rows, where] = logit.astype(bf16)
            gated_ref[rows, where] = (token + token * sigmoid(logit)).astype(bf16)
    found = tile.at[0]
    found[...] = product(gated_ref[...], reduce_ref[...].reshape(C, B))
    first = jnp.zeros((8, B), f32)
    second = jnp.zeros((8, B), f32)
    for _, rows in chunks():
        value = found[rows]
        pre_ref[rows] = value
        first = first + fold(value)
        second = second + fold(value * value)
    add_moments(sums_ref, slice(0, B), first, second)


def gate_block(me, pair, tokens, mixed):
    rows = tokens.shape[0]
    return kernel_call(
        gate_kernel,
        rows // HALF,
        [SCALAR] + [ANY] * 4 + [half_spec(C), half_spec(R)],
        [half_spec(C), half_spec(C), half_spec(B), whole_out((2, B))],
        [jax.ShapeDtypeStruct((rows, C), bf16), jax.ShapeDtypeStruct((rows, C), bf16),
         jax.ShapeDtypeStruct((rows, B), f32), jax.ShapeDtypeStruct((2, B), f32)],
        [pltpu.VMEM((2, HALF, WIDE), f32),
         pltpu.VMEM((32, R // 4, TILE), bf16), pltpu.VMEM((32, C // 32, B), bf16),
         pltpu.SemaphoreType.DMA((2, 32)), pltpu.SemaphoreType.DMA((32,))],
        4 * rows * C * R,
        2 * rows * C,
    )(me, *pair, tokens, mixed)


SPATIAL_ROWS = 9 * 16
RESTORE_ROWS = 64
CLASS_ROWS = 32
LATE_ROWS = RESTORE_ROWS + CLASS_ROWS


def restore_copy(late_ref, target, semaphore):
    return pltpu.make_async_copy(late_ref.at[:, 0:RESTORE_ROWS], target, semaphore)


def second_kernel(count, me_ref, *refs):
    blocks, refs = refs[:8], refs[8:]
    pre_ref, in_sums_ref, affine_ref, hidden_ref, out_ref, copies_ref, *refs = refs
    natural, padded, tile, spatial_ref, sums_ref, semaphores = refs
    copies = block_copies(me_ref[0], blocks, spatial_ref, semaphores)

    @pl.when(first_step())
    def _():
        start(copies)
        sums_ref[...] = jnp.zeros_like(sums_ref)
        clear_border(padded)

    border = SIDE * 16
    hidden_ref[0, 0:border] = jnp.zeros((border, 3 * B), bf16)
    hidden_ref[0, border + HALF :] = jnp.zeros((border, 3 * B), bf16)

    def hidden_step(step, carry):
        where = lanes(step, LANES)
        mean, inverse, gain, shift = (
            spread(row) for row in constants(in_sums_ref[:, where], affine_ref[:, where], count)
        )
        for chunk in range(HALF // 16):
            rows = slice(chunk * 16, chunk * 16 + 16)
            norm = (pre_ref[rows, where] - mean) * inverse * gain + shift
            natural[rows] = norm * sigmoid(norm)
        for cell in range(CELLS):
            padded[cell_place(cell)] = natural[pl.ds(cell, 16, stride=CELLS)].astype(bf16)
        for side in range(3):
            at = lanes(side * 4 + step, LANES)
            for cell in range(CELLS):
                hidden_ref[0, border + cell * 16 : border + cell * 16 + 16, at] = padded[
                    tap_place(cell, 3 + side)
                ]
        return carry

    lax.fori_loop(0, 4, hidden_step, 0)

    @pl.when(first_step())
    def _():
        wait(copies)

    found = None
    for row in range(3):
        taps = [
            spatial_ref[:, tap * 16 : tap * 16 + 16].reshape(B, B)
            for tap in range(3 * row, 3 * row + 3)
        ]
        part = product(
            hidden_ref[0, row * border : row * border + HALF], jnp.concatenate(taps, axis=0)
        )
        found = part if found is None else found + part
    tile[...] = found
    first = jnp.zeros((8, B), f32)
    second = jnp.zeros((8, B), f32)
    for chunk in range(HALF // 16):
        rows = slice(chunk * 16, chunk * 16 + 16)
        value = tile[rows]
        out_ref[rows] = value
        first = first + fold(value)
        second = second + fold(value * value)
    add_moments(sums_ref, slice(0, B), first, second)
    store_copies(copies_ref, sums_ref)


def second_block(me, spatial, pre_one, sums, affine, count):
    rows = pre_one.shape[0]
    devices = lax.axis_size(AXES)
    steps = rows // HALF
    deep = HALF + 2 * SIDE * 16
    return kernel_call(
        functools.partial(second_kernel, count),
        steps,
        [SCALAR] + [ANY] * 8 + [half_spec(B), whole_spec(sums.shape), whole_spec((2, B))],
        [pl.BlockSpec((1, deep, 3 * B), lambda step: (step, 0, 0)), half_spec(B),
         whole_out((devices, 2, B))],
        [jax.ShapeDtypeStruct((steps, deep, 3 * B), bf16), jax.ShapeDtypeStruct((rows, B), f32),
         jax.ShapeDtypeStruct((devices, 2, B), f32)],
        [pltpu.VMEM((STRIDED, LANES), f32), pltpu.VMEM((PADDED * PADDED, 16, LANES), bf16),
         pltpu.VMEM((HALF, B), f32), pltpu.VMEM((32, SPATIAL_ROWS, B), bf16),
         pltpu.VMEM((2, B), f32),
         pltpu.SemaphoreType.DMA((32,))],
        18 * rows * B * B,
        2 * rows * B,
    )(me, *spatial, pre_one, sums, affine)


def third_kernel(count, pre_ref, in_sums_ref, affine_ref, late_ref,
                 hidden_ref, out_ref, centre_ref, sums_ref, natural, tile, middle, restore_ref,
                 semaphore):
    copy = restore_copy(late_ref, restore_ref, semaphore)

    @pl.when(first_step())
    def _():
        copy.start()
        sums_ref[...] = jnp.zeros_like(sums_ref)

    def hidden_step(step, carry):
        where = lanes(step, LANES)
        mean, inverse, gain, shift = (
            spread(row) for row in constants(in_sums_ref[:, where], affine_ref[:, where], count)
        )
        for cell in range(CELLS):
            rows = slice(cell * 16, cell * 16 + 16)
            norm = (pre_ref[rows, where] - mean) * inverse * gain + shift
            natural[pl.ds(cell, 16, stride=CELLS)] = norm * sigmoid(norm)
        hidden_ref[:, where] = natural[0:HALF].astype(bf16)
        middle[:, where] = spread(jnp.mean(natural[0:HALF], 0, keepdims=True)).astype(bf16)
        return carry

    lax.fori_loop(0, 4, hidden_step, 0)

    @pl.when(first_step())
    def _():
        copy.wait()

    blocks = restore_ref.reshape(8, 4, RESTORE_ROWS, B)
    for group in range(GROUPS):
        where, found = group_at(group), tile.at[group % 2]
        columns = blocks[:, group].reshape(B, WIDE)
        found[...] = product(hidden_ref[...], columns)
        centre = product(middle[...], columns)
        centre_ref[0, :, where] = centre[0:1]
        first = jnp.zeros((8, WIDE), f32)
        second = jnp.zeros((8, WIDE), f32)
        for _, rows in chunks():
            value = found[rows]
            out_ref[rows, where] = (value - centre).astype(bf16)
            first = first + fold(value)
            second = second + fold(value * value)
        add_moments(sums_ref, where, first, second)


def third_block(pre_two, sums, affine, late, count):
    rows = pre_two.shape[0]
    return kernel_call(
        functools.partial(third_kernel, count),
        rows // HALF,
        [half_spec(B), whole_spec(sums.shape), whole_spec((2, B)), ANY],
        [half_spec(B), half_spec(C), pl.BlockSpec((1, 1, C), lambda step: (step, 0, 0)),
         whole_out((2, C))],
        [jax.ShapeDtypeStruct((rows, B), bf16), jax.ShapeDtypeStruct((rows, C), bf16),
         jax.ShapeDtypeStruct((rows // HALF, 1, C), f32), jax.ShapeDtypeStruct((2, C), f32)],
        [pltpu.VMEM((STRIDED, LANES), f32), pltpu.VMEM((2, HALF, WIDE), f32),
         pltpu.VMEM((16, B), bf16),
         pltpu.VMEM((32, RESTORE_ROWS, B), bf16), pltpu.SemaphoreType.DMA(())],
        2 * rows * B * C,
        2 * rows * B,
    )(pre_two, sums, affine, late)


def view_rows(chunk):
    return (chunk * 16) // PER_VIEW, (chunk * 16 + 8) // PER_VIEW


def class_copy(late_ref, target, semaphore):
    return pltpu.make_async_copy(late_ref.at[:, RESTORE_ROWS:], target, semaphore)


def order_classes(late, classes):
    for block in range(32):
        for half in range(2):
            top = (2 * block + half) * CLASS_ROWS
            classes[top : top + CLASS_ROWS] = late[block, :, half * TILE : (half + 1) * TILE]


def fourth_kernel(count, pre_ref, centre_ref, gated_ref, in_sums_ref, affine_ref,
                  late_ref, bias_ref, out_ref, slope_ref, views_ref, logits_ref, pooled_ref,
                  classes, late, sums, semaphore):
    copy = class_copy(late_ref, late, semaphore)
    step = pl.program_id(0)

    @pl.when(first_step())
    def _():
        copy.start()
        sums[...] = jnp.zeros_like(sums)

    for part in range(C // TILE):
        where = slice(part * TILE, (part + 1) * TILE)
        mean, inverse, gain, shift = (
            spread(row) for row in constants(in_sums_ref[:, where], affine_ref[:, where], count)
        )
        mean = mean - spread(centre_ref[0, :, where])
        totals = [[jnp.zeros((8, TILE), f32) for _ in range(2)] for _ in range(3)]
        for chunk in range(HALF // 16):
            rows = slice(chunk * 16, chunk * 16 + 16)
            unit = (pre_ref[rows, where].astype(f32) - mean) * inverse
            summed = unit * gain + shift + gated_ref[rows, where].astype(f32)
            sigma = sigmoid(summed)
            output = summed * sigma
            slope = sigma + output * (1.0 - sigma)
            out_ref[rows, where] = output.astype(bf16)
            slope_ref[rows, where] = slope.astype(bf16)
            low, high = view_rows(chunk)
            for kind, value in enumerate((output, slope, slope * unit)):
                if low == high:
                    totals[kind][low] = totals[kind][low] + fold(value)
                else:
                    totals[kind][low] = totals[kind][low] + value[0:8]
                    totals[kind][high] = totals[kind][high] + value[8:16]
        for kind in range(3):
            for view in range(2):
                at = 2 * kind + view
                row = jnp.sum(totals[kind][view], 0, keepdims=True)
                views_ref[0, at : at + 1, where] = row
                if kind == 0:
                    sums[pl.ds(2 * step + view, 1), where] = row
        views_ref[0, 6:8, where] = jnp.zeros((2, TILE), f32)

    @pl.when(step == pl.num_programs(0) - 1)
    def _():
        copy.wait()
        order_classes(late, classes)
        pooled = (sums[...] / PER_VIEW).astype(bf16)
        pooled_ref[...] = pooled
        logits_ref[...] = product(pooled, classes[...]) + bias_ref[...]


def fourth_block(pre_three, centres, gated, sums, affine, late, bias, count):
    rows = pre_three.shape[0]
    steps = rows // HALF
    return kernel_call(
        functools.partial(fourth_kernel, count),
        steps,
        [half_spec(C), pl.BlockSpec((1, 1, C), lambda step: (step, 0, 0)), half_spec(C),
         whole_spec(sums.shape), whole_spec((2, C)), ANY, whole_spec((1, TILE))],
        [half_spec(C), half_spec(C), pl.BlockSpec((1, 8, C), lambda step: (step, 0, 0)),
         whole_out((16, TILE)), whole_out((16, C))],
        [jax.ShapeDtypeStruct((rows, C), bf16), jax.ShapeDtypeStruct((rows, C), bf16),
         jax.ShapeDtypeStruct((steps, 8, C), f32), jax.ShapeDtypeStruct((16, TILE), f32),
         jax.ShapeDtypeStruct((16, C), bf16)],
        [pltpu.VMEM((C, TILE), bf16), pltpu.VMEM((32, CLASS_ROWS, B), bf16),
         pltpu.VMEM((16, C), f32), pltpu.SemaphoreType.DMA(())],
        20 * rows * C,
        2 * rows * C,
    )(pre_three, centres, gated, sums, affine, late, bias)


def video_kernel(view_count, before_ref, own_ref, after_ref, marks_ref, target_ref, views_ref,
                 late_ref, part_ref, pooled_ref, grad_ref, classes, late, semaphore):
    copy = class_copy(late_ref, late, semaphore)
    copy.start()
    marks = marks_ref[...]
    video_logits = jnp.zeros((8, TILE), f32)
    near = (before_ref, own_ref, after_ref)
    for index in range(3 * view_count):
        row = near[index // view_count][index % view_count : index % view_count + 1]
        video_logits = video_logits + marks[:, index : index + 1] * row
    known = lax.broadcasted_iota(jnp.int32, (8, TILE), 1) < CLASSES
    top = jnp.max(jnp.where(known, video_logits, -jnp.inf), 1, keepdims=True)
    weights = jnp.where(known, jnp.exp(jnp.minimum(video_logits - top, 0.0)), 0.0)
    total_weight = jnp.sum(weights, 1, keepdims=True)
    target = target_ref[...]
    entropy = jnp.log(total_weight) + top - jnp.sum(target * video_logits, 1, keepdims=True)
    video_grad = loss_scale * (weights / total_weight - target)
    first = marks[:, 3 * view_count + 1 : 3 * view_count + 2]
    view_grad = (video_grad * marks[:, 3 * view_count : 3 * view_count + 1]).astype(bf16)
    grad_ref[...] = view_grad
    place = lax.broadcasted_iota(jnp.int32, (8, TILE), 1)
    row = jnp.sum(first * jnp.where(place == CLASSES, entropy, video_grad), 0, keepdims=True)
    copy.wait()
    order_classes(late, classes)
    pooled = dot_nt(view_grad, classes[...]) * (1.0 / PER_VIEW)
    parts = [jnp.zeros((1, C), f32), jnp.zeros((1, C), f32)]
    for view in range(view_count):
        half, place = view // 2, view % 2
        pooled_ref[half, place : place + 1] = pooled[view : view + 1]
        for kind in range(2):
            at = 2 * (kind + 1) + place
            parts[kind] = parts[kind] + pooled[view : view + 1] * views_ref[half, at : at + 1]
    part_ref[0:1] = parts[0]
    part_ref[1:2] = parts[1]
    part_ref[2:3] = jnp.zeros((1, C), f32)
    part_ref[2:3, 0:TILE] = row


def video_block(before, own, following, marks, target, views, late, view_count):
    outs = [((3, C), f32), ((view_count // 2, 2, C), f32), ((8, TILE), bf16)]
    operands = (before, own, following, marks, target, views)
    return kernel_call(
        functools.partial(video_kernel, view_count),
        1,
        [whole_spec(operand.shape) for operand in operands] + [ANY],
        [whole_out(shape) for shape, _ in outs],
        [jax.ShapeDtypeStruct(shape, kind) for shape, kind in outs],
        [pltpu.VMEM((C, TILE), bf16), pltpu.VMEM((32, CLASS_ROWS, B), bf16),
         pltpu.SemaphoreType.DMA(())],
        1000000,
    )(*operands, late)


def view_scale(pooled_ref, view, where):
    return spread(pooled_ref[0, view : view + 1, where], 8)


def view_grad_rows(slope, pooled, chunk):
    low, high = view_rows(chunk)
    return slope * jnp.concatenate([pooled[low], pooled[high]], axis=0)


def fifth_kernel(count, slope_ref, pre_three_ref, centre_ref, pooled_ref, sums_three_ref, affine_three_ref,
                 grads_three_ref, late_ref, pre_two_ref, sums_two_ref, affine_two_ref,
                 low_ref, out_ref, copies_ref, natural, restore_ref, sums_ref, semaphore):
    copy = restore_copy(late_ref, restore_ref, semaphore)

    @pl.when(first_step())
    def _():
        copy.start()
        sums_ref[...] = jnp.zeros_like(sums_ref)

    for group in range(GROUPS):
        where = group_at(group)
        mean, inverse, gain, _ = constants(
            sums_three_ref[:, where], affine_three_ref[:, where], count
        )
        scale = spread(gain * inverse)
        offset = spread(grads_three_ref[0:1, where] / count)
        along = spread(grads_three_ref[1:2, where] / count * inverse)
        mean = spread(mean - centre_ref[0, :, where])
        pooled = [view_scale(pooled_ref, view, where) for view in range(2)]
        for chunk, rows in chunks():
            grad = view_grad_rows(slope_ref[rows, where].astype(f32), pooled, chunk)
            centred = pre_three_ref[rows, where].astype(f32) - mean
            low_ref[rows, where] = (scale * (grad - offset - centred * along)).astype(bf16)

    @pl.when(first_step())
    def _():
        copy.wait()

    blocks = restore_ref.reshape(8, 4, RESTORE_ROWS, B)
    grad = None
    for group in range(GROUPS):
        part = dot_nt(low_ref[:, group_at(group)], blocks[:, group].reshape(B, WIDE))
        grad = part if grad is None else grad + part
    for step in range(4):
        natural[step, 0:HALF] = grad[:, step * LANES : (step + 1) * LANES]

    def slope_step(step, carry):
        where = lanes(step, LANES)
        mean, inverse, gain, shift = (
            spread(row) for row in constants(sums_two_ref[:, where], affine_two_ref[:, where], count)
        )
        first = jnp.zeros((16, LANES), f32)
        second = jnp.zeros((16, LANES), f32)
        for cell in range(CELLS):
            rows = slice(cell * 16, cell * 16 + 16)
            unit = (pre_two_ref[rows, where] - mean) * inverse
            norm = unit * gain + shift
            sigma = sigmoid(norm)
            grad = natural[step, pl.ds(cell, 16, stride=CELLS)]
            grad = grad * (sigma * (1.0 + norm * (1.0 - sigma)))
            out_ref[rows, where] = grad
            first = first + grad
            second = second + grad * unit
        add_moments(sums_ref, where, first, second)
        return carry

    lax.fori_loop(0, 4, slope_step, 0)
    store_copies(copies_ref, sums_ref)


def fifth_block(slope, pre_three, centres, pooled, sums_three, affine_three, grads_three, late,
                pre_two, sums_two, affine_two, count, after=()):
    rows = slope.shape[0]
    devices = lax.axis_size(AXES)
    return kernel_call(
        functools.partial(fifth_kernel, count),
        rows // HALF,
        [half_spec(C), half_spec(C), pl.BlockSpec((1, 1, C), lambda step: (step, 0, 0)),
         pl.BlockSpec((1, 2, C), lambda step: (step, 0, 0)),
         whole_spec(sums_three.shape), whole_spec((2, C)), whole_spec(grads_three.shape), ANY,
         half_spec(B), whole_spec(sums_two.shape), whole_spec((2, B))],
        [half_spec(C), half_spec(B), whole_out((devices, 2, B))],
        [jax.ShapeDtypeStruct((rows, C), bf16), jax.ShapeDtypeStruct((rows, B), f32),
         jax.ShapeDtypeStruct((devices, 2, B), f32)],
        [pltpu.VMEM((4, STRIDED, LANES), f32), pltpu.VMEM((32, RESTORE_ROWS, B), bf16),
         pltpu.VMEM((2, B), f32),
         pltpu.SemaphoreType.DMA(())],
        2 * rows * B * C,
        2 * rows * B,
        after=after,
    )(slope, pre_three, centres, pooled, sums_three, affine_three, grads_three, late,
      pre_two, sums_two, affine_two)


def sixth_kernel(count, me_ref, *refs):
    blocks, refs = refs[:8], refs[8:]
    grad_ref, pre_two_ref, sums_two_ref, affine_two_ref, grads_two_ref, *refs = refs
    pre_one_ref, sums_one_ref, affine_one_ref, factors_ref, *refs = refs
    low_ref, out_ref, copies_ref, *refs = refs
    padded, shifted, tile, natural, spatial_ref, sums_ref, semaphores = refs
    border = SIDE * 16
    copies = block_copies(me_ref[0], blocks, spatial_ref, semaphores)

    @pl.when(first_step())
    def _():
        start(copies)
        sums_ref[...] = jnp.zeros_like(sums_ref)
        clear_border(padded)
        shifted[0:border] = jnp.zeros((border, 3 * B), bf16)
        shifted[border + HALF :] = jnp.zeros((border, 3 * B), bf16)

    def low_step(step, carry):
        where = lanes(step, LANES)
        mean, inverse, gain, _ = constants(sums_two_ref[:, where], affine_two_ref[:, where], count)
        scale = spread(gain * inverse)
        offset = spread(grads_two_ref[0:1, where] / count)
        along = spread(grads_two_ref[1:2, where] / count * inverse)
        mean = spread(mean)
        for cell in range(CELLS):
            rows = slice(cell * 16, cell * 16 + 16)
            centred = pre_two_ref[rows, where] - mean
            low = (scale * (grad_ref[rows, where] - offset - centred * along)).astype(bf16)
            low_ref[rows, where] = low
            padded[cell_place(cell)] = low
        for side in range(3):
            at = lanes(side * 4 + step, LANES)
            for cell in range(CELLS):
                shifted[border + cell * 16 : border + cell * 16 + 16, at] = padded[
                    tap_place(cell, 3 + side)
                ]
        return carry

    lax.fori_loop(0, 4, low_step, 0)

    @pl.when(first_step())
    def _():
        wait(copies)

    grad = None
    for tap in range(9):
        top = (tap // 3) * border
        at = (tap % 3) * B
        back = (8 - tap) * 16
        part = dot_nt(
            shifted[top : top + HALF, at : at + B],
            spatial_ref[:, back : back + 16].reshape(B, B),
        )
        grad = part if grad is None else grad + part
    tile[...] = grad
    for group in range(4):
        for cell in range(CELLS):
            natural[group, pl.ds(cell, 16, stride=CELLS)] = tile[
                cell * 16 : cell * 16 + 16, group * LANES : (group + 1) * LANES
            ]

    def slope_step(step, carry):
        where = lanes(step, LANES)
        mean, inverse, gain, shift = (
            spread(row) for row in constants(sums_one_ref[:, where], affine_one_ref[:, where], count)
        )
        first = jnp.zeros((16, LANES), f32)
        second = jnp.zeros((16, LANES), f32)
        for chunk in range(HALF // 16):
            rows = slice(chunk * 16, chunk * 16 + 16)
            unit = (pre_one_ref[rows, where] - mean) * inverse
            norm = unit * gain + shift
            sigma = sigmoid(norm)
            grad = natural[step, rows] * (sigma * (1.0 + norm * (1.0 - sigma)))
            out_ref[rows, where] = grad
            first = first + grad
            second = second + grad * unit
        add_moments(sums_ref, where, first, second)
        return carry

    lax.fori_loop(0, 4, slope_step, 0)
    store_copies(copies_ref, sums_ref, factors_ref)


def sixth_block(me, spatial, grad, pre_two, sums_two, affine_two, grads_two, pre_one, sums_one,
                affine_one, factors, count):
    rows = grad.shape[0]
    devices = lax.axis_size(AXES)
    deep = HALF + 2 * SIDE * 16
    return kernel_call(
        functools.partial(sixth_kernel, count),
        rows // HALF,
        [SCALAR] + [ANY] * 8 + [half_spec(B), half_spec(B), whole_spec(sums_two.shape),
         whole_spec((2, B)), whole_spec(grads_two.shape), half_spec(B), whole_spec(sums_one.shape),
         whole_spec((2, B)), whole_spec(factors.shape)],
        [half_spec(B), half_spec(B), whole_out((devices, 2 + factors.shape[1], B))],
        [jax.ShapeDtypeStruct((rows, B), bf16), jax.ShapeDtypeStruct((rows, B), f32),
         jax.ShapeDtypeStruct((devices, 2 + factors.shape[1], B), f32)],
        [pltpu.VMEM((PADDED * PADDED, 16, LANES), bf16), pltpu.VMEM((deep, 3 * B), bf16),
         pltpu.VMEM((HALF, B), f32), pltpu.VMEM((4, STRIDED, LANES), f32),
         pltpu.VMEM((32, SPATIAL_ROWS, B), bf16),
         pltpu.VMEM((2, B), f32), pltpu.SemaphoreType.DMA((32,))],
        18 * rows * B * B,
        2 * rows * B,
    )(me, *spatial, grad, pre_two, sums_two, affine_two, grads_two, pre_one, sums_one,
      affine_one, factors)


def low_kernel(count, grad_ref, pre_ref, sums_ref, affine_ref, grads_ref, low_ref):
    def low_step(step, carry):
        where = lanes(step, LANES)
        mean, inverse, gain, _ = constants(sums_ref[:, where], affine_ref[:, where], count)
        scale = spread(gain * inverse)
        offset = spread(grads_ref[0:1, where] / count)
        along = spread(grads_ref[1:2, where] / count * inverse)
        mean = spread(mean)
        for chunk in range(HALF // 16):
            rows = slice(chunk * 16, chunk * 16 + 16)
            centred = pre_ref[rows, where] - mean
            low_ref[rows, where] = (
                scale * (grad_ref[rows, where] - offset - centred * along)
            ).astype(bf16)
        return carry

    lax.fori_loop(0, 4, low_step, 0)


def low_outer_kernel(count, grain, me_ref, grad_ref, pre_ref, sums_ref, affine_ref, grads_ref,
                     wide_ref, low_ref, keep_ref, send_ref, plain, turned):
    @pl.when(first_step())
    def _():
        for half in range(low_ref.shape[0] // HALF):
            rows = pl.ds(half * HALF, HALF)
            low_kernel(
                count, grad_ref.at[rows], pre_ref.at[rows], sums_ref, affine_ref, grads_ref,
                low_ref.at[rows],
            )
        turn(me_ref[0], low_ref[...], grain, plain, turned)

    store_tiles(product(turned[...], wide_ref[...]), keep_ref, send_ref)


def low_outer_block(me, grad, pre, sums, affine, grads, wide_values, count):
    rows, inner = grad.shape
    blocks = wide_values.shape[1] // TILE
    half = pl.BlockSpec((2, inner // 2, TILE), lambda step: (step, 0, 0))
    low, keep, send = kernel_call(
        functools.partial(low_outer_kernel, count, inner // 4),
        blocks // 2,
        [SCALAR, whole_spec(grad.shape), whole_spec(grad.shape), whole_spec(sums.shape),
         whole_spec((2, B)), whole_spec(grads.shape),
         pl.BlockSpec((rows, 2 * TILE), lambda step: (0, step))],
        [whole_out(grad.shape), half, half],
        [jax.ShapeDtypeStruct(grad.shape, bf16),
         jax.ShapeDtypeStruct((blocks, inner // 2, TILE), bf16),
         jax.ShapeDtypeStruct((blocks, inner // 2, TILE), bf16)],
        [pltpu.VMEM((inner, rows), bf16), pltpu.VMEM((inner, rows), bf16)],
        2 * rows * inner * wide_values.shape[1],
    )(me, grad, pre, sums, affine, grads, wide_values)
    return low, (keep, send)


def gate_back_kernel(me_ref, block_a, block_b, block_c, block_d, low_ref,
                     slope_ref, pooled_ref, tokens_ref, logit_ref,
                     logit_grad_ref, part_ref, tile, reduce_ref, semaphores):
    copies = reduce_copies(me_ref[0], (block_a, block_b, block_c, block_d), reduce_ref, semaphores)

    @pl.when(first_step())
    def _():
        start(copies)
        wait(copies)

    for group in range(GROUPS):
        where, found = group_at(group), tile.at[group % 2]
        found[...] = dot_nt(low_ref[...], reduce_ref[8 * group : 8 * group + 8].reshape(WIDE, B))
        pooled = [view_scale(pooled_ref, view, where) for view in range(2)]
        for chunk, rows in chunks():
            slope = slope_ref[rows, where].astype(f32)
            grad = found[rows] + view_grad_rows(slope, pooled, chunk)
            gate = sigmoid(logit_ref[rows, where].astype(f32))
            part = grad * gate
            part_ref[rows, where] = (grad + part).astype(bf16)
            token = tokens_ref[rows, where].astype(f32)
            logit_grad_ref[rows, where] = (part * (1.0 - gate) * token).astype(bf16)


def gate_back_block(me, pair, low_one, slope, pooled, tokens, logit):
    rows = low_one.shape[0]
    return kernel_call(
        gate_back_kernel,
        rows // HALF,
        [SCALAR, ANY, ANY, ANY, ANY, half_spec(B), half_spec(C),
         pl.BlockSpec((1, 2, C), lambda step: (step, 0, 0)), half_spec(C), half_spec(C)],
        [half_spec(C), half_spec(C)],
        [jax.ShapeDtypeStruct((rows, C), bf16), jax.ShapeDtypeStruct((rows, C), bf16)],
        [pltpu.VMEM((2, HALF, WIDE), f32), pltpu.VMEM((32, C // 32, B), bf16),
         pltpu.SemaphoreType.DMA((32,))],
        2 * rows * C * R,
        2 * rows * C,
    )(me, *pair, low_one, slope, pooled, tokens, logit)


def mixing_back_kernel(me_ref, block_a, block_b, block_c, block_d, logit_grad_ref,
                       upcoming_ref, differ_ref, next_ref, scale_ref, squeezed_ref, kernels_ref,
                       natural, later, ahead, padded, expand_ref, semaphores):
    @pl.when(first_step())
    def _():
        copies = expand_copies(
            me_ref[0], (block_a, block_b, block_c, block_d), expand_ref, semaphores
        )
        start(copies)
        kernels_ref[...] = jnp.zeros_like(kernels_ref)
        clear_border(ahead)
        clear_border(padded)
        later[0:CELLS] = jnp.zeros((CELLS, LANES), f32)
        wait(copies)

    grad = None
    for group in range(GROUPS):
        columns = [
            expand_ref[top : top + 4].reshape(R, TILE) for top in (8 * group, 8 * group + 4)
        ]
        part = dot_nt(logit_grad_ref[:, group_at(group)], jnp.concatenate(columns, axis=1))
        grad = part if grad is None else grad + part
    for step in range(4):
        natural[step, 0:HALF] = grad[:, step * LANES : (step + 1) * LANES]
    segment = lax.broadcasted_iota(jnp.int32, (16, LANES), 0) % SEG
    not_last = (segment != SEG - 1).astype(f32)

    def mixing_step(step, carry):
        where = lanes(step, LANES)
        scale_rows = [spread(scale_ref[tap : tap + 1, where]) for tap in range(9)]
        mean = jnp.zeros((16, LANES), f32)
        for cell in range(CELLS):
            grad = natural[step, pl.ds(cell, 16, stride=CELLS)]
            padded[cell_place(cell)] = grad
            mean = mean + grad
            ahead[cell_place(cell)] = differ_ref[cell * 16 : cell * 16 + 16, where]
        mean = mean * (1.0 / CELLS)
        sums = [jnp.zeros((16, LANES), f32) for _ in range(9)]
        for cell in range(CELLS):
            grad = padded[cell_place(cell)]
            for tap in range(9):
                sums[tap] = sums[tap] + ahead[tap_place(cell, tap)] * grad
        for tap in range(9):
            kernels_ref[9 + tap : 10 + tap, where] += jnp.sum(sums[tap], 0, keepdims=True)
        for cell in range(CELLS):
            grad = padded[cell_place(cell)] + mean
            for tap in range(9):
                grad = grad + padded[tap_place(cell, tap)] * scale_rows[8 - tap]
            ahead[cell_place(cell)] = grad
        next_rows = [spread(next_ref[tap : tap + 1, where]) for tap in range(9)]
        for cell in range(CELLS):
            padded[cell_place(cell)] = upcoming_ref[cell * 16 : cell * 16 + 16, where]
        sums = [jnp.zeros((16, LANES), f32) for _ in range(9)]
        for cell in range(CELLS):
            grad = ahead[cell_place(cell)]
            for tap in range(9):
                sums[tap] = sums[tap] + padded[tap_place(cell, tap)] * grad
        for tap in range(9):
            kernels_ref[tap : tap + 1, where] += jnp.sum(sums[tap], 0, keepdims=True)
        for cell in range(CELLS):
            back = ahead[tap_place(cell, 0)] * next_rows[8]
            for tap in range(1, 9):
                back = back + ahead[tap_place(cell, tap)] * next_rows[8 - tap]
            later[pl.ds(cell + CELLS, 16, stride=CELLS)] = back * not_last
            natural[step, pl.ds(cell, 16, stride=CELLS)] = -ahead[cell_place(cell)]
        for chunk in range(HALF // 16):
            rows = slice(chunk * 16, chunk * 16 + 16)
            squeezed_ref[rows, where] = (natural[step, rows] + later[rows]).astype(bf16)
        return carry

    lax.fori_loop(0, 4, mixing_step, 0)


def mixing_back_block(me, pair, logit_grad, upcoming, differ, next_kernel, scale_kernel,
                      after=()):
    rows = logit_grad.shape[0]
    return kernel_call(
        mixing_back_kernel,
        rows // HALF,
        [SCALAR, ANY, ANY, ANY, ANY, half_spec(C), half_spec(R), half_spec(R),
         whole_spec((9, R)), whole_spec((9, R))],
        [half_spec(R), whole_out((18, R))],
        [jax.ShapeDtypeStruct((rows, R), bf16), jax.ShapeDtypeStruct((18, R), f32)],
        [pltpu.VMEM((4, STRIDED, LANES), f32), pltpu.VMEM((STRIDED, LANES), f32),
         pltpu.VMEM((PADDED * PADDED, 16, LANES), f32),
         pltpu.VMEM((PADDED * PADDED, 16, LANES), f32), pltpu.VMEM((32, R // 4, TILE), bf16),
         pltpu.SemaphoreType.DMA((2, 32))],
        2 * rows * C * R,
        after=after,
    )(me, *pair, logit_grad, upcoming, differ, next_kernel, scale_kernel)


def tokens_kernel(me_ref, block_a, block_b, block_c, block_d, part_ref, squeezed_ref, out_ref,
                  squeeze_ref, semaphores):
    @pl.when(first_step())
    def _():
        copies = block_copies(
            me_ref[0], (block_a, block_b, block_c, block_d), squeeze_ref, semaphores, slice(0, 64)
        )
        start(copies)
        wait(copies)

    found = dot_nt(squeezed_ref[...], squeeze_ref[...].reshape(C, R))
    out_ref[...] = (found + part_ref[...].astype(f32)).astype(bf16)


def tokens_block(me, squeeze, part, squeezed_grad):
    rows = part.shape[0]
    return kernel_call(
        tokens_kernel,
        rows // HALF,
        [SCALAR, ANY, ANY, ANY, ANY, half_spec(C), half_spec(R)],
        half_spec(C),
        jax.ShapeDtypeStruct((rows, C), bf16),
        [pltpu.VMEM((32, C // 32, R), bf16), pltpu.SemaphoreType.DMA((32,))],
        2 * rows * C * R,
    )(me, *squeeze, part, squeezed_grad)


def turn(me, values, grain, plain, turned):
    core = me & 1
    plain[...] = values.T
    half = turned.shape[0] // 2
    for group in range(half // grain):
        mine = pl.multiple_of((2 * group + core) * grain, grain)
        other = pl.multiple_of((2 * group + 1 - core) * grain, grain)
        turned[group * grain : (group + 1) * grain] = plain[pl.ds(mine, grain)]
        turned[half + group * grain : half + (group + 1) * grain] = plain[pl.ds(other, grain)]


def store_tiles(found, keep_ref, send_ref):
    half = found.shape[0] // 2
    for tile in range(2):
        at = slice(tile * TILE, (tile + 1) * TILE)
        keep_ref[tile, 0:half] = found[0:half, at].astype(bf16)
        send_ref[tile, 0:half] = found[half:, at].astype(bf16)


def outer_kernel(grain, me_ref, narrow_ref, wide_ref, keep_ref, send_ref, plain, turned):
    @pl.when(first_step())
    def _():
        turn(me_ref[0], narrow_ref[...], grain, plain, turned)

    store_tiles(product(turned[...], wide_ref[...]), keep_ref, send_ref)


def outer_block(me, narrow_values, wide_values, grain):
    rows, inner = narrow_values.shape
    blocks = wide_values.shape[1] // TILE
    half = pl.BlockSpec((2, inner // 2, TILE), lambda step: (step, 0, 0))
    return kernel_call(
        functools.partial(outer_kernel, grain),
        blocks // 2,
        [SCALAR, whole_spec((rows, inner)), pl.BlockSpec((rows, 2 * TILE), lambda step: (0, step))],
        [half, half],
        [jax.ShapeDtypeStruct((blocks, inner // 2, TILE), bf16)] * 2,
        [pltpu.VMEM((inner, rows), bf16), pltpu.VMEM((inner, rows), bf16)],
        2 * rows * inner * wide_values.shape[1],
    )(me, narrow_values, wide_values)


def outer_block_of(grain):
    return functools.partial(outer_block, grain=grain)


FEW_ROWS = 40


SHARED = GROUPS + 9


def store_shared(found, keep_ref, send_ref):
    half = found.shape[0] // 2
    keep_ref[...] = found[:half].astype(bf16).reshape(16, 16, WIDE)
    send_ref[...] = found[half:].astype(bf16).reshape(16, 16, WIDE)


def add_kernel(first_ref, second_ref, out_ref):
    out_ref[...] = (first_ref[...].astype(f32) + second_ref[...].astype(f32)).astype(bf16)


def add_block(first, second):
    part = pl.BlockSpec((first.shape[0] // 4,) + first.shape[1:], lambda step: (step, 0, 0))
    return kernel_call(
        add_kernel,
        4,
        [part, part],
        part,
        jax.ShapeDtypeStruct(first.shape, bf16),
        [],
        first.size,
    )(first, second)


def restore_outer_kernel(me_ref, narrow_ref, wide_ref, keep_ref, send_ref, plain, turned):
    @pl.when(first_step())
    def _():
        turn(me_ref[0], narrow_ref[...], 16, plain, turned)

    store_shared(product(turned[...], wide_ref[...]), keep_ref, send_ref)


def restore_outer_block(me, hidden, low_three):
    rows = hidden.shape[0]
    out = pl.BlockSpec((16, 16, WIDE), lambda step: (0, step, 0))
    return kernel_call(
        restore_outer_kernel,
        GROUPS,
        [SCALAR, whole_spec((rows, B)), pl.BlockSpec((rows, WIDE), lambda step: (0, step))],
        [out, out],
        [jax.ShapeDtypeStruct((16, 16 * SHARED, WIDE), bf16)] * 2,
        [pltpu.VMEM((B, rows), bf16), pltpu.VMEM((B, rows), bf16)],
        2 * rows * B * C,
    )(me, hidden, low_three)


def spatial_kernel(me_ref, kept_ref, sent_ref, hidden_ref, low_ref, keep_ref, send_ref, plain,
                   turned, padded):
    border = SIDE * 16
    halves = hidden_ref.shape[0]

    @pl.when(first_step())
    def _():
        for half in range(halves):
            padded[half, 0 : 2 * border] = jnp.zeros((2 * border, B), bf16)
            padded[half, 2 * border : 2 * border + HALF] = low_ref[half * HALF : (half + 1) * HALF]
            padded[half, 2 * border + HALF :] = jnp.zeros((2 * border, B), bf16)

    step = pl.program_id(0)

    @pl.when(step % 3 == 0)
    def _():
        for half in range(halves):
            turn(me_ref[0], hidden_ref[half], 16, plain, turned.at[half])

    top = pl.multiple_of((2 - step % 3) * border, 16)
    found = None
    for half in range(halves):
        part = product(turned[half], padded[half, pl.ds(top, HALF + 2 * border)])
        found = part if found is None else found + part
    store_shared(found, keep_ref, send_ref)


def spatial_block(me, buffers, hidden, low_two):
    halves, deep, _ = hidden.shape
    out = pl.BlockSpec((16, 16, B), lambda step: (0, GROUPS + (step % 3) * 3 + step // 3, 0))
    return kernel_call(
        spatial_kernel,
        9,
        [SCALAR, ANY, ANY, pl.BlockSpec((halves, deep, B), lambda step: (0, 0, step // 3)),
         whole_spec(low_two.shape)],
        [out, out],
        [jax.ShapeDtypeStruct(buffers[0].shape, bf16)] * 2,
        [pltpu.VMEM((B, deep), bf16), pltpu.VMEM((halves, B, deep), bf16),
         pltpu.VMEM((halves, deep + 2 * SIDE * 16, B), bf16)],
        18 * low_two.shape[0] * B * B,
        aliases={1: 0, 2: 1},
    )(me, *buffers, hidden, low_two)


STEM = 64
STEM_SIDE = 16
CHANNELS = 12
SLABS = 19
STEM_LANES = STEM_SIDE * STEM
INPUT_LANES = CHANNELS * 2 * STEM_SIDE
WINDOW = 7


def frames_kernel(frames_ref, out_ref, rows):
    segments = frames_ref.shape[0]
    side = 2 * STEM_SIDE

    def segment_step(segment, carry):
        pieces = [
            frames_ref[segment, index + 1, colour].astype(f32)
            - frames_ref[segment, index, colour].astype(f32)
            for index in range(4)
            for colour in range(3)
        ]
        for group in range(3):
            rows[group, pl.ds(segment, side, stride=segments)] = jnp.concatenate(
                pieces[4 * group : 4 * group + 4], axis=1
            )
        return carry

    lax.fori_loop(0, segments, segment_step, 0)
    empty = jnp.zeros((segments, INPUT_LANES), bf16)
    for parity in range(2):
        for slab in (0, 1, SLABS - 1):
            out_ref[parity, slab] = empty
    for row in range(side):
        for group in range(3):
            out_ref[row % 2, row // 2 + 2, :, group * LANES : (group + 1) * LANES] = rows[
                group, row * segments : (row + 1) * segments
            ].astype(bf16)


def frames_block(frames):
    segments = frames.shape[0] * frames.shape[1]
    ordered = frames.transpose(0, 1, 2, 5, 3, 4).reshape(
        (segments, frames.shape[2], 3) + frames.shape[3:5]
    )
    shape = (2, SLABS, segments, INPUT_LANES)
    return kernel_call(
        frames_kernel,
        1,
        [whole_spec(ordered.shape)],
        whole_out(shape),
        jax.ShapeDtypeStruct(shape, bf16),
        [pltpu.VMEM((3, (2 * STEM_SIDE + 1) * segments, LANES), f32)],
        ordered.size * 100,
    )(ordered)


def stem_rows(input_ref, offset):
    parity = 1 - offset % 2
    top = (offset - 3) // 2 + 2 if parity == 0 else (offset - 4) // 2 + 2
    found = input_ref[parity, top : top + STEM_SIDE]
    return found.reshape(-1, INPUT_LANES)


def band_select(turned=False):
    shape = [STEM_SIDE // 2, CHANNELS, 2 * STEM_SIDE, 2, LANES]
    axes = [0, 1, 2, 3, 4]
    if turned:
        shape, axes = [shape[axis] for axis in (0, 3, 4, 1, 2)], [0, 3, 4, 1, 2]
    pair, channel, place, which, entry = (
        lax.broadcasted_iota(jnp.int32, shape, axis) for axis in axes
    )
    met = (entry % CHANNELS == channel) & (entry < WINDOW * CHANNELS)
    met = met & (place == 2 * (2 * pair + which) + entry // CHANNELS - 3)
    ends = (2 * LANES, INPUT_LANES) if turned else (INPUT_LANES, 2 * LANES)
    return met.astype(bf16).reshape((STEM_SIDE // 2,) + ends)


def pair_weights(stem_weight):
    rows = stem_weight.reshape(WINDOW, WINDOW * CHANNELS, STEM)
    rows = jnp.pad(rows, ((0, 0), (0, LANES - WINDOW * CHANNELS), (0, 0)))
    none = jnp.zeros_like(rows)
    return jnp.concatenate(
        [jnp.concatenate([rows, none], 2), jnp.concatenate([none, rows], 2)], 1
    )


PAIRS = STEM_SIDE // 2


def stem_kernel(input_ref, select_ref, weights_ref, pre_ref, sums_ref, bands):
    selects = select_ref[...].reshape(PAIRS * INPUT_LANES, 2 * LANES)
    for offset in range(WINDOW):
        band = product(selects, weights_ref[offset]).astype(bf16)
        top = offset * INPUT_LANES
        for pair in range(PAIRS):
            bands[top : top + INPUT_LANES, pair * LANES : (pair + 1) * LANES] = band[
                pair * INPUT_LANES : (pair + 1) * INPUT_LANES
            ]
    rows = jnp.concatenate([stem_rows(input_ref, offset) for offset in range(WINDOW)], axis=1)
    for half in range(2):
        where = slice(half * WIDE, (half + 1) * WIDE)
        found = product(rows, bands[:, where])
        pre_ref[:, where] = found
        sums_ref[0:1, where] = jnp.sum(found, 0, keepdims=True)
        sums_ref[1:2, where] = jnp.sum(found * found, 0, keepdims=True)


def stem_block(inputs, select, weights, after=()):
    rows = inputs.shape[2] * STEM_SIDE
    return kernel_call(
        stem_kernel,
        1,
        [whole_spec(inputs.shape), whole_spec(select.shape), whole_spec(weights.shape)],
        [whole_out((rows, STEM_LANES)), whole_out((2, STEM_LANES))],
        [jax.ShapeDtypeStruct((rows, STEM_LANES), f32),
         jax.ShapeDtypeStruct((2, STEM_LANES), f32)],
        [pltpu.VMEM((WINDOW * INPUT_LANES, STEM_LANES), bf16)],
        2 * WINDOW * rows * INPUT_LANES * STEM_LANES,
        after=after,
    )(inputs, select, weights)


def stem_norm_kernel(count, pre_ref, in_sums_ref, affine_ref, cotangent_ref,
                     out_ref, grad_ref, sums_ref):
    def step_body(step, carry):
        where = lanes(step, LANES)
        mean, inverse, gain, shift = (
            spread(row) for row in constants(in_sums_ref[:, where], affine_ref[:, where], count)
        )
        first = jnp.zeros((16, LANES), f32)
        second = jnp.zeros((16, LANES), f32)
        for chunk in range(pre_ref.shape[0] // 16):
            rows = slice(chunk * 16, chunk * 16 + 16)
            unit = (pre_ref[rows, where] - mean) * inverse
            norm = unit * gain + shift
            sigma = sigmoid(norm)
            output = norm * sigma
            out_ref[rows, where] = output.astype(bf16)
            grad = cotangent_ref[rows, where].astype(f32) * (sigma + output * (1.0 - sigma))
            grad_ref[rows, where] = grad
            first = first + grad
            second = second + grad * unit
        sums_ref[0:1, where] = jnp.sum(first, 0, keepdims=True)
        sums_ref[1:2, where] = jnp.sum(second, 0, keepdims=True)
        return carry

    lax.fori_loop(0, STEM_LANES // LANES, step_body, 0)


def stem_norm_block(pre, sums, affine, cotangent, count, after=()):
    shape = pre.shape
    return kernel_call(
        functools.partial(stem_norm_kernel, count),
        1,
        [whole_spec(shape), whole_spec(sums.shape), whole_spec(affine.shape), whole_spec(shape)],
        [whole_out(shape), whole_out(shape), whole_out((2, STEM_LANES))],
        [jax.ShapeDtypeStruct(shape, bf16), jax.ShapeDtypeStruct(shape, f32),
         jax.ShapeDtypeStruct((2, STEM_LANES), f32)],
        [],
        4000 * pre.size,
        after=after,
    )(pre, sums, affine, cotangent)


def stem_back_kernel(count, input_ref, select_ref, pre_ref, in_sums_ref, affine_ref, grad_ref,
                     grads_ref, kernels_ref, out_ref, low):
    def low_step(step, carry):
        where = lanes(step, LANES)
        mean, inverse, gain, _ = constants(in_sums_ref[:, where], affine_ref[:, where], count)
        scale = spread(gain * inverse)
        offset = spread(grads_ref[0:1, where] / count)
        along = spread(grads_ref[1:2, where] / count * inverse)
        mean = spread(mean)
        for chunk in range(pre_ref.shape[0] // 16):
            rows = slice(chunk * 16, chunk * 16 + 16)
            centred = pre_ref[rows, where] - mean
            low[rows, where] = (
                scale * (grad_ref[rows, where] - offset - centred * along)
            ).astype(bf16)
        return carry

    lax.fori_loop(0, STEM_LANES // LANES, low_step, 0)
    selects = jnp.concatenate([select_ref[pair] for pair in range(PAIRS)], axis=1)
    pieces = []
    for offset in range(WINDOW):
        band = product(stem_rows(input_ref, offset).T, low[...]).astype(bf16)
        lined = [band[:, pair * LANES : (pair + 1) * LANES] for pair in range(PAIRS)]
        found = product(selects, jnp.concatenate(lined, axis=0))
        found = found[:LANES, :STEM] + found[LANES:, STEM:]
        pieces.append(found[: WINDOW * CHANNELS])
    pieces.append(jnp.zeros((3 * TILE - WINDOW * WINDOW * CHANNELS, STEM), f32))
    turned = jnp.concatenate(pieces, axis=0).T
    out_ref[...] = jnp.zeros_like(out_ref)
    own = R // 8
    for index in range(8):
        for piece in range(3):
            out_ref[index, piece * 8 : piece * 8 + 8] = turned[
                index * 8 : index * 8 + 8, piece * TILE : (piece + 1) * TILE
            ]
        for kind in range(2):
            out_ref[index, 24:33, kind * LANES : kind * LANES + own] = kernels_ref[
                9 * kind : 9 * kind + 9, index * own : (index + 1) * own
            ]


def stem_back_block(inputs, select, pre, sums, affine, grad, grads, kernel_grads, count):
    shape = pre.shape
    out = (8, FEW_ROWS, TILE)
    return kernel_call(
        functools.partial(stem_back_kernel, count),
        1,
        [whole_spec(inputs.shape), whole_spec(select.shape), whole_spec(shape),
         whole_spec(sums.shape), whole_spec(affine.shape), whole_spec(shape),
         whole_spec(grads.shape), whole_spec(kernel_grads.shape)],
        whole_out(out),
        jax.ShapeDtypeStruct(out, f32),
        [pltpu.VMEM(shape, bf16)],
        2 * WINDOW * shape[0] * INPUT_LANES * STEM_LANES,
    )(inputs, select, pre, sums, affine, grad, grads, kernel_grads)


SMALL_ROWS = 32
FIRST_ROWS = 64 + SMALL_ROWS


def cut_kernel(me_ref, squeeze_ref, expand_ref, reduce_ref, spatial_ref,
               stem_ref, next_ref, scale_ref, outer_ref, gain_one_ref, shift_one_ref,
               gain_two_ref, shift_two_ref, stem_gain_ref, stem_shift_ref,
               first_out, pair_out, spatial_out, small):
    part = me_ref[0] & 3
    first_out[0:64] = squeeze_ref[pl.ds(pl.multiple_of(part * 64, 64), 64)]
    small[...] = jnp.zeros_like(small)
    edge = stem_ref.shape[1] - B
    small[0:8] = stem_ref[:, 0:B].astype(f32)
    small[8:16, 0:edge] = stem_ref[:, B:].astype(f32)
    small[16:25, 0 : next_ref.shape[1]] = next_ref[...].astype(f32)
    small[16:25, LANES : LANES + scale_ref.shape[1]] = scale_ref[...].astype(f32)
    small[25:26] = outer_ref[...].astype(f32)
    for place, ref in enumerate((gain_one_ref, shift_one_ref, gain_two_ref, shift_two_ref)):
        small[26:27, place * LANES : place * LANES + ref.shape[1]] = ref[...].astype(f32)
    small[27:28, 0 : stem_gain_ref.shape[1]] = stem_gain_ref[...].astype(f32)
    small[27:28, LANES : LANES + stem_shift_ref.shape[1]] = stem_shift_ref[...].astype(f32)
    first_out[64:] = small[...].astype(bf16)
    pair_out[0:PAIR_ROWS] = reduce_ref[pl.ds(pl.multiple_of(part * 64, 64), 64)]
    for half in range(2):
        pair_out[PAIR_ROWS:, half * TILE : (half + 1) * TILE] = expand_ref[
            pl.ds(pl.multiple_of(part * 128 + half * 64, 64), 64)
        ]
    for tap in range(9):
        spatial_out[tap * 16 : tap * 16 + 16] = spatial_ref[
            tap, pl.ds(pl.multiple_of(part * 16, 16), 16)
        ]


def late_cut_kernel(me_ref, restore_ref, class_ref, late_out):
    part = me_ref[0] & 3
    late_out[0:RESTORE_ROWS] = restore_ref[:, pl.ds(pl.multiple_of(part * B, B), B)]
    for half in range(2):
        rows = pl.ds(pl.multiple_of(part * 64 + half * 32, 32), 32)
        late_out[RESTORE_ROWS:, half * TILE : (half + 1) * TILE] = class_ref[rows]


def late_cut_block(me, restore, classes):
    return kernel_call(
        late_cut_kernel,
        1,
        [SCALAR, whole_spec(restore.shape), whole_spec(classes.shape)],
        whole_out((LATE_ROWS, B)),
        jax.ShapeDtypeStruct((LATE_ROWS, B), bf16),
        [],
        1000000,
    )(me, restore, classes)


def cut_block(me, *weights):
    shapes = [(FIRST_ROWS, B), (2 * PAIR_ROWS, B), (SPATIAL_ROWS, B)]
    return kernel_call(
        cut_kernel,
        1,
        [SCALAR] + [whole_spec(weight.shape) for weight in weights],
        [whole_out(shape) for shape in shapes],
        [jax.ShapeDtypeStruct(shape, bf16) for shape in shapes],
        [pltpu.VMEM((SMALL_ROWS, B), f32)],
        1000000,
    )(me, *weights)


def unpack_kernel(me_ref, first_ref, squeeze_out, weights_out, next_out, scale_out,
                  one_out, two_out, three_out, stem_out):
    squeeze_out[...] = first_ref[:, 0:64]
    wide = first_ref.shape[0]
    small = []
    for index in range(wide):
        mask = (me_ref[0] >> 2) ^ index
        entry = (mask & 1) * 4 + (mask >> 1)
        small.append(first_ref[entry, 64:].astype(f32))

    def joined(row, at, width, rows=1):
        return jnp.concatenate(
            [values[row : row + rows, at : at + width] for values in small], axis=1
        )

    own = B // wide
    next_out[...] = joined(16, 0, own, 9)
    scale_out[...] = joined(16, LANES, own, 9)
    one_out[0:1] = joined(26, 0, own)
    one_out[1:2] = joined(26, LANES, own)
    two_out[0:1] = joined(26, 2 * LANES, own)
    two_out[1:2] = joined(26, 3 * LANES, own)
    three_out[0:1] = joined(25, 0, TILE)
    three_out[1:2] = joined(25, TILE, TILE)
    for row in range(2):
        stem = joined(27, row * LANES, STEM // wide)
        stem_out[row : row + 1] = jnp.concatenate([stem] * STEM_SIDE, axis=1)
    columns = jnp.concatenate(
        [jnp.concatenate([values[0:8], values[8:16, 0:LANES]], axis=1) for values in small], axis=0
    )
    rows = columns.T
    place = lax.broadcasted_iota(jnp.int32, (LANES, STEM), 0)
    none = jnp.zeros((LANES, STEM), f32)
    for offset in range(WINDOW):
        top = offset * WINDOW * CHANNELS
        block = jnp.where(place < WINDOW * CHANNELS, rows[top : top + LANES], 0.0)
        weights_out[offset, 0:LANES] = jnp.concatenate([block, none], axis=1).astype(bf16)
        weights_out[offset, LANES:] = jnp.concatenate([none, block], axis=1).astype(bf16)


def unpack_block(me, first):
    shapes = [
        ((first.shape[0], 64, B), bf16), ((WINDOW, 2 * LANES, LANES), bf16), ((9, R), f32), ((9, R), f32), ((2, B), f32),
        ((2, B), f32), ((2, C), f32), ((2, STEM_LANES), f32),
    ]
    return kernel_call(
        unpack_kernel,
        1,
        [SCALAR, whole_spec(first.shape)],
        [whole_out(shape) for shape, _ in shapes],
        [jax.ShapeDtypeStruct(shape, kind) for shape, kind in shapes],
        [],
        1000000,
    )(me, first)


def shards(
    frames,
    tokens,
    stem_cotangent,
    crop_counts,
    labels,
    stem_weight,
    stem_gain,
    stem_shift,
    w_squeeze,
    next_kernel,
    scale_kernel,
    w_expand,
    w_reduce,
    gain_one,
    shift_one,
    w_spatial,
    gain_two,
    shift_two,
    w_restore,
    gain_three,
    shift_three,
    w_class,
    class_bias,
):
    view_count = frames.shape[0]
    row_count = tokens.shape[0]
    devices = lax.axis_size(AXES)
    wide = lax.axis_size("wide")
    narrow = lax.axis_size("narrow")
    count = float(row_count * devices)
    segments = view_count * SEG
    stem_rows_here = segments * STEM_SIDE
    stem_count = float(stem_rows_here * STEM_SIDE * devices)
    direct = wide == C // TILE and narrow == 4
    me = lax.axis_index(AXES)
    me_array = (me if direct else 0 * me).astype(jnp.int32).reshape(1)

    stem_width = stem_weight.shape[1]
    inner_width = gain_one.shape[0]
    outer_width = gain_three.shape[0]

    def by_segment(values):
        values = values.reshape(STEM_SIDE, segments, STEM_LANES)
        return values.transpose(1, 0, 2).reshape(-1, STEM)

    def by_output_row(values):
        values = values.reshape(segments, STEM_SIDE, STEM_LANES)
        return values.transpose(1, 0, 2).reshape(stem_rows_here, STEM_LANES)

    if direct:
        first_own, pair_own, spatial_own = cut_block(
            me_array, w_squeeze, w_expand, w_reduce, w_spatial, stem_weight.T, next_kernel,
            scale_kernel, jnp.concatenate([gain_three, shift_three])[None], gain_one[None],
            shift_one[None], gain_two[None], shift_two[None], stem_gain[None], stem_shift[None],
        )
        firsts, pairs, spatials = Gather(first_own), Gather(pair_own), HalvedGather(spatial_own)
        (inputs, select), came, _ = beside(
            lambda images: (frames_block(images), band_select()), [frames], firsts.depth()
        )
        firsts.take_depth(came)
        late_own, came, _ = beside(
            lambda mine, restore, classes: late_cut_block(
                mine, restore, jnp.pad(classes, ((0, 0), (0, TILE - CLASSES)))
            ),
            [me_array, w_restore, w_class], firsts.second() + pairs.depth(),
        )
        firsts.take_second(came[:1])
        pairs.take_depth(came[1:])
        (
            squeeze_own, weights, full_next, full_scale, affine_one, affine_two, affine_three, stem_affine,
        ) = unpack_block(me_array, firsts.eight)
        (stem_pre, stem_part), came, _ = beside(
            stem_block, [inputs, select, weights],
            [(squeeze_own, 2)] + pairs.second() + spatials.depth(),
        )
        squeeze_far = came[0]
        pairs.take_second(came[1:2])
        spatials.take_depth(came[2:])
        (stem_pre, late_own), came, _ = beside(
            lambda *values: values, [stem_pre, late_own], [(squeeze_own, 1), (squeeze_far, 1)]
        )
        late = lax.all_gather(late_own, AXES)
        squeeze = (squeeze_own, squeeze_far) + tuple(came)
    else:
        squeeze, pair, spatial, late = gathered(
            w_squeeze, w_expand, w_reduce, w_spatial, w_restore, w_class
        )

        def whole(values):
            return lax.all_gather(values, "wide", axis=values.ndim - 1, tiled=True).astype(f32)

        weights = pair_weights(whole(stem_weight).astype(bf16))
        full_next, full_scale = whole(next_kernel), whole(scale_kernel)
        affine_one = jnp.stack([whole(gain_one), whole(shift_one)])
        affine_two = jnp.stack([whole(gain_two), whole(shift_two)])
        affine_three = jnp.stack([whole(gain_three), whole(shift_three)])
        stem_affine = jnp.tile(jnp.stack([whole(stem_gain), whole(stem_shift)]), (1, STEM_SIDE))
        inputs, select, cotangent = frames_block(frames), band_select(), by_output_row(stem_cotangent)
        stem_pre, stem_part = stem_block(inputs, select, weights)
    stem_part = stem_part.reshape(2, STEM_SIDE, STEM).sum(1).reshape(1, 2 * STEM)

    def stem_lanes(sums):
        return jnp.tile(sums[2, : 2 * STEM].reshape(2, STEM), (1, STEM_SIDE))

    def with_row(sums, row):
        return jnp.concatenate([sums, jnp.pad(row, ((0, 0), (0, sums.shape[1] - row.shape[1])))])

    mixing_operands = [me_array, squeeze, tokens, full_next, full_scale]
    if direct:
        (upcoming, differ, mixed_low), came, _ = beside(
            mixing_block, mixing_operands, pairs.third() + spatials.second()
        )
        pairs.take_third(came[:1])
        spatials.take_second(came[1:])
        mixed_low, came, _ = beside(lambda values: values, [mixed_low], pairs.core())
        pairs.take_core(came)
        pair = pairs.arrays
    else:
        upcoming, differ, mixed_low = mixing_block(*mixing_operands)
    gate_operands = [me_array, pair, tokens, mixed_low]
    if direct:
        (logit, gated_low, pre_one, one_part), came, _ = beside(
            gate_block, gate_operands, spatials.third_of(0)
        )
        spatials.take_third_of(0, came)
        (one_sums, cotangent), came, _ = beside(
            lambda copies, grads: (swap_total(copies), by_output_row(grads)),
            [to_all(with_row(one_part, stem_part)), stem_cotangent],
            spatials.third_of(1) + spatials.core_of(0),
        )
        spatials.take_third_of(1, came[:1])
        spatials.take_core_of(0, came[1:])
        one_sums, came, _ = beside(lambda values: values, [one_sums], spatials.core_of(1))
        spatials.take_core_of(1, came)
        spatial = spatials.arrays
    else:
        logit, gated_low, pre_one, one_part = gate_block(*gate_operands)
        one_sums = swap_total(to_all(with_row(one_part, stem_part)))
    stem_sums = stem_lanes(one_sums)
    hidden_one, pre_two, two_part = second_block(
        me_array, spatial, pre_one, one_sums, affine_one, count
    )
    stem_out, stem_norm_grad, stem_part = stem_norm_block(
        stem_pre, stem_sums, stem_affine, cotangent, stem_count
    )
    stem_part = stem_part.reshape(2, STEM_SIDE, STEM).sum(1).reshape(1, 2 * STEM)
    two_sums = swap_total(two_part)
    hidden_two, pre_three, centres, three_part = third_block(pre_two, two_sums, affine_two, late, count)
    three_sums, (stem_features, select_turned) = total_beside(
        with_row(three_part, stem_part),
        lambda values: (by_segment(values).T, band_select(True)), [stem_out],
    )
    stem_features = stem_features.T
    stem_grads = stem_lanes(three_sums)
    bias = jnp.pad(class_bias.astype(f32), (0, TILE - CLASSES))[None]
    activations, slope, view_sums, view_logits, pooled_low = fourth_block(
        pre_three, centres, gated_low, three_sums, affine_three, late, bias, count
    )
    pooled_low = pooled_low[:view_count]

    ends = jnp.cumsum(crop_counts)
    starts = ends - crop_counts
    positions = (me - 1) * view_count + jnp.arange(3 * view_count, dtype=jnp.int32)
    video = jnp.sum((ends[None, :] <= positions[:, None]).astype(jnp.int32), 1)
    own_video = video[view_count : 2 * view_count]
    belongs = (
        own_video[:, None] == jnp.arange(crop_counts.shape[0], dtype=jnp.int32)[None, :]
    ).astype(jnp.int32)
    own_count = jnp.sum(belongs * crop_counts[None, :], 1).astype(f32)
    own_label = jnp.sum(belongs * labels[None, :], 1)
    own_start = jnp.sum(belongs * starts[None, :], 1)
    first = (own_start == positions[view_count : 2 * view_count]).astype(f32)
    same = (own_video[:, None] == video[None, :]).astype(f32) / own_count[:, None]
    target = (own_label[:, None] == jnp.arange(TILE, dtype=jnp.int32)[None, :]).astype(f32)
    marks = jnp.concatenate([same, 1.0 / own_count[:, None], first[:, None]], axis=1)
    marks = jnp.pad(marks, ((0, 8 - view_count), (0, LANES - marks.shape[1])))
    target = jnp.pad(target, ((0, 8 - view_count), (0, 0)))

    before = lax.ppermute(view_logits, AXES, [(i, i + 1) for i in range(devices - 1)])
    following = lax.ppermute(view_logits, AXES, [(i + 1, i) for i in range(devices - 1)])
    three_part, pooled_grad, view_grad_low = video_block(
        before, view_logits, following, marks, target, view_sums, late, view_count
    )
    view_grad_low = view_grad_low[:view_count]

    own_parts = pooled_low.reshape(view_count, wide, outer_width).swapaxes(0, 1)
    grad_parts = jnp.broadcast_to(
        view_grad_low, (wide, view_count, TILE)
    )
    factors = jnp.concatenate([own_parts, grad_parts], axis=2)
    factors = jnp.broadcast_to(factors[:, None], (wide, narrow) + factors.shape[1:])
    factors = factors.reshape((devices,) + factors.shape[2:])
    factors = jnp.pad(factors, ((0, 0), (0, 0), (0, B - factors.shape[2])))

    three_grads = total(three_part)
    class_bias_grad = three_grads[2, :CLASSES]
    loss = three_grads[2, CLASSES] / crop_counts.shape[0]

    fifth_operands = [
        slope, pre_three, centres, pooled_grad, three_sums, affine_three, three_grads, late,
        pre_two, two_sums, affine_two,
    ]
    run_fifth = functools.partial(fifth_block, count=count)
    run_sixth = functools.partial(sixth_block, count=count)
    run_stem_back = functools.partial(stem_back_block, count=stem_count)

    def stem_back_operands():
        return [
            inputs, select_turned, stem_pre, stem_sums, stem_affine, stem_norm_grad, stem_grads,
            kernel_grads,
        ]
    run_outer = outer_block_of(R // 4)

    def sixth_operands():
        return [
            me_array, spatial, norm_two_grad, pre_two, two_sums, affine_two, two_grads, pre_one,
            one_sums, affine_one, factors,
        ]

    def low_operands():
        return [me_array, norm_one_grad, pre_one, one_sums, affine_one, one_grads, gated_low]

    def gate_back_operands():
        return [me_array, pair, low_one, slope, pooled_grad, tokens, logit]

    def mixing_back_operands():
        return [me_array, pair, logit_grad, upcoming, differ, full_next, full_scale]

    if direct:
        low_three, norm_two_grad, two_part = run_fifth(*fifth_operands)
        (buffers, two_grads), _, _ = beside(
            lambda mine, hidden, low, part: (
                restore_outer_block(mine, hidden, low), swap_total(part)
            ),
            [me_array, hidden_two, low_three, two_part], [],
        )
        low_two, norm_one_grad, one_part = run_sixth(*sixth_operands())
        ((keep, send), one_grads), _, _ = beside(
            lambda mine, shared, hidden, low, part: (
                spatial_block(mine, shared, hidden, low), swap(part)
            ),
            [me_array, buffers, hidden_one, low_two, one_part], [],
        )
        one_grads, factors = apart(one_grads)
        quarter = (4, 2, 2, R // 4, TILE)
        (low_one, reduce_half), came, _ = beside(
            functools.partial(low_outer_block, count=count), low_operands(), [(send, 1)]
        )
        buffer = add_block(keep, came[0])
        reduced_sum = Sum(reduce_half, quarter, 0)
        (low_one, buffer), came, _ = beside(
            lambda *values: values, [low_one, buffer], reduced_sum.core()
        )
        buffer = lax.psum_scatter(
            buffer.reshape(8, -1, WIDE), "wide", scatter_dimension=0, tiled=False
        )
        reduced_sum.take_core(came)
        (logit_grad, tokens_part), came, _ = beside(
            gate_back_block, gate_back_operands(), reduced_sum.split("x")
        )
        reduced_sum.take(came)
        expand_half, came, _ = beside(
            run_outer, [me_array, mixed_low, logit_grad], reduced_sum.split("y")
        )
        reduced_sum.take(came)
        expand_sum = Sum(expand_half, quarter, 0)
        logit_grad, came, _ = beside(lambda values: values, [logit_grad], expand_sum.core())
        expand_sum.take_core(came)
        (low_squeezed, kernel_grads), came, _ = beside(
            mixing_back_block, mixing_back_operands(),
            expand_sum.split("x"),
        )
        expand_sum.take(came)
        squeeze_half, came, _ = beside(
            run_outer, [me_array, low_squeezed, tokens],
            expand_sum.split("y"),
        )
        expand_sum.take(came)
        both_sum = Sum((None, None), (), 1)
        both_sum.axes = "z"
        both_sum.values = jnp.stack([reduced_sum.values, expand_sum.values])
        shared = Sum((None, None), (), 0)
        shared.axes = "x"
        shared.values = buffer.reshape(2, -1, WIDE)
        squeezed = Sum(squeeze_half, quarter, 0)
        tokens_part, came, _ = beside(lambda values: values, [tokens_part], squeezed.core())
        squeezed.take_core(came)
        stem_back, came, _ = beside(
            run_stem_back, stem_back_operands(),
            squeezed.split("x") + both_sum.split("z") + shared.split("x"),
        )
        squeezed.take(came[:1])
        both_sum.take(came[1:4])
        shared.take(came[4:])
        few = Sum((None, None), (), 0)
        few.axes = "zy"
        few.values = stem_back.reshape(4, 2, FEW_ROWS, TILE)
        tokens_grad, came, _ = beside(
            tokens_block, [me_array, squeeze, tokens_part, low_squeezed],
            squeezed.split("y") + few.split("y") + both_sum.spread(),
        )
        squeezed.take(came[:1])
        few.take(came[1:2])
        both_sum.take_spread(came[2:])
        squeezed.values = jnp.concatenate([squeezed.values, few.values], axis=1)
        _, came, _ = beside(lambda: None, [], squeezed.split("z") + shared.spread())
        squeezed.take(came[:3])
        shared.take_spread(came[3:])
        last = Sum((None, None), (), 0)
        last.values = squeezed.values.astype(bf16)
        _, came, _ = beside(lambda: None, [], last.spread())
        last.take_spread(came)
        squeezed.whole = last.whole[:, : R // 4]
        few = jnp.sum(last.whole[:, R // 4 :], 0)
        buffer = shared.whole
        sum_stem = few[:24].reshape(3, 8, TILE).swapaxes(0, 1).reshape(8, 3 * TILE)
        sum_stem = sum_stem[:, : stem_weight.shape[0]].T
        sum_next = few[24:33, :inner_width]
        sum_scale = few[24:33, LANES : LANES + inner_width]
        buffer = buffer.reshape(4, SHARED, 16, WIDE)
        sum_restore = buffer[:, :GROUPS].swapaxes(1, 2).reshape(w_restore.shape)
        sum_spatial = buffer[:, GROUPS:].swapaxes(0, 1)
        sum_spatial = sum_spatial.reshape(w_spatial.shape)
        sum_reduce = both_sum.whole[:, 0].reshape(B, TILE).T
        sum_expand = both_sum.whole[:, 1].reshape(R, TILE)
        sum_squeeze = squeezed.whole.reshape(R, TILE).T
    else:
        low_three, norm_two_grad, two_part = run_fifth(*fifth_operands)
        buffers = restore_outer_block(me_array, hidden_two, low_three)
        two_grads = swap_total(two_part)
        low_two, norm_one_grad, one_part = run_sixth(*sixth_operands())
        one_grads, factors = apart(swap(one_part))
        buffers = spatial_block(me_array, buffers, hidden_one, low_two)
        low_one, reduce_half = low_outer_block(*low_operands(), count)
        logit_grad, tokens_part = gate_back_block(*gate_back_operands())
        expand_half = run_outer(me_array, mixed_low, logit_grad)
        low_squeezed, kernel_grads = mixing_back_block(*mixing_back_operands())
        few = run_stem_back(*stem_back_operands())
        squeeze_half = run_outer(me_array, low_squeezed, tokens)
        tokens_grad = tokens_block(me_array, squeeze, tokens_part, low_squeezed)
        few = lax.psum(few, AXES)
        sum_stem = few[:, :24].reshape(8, 3, 8, TILE).swapaxes(1, 2).reshape(STEM, 3 * TILE)
        sum_stem = sum_stem[:, : stem_weight.shape[0]].T
        sum_next, sum_scale = (
            few[:, 24:33, at : at + R // 8].swapaxes(0, 1).reshape(9, R) for at in (0, LANES)
        )

        def own_columns(values, width):
            return lax.dynamic_slice_in_dim(values, lax.axis_index("wide") * width, width, 1)

        sum_stem = own_columns(sum_stem, stem_width)
        sum_next = own_columns(sum_next, inner_width)
        sum_scale = own_columns(sum_scale, inner_width)
        sum_restore, sum_spatial, sum_reduce, sum_expand, sum_squeeze = reduced(
            buffers, reduce_half, expand_half, squeeze_half
        )
    factors = factors.reshape(devices * view_count, B)
    sum_class = product_left(
        factors[:, :outer_width], factors[:, outer_width : outer_width + CLASSES]
    )

    def own_slice(values, width):
        return lax.dynamic_slice_in_dim(values, lax.axis_index("wide") * width, width)

    return (
        activations,
        stem_features,
        tokens_grad,
        sum_stem,
        own_slice(stem_grads[1, :STEM], stem_width),
        own_slice(stem_grads[0, :STEM], stem_width),
        sum_squeeze,
        sum_next,
        sum_scale,
        sum_expand,
        sum_reduce,
        own_slice(one_grads[1], inner_width),
        own_slice(one_grads[0], inner_width),
        sum_spatial,
        own_slice(two_grads[1], inner_width),
        own_slice(two_grads[0], inner_width),
        sum_restore,
        own_slice(three_grads[1], outer_width),
        own_slice(three_grads[0], outer_width),
        sum_class,
        class_bias_grad,
        loss,
    )


def solution(mesh):
    in_specs = (
        P(("wide", "narrow"), None, None, None, None, None),
        P(("wide", "narrow"), None),
        P(("wide", "narrow"), None),
        P(),
        P(),
        P(None, "wide"),
        P("wide"),
        P("wide"),
        P("wide", None),
        P(None, "wide"),
        P(None, "wide"),
        P(None, "wide"),
        P("wide", None),
        P("wide"),
        P("wide"),
        P(None, "wide", None),
        P("wide"),
        P("wide"),
        P("wide", None),
        P("wide"),
        P("wide"),
        P("wide", None),
        P(),
    )
    out_specs = (
        P(("wide", "narrow"), None),
        P(("wide", "narrow"), None),
        P(("wide", "narrow"), None),
        P(None, "wide"),
        P("wide"),
        P("wide"),
        P("wide", None),
        P(None, "wide"),
        P(None, "wide"),
        P(None, "wide"),
        P("wide", None),
        P("wide"),
        P("wide"),
        P(None, "wide", None),
        P("wide"),
        P("wide"),
        P("wide", None),
        P("wide"),
        P("wide"),
        P("wide", None),
        P(),
        P(),
    )
    return jax.shard_map(shards, mesh=mesh, in_specs=in_specs, out_specs=out_specs, check_vma=False)
```
